32 devices in a mesh: dp: 16 (over z, y, x), seq: 2 (over core).
Axes of the slice: x: 2, y: 2, z: 4, core: 2. Of those that a mesh axis runs over, the one named last changes fastest.
Arguments:
- labels: int32 [32], P('dp'), may hold values from 0 to 1000
- targets: int32 [32, 256], P('dp', 'seq'), may hold values from 0 to 16383
- heights: int32 [32], P('dp'), may hold values from 8 to 16, as said below
- loss_mask: int32 [32, 256], P('dp', 'seq'), may hold values from 0 to 1
- class_table: float32 [1001, 768], P(None, ('dp', 'seq')), may hold values from -1.8 to 1.8
- code_table: float32 [16384, 768], P(('dp', 'seq')), may hold values from -1.8 to 1.8
- attend_in: float32 [768, 2304], P(('dp', 'seq')), may hold values from -0.21875 to 0.21875
- attend_mix: float32 [768, 768], P(('dp', 'seq')), may hold values from -0.625 to 0.625
- expand_in: float32 [768, 4096], P(('dp', 'seq')), may hold values from -0.21875 to 0.21875
- shrink_out: float32 [2048, 768], P(('dp', 'seq')), may hold values from -0.125 to 0.125
- head_weight: float32 [768, 16384], P(None, ('dp', 'seq')), may hold values from -0.21875 to 0.21875
- norm_gains: float32 [3, 768], P(None, ('dp', 'seq')), may hold values from 0.34 to 2.3
- drift_class: float32 [1001, 768], P(None, ('dp', 'seq')), may hold values from -1.1920929e-07 to 1.1920929e-07
- drift_code: float32 [16384, 768], P(('dp', 'seq')), may hold values from -2.9802322e-07 to 2.9802322e-07
- drift_attend: float32 [768, 2304], P(('dp', 'seq')), may hold values from -2.861023e-06 to 2.861023e-06
- drift_mix: float32 [768, 768], P(('dp', 'seq')), may hold values from -2.861023e-06 to 2.861023e-06
- drift_expand: float32 [768, 4096], P(('dp', 'seq')), may hold values from -2.861023e-06 to 2.861023e-06
- drift_shrink: float32 [2048, 768], P(('dp', 'seq')), may hold values from -2.861023e-06 to 2.861023e-06
- drift_head: float32 [768, 16384], P(None, ('dp', 'seq')), may hold values from -2.861023e-06 to 2.861023e-06
- drift_gains: float32 [3, 768], P(None, ('dp', 'seq')), may hold values from -1.1444092e-05 to 1.1444092e-05
- square_class: float32 [1001, 768], P(None, ('dp', 'seq')), may hold values from 1.4031683e-16 to 1.1204005e-15
- square_code: float32 [16384, 768], P(('dp', 'seq')), may hold values from 7.942518e-16 to 6.3419343e-15
- square_attend: float32 [768, 2304], P(('dp', 'seq')), may hold values from 7.966128e-14 to 1.2721573e-12
- square_mix: float32 [768, 768], P(('dp', 'seq')), may hold values from 7.966128e-14 to 1.2721573e-12
- square_expand: float32 [768, 4096], P(('dp', 'seq')), may hold values from 7.966128e-14 to 1.2721573e-12
- square_shrink: float32 [2048, 768], P(('dp', 'seq')), may hold values from 7.966128e-14 to 1.2721573e-12
- square_head: float32 [768, 16384], P(None, ('dp', 'seq')), may hold values from 7.966128e-14 to 1.2721573e-12
- square_gains: float32 [3, 768], P(None, ('dp', 'seq')), may hold values from 1.2721573e-12 to 2.0293938e-11
Outputs:
- class_new: float32 [1001, 768], P(None, ('dp', 'seq'))
- code_new: float32 [16384, 768], P(('dp', 'seq'))
- attend_new: float32 [768, 2304], P(('dp', 'seq'))
- mix_new: float32 [768, 768], P(('dp', 'seq'))
- expand_new: float32 [768, 4096], P(('dp', 'seq'))
- shrink_new: float32 [2048, 768], P(('dp', 'seq'))
- head_new: float32 [768, 16384], P(None, ('dp', 'seq'))
- gains_new: float32 [3, 768], P(None, ('dp', 'seq'))
- momentum_class: float32 [1001, 768], P(None, ('dp', 'seq'))
- momentum_code: float32 [16384, 768], P(('dp', 'seq'))
- momentum_attend: float32 [768, 2304], P(('dp', 'seq'))
- momentum_mix: float32 [768, 768], P(('dp', 'seq'))
- momentum_expand: float32 [768, 4096], P(('dp', 'seq'))
- momentum_shrink: float32 [2048, 768], P(('dp', 'seq'))
- momentum_head: float32 [768, 16384], P(None, ('dp', 'seq'))
- momentum_gains: float32 [3, 768], P(None, ('dp', 'seq'))
- variance_class: float32 [1001, 768], P(None, ('dp', 'seq'))
- variance_code: float32 [16384, 768], P(('dp', 'seq'))
- variance_attend: float32 [768, 2304], P(('dp', 'seq'))
- variance_mix: float32 [768, 768], P(('dp', 'seq'))
- variance_expand: float32 [768, 4096], P(('dp', 'seq'))
- variance_shrink: float32 [2048, 768], P(('dp', 'seq'))
- variance_head: float32 [768, 16384], P(None, ('dp', 'seq'))
- variance_gains: float32 [3, 768], P(None, ('dp', 'seq'))
- grad_norm: float32 [], replicated
- loss_sum: float32 [], replicated
- loss_count: float32 [], replicated
The draws below stay inside these ranges and needn't reach their ends.
Inputs may be any that keep to these rules, and one draw needn't show every extreme that they name: `heights`: in each aligned block of 2 images (those of one index of dp) at least one image has 16 rows.
All inputs are finite; a program needn't handle non-finite values.
Results may differ from the reference program's by a relative error of at most 0.02.
The reference program's roundings to bfloat16 on the way count: a program that leaves them out, or rounds other values in their place, can miss the bound.
Values may be sent and summed in bfloat16 or wider, within the bound.
A program may use at most 320 MiB of HBM per device.

```python
import math
import jax
import jax.numpy as jnp
import numpy as np
from jax import lax

D = 768
HEADS = 12
HD = 64
FF = 2048
V = 16384
CLASSES = 1001
GRID = 16
HMAX = 16
HMIN = 8
STEP = 10
IMG_DEV = 2
L = 256
IMAGES = 32
PARAMS = 33014784


def draw_heights(key, part):
    key = jax.random.fold_in(key, 11)
    key_pick, key_full = jax.random.split(key)
    blocks = IMAGES // IMG_DEV
    block = jnp.arange(IMAGES) // IMG_DEV
    span = (HMAX - HMIN) * (block + 1) // blocks
    pick = jax.random.randint(key_pick, (IMAGES,), 0, 1 << 20) % (span + 1)
    chosen = jax.random.randint(key_full, (blocks,), 0, IMG_DEV)
    forced = jnp.arange(IMAGES) % IMG_DEV == chosen[block]
    return jnp.where(forced, HMAX, HMIN + pick).astype(jnp.int32)


def draw_loss_mask(key, part):
    key = jax.random.fold_in(key, 12)
    blocks = IMAGES // IMG_DEV
    block = jnp.arange(IMAGES) // IMG_DEV
    rate_block = 250 + 750 * block // max(blocks - 1, 1)
    rate_place = 400 + 600 * jnp.arange(L) // (L - 1)
    rate = rate_block[:, None] * rate_place[None, :] // 1000
    ticket = jax.random.randint(key, (IMAGES, L), 0, 1000)
    return (ticket < rate).astype(jnp.int32)


def draw_norm_gains(key, part):
    key = jax.random.fold_in(key, 13)
    ramp = jnp.arange(D, dtype=jnp.float32) / (D - 1)
    lower, upper = (0.6, 1.8)
    jitter = jax.random.uniform(key, (3, D), jnp.float32, 0.85, 1.15)
    return (lower + (upper - lower) * ramp)[None, :] * jitter


def set_ends(result, key, least, top_value):
    extent = result.shape
    spot = [jax.random.randint(jax.random.fold_in(key, axis), (), 0, extent[axis]) for axis in range(len(extent))]
    result = result.at[tuple(spot)].set(least)
    longest = extent.index(max(extent))
    spot[longest] = (spot[longest] + 1) % extent[longest]
    return result.at[tuple(spot)].set(top_value)


def block_levels(key, dims, shards, least, high):
    def one(axis_at, shards_of):
        draws = jax.random.uniform(jax.random.fold_in(jax.random.fold_in(key, 6), axis_at), (shards_of,), jnp.float32, least / len(shards), high / len(shards))
        return jnp.repeat(jnp.exp(draws), dims[axis_at] // shards_of).reshape((-1,) + (1,) * (len(dims) - axis_at - 1))

    level = one(*shards[0])
    for cut in shards[1:]:
        level = level * one(*cut)
    return level


def cumulative_ranks(count, slope):
    loads = [(1 << 20) // math.isqrt(grade ** slope) + 1 for grade in range(1, count + 1)]
    spread = 1 + sum(loads) // (1 << 30)
    return np.cumsum(np.array([max(1, weight // spread) for weight in loads]))


def skewed_ids(own_key, extent, amount, slope):
    listing = cumulative_ranks(amount, slope)
    lot = jax.random.randint(jax.random.fold_in(own_key, 1), extent, 0, int(listing[amount - 1]))
    grade = jnp.searchsorted(jnp.asarray(listing, jnp.int32), lot, side="right")
    return jax.random.permutation(jax.random.fold_in(own_key, 2), amount)[grade].astype(jnp.int32)


def gaussian(stream_key, extent, scale, bound, pieces=(), held_as=jnp.bfloat16):
    array = scale * jax.random.normal(stream_key, extent, jnp.float32)
    if pieces:
        array = array * block_levels(stream_key, extent, pieces, -0.22, 0.18)
    return jnp.clip(array, -bound, bound).astype(held_as)


def setup_inputs(seed: int = 0) -> dict:
    seeds = jax.random.split(jax.random.key(seed), 29)
    return {
        "labels": set_ends(jax.random.randint(seeds[0], (IMAGES,), 0, CLASSES), jax.random.fold_in(seeds[0], 1), 0, CLASSES - 1).astype(jnp.int32),
        "targets": set_ends(skewed_ids(seeds[1], (IMAGES, L), V, 1), jax.random.fold_in(seeds[1], 3), 0, V - 1).astype(jnp.int32),
        "heights": draw_heights(jax.random.fold_in(seeds[28], 71), 0),
        "loss_mask": draw_loss_mask(jax.random.fold_in(seeds[28], 71), 0),
        "class_table": gaussian(seeds[4], (CLASSES, D), 0.3, 1.8, ((1, 32),), jnp.float32),
        "code_table": gaussian(seeds[5], (V, D), 0.3, 1.8, ((0, 32),), jnp.float32),
        "attend_in": gaussian(seeds[6], (D, 3 * D), D ** -0.5, 0.21875, ((0, 32),), jnp.float32),
        "attend_mix": gaussian(seeds[7], (D, D), (D // 8) ** -0.5, 0.625, ((0, 32),), jnp.float32),
        "expand_in": gaussian(seeds[8], (D, 2 * FF), D ** -0.5, 0.21875, ((0, 32),), jnp.float32),
        "shrink_out": gaussian(seeds[9], (FF, D), FF ** -0.5, 0.125, ((0, 32),), jnp.float32),
        "head_weight": gaussian(seeds[10], (D, V), D ** -0.5, 0.21875, ((1, 32),), jnp.float32),
        "norm_gains": draw_norm_gains(jax.random.fold_in(seeds[28], 71), 0),
        "drift_class": gaussian(seeds[12], (CLASSES, D), (0.00111 * (0.0105 / (CLASSES * D * L)) ** 0.5), 1.1920928955078125e-07, ((1, 32),), jnp.float32),
        "drift_code": gaussian(seeds[13], (V, D), (0.00111 * (0.0038 / (V * D)) ** 0.5), 2.980232238769531e-07, ((0, 32),), jnp.float32),
        "drift_attend": gaussian(seeds[14], (D, 3 * D), (0.111 * 0.01 / PARAMS ** 0.5), 2.86102294921875e-06, ((0, 32),), jnp.float32),
        "drift_mix": gaussian(seeds[15], (D, D), (0.111 * 0.01 / PARAMS ** 0.5), 2.86102294921875e-06, ((0, 32),), jnp.float32),
        "drift_expand": gaussian(seeds[16], (D, 2 * FF), (0.111 * 0.01 / PARAMS ** 0.5), 2.86102294921875e-06, ((0, 32),), jnp.float32),
        "drift_shrink": gaussian(seeds[17], (FF, D), (0.111 * 0.01 / PARAMS ** 0.5), 2.86102294921875e-06, ((0, 32),), jnp.float32),
        "drift_head": gaussian(seeds[18], (D, V), (0.111 * 0.01 / PARAMS ** 0.5), 2.86102294921875e-06, ((1, 32),), jnp.float32),
        "drift_gains": gaussian(seeds[19], (3, D), (0.444 * 0.01 / PARAMS ** 0.5), 1.1444091796875e-05, ((1, 32),), jnp.float32),
        "square_class": jnp.clip(jnp.exp(math.log(1.1204005490028906e-15) - 2.0775386 * jax.random.uniform(seeds[20], (CLASSES, D), jnp.float32) ** block_levels(seeds[20], (CLASSES, D), ((1, 32),), -0.2, 0.2)), 1.4031683106418722e-16, 1.1204005490028906e-15),
        "square_code": jnp.clip(jnp.exp(math.log(6.341934305319078e-15) - 2.0775386 * jax.random.uniform(seeds[21], (V, D), jnp.float32) ** block_levels(seeds[21], (V, D), ((0, 32),), -0.2, 0.2)), 7.942517832120431e-16, 6.341934305319078e-15),
        "square_attend": jnp.clip(jnp.exp(math.log(1.2721572927032465e-12) - 2.7706857 * jax.random.uniform(seeds[22], (D, 3 * D), jnp.float32) ** block_levels(seeds[22], (D, 3 * D), ((0, 32),), -0.2, 0.2)), 7.966128028492198e-14, 1.2721572927032465e-12),
        "square_mix": jnp.clip(jnp.exp(math.log(1.2721572927032465e-12) - 2.7706857 * jax.random.uniform(seeds[23], (D, D), jnp.float32) ** block_levels(seeds[23], (D, D), ((0, 32),), -0.2, 0.2)), 7.966128028492198e-14, 1.2721572927032465e-12),
        "square_expand": jnp.clip(jnp.exp(math.log(1.2721572927032465e-12) - 2.7706857 * jax.random.uniform(seeds[24], (D, 2 * FF), jnp.float32) ** block_levels(seeds[24], (D, 2 * FF), ((0, 32),), -0.2, 0.2)), 7.966128028492198e-14, 1.2721572927032465e-12),
        "square_shrink": jnp.clip(jnp.exp(math.log(1.2721572927032465e-12) - 2.7706857 * jax.random.uniform(seeds[25], (FF, D), jnp.float32) ** block_levels(seeds[25], (FF, D), ((0, 32),), -0.2, 0.2)), 7.966128028492198e-14, 1.2721572927032465e-12),
        "square_head": jnp.clip(jnp.exp(math.log(1.2721572927032465e-12) - 2.7706857 * jax.random.uniform(seeds[26], (D, V), jnp.float32) ** block_levels(seeds[26], (D, V), ((1, 32),), -0.2, 0.2)), 7.966128028492198e-14, 1.2721572927032465e-12),
        "square_gains": jnp.clip(jnp.exp(math.log(2.0293938404747358e-11) - 2.769608 * jax.random.uniform(seeds[27], (3, D), jnp.float32) ** block_levels(seeds[27], (3, D), ((1, 32),), -0.2, 0.2)), 1.2721572927032465e-12, 2.0293938404747358e-11),
    }


@jax.custom_vjp
def low(v):
    return lax.optimization_barrier(v.astype(jnp.bfloat16)).astype(jnp.float32)

@jax.custom_vjp
def low_back(v):
    return v

def low_keep(v):
    return (low(v), None)

def low_pass(kept, grad):
    return (grad,)

def back_keep(v):
    return (v, None)

def back_low(kept, grad):
    return (low(grad),)
low.defvjp(low_keep, low_pass)
low_back.defvjp(back_keep, back_low)
EPS_NORM = 1e-05
BETA_ONE = 0.9
BETA_TWO = 0.95
ADAM_EPS = 1e-08
CLIP_NORM = 0.01
NEGATIVE_FILL = -1000000000.0
FULL_PRECISION = lax.Precision.HIGHEST
RATES = (0.8, 0.8, 0.08, 0.08, 0.08, 0.08, 0.08, 0.8)
DECAYS = (0.1, 0.1, 0.1, 0.1, 0.1, 0.1, 0.1, 0.0)

def matmul(left, right):
    return jnp.dot(left, right, precision=FULL_PRECISION, preferred_element_type=jnp.float32)

def rms_gain(values, gain):
    return values * lax.rsqrt(lax.optimization_barrier(jnp.mean(values * values, axis=-1, keepdims=True)) + EPS_NORM) * gain

def turn_half(tensor):
    quarter = tensor.shape[-1] // 4
    return jnp.concatenate([-tensor[..., quarter:2 * quarter], tensor[..., :quarter], -tensor[..., 3 * quarter:], tensor[..., 2 * quarter:3 * quarter]], axis=-1)

def rope_tables(positions, width):
    quarter = width // 4
    freq = 10000.0 ** (-jnp.arange(quarter, dtype=jnp.float32) / quarter)
    row_angle = (positions // GRID).astype(jnp.float32)[:, None] * freq
    col_angle = (positions % GRID).astype(jnp.float32)[:, None] * freq
    angles = jnp.concatenate([row_angle, row_angle, col_angle, col_angle], axis=-1)
    return (jnp.cos(angles), jnp.sin(angles))

def rotate(tensor, cosine, sine):
    return tensor * cosine[None, :, None, :] + turn_half(tensor) * sine[None, :, None, :]

def group_loss(masters, labels, targets, heights, loss_mask):
    class_w, code_w, qkv_w, mix_w, expand_w, shrink_w, head_w, gain_w = [low(member) for member in masters]
    images = targets.shape[0]
    places = jnp.arange(L)
    codes = jnp.concatenate([jnp.zeros((images, 1), jnp.int32), targets[:, :L - 1]], axis=1)
    start = jnp.where((places == 0)[None, :, None], class_w[labels][:, None, :], code_w[codes])
    start = start.reshape(images * L, D)
    normed_one = low(rms_gain(start, gain_w[0]))
    mixed = low_back(matmul(normed_one, qkv_w)).reshape(images, L, 3, HEADS, HD)
    cosine, sine = rope_tables(places, HD)
    query = low_back(low(rotate(mixed[:, :, 0], cosine, sine)))
    keys = low_back(low(rotate(mixed[:, :, 1], cosine, sine)))
    values = low_back(low(mixed[:, :, 2]))
    scores = low_back(jnp.einsum('bqhd,bkhd->bhqk', query, keys, precision=FULL_PRECISION) * HD ** (-0.5))
    lengths = GRID * heights
    allowed = (places[None, :] <= places[:, None])[None, None] & (places[None, :] < lengths[:, None])[:, None, None, :]
    scores = jnp.where(allowed, scores, NEGATIVE_FILL)
    score_peak = lax.optimization_barrier(jnp.max(scores, axis=-1, keepdims=True))
    exponent = jnp.exp(scores - score_peak)
    probs = low(exponent / lax.optimization_barrier(jnp.sum(exponent, axis=-1, keepdims=True)))
    attended = jnp.einsum('bhqk,bkhd->bqhd', probs, values, precision=FULL_PRECISION)
    attended = low_back(low(attended)).reshape(images * L, D)
    middle = start + low_back(matmul(attended, mix_w))
    normed_two = low(rms_gain(middle, gain_w[1]))
    both = low_back(matmul(normed_two, expand_w))
    hidden = low(jax.nn.silu(both[:, :FF]) * both[:, FF:])
    final = middle + low_back(matmul(hidden, shrink_w))
    normed_top = low(rms_gain(final, gain_w[2]))
    logits = low_back(matmul(normed_top, head_w))
    logit_peak = lax.optimization_barrier(jnp.max(logits, axis=1, keepdims=True))
    log_total = logit_peak[:, 0] + jnp.log(lax.optimization_barrier(jnp.sum(jnp.exp(logits - logit_peak), axis=1)))
    picked = jnp.take_along_axis(logits, targets.reshape(-1, 1), axis=1)[:, 0]
    counted = (loss_mask * (places[None, :] < lengths[:, None])).astype(jnp.float32).reshape(-1)
    return jnp.sum((log_total - picked) * counted)

def adam_update(master, drift, square, grad, rate, decay):
    moment = BETA_ONE * drift + (1.0 - BETA_ONE) * grad
    second = BETA_TWO * square + (1.0 - BETA_TWO) * grad * grad
    stride = moment / (1.0 - BETA_ONE ** STEP) / (jnp.sqrt(second / (1.0 - BETA_TWO ** STEP)) + ADAM_EPS)
    return (master - rate * (stride + decay * master), moment, second)

def reference(labels, targets, heights, loss_mask, class_table, code_table, attend_in, attend_mix, expand_in, shrink_out, head_weight, norm_gains, drift_class, drift_code, drift_attend, drift_mix, drift_expand, drift_shrink, drift_head, drift_gains, square_class, square_code, square_attend, square_mix, square_expand, square_shrink, square_head, square_gains):
    masters = (class_table, code_table, attend_in, attend_mix, expand_in, shrink_out, head_weight, norm_gains)
    drifts = (drift_class, drift_code, drift_attend, drift_mix, drift_expand, drift_shrink, drift_head, drift_gains)
    squares = (square_class, square_code, square_attend, square_mix, square_expand, square_shrink, square_head, square_gains)
    groups = IMAGES // IMG_DEV
    batches = (labels.reshape(groups, IMG_DEV), targets.reshape(groups, IMG_DEV, L), heights.reshape(groups, IMG_DEV), loss_mask.reshape(groups, IMG_DEV, L))

    def group_step(carry, batch):
        lab, tgt, hgt, msk = batch
        value, pull = jax.vjp(lambda *weights: group_loss(weights, lab, tgt, hgt, msk), *masters)
        grads = pull(jnp.ones((), value.dtype))
        counted = jnp.sum((msk * (jnp.arange(L)[None, :] < GRID * hgt[:, None])).astype(value.dtype))
        summed = tuple((before + after for before, after in zip(carry[0], grads)))
        return ((summed, carry[1] + value, carry[2] + counted), None)
    zero = jnp.zeros((), class_table.dtype)
    start = (tuple((jnp.zeros_like(member) for member in masters)), zero, zero)
    (grads, loss_total, loss_count), _ = lax.scan(group_step, start, batches)
    grads = [member / loss_count for member in grads]
    grad_norm = jnp.sqrt(sum((jnp.sum(member * member) for member in grads)))
    factor = CLIP_NORM / jnp.maximum(grad_norm, CLIP_NORM)
    news, firsts, seconds = ([], [], [])
    for member in range(8):
        fresh, moment, second = adam_update(masters[member], drifts[member], squares[member], grads[member] * factor, RATES[member], DECAYS[member])
        news.append(fresh)
        firsts.append(moment)
        seconds.append(second)
    return (news[0], news[1], news[2], news[3], news[4], news[5], news[6], news[7], firsts[0], firsts[1], firsts[2], firsts[3], firsts[4], firsts[5], firsts[6], firsts[7], seconds[0], seconds[1], seconds[2], seconds[3], seconds[4], seconds[5], seconds[6], seconds[7], grad_norm, loss_total, loss_count)
```

```python
import functools

import jax
import jax.numpy as jnp
from jax import lax
from jax.experimental import pallas as pl
from jax.experimental.pallas import tpu as pltpu
from jax.sharding import PartitionSpec as P

HD = 64
GRID = 16
STEP = 10

EPS_NORM = 1e-05
BETA_ONE = 0.9
BETA_TWO = 0.95
ADAM_EPS = 1e-08
CLIP_NORM = 0.01
NEGATIVE_FILL = -1000000000.0
RATES = (0.8, 0.8, 0.08, 0.08, 0.08, 0.08, 0.08, 0.8)
DECAYS = (0.1, 0.1, 0.1, 0.1, 0.1, 0.1, 0.1, 0.0)

MESH = pl.DeviceIdType.MESH
ANY = pl.BlockSpec(memory_space=pl.ANY)
VMEM = pl.BlockSpec(memory_space=pltpu.VMEM)
BF = jnp.bfloat16
F32 = jnp.float32


def dims_of(dp):
    bits = dp.bit_length() - 1
    nz = 1 << (bits // 2)
    rest = dp // nz
    ny = 1 << ((rest.bit_length() - 1) // 2)
    return (nz, ny, rest // ny)


class Place:
    def __init__(self, dims):
        self.dims = dims
        nz, ny, nx = dims
        chip = lax.axis_index("dp")
        self.c = lax.axis_index("seq")
        self.z = chip // (ny * nx)
        self.y = (chip // nx) % ny
        self.x = chip % nx

    def zs(self, back):
        return (self.z + self.dims[0] - back) % self.dims[0]

    def ys(self, back):
        return (self.y + self.dims[1] - back) % self.dims[1]

    def xs(self, back):
        return (self.x + self.dims[2] - back) % self.dims[2]

    def dev(self, z=0, y=0, x=0, c=0):
        nz, ny, nx = self.dims
        z, y, x = ((self.z + z) % nz, (self.y + y) % ny, (self.x + x) % nx)
        return ((z * ny + y) * nx + x, (self.c + c) % 2)


def line_offsets(dims):
    nz, ny, nx = dims
    return (
        [(s, 0, 0, 0) for s in range(1, nz)]
        + [(0, s, 0, 0) for s in range(1, ny)]
        + [(0, 0, s, 0) for s in range(1, nx)]
        + [(0, 0, 0, 1)]
    )


def plane_offsets(dims):
    return [(0, v, u, 0) for v in range(dims[1]) for u in range(dims[2]) if v or u]


def greet(place, offsets):
    offsets = sorted(set(offsets))
    sem = pltpu.get_barrier_semaphore()
    for off in offsets:
        pl.semaphore_signal(sem, inc=1, device_id=place.dev(*off), device_id_type=MESH)
    pl.semaphore_wait(sem, len(offsets))


class Comm:
    def __init__(self, send_sems, recv_sems, local_sems):
        self.send_sems, self.recv_sems, self.local_sems = (send_sems, recv_sems, local_sems)
        self.sent, self.held, self.count, self.locals = ([], [], 0, 0)

    def send(self, src, dst, device):
        k = self.count
        self.count += 1
        copy = pltpu.make_async_remote_copy(
            src_ref=src,
            dst_ref=dst,
            send_sem=self.send_sems.at[k],
            recv_sem=self.recv_sems.at[k],
            device_id=device,
            device_id_type=MESH,
        )
        copy.start()
        self.sent.append(copy)
        return copy

    def keep(self, src, dst):
        copy = pltpu.make_async_copy(src, dst, self.local_sems.at[self.locals])
        self.locals += 1
        copy.start()
        self.held.append(copy)
        return copy

    def finish(self, but=()):
        for copy in self.sent:
            copy.wait_send()
        for copy in self.held:
            if copy not in but:
                copy.wait()


def small_gather(comm, place, src, out):
    nz, ny, nx = place.dims
    z, y, x, c = (place.z, place.y, place.x, place.c)
    mine = comm.keep(src, out.at[z, y, x, c])
    comm.held.remove(mine)
    got = [comm.send(src, out.at[z, y, x, c], place.dev(c=1))]
    yield
    for copy in got:
        copy.wait_recv()
    mine.wait()
    got = [comm.send(out.at[z, y, x], out.at[z, y, x], place.dev(x=t)) for t in range(1, nx)]
    yield
    for copy in got:
        copy.wait_recv()
    got = [comm.send(out.at[z, y], out.at[z, y], place.dev(y=t)) for t in range(1, ny)]
    yield
    for copy in got:
        copy.wait_recv()
    got = [comm.send(out.at[z], out.at[z], place.dev(z=t)) for t in range(1, nz)]
    yield
    for copy in got:
        copy.wait_recv()


def drain(stages):
    for _ in stages:
        pass


def sems(count):
    return pltpu.SemaphoreType.DMA((count,))


def shape(dims, dtype):
    return jax.ShapeDtypeStruct(tuple(dims), dtype)


def call(kernel, outs, in_specs, out_specs, scratch, cid, name, args, vmem=None):
    return pl.pallas_call(
        kernel,
        out_shape=outs,
        in_specs=in_specs,
        out_specs=out_specs,
        scratch_shapes=scratch,
        compiler_params=pltpu.CompilerParams(
            collective_id=cid, has_side_effects=True, vmem_limit_bytes=vmem
        ),
        name=name,
    )(*args)


def small_sends(dims):
    return sum(dims) - 2


def gather_first(dims, layers, table, meta, cid):
    nz, ny, nx = dims
    n = len(layers)

    def kernel(*refs):
        ins, rest = (refs[: n + 2], refs[n + 2 :])
        outs, (ssem, rsem, lsem) = (rest[: n + 2], rest[n + 2 :])
        place = Place(dims)
        z, y, x, c = (place.z, place.y, place.x, place.c)
        greet(place, line_offsets(dims) + plane_offsets(dims))
        comm = Comm(ssem, rsem, lsem)
        small = small_gather(comm, place, ins[n + 1], outs[n + 1])
        next(small)
        tab, whole = (ins[n], outs[n])
        slot = whole.at[y, x, c]
        near = [
            (off, comm.send(tab, slot, place.dev(*off))) for off in plane_offsets(dims)
        ]
        waits = []
        for a in range(n):
            comm.keep(ins[a], outs[a].at[z])
            for s in range(1, nz):
                waits.append(comm.send(ins[a], outs[a].at[z], place.dev(z=s)))
        comm.keep(tab, slot)
        waits.append(comm.send(tab, slot, place.dev(c=1)))
        next(small)
        next(small)
        next(small)
        for off, copy in near:
            copy.wait_recv()
            block = whole.at[place.ys(off[1]), place.xs(off[2]), c]
            waits.append(comm.send(block, block, place.dev(c=1)))
        drain(small)
        for copy in waits:
            copy.wait_recv()
        comm.finish()

    count = n * (nz - 1) + 2 * ny * nx + small_sends(dims)
    outs = [shape((nz,) + v.shape, v.dtype) for v in layers]
    outs += [shape((ny, nx, 2) + table.shape, table.dtype), shape(dims + (2,) + meta.shape, meta.dtype)]
    return call(
        kernel, outs, [ANY] * (n + 2), [ANY] * (n + 2), [sems(count), sems(count), sems(n + 2)],
        cid, "gather_first", (*layers, table, meta),
    )


def gather_second(dims, lines, first_axes, rows, small, cid):
    nz, ny, nx = dims
    n = len(lines)
    parts = 2 if nz <= 4 else 1
    step = nz // parts

    def kernel(*refs):
        ins, rest = (refs[: n + 2], refs[n + 2 :])
        outs, (ssem, rsem, lsem) = (rest[: n + 2], rest[n + 2 :])
        place = Place(dims)
        z, y, x, c = (place.z, place.y, place.x, place.c)
        greet(place, line_offsets(dims))
        comm = Comm(ssem, rsem, lsem)
        gather = small_gather(comm, place, ins[n + 1], outs[n + 1])
        next(gather)
        waits = []
        for s in range(1, nz):
            waits.append(comm.send(ins[n].at[place.zs(nz - s)], outs[n].at[z], place.dev(z=s)))
        comm.keep(ins[n].at[z], outs[n].at[z])
        firsts, seconds = ([], [])
        for g in range(parts):
            span = pl.ds(g * step, step)
            for a in range(n):
                src, dst = (ins[a].at[span], outs[a].at[span, y, x, c])
                comm.keep(src, dst)
                waits.append(comm.send(src, dst, place.dev(c=1)))
                first = first_axes[a]
                second = "y" if first == "x" else "x"
                sizes = {"x": nx, "y": ny}
                for t in range(1, sizes[first]):
                    firsts.append((a, span, first, second, sizes[second], t, comm.send(src, dst, place.dev(**{first: t}))))
                for t in range(1, sizes[second]):
                    yy, xx = (place.ys(t), x) if second == "y" else (y, place.xs(t))
                    seconds.append((a, span, yy, xx, comm.send(src, dst, place.dev(**{second: t}))))
        next(gather)
        next(gather)
        next(gather)
        for a, span, first, second, size, t, copy in firsts:
            copy.wait_recv()
            yy, xx = (place.ys(t), x) if first == "y" else (y, place.xs(t))
            block = outs[a].at[span, yy, xx, c]
            for u in range(1, size):
                y2, x2 = (place.ys(u), xx) if second == "y" else (yy, place.xs(u))
                seconds.append((a, span, y2, x2, comm.send(block, block, place.dev(**{second: u}))))
            waits.append(comm.send(block, block, place.dev(c=1)))
        drain(gather)
        for a, span, yy, xx, copy in seconds:
            copy.wait_recv()
            block = outs[a].at[span, yy, xx, c]
            waits.append(comm.send(block, block, place.dev(c=1)))
        for copy in waits:
            copy.wait_recv()
        comm.finish()

    count = n * parts * (2 * ny * nx - 1) + nz + small_sends(dims)
    outs = [shape(dims + (2,) + v.shape[1:], v.dtype) for v in lines]
    outs += [shape(rows.shape, rows.dtype), shape(dims + (2,) + small.shape, small.dtype)]
    return call(
        kernel, outs, [ANY] * (n + 2), [ANY] * (n + 2),
        [sems(count), sems(count), sems(n * parts + 2)],
        cid, "gather_second", (*lines, rows, small),
    )


def line_gather(dims, block, cid, name):
    nz = dims[0]

    def kernel(src, out, ssem, rsem, lsem):
        place = Place(dims)
        greet(place, [(s, 0, 0, 0) for s in range(1, nz)])
        comm = Comm(ssem, rsem, lsem)
        waits = [comm.send(src, out.at[place.z], place.dev(z=s)) for s in range(1, nz)]
        comm.keep(src, out.at[place.z])
        for copy in waits:
            copy.wait_recv()
        comm.finish()

    return call(
        kernel, shape((nz,) + block.shape, block.dtype), [ANY], ANY,
        [sems(nz), sems(nz), sems(1)], cid, name, (block,),
    )


def all_small(dims, block, cid, name):
    def kernel(src, out, ssem, rsem, lsem):
        place = Place(dims)
        greet(place, line_offsets(dims))
        comm = Comm(ssem, rsem, lsem)
        drain(small_gather(comm, place, src, out))
        comm.finish()

    count = small_sends(dims)
    return call(
        kernel, shape(dims + (2,) + block.shape, block.dtype), [ANY], ANY,
        [sems(count), sems(count), sems(1)], cid, name, (block,),
    )


def add_blocks(out, terms):
    lead = out.shape[:-2]

    def visit(index):
        if len(index) < len(lead):

            @pl.loop(0, lead[len(index)])
            def _(i):
                visit(index + (i,))

        else:
            total = terms[0][index].astype(F32)
            for term in terms[1:]:
                total = total + term[index].astype(F32)
            out[index] = total.astype(out.dtype)

    visit(())


def scatter_first(dims, grads, first_axes, rows, small, cid):
    nz, ny, nx = dims
    n = len(grads)

    def kernel(*refs):
        ins, rest = (refs[: n + 2], refs[n + 2 :])
        outs, rest = (rest[: n + 2], rest[n + 2 :])
        halves, ones, twos, (ssem, rsem, lsem) = (
            rest[:n], rest[n : 2 * n], rest[2 * n : 3 * n], rest[3 * n :]
        )
        place = Place(dims)
        z, y, x, c = (place.z, place.y, place.x, place.c)
        greet(place, line_offsets(dims))
        comm = Comm(ssem, rsem, lsem)
        gather = small_gather(comm, place, ins[n + 1], outs[n + 1])
        pair = []
        for a in range(n):
            pair.append(comm.send(ins[a].at[:, :, :, 1 - c], halves[a], place.dev(c=1)))
        next(gather)
        waits = [comm.send(ins[n], outs[n].at[z], place.dev(z=s)) for s in range(1, nz)]
        comm.keep(ins[n], outs[n].at[z])
        got_one = []
        for a in range(n):
            pair[a].wait_recv()
            add_blocks(halves[a], [halves[a], ins[a].at[:, :, :, c]])
            if first_axes[a] == "y":
                got_one.append([
                    comm.send(halves[a].at[:, place.ys(ny - t)], ones[a].at[t - 1], place.dev(y=t))
                    for t in range(1, ny)
                ])
            else:
                got_one.append([
                    comm.send(halves[a].at[:, :, place.xs(nx - t)], ones[a].at[t - 1], place.dev(x=t))
                    for t in range(1, nx)
                ])
        next(gather)
        next(gather)
        next(gather)
        got_two = []
        for a in range(n):
            for copy in got_one[a]:
                copy.wait_recv()
            if first_axes[a] == "y":
                mine = halves[a].at[:, y]
                add_blocks(mine, [mine] + [ones[a].at[t] for t in range(ny - 1)])
                got_two.append([
                    comm.send(halves[a].at[:, y, place.xs(nx - t)], twos[a].at[t - 1], place.dev(x=t))
                    for t in range(1, nx)
                ])
            else:
                mine = halves[a].at[:, :, x]
                add_blocks(mine, [mine] + [ones[a].at[t] for t in range(nx - 1)])
                got_two.append([
                    comm.send(halves[a].at[:, place.ys(ny - t), x], twos[a].at[t - 1], place.dev(y=t))
                    for t in range(1, ny)
                ])
        drain(gather)
        for a in range(n):
            for copy in got_two[a]:
                copy.wait_recv()
            terms = [twos[a].at[t] for t in range(twos[a].shape[0])]
            add_blocks(outs[a], [halves[a].at[:, y, x]] + terms)
        for copy in waits:
            copy.wait_recv()
        comm.finish()

    count = n * (ny + nx - 1) + nz + small_sends(dims)
    scratch = [pltpu.VMEM((nz, ny, nx) + g.shape[4:], g.dtype) for g in grads]
    for g, axis in zip(grads, first_axes):
        near, far = (ny, nx) if axis == "y" else (nx, ny)
        scratch.append(pltpu.VMEM((near - 1, nz, far) + g.shape[4:], g.dtype))
    for g, axis in zip(grads, first_axes):
        scratch.append(pltpu.VMEM(((nx if axis == "y" else ny) - 1, nz) + g.shape[4:], g.dtype))
    outs = [shape((nz,) + g.shape[4:], g.dtype) for g in grads]
    outs += [shape((nz,) + rows.shape, rows.dtype), shape(dims + (2,) + small.shape, small.dtype)]
    return call(
        kernel, outs, [VMEM] * n + [ANY] * 2, [VMEM] * n + [ANY] * 2,
        scratch + [sems(count), sems(count), sems(2)],
        cid, "scatter_first", (*grads, rows, small), 60 * 2**20,
    )


def scatter_second(dims, lines, table, cid):
    nz, ny, nx = dims
    n = len(lines)
    block = table.shape[3:]

    def kernel(*refs):
        ins, rest = (refs[: n + 1], refs[n + 1 :])
        outs, rest = (rest[: n + 1], rest[n + 1 :])
        got, half, near, ssem, rsem, lsem = (rest[:n], *rest[n:])
        place = Place(dims)
        z, y, x, c = (place.z, place.y, place.x, place.c)
        offsets = plane_offsets(dims)
        greet(place, line_offsets(dims) + offsets)
        comm = Comm(ssem, rsem, lsem)
        pair = comm.send(ins[n].at[:, :, 1 - c], half, place.dev(c=1))
        lines_in = [
            [
                comm.send(ins[a].at[place.zs(nz - s)], got[a].at[s - 1], place.dev(z=s))
                for s in range(1, nz)
            ]
            for a in range(n)
        ]
        pair.wait_recv()
        add_blocks(half, [half, ins[n].at[:, :, c]])
        arriving = [
            comm.send(half.at[place.ys(ny - off[1]), place.xs(nx - off[2])], near.at[k], place.dev(*off))
            for k, off in enumerate(offsets)
        ]
        for a in range(n):
            for copy in lines_in[a]:
                copy.wait_recv()
            add_blocks(outs[a], [ins[a].at[z]] + [got[a].at[s] for s in range(nz - 1)])
        for copy in arriving:
            copy.wait_recv()
        add_blocks(outs[n], [half.at[y, x]] + [near.at[k] for k in range(len(offsets))])
        comm.finish()

    count = n * (nz - 1) + ny * nx
    scratch = [pltpu.VMEM((nz - 1,) + v.shape[1:], v.dtype) for v in lines]
    scratch += [pltpu.VMEM((ny, nx) + block, BF), pltpu.VMEM((ny * nx - 1,) + block, BF)]
    outs = [shape(v.shape[1:], F32) for v in lines] + [shape(block, F32)]
    return call(
        kernel, outs, [VMEM] * (n + 1), [VMEM] * (n + 1),
        scratch + [sems(count), sems(count), sems(1)],
        cid, "scatter_second", (*lines, table), 60 * 2**20,
    )


def matmul(left, right):
    return jnp.dot(left, right, preferred_element_type=F32)


def norm_forward(values, gain):
    inverse = lax.rsqrt(jnp.mean(values * values, axis=-1, keepdims=True) + EPS_NORM)
    normed = values * inverse
    return (normed * gain, normed, inverse)


def norm_backward(grad, normed, inverse, gain):
    scaled = grad * gain
    inner = jnp.mean(scaled * normed, axis=-1, keepdims=True)
    return (inverse * (scaled - normed * inner), jnp.sum(grad * normed, axis=0))


def turn_half(tensor):
    quarter = tensor.shape[-1] // 4
    return jnp.concatenate(
        [
            -tensor[..., quarter : 2 * quarter],
            tensor[..., :quarter],
            -tensor[..., 3 * quarter :],
            tensor[..., 2 * quarter : 3 * quarter],
        ],
        axis=-1,
    )


def rope_tables(positions, width):
    quarter = width // 4
    freq = 10000.0 ** (-jnp.arange(quarter, dtype=F32) / quarter)
    row_angle = (positions // GRID).astype(F32)[:, None] * freq
    col_angle = (positions % GRID).astype(F32)[:, None] * freq
    angles = jnp.concatenate([row_angle, row_angle, col_angle, col_angle], axis=-1)
    return (jnp.cos(angles)[:, None, :], jnp.sin(angles)[:, None, :])


def rotate(tensor, cosine, sine):
    return tensor * cosine + turn_half(tensor) * sine


def rotate_back(grad, cosine, sine):
    return grad * cosine - turn_half(grad * sine)


def masked_scores(query, keys, height):
    scores = jnp.einsum("qhd,khd->hqk", query, keys, preferred_element_type=F32) * HD ** (-0.5)
    places = jnp.arange(query.shape[0])
    allowed = (places[None, :] <= places[:, None]) & (places[None, :] < GRID * height)
    return jnp.where(allowed[None], scores, NEGATIVE_FILL)


def attend(query, keys, values, height):
    scores = masked_scores(query, keys, height)
    score_peak = jnp.max(scores, axis=-1, keepdims=True)
    exponent = jnp.exp(scores - score_peak)
    score_total = jnp.sum(exponent, axis=-1, keepdims=True)
    probs = exponent / score_total
    output = jnp.einsum("hqk,khd->qhd", probs.astype(BF), values, preferred_element_type=F32)
    return (output.astype(BF).reshape(query.shape[0], -1), probs)


def attend_back(query, keys, values, probs, grad_out):
    grad_heads = grad_out.reshape(query.shape)
    grad_probs = jnp.einsum("qhd,khd->hqk", grad_heads, values, preferred_element_type=F32)
    grad_scores = probs * (grad_probs - jnp.sum(probs * grad_probs, axis=-1, keepdims=True))
    grad_scores = grad_scores.astype(BF)
    scale = HD ** (-0.5)
    grad_query = jnp.einsum("hqk,khd->qhd", grad_scores, keys, preferred_element_type=F32) * scale
    grad_keys = jnp.einsum("hqk,qhd->khd", grad_scores, query, preferred_element_type=F32) * scale
    grad_values = jnp.einsum(
        "hqk,qhd->khd", probs.astype(BF), grad_heads, preferred_element_type=F32
    )
    return (grad_query.astype(BF), grad_keys.astype(BF), grad_values.astype(BF))


def adam_update(master, drift, square, grad, rate, decay):
    moment = BETA_ONE * drift + (1.0 - BETA_ONE) * grad
    second = BETA_TWO * square + (1.0 - BETA_TWO) * grad * grad
    stride = (
        moment / (1.0 - BETA_ONE**STEP) / (jnp.sqrt(second / (1.0 - BETA_TWO**STEP)) + ADAM_EPS)
    )
    return (master - rate * (stride + decay * master), moment, second)


def pad_rows(value, rows):
    flat = value.reshape(-1)
    return jnp.pad(flat, (0, rows * 128 - flat.shape[0])).reshape(rows, 128)


def block_form(rows, columns):
    return (rows, columns) if rows % 8 == 0 else (rows * columns // 128, 128)


FIRST_AXES = ("x", "x", "y", "x")


def on_device(dims, *args):
    labels, targets, heights, loss_mask = args[:4]
    masters, drifts, squares = (args[4:12], args[12:20], args[20:28])
    class_table, code_table, attend_in, attend_mix, expand_in, shrink_out, head_weight, norm_gains = masters
    nz, ny, nx = dims
    plane = ny * nx
    chips = nz * plane
    images, local_len = targets.shape
    length = local_len * 2
    width = code_table.shape[1]
    device_codes = code_table.shape[0]
    line_codes = device_codes * plane * 2
    gain_columns = norm_gains.shape[1]
    chip, core = (lax.axis_index("dp"), lax.axis_index("seq"))
    z, y, x = (chip // plane, (chip // nx) % ny, chip % nx)
    plane_groups = [[k * plane + i for i in range(plane)] for k in range(nz)]
    line_groups = [[k * plane + i for k in range(nz)] for i in range(plane)]

    head_near = lax.all_gather(head_weight.astype(BF), "dp", axis_index_groups=plane_groups)
    head_near = lax.all_gather(head_near, "seq")

    layers = [v.astype(BF) for v in (attend_in, attend_mix, expand_in, shrink_out)]
    tail = jnp.concatenate([labels, heights])
    meta = jnp.concatenate([targets, loss_mask, pad_rows(tail, 4)], axis=0)
    *lines, table, metas = gather_first(dims, layers, code_table.astype(BF), meta, 0)
    table = table.reshape(line_codes, width)

    own_tokens = lax.dynamic_slice_in_dim(metas, core, 1, axis=4)[:, :, :, :, 0]
    own_masks = lax.dynamic_slice_in_dim(metas, 2 + core, 1, axis=4)[:, :, :, :, 0]

    def of_line(value):
        value = lax.dynamic_slice_in_dim(value, y, 1, axis=1)
        return lax.dynamic_slice_in_dim(value, x, 1, axis=2).reshape(nz, -1)

    line_targets = of_line(own_tokens)
    line_heights = of_line(lax.dynamic_slice_in_dim(metas[:, :, :, 0, 4], images + core, 1, axis=3))
    places = jnp.arange(length)
    line_counted = (of_line(own_masks) * (places[None, :] < GRID * line_heights)).astype(F32)
    all_labels = metas[:, :, :, 0, 4, :images].reshape(-1)
    before = jnp.concatenate(
        [jnp.full((nz, 1), -1, jnp.int32), line_targets[:, :-1] - z * line_codes], axis=1
    ).reshape(-1)
    code_pick = (before[:, None] == jnp.arange(line_codes)[None, :]).astype(BF)
    rows = matmul(code_pick, table).astype(BF).reshape(nz, length, width)
    class_pick = all_labels[:, None] == jnp.arange(class_table.shape[0])[None, :]
    class_part = matmul(class_pick.astype(BF), class_table.astype(BF))
    gains_low = norm_gains.astype(BF).astype(F32)
    small = jnp.concatenate([pad_rows(class_part, 6), pad_rows(gains_low, 2)], axis=0)

    *weights, row_parts, smalls = gather_second(dims, lines, FIRST_AXES, rows, small, 1)
    qkv_w, mix_w, expand_w, shrink_w = (v.reshape(-1, v.shape[-1]) for v in weights)
    smalls = smalls.reshape(chips * 2, -1)
    class_rows = smalls[:, : 6 * 128].reshape(chips * 2, chips * images, -1)
    class_row = lax.dynamic_slice_in_dim(class_rows, chip * images + core, 1, axis=1).reshape(1, -1)
    gain = smalls[:, 6 * 128 : 6 * 128 + 3 * gain_columns].reshape(chips * 2, 3, gain_columns)
    gain = gain.transpose(1, 0, 2).reshape(3, -1)
    start = jnp.sum(row_parts.astype(F32), axis=0)
    start = jnp.where((places == 0)[:, None], class_row, start)
    height = lax.dynamic_slice_in_dim(line_heights, z, 1, axis=0).reshape(())

    cosine, sine = rope_tables(places, HD)
    normed_one, norm_one, inverse_one = norm_forward(start, gain[0])
    normed_one = normed_one.astype(BF)
    mixed = matmul(normed_one, qkv_w).reshape(length, 3, -1, HD)
    query = rotate(mixed[:, 0], cosine, sine).astype(BF)
    keys = rotate(mixed[:, 1], cosine, sine).astype(BF)
    values = mixed[:, 2].astype(BF)
    attended, probs = attend(query, keys, values, height)
    middle = start + matmul(attended, mix_w)
    normed_two, norm_two, inverse_two = norm_forward(middle, gain[1])
    normed_two = normed_two.astype(BF)
    both = matmul(normed_two, expand_w)
    inner = both.shape[1] // 2
    gate_part, up_part = (both[:, :inner], both[:, inner:])
    hidden = (jax.nn.silu(gate_part) * up_part).astype(BF)
    final = middle + matmul(hidden, shrink_w)
    normed_top, norm_top, inverse_top = norm_forward(final, gain[2])
    normed_top = normed_top.astype(BF)

    tops = line_gather(dims, normed_top, 2, "top_rows").reshape(nz * length, width)
    head_w = head_near.transpose(2, 1, 0, 3).reshape(width, line_codes)
    logits = matmul(tops, head_w)
    local_targets = (line_targets - z * line_codes).reshape(-1, 1)
    onehot = local_targets == jnp.arange(line_codes)[None, :]
    peak = jnp.max(logits, axis=1)
    total = jnp.sum(jnp.exp(logits - peak[:, None]), axis=1)
    picked = jnp.sum(jnp.where(onehot, logits, 0.0), axis=1)
    stats = jnp.concatenate([v.reshape(-1, 128) for v in (peak, total, picked)], axis=0)
    stats = line_gather(dims, stats, 3, "row_stats").reshape(nz, 3, -1)
    peaks = jnp.max(stats[:, 0], axis=0)
    totals = jnp.sum(stats[:, 1] * jnp.exp(stats[:, 0] - peaks[None, :]), axis=0)
    log_total = peaks + jnp.log(totals)
    counted = line_counted.reshape(-1)
    losses = (log_total - jnp.sum(stats[:, 2], axis=0)) * counted
    loss_local = jnp.sum(lax.dynamic_slice_in_dim(losses.reshape(nz, -1), z, 1, axis=0))
    count_local = jnp.sum(lax.dynamic_slice_in_dim(line_counted, z, 1, axis=0))
    softmax = jnp.exp(logits - peaks[:, None]) / totals[:, None]
    grad_logits = ((softmax - onehot.astype(F32)) * counted[:, None]).astype(BF)
    grad_tops = matmul(grad_logits, head_w.T).astype(BF).reshape(nz, length, width)
    grad_top = lax.psum_scatter(grad_tops, "dp", axis_index_groups=line_groups)
    grad_head = matmul(tops.T, grad_logits).astype(BF).reshape(width, plane, 2, -1)
    grad_head = lax.psum_scatter(grad_head, "seq", scatter_dimension=2)
    grad_head = lax.psum_scatter(
        grad_head, "dp", scatter_dimension=1, axis_index_groups=plane_groups
    ).astype(F32)

    grad_final, gain_top = norm_backward(grad_top.astype(F32), norm_top, inverse_top, gain[2])
    back_down = grad_final.astype(BF)
    grad_shrink = matmul(hidden.T, back_down)
    grad_hidden = matmul(back_down, shrink_w.T)
    sigma = jax.nn.sigmoid(gate_part)
    grad_gate = grad_hidden * up_part * sigma * (1.0 + gate_part * (1.0 - sigma))
    grad_up = grad_hidden * gate_part * sigma
    grad_both = jnp.concatenate([grad_gate, grad_up], axis=1).astype(BF)
    grad_expand = matmul(normed_two.T, grad_both)
    grad_norm_two, gain_two = norm_backward(
        matmul(grad_both, expand_w.T), norm_two, inverse_two, gain[1]
    )
    grad_middle = grad_final + grad_norm_two
    back_mix = grad_middle.astype(BF)
    grad_mix = matmul(attended.T, back_mix)
    grad_attended = matmul(back_mix, mix_w.T).astype(BF)
    grad_query, grad_keys, grad_values = attend_back(query, keys, values, probs, grad_attended)
    grad_mixed = jnp.stack(
        [
            rotate_back(grad_query.astype(F32), cosine, sine).astype(BF),
            rotate_back(grad_keys.astype(F32), cosine, sine).astype(BF),
            grad_values,
        ],
        axis=1,
    ).reshape(length, -1)
    grad_qkv = matmul(normed_one.T, grad_mixed)
    grad_norm_one, gain_one = norm_backward(
        matmul(grad_mixed, qkv_w.T), norm_one, inverse_one, gain[0]
    )
    grad_start = grad_middle + grad_norm_one

    grads_in = []
    for grad, shard in zip((grad_qkv, grad_mix, grad_expand, grad_shrink), layers):
        grads_in.append(grad.astype(BF).reshape(dims + (2,) + block_form(*shard.shape)))
    small = jnp.concatenate(
        [
            pad_rows(grad_start[0], width // 128),
            pad_rows(jnp.concatenate([gain_one, gain_two, gain_top]), 3 * width // 128),
        ],
        axis=0,
    )
    *line_grads, row_grads, smalls = scatter_first(
        dims, grads_in, FIRST_AXES, grad_start.astype(BF), small, 4
    )
    row_grads = row_grads.reshape(nz * length, width)
    table_grad = lax.dot_general(
        code_pick, row_grads, (((0,), (0,)), ((), ())), preferred_element_type=F32
    )
    table_grad = table_grad.astype(BF).reshape(ny, nx, 2, device_codes, width)
    *layer_shares, code_share = scatter_second(dims, line_grads, table_grad, 5)
    layer_shares = [g.reshape(v.shape) for g, v in zip(layer_shares, layers)]
    smalls = smalls.reshape(chips * 2, 4, -1)
    device = chip * 2 + core
    small_mine = lax.dynamic_slice_in_dim(smalls, device * gain_columns, gain_columns, axis=2)
    class_share = jnp.dot(
        class_pick.astype(F32).T,
        small_mine[:, 0],
        precision=lax.Precision.HIGHEST,
        preferred_element_type=F32,
    )
    gain_share = jnp.sum(small_mine[:, 1:], axis=0)
    shares = (class_share, code_share, *layer_shares, grad_head, gain_share)

    square_local = sum((jnp.sum(member * member) for member in shares))
    sums = pad_rows(jnp.stack([square_local, loss_local, count_local]), 8)
    sums = jnp.sum(all_small(dims, sums, 6, "last_sums").reshape(chips * 2, -1), axis=0)
    total_square, loss_sum, loss_count = (sums[0], sums[1], sums[2])
    grad_norm = jnp.sqrt(total_square) / loss_count
    factor = CLIP_NORM / jnp.maximum(grad_norm, CLIP_NORM) / loss_count
    news, firsts, seconds = ([], [], [])
    for member in range(8):
        fresh, moment, second = adam_update(
            masters[member],
            drifts[member],
            squares[member],
            shares[member] * factor,
            RATES[member],
            DECAYS[member],
        )
        news.append(fresh)
        firsts.append(moment)
        seconds.append(second)
    return tuple(news) + tuple(firsts) + tuple(seconds) + (grad_norm, loss_sum, loss_count)


def solution(mesh):
    rows, columns = (P(("dp", "seq"), None), P(None, ("dp", "seq")))
    eight = (columns, rows, rows, rows, rows, rows, columns, columns)
    return jax.shard_map(
        functools.partial(on_device, dims_of(mesh.shape["dp"])),
        mesh=mesh,
        in_specs=(P("dp"), P("dp", "seq"), P("dp"), P("dp", "seq")) + eight * 3,
        out_specs=eight * 3 + (P(), P(), P()),
        check_vma=False,
    )
```

```python
import functools

import jax
import jax.numpy as jnp
from jax import lax
from jax.experimental import pallas as pl
from jax.experimental.pallas import tpu as pltpu
from jax.sharding import PartitionSpec as P

HD = 64
GRID = 16
STEP = 10

EPS_NORM = 1e-05
BETA_ONE = 0.9
BETA_TWO = 0.95
ADAM_EPS = 1e-08
CLIP_NORM = 0.01
NEGATIVE_FILL = -1000000000.0
RATES = (0.8, 0.8, 0.08, 0.08, 0.08, 0.08, 0.08, 0.8)
DECAYS = (0.1, 0.1, 0.1, 0.1, 0.1, 0.1, 0.1, 0.0)

MESH = pl.DeviceIdType.MESH
ANY = pl.BlockSpec(memory_space=pl.ANY)
VMEM = pl.BlockSpec(memory_space=pltpu.VMEM)
BF = jnp.bfloat16
F32 = jnp.float32


def dims_of(dp):
    bits = dp.bit_length() - 1
    nz = 1 << (bits // 2)
    rest = dp // nz
    ny = 1 << ((rest.bit_length() - 1) // 2)
    return (nz, ny, rest // ny)


class Place:
    def __init__(self, dims):
        self.dims = dims
        nz, ny, nx = dims
        chip = lax.axis_index("dp")
        self.c = lax.axis_index("seq")
        self.z = chip // (ny * nx)
        self.y = (chip // nx) % ny
        self.x = chip % nx

    def zs(self, back):
        return (self.z + self.dims[0] - back) % self.dims[0]

    def ys(self, back):
        return (self.y + self.dims[1] - back) % self.dims[1]

    def xs(self, back):
        return (self.x + self.dims[2] - back) % self.dims[2]

    def dev(self, z=0, y=0, x=0, c=0):
        nz, ny, nx = self.dims
        z, y, x = ((self.z + z) % nz, (self.y + y) % ny, (self.x + x) % nx)
        return ((z * ny + y) * nx + x, (self.c + c) % 2)


def line_offsets(dims):
    nz, ny, nx = dims
    return (
        [(s, 0, 0, 0) for s in range(1, nz)]
        + [(0, s, 0, 0) for s in range(1, ny)]
        + [(0, 0, s, 0) for s in range(1, nx)]
        + [(0, 0, 0, 1)]
    )


def plane_offsets(dims):
    return [(0, v, u, 0) for v in range(dims[1]) for u in range(dims[2]) if v or u]


def greet(place, offsets):
    offsets = sorted(set(offsets))
    sem = pltpu.get_barrier_semaphore()
    for off in offsets:
        pl.semaphore_signal(sem, inc=1, device_id=place.dev(*off), device_id_type=MESH)
    pl.semaphore_wait(sem, len(offsets))


class Comm:
    def __init__(self, send_sems, recv_sems, local_sems):
        self.send_sems, self.recv_sems, self.local_sems = (send_sems, recv_sems, local_sems)
        self.sent, self.held, self.count, self.locals = ([], [], 0, 0)

    def send(self, src, dst, device):
        k = self.count
        self.count += 1
        copy = pltpu.make_async_remote_copy(
            src_ref=src,
            dst_ref=dst,
            send_sem=self.send_sems.at[k],
            recv_sem=self.recv_sems.at[k],
            device_id=device,
            device_id_type=MESH,
        )
        copy.start()
        self.sent.append(copy)
        return copy

    def keep(self, src, dst):
        copy = pltpu.make_async_copy(src, dst, self.local_sems.at[self.locals])
        self.locals += 1
        copy.start()
        self.held.append(copy)
        return copy

    def finish(self, but=()):
        for copy in self.sent:
            copy.wait_send()
        for copy in self.held:
            if copy not in but:
                copy.wait()


def small_gather(comm, place, src, out):
    nz, ny, nx = place.dims
    z, y, x, c = (place.z, place.y, place.x, place.c)
    mine = comm.keep(src, out.at[z, y, x, c])
    comm.held.remove(mine)
    got = [comm.send(src, out.at[z, y, x, c], place.dev(c=1))]
    yield
    for copy in got:
        copy.wait_recv()
    mine.wait()
    got = [comm.send(out.at[z, y, x], out.at[z, y, x], place.dev(x=t)) for t in range(1, nx)]
    yield
    for copy in got:
        copy.wait_recv()
    got = [comm.send(out.at[z, y], out.at[z, y], place.dev(y=t)) for t in range(1, ny)]
    yield
    for copy in got:
        copy.wait_recv()
    got = [comm.send(out.at[z], out.at[z], place.dev(z=t)) for t in range(1, nz)]
    yield
    for copy in got:
        copy.wait_recv()


def drain(stages):
    for _ in stages:
        pass


def sems(count):
    return pltpu.SemaphoreType.DMA((count,))


def shape(dims, dtype):
    return jax.ShapeDtypeStruct(tuple(dims), dtype)


def call(kernel, outs, in_specs, out_specs, scratch, cid, name, args, vmem=None):
    return pl.pallas_call(
        kernel,
        out_shape=outs,
        in_specs=in_specs,
        out_specs=out_specs,
        scratch_shapes=scratch,
        compiler_params=pltpu.CompilerParams(
            collective_id=cid, has_side_effects=True, vmem_limit_bytes=vmem
        ),
        name=name,
    )(*args)


def small_sends(dims):
    return sum(dims) - 2


def gather_first(dims, layers, table, meta, cid):
    nz, ny, nx = dims
    n = len(layers)

    def kernel(*refs):
        ins, rest = (refs[: n + 2], refs[n + 2 :])
        outs, (ssem, rsem, lsem) = (rest[: n + 2], rest[n + 2 :])
        place = Place(dims)
        z, y, x, c = (place.z, place.y, place.x, place.c)
        greet(place, line_offsets(dims) + plane_offsets(dims))
        comm = Comm(ssem, rsem, lsem)
        small = small_gather(comm, place, ins[n + 1], outs[n + 1])
        next(small)
        tab, whole = (ins[n], outs[n])
        slot = whole.at[y, x, c]
        near = [
            (off, comm.send(tab, slot, place.dev(*off))) for off in plane_offsets(dims)
        ]
        waits = []
        for a in range(n):
            comm.keep(ins[a], outs[a].at[z])
            for s in range(1, nz):
                waits.append(comm.send(ins[a], outs[a].at[z], place.dev(z=s)))
        comm.keep(tab, slot)
        waits.append(comm.send(tab, slot, place.dev(c=1)))
        next(small)
        next(small)
        next(small)
        for off, copy in near:
            copy.wait_recv()
            block = whole.at[place.ys(off[1]), place.xs(off[2]), c]
            waits.append(comm.send(block, block, place.dev(c=1)))
        drain(small)
        for copy in waits:
            copy.wait_recv()
        comm.finish()

    count = n * (nz - 1) + 2 * ny * nx + small_sends(dims)
    outs = [shape((nz,) + v.shape, v.dtype) for v in layers]
    outs += [shape((ny, nx, 2) + table.shape, table.dtype), shape(dims + (2,) + meta.shape, meta.dtype)]
    return call(
        kernel, outs, [ANY] * (n + 2), [ANY] * (n + 2), [sems(count), sems(count), sems(n + 2)],
        cid, "gather_first", (*layers, table, meta),
    )


def gather_second(dims, lines, first_axes, rows, small, cid):
    nz, ny, nx = dims
    n = len(lines)
    parts = 2 if nz <= 4 else 1
    step = nz // parts

    def kernel(*refs):
        ins, rest = (refs[: n + 2], refs[n + 2 :])
        outs, (ssem, rsem, lsem) = (rest[: n + 2], rest[n + 2 :])
        place = Place(dims)
        z, y, x, c = (place.z, place.y, place.x, place.c)
        greet(place, line_offsets(dims))
        comm = Comm(ssem, rsem, lsem)
        gather = small_gather(comm, place, ins[n + 1], outs[n + 1])
        next(gather)
        waits = []
        for s in range(1, nz):
            waits.append(comm.send(ins[n].at[place.zs(nz - s)], outs[n].at[z], place.dev(z=s)))
        comm.keep(ins[n].at[z], outs[n].at[z])
        firsts, seconds = ([], [])
        for g in range(parts):
            span = pl.ds(g * step, step)
            for a in range(n):
                src, dst = (ins[a].at[span], outs[a].at[span, y, x, c])
                comm.keep(src, dst)
                waits.append(comm.send(src, dst, place.dev(c=1)))
                first = first_axes[a]
                second = "y" if first == "x" else "x"
                sizes = {"x": nx, "y": ny}
                for t in range(1, sizes[first]):
                    firsts.append((a, span, first, second, sizes[second], t, comm.send(src, dst, place.dev(**{first: t}))))
                for t in range(1, sizes[second]):
                    yy, xx = (place.ys(t), x) if second == "y" else (y, place.xs(t))
                    seconds.append((a, span, yy, xx, comm.send(src, dst, place.dev(**{second: t}))))
        next(gather)
        next(gather)
        next(gather)
        for a, span, first, second, size, t, copy in firsts:
            copy.wait_recv()
            yy, xx = (place.ys(t), x) if first == "y" else (y, place.xs(t))
            block = outs[a].at[span, yy, xx, c]
            for u in range(1, size):
                y2, x2 = (place.ys(u), xx) if second == "y" else (yy, place.xs(u))
                seconds.append((a, span, y2, x2, comm.send(block, block, place.dev(**{second: u}))))
            waits.append(comm.send(block, block, place.dev(c=1)))
        drain(gather)
        for a, span, yy, xx, copy in seconds:
            copy.wait_recv()
            block = outs[a].at[span, yy, xx, c]
            waits.append(comm.send(block, block, place.dev(c=1)))
        for copy in waits:
            copy.wait_recv()
        comm.finish()

    count = n * parts * (2 * ny * nx - 1) + nz + small_sends(dims)
    outs = [shape(dims + (2,) + v.shape[1:], v.dtype) for v in lines]
    outs += [shape(rows.shape, rows.dtype), shape(dims + (2,) + small.shape, small.dtype)]
    return call(
        kernel, outs, [ANY] * (n + 2), [ANY] * (n + 2),
        [sems(count), sems(count), sems(n * parts + 2)],
        cid, "gather_second", (*lines, rows, small),
    )


def line_gather(dims, block, cid, name):
    nz = dims[0]

    def kernel(src, out, ssem, rsem, lsem):
        place = Place(dims)
        greet(place, [(s, 0, 0, 0) for s in range(1, nz)])
        comm = Comm(ssem, rsem, lsem)
        waits = [comm.send(src, out.at[place.z], place.dev(z=s)) for s in range(1, nz)]
        comm.keep(src, out.at[place.z])
        for copy in waits:
            copy.wait_recv()
        comm.finish()

    return call(
        kernel, shape((nz,) + block.shape, block.dtype), [ANY], ANY,
        [sems(nz), sems(nz), sems(1)], cid, name, (block,),
    )


def add_blocks(out, terms):
    lead = out.shape[:-2]

    def visit(index):
        if len(index) < len(lead):

            @pl.loop(0, lead[len(index)])
            def _(i):
                visit(index + (i,))

        else:
            total = terms[0][index].astype(F32)
            for term in terms[1:]:
                total = total + term[index].astype(F32)
            out[index] = total.astype(out.dtype)

    visit(())


def scatter_first(dims, grads, first_axes, rows, small, cid):
    nz, ny, nx = dims
    n = len(grads)

    def kernel(*refs):
        ins, rest = (refs[: n + 2], refs[n + 2 :])
        outs, rest = (rest[: n + 2], rest[n + 2 :])
        halves, ones, twos, (ssem, rsem, lsem) = (
            rest[:n], rest[n : 2 * n], rest[2 * n : 3 * n], rest[3 * n :]
        )
        place = Place(dims)
        z, y, x, c = (place.z, place.y, place.x, place.c)
        greet(place, line_offsets(dims))
        comm = Comm(ssem, rsem, lsem)
        gather = small_gather(comm, place, ins[n + 1], outs[n + 1])
        pair = []
        for a in range(n):
            pair.append(comm.send(ins[a].at[:, :, :, 1 - c], halves[a], place.dev(c=1)))
        next(gather)
        waits = [comm.send(ins[n], outs[n].at[z], place.dev(z=s)) for s in range(1, nz)]
        comm.keep(ins[n], outs[n].at[z])
        got_one = []
        for a in range(n):
            pair[a].wait_recv()
            add_blocks(halves[a], [halves[a], ins[a].at[:, :, :, c]])
            if first_axes[a] == "y":
                got_one.append([
                    comm.send(halves[a].at[:, place.ys(ny - t)], ones[a].at[t - 1], place.dev(y=t))
                    for t in range(1, ny)
                ])
            else:
                got_one.append([
                    comm.send(halves[a].at[:, :, place.xs(nx - t)], ones[a].at[t - 1], place.dev(x=t))
                    for t in range(1, nx)
                ])
        next(gather)
        next(gather)
        next(gather)
        got_two = []
        for a in range(n):
            for copy in got_one[a]:
                copy.wait_recv()
            if first_axes[a] == "y":
                mine = halves[a].at[:, y]
                add_blocks(mine, [mine] + [ones[a].at[t] for t in range(ny - 1)])
                got_two.append([
                    comm.send(halves[a].at[:, y, place.xs(nx - t)], twos[a].at[t - 1], place.dev(x=t))
                    for t in range(1, nx)
                ])
            else:
                mine = halves[a].at[:, :, x]
                add_blocks(mine, [mine] + [ones[a].at[t] for t in range(nx - 1)])
                got_two.append([
                    comm.send(halves[a].at[:, place.ys(ny - t), x], twos[a].at[t - 1], place.dev(y=t))
                    for t in range(1, ny)
                ])
        drain(gather)
        for a in range(n):
            for copy in got_two[a]:
                copy.wait_recv()
            terms = [twos[a].at[t] for t in range(twos[a].shape[0])]
            add_blocks(outs[a], [halves[a].at[:, y, x]] + terms)
        for copy in waits:
            copy.wait_recv()
        comm.finish()

    count = n * (ny + nx - 1) + nz + small_sends(dims)
    scratch = [pltpu.VMEM((nz, ny, nx) + g.shape[4:], g.dtype) for g in grads]
    for g, axis in zip(grads, first_axes):
        near, far = (ny, nx) if axis == "y" else (nx, ny)
        scratch.append(pltpu.VMEM((near - 1, nz, far) + g.shape[4:], g.dtype))
    for g, axis in zip(grads, first_axes):
        scratch.append(pltpu.VMEM(((nx if axis == "y" else ny) - 1, nz) + g.shape[4:], g.dtype))
    outs = [shape((nz,) + g.shape[4:], g.dtype) for g in grads]
    outs += [shape((nz,) + rows.shape, rows.dtype), shape(dims + (2,) + small.shape, small.dtype)]
    return call(
        kernel, outs, [VMEM] * n + [ANY] * 2, [VMEM] * n + [ANY] * 2,
        scratch + [sems(count), sems(count), sems(2)],
        cid, "scatter_first", (*grads, rows, small), 60 * 2**20,
    )


def scatter_second(dims, lines, table, head, partial, cid):
    nz, ny, nx = dims
    n = len(lines)
    block = table.shape[3:]

    def kernel(*refs):
        ins, rest = (refs[: n + 3], refs[n + 3 :])
        outs, rest = (rest[: n + 2], rest[n + 2 :])
        got, (half, near, mine, every, ssem, rsem, lsem) = (rest[:n], rest[n:])
        place = Place(dims)
        z, y, x, c = (place.z, place.y, place.x, place.c)
        offsets = plane_offsets(dims)
        greet(place, line_offsets(dims) + offsets)
        comm = Comm(ssem, rsem, lsem)
        pair = comm.send(ins[n].at[:, :, 1 - c], half, place.dev(c=1))
        lines_in = [
            [
                comm.send(ins[a].at[place.zs(nz - s)], got[a].at[s - 1], place.dev(z=s))
                for s in range(1, nz)
            ]
            for a in range(n)
        ]
        pair.wait_recv()
        add_blocks(half, [half, ins[n].at[:, :, c]])
        arriving = [
            comm.send(half.at[place.ys(ny - off[1]), place.xs(nx - off[2])], near.at[k], place.dev(*off))
            for k, off in enumerate(offsets)
        ]
        share = ins[n + 1][...].astype(F32)
        square = jnp.sum(share * share)
        for a in range(n):
            for copy in lines_in[a]:
                copy.wait_recv()
            add_blocks(outs[a], [ins[a].at[z]] + [got[a].at[s] for s in range(nz - 1)])
            square = square + jnp.sum(outs[a][...] * outs[a][...])
        for copy in arriving:
            copy.wait_recv()
        add_blocks(outs[n], [half.at[y, x]] + [near.at[k] for k in range(len(offsets))])
        square = square + jnp.sum(outs[n][...] * outs[n][...])
        held = ins[n + 2][...]
        first = (lax.broadcasted_iota(jnp.int32, held.shape, 0) == 0) & (
            lax.broadcasted_iota(jnp.int32, held.shape, 1) == 0
        )
        mine[...] = held + jnp.where(first, square, 0.0)
        drain(small_gather(comm, place, mine, every))
        outs[n + 1][...] = jnp.zeros_like(held)
        sums = outs[n + 1]

        @pl.loop(0, nz)
        def _(k):
            for j in range(ny):
                for i in range(nx):
                    sums[...] += every[k, j, i, 0] + every[k, j, i, 1]

        comm.finish()

    count = n * (nz - 1) + ny * nx + small_sends(dims)
    scratch = [pltpu.VMEM((nz - 1,) + v.shape[1:], v.dtype) for v in lines]
    scratch += [pltpu.VMEM((ny, nx) + block, BF), pltpu.VMEM((ny * nx - 1,) + block, BF)]
    scratch += [pltpu.VMEM(partial.shape, F32), pltpu.VMEM(dims + (2,) + partial.shape, F32)]
    outs = [shape(v.shape[1:], F32) for v in lines] + [shape(block, F32), shape(partial.shape, F32)]
    return call(
        kernel, outs, [VMEM] * (n + 3), [VMEM] * (n + 2),
        scratch + [sems(count), sems(count), sems(1)],
        cid, "scatter_second", (*lines, table, head, partial), 60 * 2**20,
    )


def matmul(left, right):
    return jnp.dot(left, right, preferred_element_type=F32)


def head_forward(tops, weights, marks):
    cores, plane, width, columns = weights.shape
    rows = tops.shape[0]
    blocks = cores * plane

    def kernel(x_ref, w_ref, mark_ref, logit_ref, stat_ref, peak, total, picked):
        k = pl.program_id(0)

        @pl.when(k == 0)
        def _():
            peak[...] = jnp.full_like(peak, -jnp.inf)
            total[...] = jnp.zeros_like(total)
            picked[...] = jnp.zeros_like(picked)

        logits = matmul(x_ref[...], w_ref[...])
        logit_ref[...] = logits
        lanes = lax.broadcasted_iota(jnp.int32, logits.shape, 1) + k * columns
        chosen = jnp.where(lanes == mark_ref[...], logits, 0.0)
        picked[...] += jnp.sum(chosen, axis=1, keepdims=True)
        old = peak[...]
        new = jnp.maximum(old, jnp.max(logits, axis=1, keepdims=True))
        exponent = jnp.sum(jnp.exp(logits - new), axis=1, keepdims=True)
        total[...] = total[...] * jnp.exp(old - new) + exponent
        peak[...] = new

        @pl.when(k == blocks - 1)
        def _():
            lane = lax.broadcasted_iota(jnp.int32, (rows, 128), 1)
            table = jnp.where(lane == 0, peak[...], jnp.where(lane == 1, total[...], picked[...]))
            stat_ref[...] = table.T[:8]

    return pl.pallas_call(
        kernel,
        grid=(blocks,),
        out_shape=[shape((blocks, rows, columns), F32), shape((8, rows), F32)],
        in_specs=[
            pl.BlockSpec((rows, width), lambda k: (0, 0)),
            pl.BlockSpec((None, None, width, columns), lambda k: (k % 2, k // 2, 0, 0)),
            pl.BlockSpec((rows, 1), lambda k: (0, 0)),
        ],
        out_specs=[
            pl.BlockSpec((None, rows, columns), lambda k: (k, 0, 0)),
            pl.BlockSpec((8, rows), lambda k: (0, 0)),
        ],
        scratch_shapes=[pltpu.VMEM((rows, 1), F32)] * 3,
        compiler_params=pltpu.CompilerParams(vmem_limit_bytes=48 * 2**20),
        cost_estimate=pl.CostEstimate(
            flops=2 * rows * width * columns * blocks,
            bytes_accessed=blocks * columns * (2 * width + 4 * rows),
            transcendentals=rows * columns * blocks,
        ),
        name="head_forward",
    )(tops, weights, marks)


def head_backward(logits, weights, marks, stats):
    blocks, rows, columns = logits.shape
    width = weights.shape[2]

    def kernel(l_ref, w_ref, mark_ref, stat_ref, grad_ref, top_ref, column, total):
        k = pl.program_id(0)

        @pl.when(k == 0)
        def _():
            column[...] = jnp.concatenate([stat_ref[...]] * 16, axis=0).T
            total[...] = jnp.zeros_like(total)

        held = column[...]
        soft = jnp.exp(l_ref[...] - held[:, 0:1]) * held[:, 1:2]
        lanes = lax.broadcasted_iota(jnp.int32, soft.shape, 1) + k * columns
        grad = (soft - jnp.where(lanes == mark_ref[...], held[:, 2:3], 0.0)).astype(BF)
        grad_ref[...] = grad
        total[...] += lax.dot_general(
            grad, w_ref[...], (((1,), (1,)), ((), ())), preferred_element_type=F32
        )

        @pl.when(k == blocks - 1)
        def _():
            top_ref[...] = total[...].astype(BF)

    return pl.pallas_call(
        kernel,
        grid=(blocks,),
        out_shape=[shape(logits.shape, BF), shape((rows, width), BF)],
        in_specs=[
            pl.BlockSpec((None, rows, columns), lambda k: (k, 0, 0)),
            pl.BlockSpec((None, None, width, columns), lambda k: (k % 2, k // 2, 0, 0)),
            pl.BlockSpec((rows, 1), lambda k: (0, 0)),
            pl.BlockSpec((8, rows), lambda k: (0, 0)),
        ],
        out_specs=[
            pl.BlockSpec((None, rows, columns), lambda k: (k, 0, 0)),
            pl.BlockSpec((rows, width), lambda k: (0, 0)),
        ],
        scratch_shapes=[pltpu.VMEM((rows, 128), F32), pltpu.VMEM((rows, width), F32)],
        compiler_params=pltpu.CompilerParams(vmem_limit_bytes=48 * 2**20),
        cost_estimate=pl.CostEstimate(
            flops=2 * rows * width * columns * blocks,
            bytes_accessed=blocks * columns * (2 * width + 6 * rows),
            transcendentals=rows * columns * blocks,
        ),
        name="head_backward",
    )(logits, weights, marks, stats)


def head_weights(tops, grads):
    blocks, rows, columns = grads.shape
    width = tops.shape[1]

    def kernel(x_ref, g_ref, out_ref, turned):
        @pl.when(pl.program_id(0) == 0)
        def _():
            turned[...] = x_ref[...].T

        out_ref[...] = matmul(turned[...], g_ref[...]).astype(BF)

    return pl.pallas_call(
        kernel,
        grid=(blocks,),
        out_shape=shape((2, blocks // 2, width, columns), BF),
        in_specs=[
            pl.BlockSpec((rows, width), lambda k: (0, 0)),
            pl.BlockSpec((None, rows, columns), lambda k: (k, 0, 0)),
        ],
        out_specs=pl.BlockSpec((None, None, width, columns), lambda k: (k % 2, k // 2, 0, 0)),
        scratch_shapes=[pltpu.VMEM((width, rows), BF)],
        compiler_params=pltpu.CompilerParams(vmem_limit_bytes=48 * 2**20),
        cost_estimate=pl.CostEstimate(
            flops=2 * rows * width * columns * blocks,
            bytes_accessed=blocks * columns * 2 * (width + rows),
            transcendentals=0,
        ),
        name="head_weights",
    )(tops, grads)


def norm_forward(values, gain):
    inverse = lax.rsqrt(jnp.mean(values * values, axis=-1, keepdims=True) + EPS_NORM)
    normed = values * inverse
    return (normed * gain, normed, inverse)


def norm_backward(grad, normed, inverse, gain):
    scaled = grad * gain
    inner = jnp.mean(scaled * normed, axis=-1, keepdims=True)
    return (inverse * (scaled - normed * inner), jnp.sum(grad * normed, axis=0))


def turn_half(tensor):
    quarter = tensor.shape[-1] // 4
    return jnp.concatenate(
        [
            -tensor[..., quarter : 2 * quarter],
            tensor[..., :quarter],
            -tensor[..., 3 * quarter :],
            tensor[..., 2 * quarter : 3 * quarter],
        ],
        axis=-1,
    )


def rope_tables(positions, width):
    quarter = width // 4
    freq = 10000.0 ** (-jnp.arange(quarter, dtype=F32) / quarter)
    row_angle = (positions // GRID).astype(F32)[:, None] * freq
    col_angle = (positions % GRID).astype(F32)[:, None] * freq
    angles = jnp.concatenate([row_angle, row_angle, col_angle, col_angle], axis=-1)
    return (jnp.cos(angles)[:, None, :], jnp.sin(angles)[:, None, :])


def rotate(tensor, cosine, sine):
    return tensor * cosine + turn_half(tensor) * sine


def rotate_back(grad, cosine, sine):
    return grad * cosine - turn_half(grad * sine)


def masked_scores(query, keys, height):
    scores = jnp.einsum("qhd,khd->hqk", query, keys, preferred_element_type=F32) * HD ** (-0.5)
    places = jnp.arange(query.shape[0])
    allowed = (places[None, :] <= places[:, None]) & (places[None, :] < GRID * height)
    return jnp.where(allowed[None], scores, NEGATIVE_FILL)


def attend(query, keys, values, height):
    scores = masked_scores(query, keys, height)
    score_peak = jnp.max(scores, axis=-1, keepdims=True)
    exponent = jnp.exp(scores - score_peak)
    score_total = jnp.sum(exponent, axis=-1, keepdims=True)
    probs = exponent / score_total
    output = jnp.einsum("hqk,khd->qhd", probs.astype(BF), values, preferred_element_type=F32)
    return (output.astype(BF).reshape(query.shape[0], -1), probs)


def attend_back(query, keys, values, probs, grad_out):
    grad_heads = grad_out.reshape(query.shape)
    grad_probs = jnp.einsum("qhd,khd->hqk", grad_heads, values, preferred_element_type=F32)
    grad_scores = probs * (grad_probs - jnp.sum(probs * grad_probs, axis=-1, keepdims=True))
    grad_scores = grad_scores.astype(BF)
    scale = HD ** (-0.5)
    grad_query = jnp.einsum("hqk,khd->qhd", grad_scores, keys, preferred_element_type=F32) * scale
    grad_keys = jnp.einsum("hqk,qhd->khd", grad_scores, query, preferred_element_type=F32) * scale
    grad_values = jnp.einsum(
        "hqk,qhd->khd", probs.astype(BF), grad_heads, preferred_element_type=F32
    )
    return (grad_query.astype(BF), grad_keys.astype(BF), grad_values.astype(BF))


def adam_update(master, drift, square, grad, rate, decay):
    moment = BETA_ONE * drift + (1.0 - BETA_ONE) * grad
    second = BETA_TWO * square + (1.0 - BETA_TWO) * grad * grad
    stride = (
        moment / (1.0 - BETA_ONE**STEP) / (jnp.sqrt(second / (1.0 - BETA_TWO**STEP)) + ADAM_EPS)
    )
    return (master - rate * (stride + decay * master), moment, second)


def pad_rows(value, rows):
    flat = value.reshape(-1)
    return jnp.pad(flat, (0, rows * 128 - flat.shape[0])).reshape(rows, 128)


def block_form(rows, columns):
    return (rows, columns) if rows % 8 == 0 else (rows * columns // 128, 128)


FIRST_AXES = ("x", "x", "y", "x")


def on_device(dims, *args):
    labels, targets, heights, loss_mask = args[:4]
    masters, drifts, squares = (args[4:12], args[12:20], args[20:28])
    class_table, code_table, attend_in, attend_mix, expand_in, shrink_out, head_weight, norm_gains = masters
    nz, ny, nx = dims
    plane = ny * nx
    chips = nz * plane
    images, local_len = targets.shape
    length = local_len * 2
    width = code_table.shape[1]
    device_codes = code_table.shape[0]
    line_codes = device_codes * plane * 2
    gain_columns = norm_gains.shape[1]
    chip, core = (lax.axis_index("dp"), lax.axis_index("seq"))
    z, y, x = (chip // plane, (chip // nx) % ny, chip % nx)
    plane_groups = [[k * plane + i for i in range(plane)] for k in range(nz)]
    line_groups = [[k * plane + i for k in range(nz)] for i in range(plane)]

    layers = [v.astype(BF) for v in (attend_in, attend_mix, expand_in, shrink_out)]
    tail = jnp.concatenate([labels, heights])
    meta = jnp.concatenate([targets, loss_mask, pad_rows(tail, 4)], axis=0)
    *lines, table, metas = gather_first(dims, layers, code_table.astype(BF), meta, 0)
    table = table.reshape(line_codes, width)

    own_tokens = lax.dynamic_slice_in_dim(metas, core, 1, axis=4)[:, :, :, :, 0]
    own_masks = lax.dynamic_slice_in_dim(metas, 2 + core, 1, axis=4)[:, :, :, :, 0]

    def of_line(value):
        value = lax.dynamic_slice_in_dim(value, y, 1, axis=1)
        return lax.dynamic_slice_in_dim(value, x, 1, axis=2).reshape(nz, -1)

    line_targets = of_line(own_tokens)
    line_heights = of_line(lax.dynamic_slice_in_dim(metas[:, :, :, 0, 4], images + core, 1, axis=3))
    places = jnp.arange(length)
    line_counted = (of_line(own_masks) * (places[None, :] < GRID * line_heights)).astype(F32)
    all_labels = metas[:, :, :, 0, 4, :images].reshape(-1)
    before = jnp.concatenate(
        [jnp.full((nz, 1), -1, jnp.int32), line_targets[:, :-1] - z * line_codes], axis=1
    ).reshape(-1)
    code_pick = (before[:, None] == jnp.arange(line_codes)[None, :]).astype(BF)
    rows = matmul(code_pick, table).astype(BF).reshape(nz, length, width)
    class_pick = all_labels[:, None] == jnp.arange(class_table.shape[0])[None, :]
    class_part = matmul(class_pick.astype(BF), class_table.astype(BF))
    gains_low = norm_gains.astype(BF).astype(F32)
    small = jnp.concatenate([pad_rows(class_part, 6), pad_rows(gains_low, 2)], axis=0)

    *weights, row_parts, smalls = gather_second(dims, lines, FIRST_AXES, rows, small, 1)
    qkv_w, mix_w, expand_w, shrink_w = (v.reshape(-1, v.shape[-1]) for v in weights)
    head_low, smalls = lax.optimization_barrier((head_weight.astype(BF), smalls))
    head_near = lax.all_gather(head_low, "dp", axis_index_groups=plane_groups)
    head_near = lax.all_gather(head_near, "seq")
    smalls = smalls.reshape(chips * 2, -1)
    class_rows = smalls[:, : 6 * 128].reshape(chips * 2, chips * images, -1)
    class_row = lax.dynamic_slice_in_dim(class_rows, chip * images + core, 1, axis=1).reshape(1, -1)
    gain = smalls[:, 6 * 128 : 6 * 128 + 3 * gain_columns].reshape(chips * 2, 3, gain_columns)
    gain = gain.transpose(1, 0, 2).reshape(3, -1)
    start = jnp.sum(row_parts.astype(F32), axis=0)
    start = jnp.where((places == 0)[:, None], class_row, start)
    height = lax.dynamic_slice_in_dim(line_heights, z, 1, axis=0).reshape(())

    cosine, sine = rope_tables(places, HD)
    normed_one, norm_one, inverse_one = norm_forward(start, gain[0])
    normed_one = normed_one.astype(BF)
    mixed = matmul(normed_one, qkv_w).reshape(length, 3, -1, HD)
    query = rotate(mixed[:, 0], cosine, sine).astype(BF)
    keys = rotate(mixed[:, 1], cosine, sine).astype(BF)
    values = mixed[:, 2].astype(BF)
    attended, probs = attend(query, keys, values, height)
    middle = start + matmul(attended, mix_w)
    normed_two, norm_two, inverse_two = norm_forward(middle, gain[1])
    normed_two = normed_two.astype(BF)
    both = matmul(normed_two, expand_w)
    inner = both.shape[1] // 2
    gate_part, up_part = (both[:, :inner], both[:, inner:])
    hidden = (jax.nn.silu(gate_part) * up_part).astype(BF)
    final = middle + matmul(hidden, shrink_w)
    normed_top, norm_top, inverse_top = norm_forward(final, gain[2])
    normed_top = normed_top.astype(BF)

    tops = line_gather(dims, normed_top, 2, "top_rows").reshape(nz * length, width)
    marks = (line_targets - z * line_codes).reshape(-1, 1)
    logits, stats = head_forward(tops, head_near, marks)
    stats = line_gather(dims, stats, 3, "row_stats")
    peaks = jnp.max(stats[:, 0], axis=0)
    totals = jnp.sum(stats[:, 1] * jnp.exp(stats[:, 0] - peaks[None, :]), axis=0)
    log_total = peaks + jnp.log(totals)
    counted = line_counted.reshape(-1)
    losses = (log_total - jnp.sum(stats[:, 2], axis=0)) * counted
    loss_local = jnp.sum(lax.dynamic_slice_in_dim(losses.reshape(nz, -1), z, 1, axis=0))
    count_local = jnp.sum(lax.dynamic_slice_in_dim(line_counted, z, 1, axis=0))
    scales = jnp.stack([peaks, counted / totals, counted])
    scales = jnp.pad(scales, ((0, 5), (0, 0)))
    grad_logits, grad_tops = head_backward(logits, head_near, marks, scales)
    grad_tops = grad_tops.reshape(nz, length, width)
    grad_top = lax.psum_scatter(grad_tops, "dp", axis_index_groups=line_groups)
    grad_head = head_weights(tops, grad_logits)
    grad_head = lax.psum_scatter(grad_head, "seq", scatter_dimension=0)
    grad_head = lax.psum_scatter(grad_head, "dp", axis_index_groups=plane_groups)

    grad_final, gain_top = norm_backward(grad_top.astype(F32), norm_top, inverse_top, gain[2])
    back_down = grad_final.astype(BF)
    grad_shrink = matmul(hidden.T, back_down)
    grad_hidden = matmul(back_down, shrink_w.T)
    sigma = jax.nn.sigmoid(gate_part)
    grad_gate = grad_hidden * up_part * sigma * (1.0 + gate_part * (1.0 - sigma))
    grad_up = grad_hidden * gate_part * sigma
    grad_both = jnp.concatenate([grad_gate, grad_up], axis=1).astype(BF)
    grad_expand = matmul(normed_two.T, grad_both)
    grad_norm_two, gain_two = norm_backward(
        matmul(grad_both, expand_w.T), norm_two, inverse_two, gain[1]
    )
    grad_middle = grad_final + grad_norm_two
    back_mix = grad_middle.astype(BF)
    grad_mix = matmul(attended.T, back_mix)
    grad_attended = matmul(back_mix, mix_w.T).astype(BF)
    grad_query, grad_keys, grad_values = attend_back(query, keys, values, probs, grad_attended)
    grad_mixed = jnp.stack(
        [
            rotate_back(grad_query.astype(F32), cosine, sine).astype(BF),
            rotate_back(grad_keys.astype(F32), cosine, sine).astype(BF),
            grad_values,
        ],
        axis=1,
    ).reshape(length, -1)
    grad_qkv = matmul(normed_one.T, grad_mixed)
    grad_norm_one, gain_one = norm_backward(
        matmul(grad_mixed, qkv_w.T), norm_one, inverse_one, gain[0]
    )
    grad_start = grad_middle + grad_norm_one

    grads_in = []
    for grad, shard in zip((grad_qkv, grad_mix, grad_expand, grad_shrink), layers):
        grads_in.append(grad.astype(BF).reshape(dims + (2,) + block_form(*shard.shape)))
    small = jnp.concatenate(
        [
            pad_rows(grad_start[0], width // 128),
            pad_rows(jnp.concatenate([gain_one, gain_two, gain_top]), 3 * width // 128),
        ],
        axis=0,
    )
    *line_grads, row_grads, smalls = scatter_first(
        dims, grads_in, FIRST_AXES, grad_start.astype(BF), small, 4
    )
    row_grads = row_grads.reshape(nz * length, width)
    table_grad = lax.dot_general(
        code_pick, row_grads, (((0,), (0,)), ((), ())), preferred_element_type=F32
    )
    table_grad = table_grad.astype(BF).reshape(ny, nx, 2, device_codes, width)
    smalls = smalls.reshape(chips * 2, 4, -1)
    device = chip * 2 + core
    small_mine = lax.dynamic_slice_in_dim(smalls, device * gain_columns, gain_columns, axis=2)
    class_share = jnp.dot(
        class_pick.astype(F32).T,
        small_mine[:, 0],
        precision=lax.Precision.HIGHEST,
        preferred_element_type=F32,
    )
    gain_share = jnp.sum(small_mine[:, 1:], axis=0)
    square_local = jnp.sum(class_share * class_share) + jnp.sum(gain_share * gain_share)
    partial = pad_rows(jnp.stack([square_local, loss_local, count_local]), 8)
    *layer_shares, code_share, sums = scatter_second(
        dims, line_grads, table_grad, grad_head, partial, 5
    )
    layer_shares = [g.reshape(v.shape) for g, v in zip(layer_shares, layers)]
    shares = (class_share, code_share, *layer_shares, grad_head.astype(F32), gain_share)
    total_square, loss_sum, loss_count = (sums[0, 0], sums[0, 1], sums[0, 2])
    grad_norm = jnp.sqrt(total_square) / loss_count
    factor = CLIP_NORM / jnp.maximum(grad_norm, CLIP_NORM) / loss_count
    news, firsts, seconds = ([], [], [])
    for member in range(8):
        fresh, moment, second = adam_update(
            masters[member],
            drifts[member],
            squares[member],
            shares[member] * factor,
            RATES[member],
            DECAYS[member],
        )
        news.append(fresh)
        firsts.append(moment)
        seconds.append(second)
    return tuple(news) + tuple(firsts) + tuple(seconds) + (grad_norm, loss_sum, loss_count)


def solution(mesh):
    rows, columns = (P(("dp", "seq"), None), P(None, ("dp", "seq")))
    eight = (columns, rows, rows, rows, rows, rows, columns, columns)
    return jax.shard_map(
        functools.partial(on_device, dims_of(mesh.shape["dp"])),
        mesh=mesh,
        in_specs=(P("dp"), P("dp", "seq"), P("dp"), P("dp", "seq")) + eight * 3,
        out_specs=eight * 3 + (P(), P(), P()),
        check_vma=False,
    )
```

```python
import functools

import jax
import jax.numpy as jnp
from jax import lax
from jax.experimental import pallas as pl
from jax.experimental.pallas import tpu as pltpu
from jax.sharding import PartitionSpec as P

HD = 64
GRID = 16
STEP = 10

EPS_NORM = 1e-05
BETA_ONE = 0.9
BETA_TWO = 0.95
ADAM_EPS = 1e-08
CLIP_NORM = 0.01
NEGATIVE_FILL = -1000000000.0
RATES = (0.8, 0.8, 0.08, 0.08, 0.08, 0.08, 0.08, 0.8)
DECAYS = (0.1, 0.1, 0.1, 0.1, 0.1, 0.1, 0.1, 0.0)

MESH = pl.DeviceIdType.MESH
ANY = pl.BlockSpec(memory_space=pl.ANY)
VMEM = pl.BlockSpec(memory_space=pltpu.VMEM)
BF = jnp.bfloat16
F32 = jnp.float32


def dims_of(dp):
    bits = dp.bit_length() - 1
    nz = 1 << (bits // 2)
    rest = dp // nz
    ny = 1 << ((rest.bit_length() - 1) // 2)
    return (nz, ny, rest // ny)


class Place:
    def __init__(self, dims):
        self.dims = dims
        nz, ny, nx = dims
        chip = lax.axis_index("dp")
        self.c = lax.axis_index("seq")
        self.z = chip // (ny * nx)
        self.y = (chip // nx) % ny
        self.x = chip % nx

    def zs(self, back):
        return (self.z + self.dims[0] - back) % self.dims[0]

    def ys(self, back):
        return (self.y + self.dims[1] - back) % self.dims[1]

    def xs(self, back):
        return (self.x + self.dims[2] - back) % self.dims[2]

    def dev(self, z=0, y=0, x=0, c=0):
        nz, ny, nx = self.dims
        z, y, x = ((self.z + z) % nz, (self.y + y) % ny, (self.x + x) % nx)
        return ((z * ny + y) * nx + x, (self.c + c) % 2)


def line_offsets(dims):
    nz, ny, nx = dims
    return (
        [(s, 0, 0, 0) for s in range(1, nz)]
        + [(0, s, 0, 0) for s in range(1, ny)]
        + [(0, 0, s, 0) for s in range(1, nx)]
        + [(0, 0, 0, 1)]
    )


def plane_offsets(dims):
    return [(0, v, u, 0) for v in range(dims[1]) for u in range(dims[2]) if v or u]


def greet(place, offsets):
    offsets = sorted(set(offsets))
    sem = pltpu.get_barrier_semaphore()
    for off in offsets:
        pl.semaphore_signal(sem, inc=1, device_id=place.dev(*off), device_id_type=MESH)
    pl.semaphore_wait(sem, len(offsets))


class Comm:
    def __init__(self, send_sems, recv_sems, local_sems):
        self.send_sems, self.recv_sems, self.local_sems = (send_sems, recv_sems, local_sems)
        self.sent, self.held, self.count, self.locals = ([], [], 0, 0)

    def send(self, src, dst, device):
        k = self.count
        self.count += 1
        copy = pltpu.make_async_remote_copy(
            src_ref=src,
            dst_ref=dst,
            send_sem=self.send_sems.at[k],
            recv_sem=self.recv_sems.at[k],
            device_id=device,
            device_id_type=MESH,
        )
        copy.start()
        self.sent.append(copy)
        return copy

    def keep(self, src, dst):
        copy = pltpu.make_async_copy(src, dst, self.local_sems.at[self.locals])
        self.locals += 1
        copy.start()
        self.held.append(copy)
        return copy

    def done(self, copy):
        copy.wait()
        self.held = [other for other in self.held if other is not copy]

    def finish(self):
        for copy in self.sent:
            copy.wait_send()
        for copy in self.held:
            copy.wait()


def all_offsets(dims):
    nz, ny, nx = dims
    spots = [(k, j, i, core) for k in range(nz) for j in range(ny) for i in range(nx) for core in range(2)]
    return spots[1:]


def small_exchange(comm, place, src, out, own):
    z, y, x, c = (place.z, place.y, place.x, place.c)
    nz, ny, nx = place.dims
    if own:
        comm.keep(src(z, y, x, c), out.at[z, y, x, c])
    got = []
    for off in all_offsets(place.dims):
        there = (place.zs(nz - off[0]), place.ys(ny - off[1]), place.xs(nx - off[2]), (c + off[3]) % 2)
        got.append(comm.send(src(*there), out.at[z, y, x, c], place.dev(*off)))
    return got


class PlaneGather:
    def __init__(self, comm, place):
        self.comm, self.place = (comm, place)
        self.firsts, self.seconds, self.mates = ([], [], [])

    def ways(self, axis):
        _, ny, nx = self.place.dims
        return range(1, ny if axis == "y" else nx)

    def back(self, axis, t, yy, xx):
        return (self.place.ys(t), xx) if axis == "y" else (yy, self.place.xs(t))

    def spread(self, block, first, src=None):
        place, second = (self.place, "y" if first == "x" else "x")
        dst = block(place.y, place.x)
        src = dst if src is None else src
        for t in self.ways(first):
            copy = self.comm.send(src, dst, place.dev(**{first: t}))
            self.firsts.append((block, first, second, t, copy))
        for t in self.ways(second):
            copy = self.comm.send(src, dst, place.dev(**{second: t}))
            self.seconds.append((block(*self.back(second, t, place.y, place.x)), copy))
        self.mates.append(self.comm.send(src, dst, place.dev(c=1)))

    def forward(self):
        place = self.place
        for block, first, second, t, copy in self.firsts:
            copy.wait_recv()
            yy, xx = self.back(first, t, place.y, place.x)
            held = block(yy, xx)
            for u in self.ways(second):
                copy = self.comm.send(held, held, place.dev(**{second: u}))
                self.seconds.append((block(*self.back(second, u, yy, xx)), copy))
            self.mates.append(self.comm.send(held, held, place.dev(c=1)))
        self.firsts = []

    def settle(self):
        for held, copy in self.seconds:
            copy.wait_recv()
            self.mates.append(self.comm.send(held, held, self.place.dev(c=1)))
        self.seconds = []

    def forward_some(self, count):
        rest = self.firsts[count:]
        self.firsts = self.firsts[:count]
        self.forward()
        self.firsts = rest

    def arrive(self):
        for copy in self.mates:
            copy.wait_recv()
        self.mates = []


def sems(count):
    return pltpu.SemaphoreType.DMA((count,))


def shape(dims, dtype):
    return jax.ShapeDtypeStruct(tuple(dims), dtype)


def call(kernel, outs, in_specs, out_specs, scratch, cid, name, args, vmem=None):
    return pl.pallas_call(
        kernel,
        out_shape=outs,
        in_specs=in_specs,
        out_specs=out_specs,
        scratch_shapes=scratch,
        compiler_params=pltpu.CompilerParams(
            collective_id=cid, has_side_effects=True, vmem_limit_bytes=vmem
        ),
        name=name,
    )(*args)


def small_sends(dims):
    return dims[0] * dims[1] * dims[2] * 2 - 1


def gather_all(dims, layers, first_axes, table, classes, gains, meta, images, cid):
    nz, ny, nx = dims
    n = len(layers)
    rows, width = table.shape
    length = meta.shape[1] * 2
    count_images = nz * ny * nx * images
    label_rows = -(-count_images // 128)
    groups = [(k,) for k in range(nz)] if nz <= 4 else [tuple(range(nz))]

    def kernel(*refs):
        ins, rest = (refs[:n], refs[n:])
        table_in, class_in, gain_in, meta_in, *rest = rest
        outs, rest = (rest[:n], rest[n:])
        parts_out, meta_out, small_out, *rest = rest
        low, rest = (rest[:n], rest[n:])
        whole, found, total, class_low, gain_row, small_in, ssem, rsem, lsem = rest
        place = Place(dims)
        z, y, x, c = (place.z, place.y, place.x, place.c)
        greet(place, all_offsets(dims))
        comm = Comm(ssem, rsem, lsem)
        metas = small_exchange(comm, place, lambda *spot: meta_in, meta_out, False)
        meta_out[z, y, x, c] = meta_in[...]
        waits = []
        whole[y, x, c] = table_in[...].astype(BF)
        tables, blocks = (PlaneGather(comm, place), PlaneGather(comm, place))
        for first, start in (("x", 0), ("y", rows // 2)):
            half = pl.ds(start, rows // 2)
            tables.spread(lambda yy, xx, half=half: whole.at[yy, xx, c, half], first)
        for a in range(n):
            low[a][...] = ins[a][...].astype(BF)
        along = {}
        for s in range(1, nz):
            for a in range(n):
                along[s, a] = comm.send(low[a], outs[a].at[z, y, x, c], place.dev(z=s))
        kept = [comm.keep(low[a], outs[a].at[z, y, x, c]) for a in range(n)]

        def spread(group):
            for a in range(n):
                for k in group:
                    if k:
                        along[k, a].wait_recv()
                if len(group) > 1:
                    comm.done(kept[a])
                    at = pl.ds(0, nz)
                else:
                    at = place.zs(group[0])
                blocks.spread(
                    lambda yy, xx, a=a, at=at: outs[a].at[at, yy, xx, c],
                    first_axes[a],
                    low[a] if group == (0,) else None,
                )

        for copy in metas:
            copy.wait_recv()

        class_low[...] = jnp.zeros_like(class_low)
        class_low[0 : class_in.shape[0], 0 : class_in.shape[1]] = class_in[...]
        small_in[...] = jnp.zeros_like(small_in)
        for r in range(label_rows):
            labels = jnp.zeros((1, 128), jnp.int32)
            for k in range(nz * ny * nx):
                labels = labels + meta_out[k // (ny * nx), k // nx % ny, k % nx, 0, 5 + r : 6 + r, :]
            pick = lax.broadcasted_iota(jnp.int32, (class_low.shape[0], 128), 0) == labels
            picked = lax.dot_general(
                jnp.where(pick, 1.0, 0.0).astype(BF),
                class_low[...].astype(BF),
                (((0,), (0,)), ((), ())),
                preferred_element_type=F32,
            )
            for i in range(min(128, count_images - 128 * r)):
                k, core = divmod(128 * r + i, 2)
                small_in[k // (ny * nx), k // nx % ny, k % nx, core, 0:1, :] = picked[i : i + 1]
        gain_row[...] = jnp.zeros_like(gain_row)
        gain_row[0:3, 0 : gain_in.shape[1]] = gain_in[...].astype(BF).astype(F32)

        @pl.loop(0, nz)
        def _(k):
            for j in range(ny):
                for i in range(nx):
                    for core in range(2):
                        small_in[k, j, i, core, 1:4, :] = gain_row[0:3]

        waits += small_exchange(comm, place, lambda *spot: small_in.at[spot], small_out, True)

        size = len(layers)
        steps = [lambda group=group: spread(group) for group in groups]
        steps.pop(0)()
        tables.forward()
        if steps:
            steps.pop(0)()
        blocks.forward_some(size)
        if steps:
            steps.pop(0)()
        tables.settle()
        blocks.forward_some(size)
        for step in steps:
            step()
        tables.arrive()

        for s in range(1, nz + 1):
            zz = place.zs(s % nz)
            columns = []
            for half in range(2):
                codes = meta_out[zz, y, x, half, pl.ds(c, 1), :].astype(F32)
                columns.append(jnp.broadcast_to(codes, (128, meta.shape[1])).T)
            column = jnp.concatenate(columns, axis=0)
            column = column - (z * ny * nx * 2 * rows).astype(F32)
            total[...] = jnp.zeros_like(total)

            @pl.loop(0, ny * nx * 2)
            def _(j):
                base = (j * rows).astype(F32)
                lane = lax.broadcasted_iota(jnp.int32, (length, 128), 1).astype(F32) + base
                picks = [
                    jnp.where(column == lane + float(128 * q), 1.0, 0.0).astype(BF)
                    for q in range(-(-rows // 128))
                ]
                pick = jnp.concatenate(picks, axis=1)[:, :rows]
                total[...] += matmul(pick, whole[j // (2 * nx), j // 2 % nx, j % 2])

            found[s % nz] = total[...].astype(BF)
            if s < nz:
                waits.append(comm.send(found.at[s], parts_out.at[nz - s], place.dev(z=nz - s)))
            blocks.forward_some(size)
        comm.keep(found.at[0], parts_out.at[0])
        blocks.forward()
        blocks.settle()
        blocks.arrive()
        for copy in waits:
            copy.wait_recv()
        comm.finish()

    count = n * (nz - 1) + (n * len(groups) + 2) * (2 * ny * nx - 1) + nz + 2 * small_sends(dims)
    small = dims + (2, 8, 128)
    outs = [shape(dims + (2,) + v.shape, BF) for v in layers]
    outs += [
        shape((nz, length, width), BF),
        shape(dims + (2,) + meta.shape, meta.dtype),
        shape(small, F32),
    ]
    scratch = [pltpu.VMEM(v.shape, BF) for v in layers]
    scratch += [
        pltpu.VMEM((ny, nx, 2) + table.shape, BF),
        pltpu.VMEM((nz, length, width), BF),
        pltpu.VMEM((length, width), F32),
        pltpu.VMEM((-(-classes.shape[0] // 128) * 128, 128), F32),
        pltpu.VMEM((8, 128), F32),
        pltpu.VMEM(small, F32),
        sems(count),
        sems(count),
        sems(n + 3),
    ]
    return call(
        kernel, outs, [VMEM] * (n + 4), [ANY] * (n + 1) + [VMEM] * 2, scratch,
        cid, "gather_all", (*layers, table, classes, gains, meta), 60 * 2**20,
    )


def line_gather(dims, block, cid, name):
    nz = dims[0]

    def kernel(src, out, ssem, rsem, lsem):
        place = Place(dims)
        greet(place, [(s, 0, 0, 0) for s in range(1, nz)])
        comm = Comm(ssem, rsem, lsem)
        waits = [comm.send(src, out.at[place.z], place.dev(z=s)) for s in range(1, nz)]
        comm.keep(src, out.at[place.z])
        for copy in waits:
            copy.wait_recv()
        comm.finish()

    return call(
        kernel, shape((nz,) + block.shape, block.dtype), [ANY], ANY,
        [sems(nz), sems(nz), sems(1)], cid, name, (block,),
    )


def head_gather(dims, block, head, cid):
    nz, ny, nx = dims
    rows = head.shape[0]

    def kernel(src, head_in, out, whole, low, ssem, rsem, lsem):
        place = Place(dims)
        z, y, x, c = (place.z, place.y, place.x, place.c)
        greet(place, line_offsets(dims))
        comm = Comm(ssem, rsem, lsem)
        low[...] = head_in[...].astype(BF)
        comm.keep(low, whole.at[c, y, x])
        gather = PlaneGather(comm, place)
        for first, start in (("x", 0), ("y", rows // 2)):
            half = pl.ds(start, rows // 2)
            gather.spread(lambda yy, xx, half=half: whole.at[c, yy, xx, half], first, low.at[half])
        waits = [comm.send(src, out.at[z], place.dev(z=s)) for s in range(1, nz)]
        comm.keep(src, out.at[z])
        gather.forward()
        gather.settle()
        gather.arrive()
        for copy in waits:
            copy.wait_recv()
        comm.finish()

    count = nz + 2 * (2 * ny * nx - 1)
    return call(
        kernel,
        [shape((nz,) + block.shape, BF), shape((2, ny, nx) + head.shape, BF)],
        [ANY, VMEM], [ANY, ANY],
        [pltpu.VMEM(head.shape, BF), sems(count), sems(count), sems(2)],
        cid, "head_gather", (block, head), 48 * 2**20,
    )


def add_blocks(out, terms):
    lead = out.shape[:-2]

    def visit(index):
        if len(index) < len(lead):

            @pl.loop(0, lead[len(index)])
            def _(i):
                visit(index + (i,))

        else:
            if len(terms) == 2 and out.dtype == BF:
                out[index] = terms[0][index] + terms[1][index]
                return
            total = terms[0][index].astype(F32)
            for term in terms[1:]:
                total = total + term[index].astype(F32)
            out[index] = total.astype(out.dtype)

    visit(())


def scatter_all(dims, grads, first_axes, rows, codes, head, small, same, partial, device_codes, cid):
    nz, ny, nx = dims
    n = len(grads)
    length, width = rows.shape
    block = (device_codes, width)
    parts = 2 if nz <= 4 else 1
    step = nz // parts
    items = [(a, g) for g in range(parts) for a in range(n)]

    def kernel(*refs):
        ins, rest = (refs[:n], refs[n:])
        rows_in, codes_in, head_in, small_in, same_in, partial_in, *rest = rest
        outs, rest = (rest[:n], rest[n:])
        table_out, small_out, sums, *rest = rest
        halves, ones, twos, threes, rest = (
            rest[:n], rest[n : 2 * n], rest[2 * n : 3 * n], rest[3 * n : 4 * n], rest[4 * n :]
        )
        lined, given, own, half, near, tops, mixed, mine, every, ssem, rsem, lsem = rest
        place = Place(dims)
        z, y, x, c = (place.z, place.y, place.x, place.c)
        offsets = plane_offsets(dims)
        greet(place, all_offsets(dims))
        comm = Comm(ssem, rsem, lsem)
        pair, got_one, got_two = ({}, {}, {})
        waits = small_exchange(comm, place, lambda *spot: small_in.at[spot], small_out, True)
        for a, g in items:
            span = pl.ds(g * step, step)
            pair[a, g] = comm.send(ins[a].at[span, :, :, 1 - c], halves[a].at[span], place.dev(c=1))
        lines = [comm.send(rows_in, lined.at[s], place.dev(z=s)) for s in range(1, nz)]
        lined[0] = rows_in[...]

        def first_step(a, g):
            span = pl.ds(g * step, step)
            pair[a, g].wait_recv()
            add_blocks(halves[a].at[span], [halves[a].at[span], ins[a].at[span, :, :, c]])
            if first_axes[a] == "y":
                got_one[a, g] = [
                    comm.send(halves[a].at[span, place.ys(ny - t)], ones[a].at[t - 1, span], place.dev(y=t))
                    for t in range(1, ny)
                ]
            else:
                got_one[a, g] = [
                    comm.send(halves[a].at[span, :, place.xs(nx - t)], ones[a].at[t - 1, span], place.dev(x=t))
                    for t in range(1, nx)
                ]

        def second_step(a, g):
            span = pl.ds(g * step, step)
            for copy in got_one[a, g]:
                copy.wait_recv()
            if first_axes[a] == "y":
                held = halves[a].at[span, y]
                add_blocks(held, [held] + [ones[a].at[t, span] for t in range(ny - 1)])
                got_two[a, g] = [
                    comm.send(halves[a].at[span, y, place.xs(nx - t)], twos[a].at[t - 1, span], place.dev(x=t))
                    for t in range(1, nx)
                ]
            else:
                held = halves[a].at[span, :, x]
                add_blocks(held, [held] + [ones[a].at[t, span] for t in range(nx - 1)])
                got_two[a, g] = [
                    comm.send(halves[a].at[span, place.ys(ny - t), x], twos[a].at[t - 1, span], place.dev(y=t))
                    for t in range(1, ny)
                ]

        for a, g in items:
            first_step(a, g)
        for a, g in items[: len(items) // 2]:
            second_step(a, g)

        for copy in lines:
            copy.wait_recv()
        held_codes = codes_in[...]
        flat = jnp.concatenate([held_codes[k : k + 1] for k in range(nz * length // 128)], axis=1)

        def product(into, core):
            @pl.loop(0, ny * nx)
            def _(j):
                code = lax.broadcasted_iota(jnp.int32, (device_codes, nz * length), 0)
                pick = code + (j * 2 + core) * device_codes == flat
                pick = jnp.where(pick, 1.0, 0.0).astype(BF)
                value = matmul(pick, lined[...].reshape(nz * length, width))
                into[j // nx, j % nx] = value.astype(BF)

        product(given, 1 - c)
        table_pair = comm.send(given, half, place.dev(c=1))
        product(own, c)
        for a, g in items[len(items) // 2 :]:
            second_step(a, g)
        table_pair.wait_recv()
        add_blocks(half, [half, own])
        arriving = [
            comm.send(half.at[place.ys(ny - off[1]), place.xs(nx - off[2])], near.at[k], place.dev(*off))
            for k, off in enumerate(offsets)
        ]

        third = {}
        for a in range(n):
            for g in range(parts):
                span = pl.ds(g * step, step)
                for copy in got_two[a, g]:
                    copy.wait_recv()
                held = halves[a].at[span, y, x]
                add_blocks(held, [held] + [twos[a].at[t, span] for t in range(twos[a].shape[0])])
            third[a] = [
                comm.send(halves[a].at[place.zs(nz - s), y, x], threes[a].at[s - 1], place.dev(z=s))
                for s in range(1, nz)
            ]
        for copy in waits:
            copy.wait_recv()
        comm.done(comm.held[0])
        mixed[...] = jnp.zeros_like(mixed)

        @pl.loop(0, nz)
        def _(k):
            for j in range(ny):
                for i in range(nx):
                    for core in range(2):
                        at = ((k * ny + j) * nx + i) * 2 + core
                        tops[pl.ds(at, 1), :] = small_out[k, j, i, core, 0:1, :]
                        mixed[...] += small_out[k, j, i, core]

        summed = jnp.dot(
            same_in[...], tops[...], precision=lax.Precision.HIGHEST, preferred_element_type=F32
        )
        row = lax.broadcasted_iota(jnp.int32, mixed.shape, 0)
        gained = jnp.where((row >= 1) & (row < 4), mixed[...], 0.0)
        square = jnp.sum(summed * tops[...]) + jnp.sum(gained * gained)
        share = head_in[...].astype(F32)
        square = square + jnp.sum(share * share)
        for a in range(n):
            for copy in third[a]:
                copy.wait_recv()
            add_blocks(outs[a], [halves[a].at[z, y, x]] + [threes[a].at[s] for s in range(nz - 1)])
            square = square + jnp.sum(outs[a][...] * outs[a][...])
        for copy in arriving:
            copy.wait_recv()
        add_blocks(table_out, [half.at[y, x]] + [near.at[k] for k in range(len(offsets))])
        square = square + jnp.sum(table_out[...] * table_out[...])
        first = (lax.broadcasted_iota(jnp.int32, mine.shape, 0) == 0) & (
            lax.broadcasted_iota(jnp.int32, mine.shape, 1) == 0
        )
        mine[...] = partial_in[...] + jnp.where(first, square, 0.0)
        for copy in small_exchange(comm, place, lambda *spot: mine, every, False):
            copy.wait_recv()
        every[z, y, x, c] = mine[...]
        sums[...] = jnp.zeros_like(sums)

        @pl.loop(0, nz)
        def _(k):
            for j in range(ny):
                for i in range(nx):
                    sums[...] += every[k, j, i, 0] + every[k, j, i, 1]

        comm.finish()

    count = n * (parts * (ny + nx - 1) + nz - 1) + nz + ny * nx + 2 * small_sends(dims)
    trail = [g.shape[4:] for g in grads]
    near_far = [(ny, nx) if axis == "y" else (nx, ny) for axis in first_axes]
    scratch = [pltpu.VMEM((nz, ny, nx) + t, BF) for t in trail]
    scratch += [pltpu.VMEM((u - 1, nz, v) + t, BF) for t, (u, v) in zip(trail, near_far)]
    scratch += [pltpu.VMEM((v - 1, nz) + t, BF) for t, (u, v) in zip(trail, near_far)]
    scratch += [pltpu.VMEM((nz - 1,) + t, BF) for t in trail]
    scratch += [
        pltpu.VMEM((nz, length, width), BF),
        pltpu.VMEM((ny, nx) + block, BF),
        pltpu.VMEM((ny, nx) + block, BF),
        pltpu.VMEM((ny, nx) + block, BF),
        pltpu.VMEM((ny * nx - 1,) + block, BF),
        pltpu.VMEM((same.shape[0], 128), F32),
        pltpu.VMEM((8, 128), F32),
        pltpu.VMEM(partial.shape, F32),
        pltpu.VMEM(dims + (2,) + partial.shape, F32),
        sems(count),
        sems(count),
        sems(2),
    ]
    outs = [shape(t, F32) for t in trail]
    outs += [shape(block, F32), shape(small.shape, F32), shape(partial.shape, F32)]
    return call(
        kernel, outs, [VMEM] * (n + 6), [VMEM] * (n + 3), scratch,
        cid, "scatter_all", (*grads, rows, codes, head, small, same, partial), 62 * 2**20,
    )


def matmul(left, right):
    return jnp.dot(left, right, preferred_element_type=F32)


def head_forward(tops, weights, marks):
    cores, plane, width, columns = weights.shape
    rows = tops.shape[0]
    blocks = cores * plane

    def kernel(x_ref, w_ref, mark_ref, logit_ref, stat_ref, peak, total, picked):
        k = pl.program_id(0)

        @pl.when(k == 0)
        def _():
            peak[...] = jnp.full_like(peak, -jnp.inf)
            total[...] = jnp.zeros_like(total)
            picked[...] = jnp.zeros_like(picked)

        logits = matmul(x_ref[...], w_ref[...])
        logit_ref[...] = logits
        lanes = lax.broadcasted_iota(jnp.int32, logits.shape, 1) + k * columns
        chosen = jnp.where(lanes == mark_ref[...], logits, 0.0)
        picked[...] += jnp.sum(chosen, axis=1, keepdims=True)
        old = peak[...]
        new = jnp.maximum(old, jnp.max(logits, axis=1, keepdims=True))
        exponent = jnp.sum(jnp.exp(logits - new), axis=1, keepdims=True)
        total[...] = total[...] * jnp.exp(old - new) + exponent
        peak[...] = new

        @pl.when(k == blocks - 1)
        def _():
            lane = lax.broadcasted_iota(jnp.int32, (rows, 128), 1)
            table = jnp.where(lane == 0, peak[...], jnp.where(lane == 1, total[...], picked[...]))
            stat_ref[...] = table.T[:8]

    return pl.pallas_call(
        kernel,
        grid=(blocks,),
        out_shape=[shape((blocks, rows, columns), F32), shape((8, rows), F32)],
        in_specs=[
            pl.BlockSpec((rows, width), lambda k: (0, 0)),
            pl.BlockSpec((None, None, width, columns), lambda k: (k % 2, k // 2, 0, 0)),
            pl.BlockSpec((rows, 1), lambda k: (0, 0)),
        ],
        out_specs=[
            pl.BlockSpec((None, rows, columns), lambda k: (k, 0, 0)),
            pl.BlockSpec((8, rows), lambda k: (0, 0)),
        ],
        scratch_shapes=[pltpu.VMEM((rows, 1), F32)] * 3,
        compiler_params=pltpu.CompilerParams(vmem_limit_bytes=48 * 2**20),
        cost_estimate=pl.CostEstimate(
            flops=2 * rows * width * columns * blocks,
            bytes_accessed=blocks * columns * (2 * width + 4 * rows),
            transcendentals=rows * columns * blocks,
        ),
        name="head_forward",
    )(tops, weights, marks)


def head_backward(logits, weights, marks, stats):
    blocks, rows, columns = logits.shape
    width = weights.shape[2]

    def kernel(l_ref, w_ref, mark_ref, stat_ref, grad_ref, top_ref, column, total):
        k = pl.program_id(0)

        @pl.when(k == 0)
        def _():
            column[...] = jnp.concatenate([stat_ref[...]] * 16, axis=0).T
            total[...] = jnp.zeros_like(total)

        held = column[...]
        soft = jnp.exp(l_ref[...] - held[:, 0:1]) * held[:, 1:2]
        lanes = lax.broadcasted_iota(jnp.int32, soft.shape, 1) + k * columns
        grad = (soft - jnp.where(lanes == mark_ref[...], held[:, 2:3], 0.0)).astype(BF)
        grad_ref[...] = grad
        total[...] += lax.dot_general(
            grad, w_ref[...], (((1,), (1,)), ((), ())), preferred_element_type=F32
        )

        @pl.when(k == blocks - 1)
        def _():
            top_ref[...] = total[...].astype(BF)

    return pl.pallas_call(
        kernel,
        grid=(blocks,),
        out_shape=[shape(logits.shape, BF), shape((rows, width), BF)],
        in_specs=[
            pl.BlockSpec((None, rows, columns), lambda k: (k, 0, 0)),
            pl.BlockSpec((None, None, width, columns), lambda k: (k % 2, k // 2, 0, 0)),
            pl.BlockSpec((rows, 1), lambda k: (0, 0)),
            pl.BlockSpec((8, rows), lambda k: (0, 0)),
        ],
        out_specs=[
            pl.BlockSpec((None, rows, columns), lambda k: (k, 0, 0)),
            pl.BlockSpec((rows, width), lambda k: (0, 0)),
        ],
        scratch_shapes=[pltpu.VMEM((rows, 128), F32), pltpu.VMEM((rows, width), F32)],
        compiler_params=pltpu.CompilerParams(vmem_limit_bytes=48 * 2**20),
        cost_estimate=pl.CostEstimate(
            flops=2 * rows * width * columns * blocks,
            bytes_accessed=blocks * columns * (2 * width + 6 * rows),
            transcendentals=rows * columns * blocks,
        ),
        name="head_backward",
    )(logits, weights, marks, stats)


def head_weights(tops, grads):
    blocks, rows, columns = grads.shape
    width = tops.shape[1]

    def kernel(x_ref, g_ref, out_ref, turned):
        @pl.when(pl.program_id(0) == 0)
        def _():
            turned[...] = x_ref[...].T

        out_ref[...] = matmul(turned[...], g_ref[...]).astype(BF)

    return pl.pallas_call(
        kernel,
        grid=(blocks,),
        out_shape=shape((2, blocks // 2, width, columns), BF),
        in_specs=[
            pl.BlockSpec((rows, width), lambda k: (0, 0)),
            pl.BlockSpec((None, rows, columns), lambda k: (k, 0, 0)),
        ],
        out_specs=pl.BlockSpec((None, None, width, columns), lambda k: (k % 2, k // 2, 0, 0)),
        scratch_shapes=[pltpu.VMEM((width, rows), BF)],
        compiler_params=pltpu.CompilerParams(vmem_limit_bytes=48 * 2**20),
        cost_estimate=pl.CostEstimate(
            flops=2 * rows * width * columns * blocks,
            bytes_accessed=blocks * columns * 2 * (width + rows),
            transcendentals=0,
        ),
        name="head_weights",
    )(tops, grads)


def norm_forward(values, gain):
    inverse = lax.rsqrt(jnp.mean(values * values, axis=-1, keepdims=True) + EPS_NORM)
    normed = values * inverse
    return (normed * gain, normed, inverse)


def norm_backward(grad, normed, inverse, gain):
    scaled = grad * gain
    inner = jnp.mean(scaled * normed, axis=-1, keepdims=True)
    return (inverse * (scaled - normed * inner), jnp.sum(grad * normed, axis=0))


def turn_half(tensor):
    quarter = tensor.shape[-1] // 4
    return jnp.concatenate(
        [
            -tensor[..., quarter : 2 * quarter],
            tensor[..., :quarter],
            -tensor[..., 3 * quarter :],
            tensor[..., 2 * quarter : 3 * quarter],
        ],
        axis=-1,
    )


def rope_tables(positions, width):
    quarter = width // 4
    freq = 10000.0 ** (-jnp.arange(quarter, dtype=F32) / quarter)
    row_angle = (positions // GRID).astype(F32)[:, None] * freq
    col_angle = (positions % GRID).astype(F32)[:, None] * freq
    angles = jnp.concatenate([row_angle, row_angle, col_angle, col_angle], axis=-1)
    return (jnp.cos(angles)[:, None, :], jnp.sin(angles)[:, None, :])


def rotate(tensor, cosine, sine):
    return tensor * cosine + turn_half(tensor) * sine


def rotate_back(grad, cosine, sine):
    return grad * cosine - turn_half(grad * sine)


def masked_scores(query, keys, height):
    scores = jnp.einsum("qhd,khd->hqk", query, keys, preferred_element_type=F32) * HD ** (-0.5)
    places = jnp.arange(query.shape[0])
    allowed = (places[None, :] <= places[:, None]) & (places[None, :] < GRID * height)
    return jnp.where(allowed[None], scores, NEGATIVE_FILL)


def attend(query, keys, values, height):
    scores = masked_scores(query, keys, height)
    score_peak = jnp.max(scores, axis=-1, keepdims=True)
    exponent = jnp.exp(scores - score_peak)
    score_total = jnp.sum(exponent, axis=-1, keepdims=True)
    probs = exponent / score_total
    output = jnp.einsum("hqk,khd->qhd", probs.astype(BF), values, preferred_element_type=F32)
    return (output.astype(BF).reshape(query.shape[0], -1), probs)


def attend_back(query, keys, values, probs, grad_out):
    grad_heads = grad_out.reshape(query.shape)
    grad_probs = jnp.einsum("qhd,khd->hqk", grad_heads, values, preferred_element_type=F32)
    grad_scores = probs * (grad_probs - jnp.sum(probs * grad_probs, axis=-1, keepdims=True))
    grad_scores = grad_scores.astype(BF)
    scale = HD ** (-0.5)
    grad_query = jnp.einsum("hqk,khd->qhd", grad_scores, keys, preferred_element_type=F32) * scale
    grad_keys = jnp.einsum("hqk,qhd->khd", grad_scores, query, preferred_element_type=F32) * scale
    grad_values = jnp.einsum(
        "hqk,qhd->khd", probs.astype(BF), grad_heads, preferred_element_type=F32
    )
    return (grad_query.astype(BF), grad_keys.astype(BF), grad_values.astype(BF))


def adam_update(master, drift, square, grad, rate, decay):
    moment = BETA_ONE * drift + (1.0 - BETA_ONE) * grad
    second = BETA_TWO * square + (1.0 - BETA_TWO) * grad * grad
    stride = (
        moment / (1.0 - BETA_ONE**STEP) / (jnp.sqrt(second / (1.0 - BETA_TWO**STEP)) + ADAM_EPS)
    )
    return (master - rate * (stride + decay * master), moment, second)


def pad_rows(value, rows):
    flat = value.reshape(-1)
    return jnp.pad(flat, (0, rows * 128 - flat.shape[0])).reshape(rows, 128)


def block_form(rows, columns):
    return (rows, columns) if rows % 8 == 0 else (rows * columns // 128, 128)


FIRST_AXES = ("x", "x", "y", "x")


def on_device(dims, *args):
    labels, targets, heights, loss_mask = args[:4]
    masters, drifts, squares = (args[4:12], args[12:20], args[20:28])
    class_table, code_table, attend_in, attend_mix, expand_in, shrink_out, head_weight, norm_gains = masters
    nz, ny, nx = dims
    plane = ny * nx
    chips = nz * plane
    images, local_len = targets.shape
    length = local_len * 2
    width = code_table.shape[1]
    device_codes = code_table.shape[0]
    line_codes = device_codes * plane * 2
    gain_columns = norm_gains.shape[1]
    chip, core = (lax.axis_index("dp"), lax.axis_index("seq"))
    z, y, x = (chip // plane, (chip // nx) % ny, chip % nx)
    plane_groups = [[k * plane + i for i in range(plane)] for k in range(nz)]
    line_groups = [[k * plane + i for k in range(nz)] for i in range(plane)]

    layers = (attend_in, attend_mix, expand_in, shrink_out)
    tail = pad_rows(jnp.concatenate([labels, heights]), 1)
    label_rows = -(-chips * images // 128)
    spread = lax.dynamic_update_slice(jnp.zeros((label_rows * 128,), jnp.int32), labels, (chip * images,))
    spread = jnp.pad(spread.reshape(label_rows, 128), ((0, 3 - label_rows), (0, 0)))
    meta = jnp.concatenate([targets, loss_mask, tail, spread], axis=0)
    *weights, row_parts, metas, smalls = gather_all(
        dims, layers, FIRST_AXES, code_table, class_table, norm_gains, meta, images, 0
    )

    own_tokens = lax.dynamic_slice_in_dim(metas, core, 1, axis=4)[:, :, :, :, 0]
    own_masks = lax.dynamic_slice_in_dim(metas, 2 + core, 1, axis=4)[:, :, :, :, 0]

    def of_line(value):
        value = lax.dynamic_slice_in_dim(value, y, 1, axis=1)
        return lax.dynamic_slice_in_dim(value, x, 1, axis=2).reshape(nz, -1)

    line_targets = of_line(own_tokens)
    line_heights = of_line(lax.dynamic_slice_in_dim(metas[:, :, :, 0, 4], images + core, 1, axis=3))
    places = jnp.arange(length)
    line_counted = (of_line(own_masks) * (places[None, :] < GRID * line_heights)).astype(F32)
    all_labels = metas[:, :, :, 0, 4, :images].reshape(-1)
    before = jnp.concatenate(
        [jnp.full((nz, 1), -1, jnp.int32), line_targets[:, :-1] - z * line_codes], axis=1
    )
    qkv_w, mix_w, expand_w, shrink_w = (v.reshape(-1, v.shape[-1]) for v in weights)

    smalls = smalls.reshape(chips * 2, 8, 128)[:, :, :gain_columns]
    class_row = smalls[:, 0].reshape(1, -1)
    gain = smalls[:, 1:4].transpose(1, 0, 2).reshape(3, -1)
    start = jnp.sum(row_parts.astype(F32), axis=0)
    start = jnp.concatenate([class_row, start[:-1]], axis=0)
    height = lax.dynamic_slice_in_dim(line_heights, z, 1, axis=0).reshape(())

    cosine, sine = rope_tables(places, HD)
    normed_one, norm_one, inverse_one = norm_forward(start, gain[0])
    normed_one = normed_one.astype(BF)
    mixed = matmul(normed_one, qkv_w).reshape(length, 3, -1, HD)
    query = rotate(mixed[:, 0], cosine, sine).astype(BF)
    keys = rotate(mixed[:, 1], cosine, sine).astype(BF)
    values = mixed[:, 2].astype(BF)
    attended, probs = attend(query, keys, values, height)
    middle = start + matmul(attended, mix_w)
    normed_two, norm_two, inverse_two = norm_forward(middle, gain[1])
    normed_two = normed_two.astype(BF)
    both = matmul(normed_two, expand_w)
    inner = both.shape[1] // 2
    gate_part, up_part = (both[:, :inner], both[:, inner:])
    hidden = (jax.nn.silu(gate_part) * up_part).astype(BF)
    final = middle + matmul(hidden, shrink_w)
    normed_top, norm_top, inverse_top = norm_forward(final, gain[2])
    normed_top = normed_top.astype(BF)

    tops, head_near = head_gather(dims, normed_top, head_weight, 2)
    tops = tops.reshape(nz * length, width)
    head_near = head_near.reshape(2, plane, width, -1)
    marks = (line_targets - z * line_codes).reshape(-1, 1)
    logits, stats = head_forward(tops, head_near, marks)
    stats = line_gather(dims, stats, 3, "row_stats")
    peaks = jnp.max(stats[:, 0], axis=0)
    totals = jnp.sum(stats[:, 1] * jnp.exp(stats[:, 0] - peaks[None, :]), axis=0)
    log_total = peaks + jnp.log(totals)
    counted = line_counted.reshape(-1)
    losses = (log_total - jnp.sum(stats[:, 2], axis=0)) * counted
    loss_local = jnp.sum(lax.dynamic_slice_in_dim(losses.reshape(nz, -1), z, 1, axis=0))
    count_local = jnp.sum(lax.dynamic_slice_in_dim(line_counted, z, 1, axis=0))
    scales = jnp.stack([peaks, counted / totals, counted])
    scales = jnp.pad(scales, ((0, 5), (0, 0)))
    grad_logits, grad_tops = head_backward(logits, head_near, marks, scales)
    grad_tops = grad_tops.reshape(nz, length, width)
    grad_top = lax.psum_scatter(grad_tops, "dp", axis_index_groups=line_groups)
    grad_head = head_weights(tops, grad_logits)
    grad_head = lax.psum_scatter(grad_head, "seq", scatter_dimension=0)
    grad_head = lax.psum_scatter(grad_head, "dp", axis_index_groups=plane_groups)

    grad_final, gain_top = norm_backward(grad_top.astype(F32), norm_top, inverse_top, gain[2])
    back_down = grad_final.astype(BF)
    grad_shrink = matmul(hidden.T, back_down)
    grad_hidden = matmul(back_down, shrink_w.T)
    sigma = jax.nn.sigmoid(gate_part)
    grad_gate = grad_hidden * up_part * sigma * (1.0 + gate_part * (1.0 - sigma))
    grad_up = grad_hidden * gate_part * sigma
    grad_both = jnp.concatenate([grad_gate, grad_up], axis=1).astype(BF)
    grad_expand = matmul(normed_two.T, grad_both)
    grad_norm_two, gain_two = norm_backward(
        matmul(grad_both, expand_w.T), norm_two, inverse_two, gain[1]
    )
    grad_middle = grad_final + grad_norm_two
    back_mix = grad_middle.astype(BF)
    grad_mix = matmul(attended.T, back_mix)
    grad_attended = matmul(back_mix, mix_w.T).astype(BF)
    grad_query, grad_keys, grad_values = attend_back(query, keys, values, probs, grad_attended)
    grad_mixed = jnp.stack(
        [
            rotate_back(grad_query.astype(F32), cosine, sine).astype(BF),
            rotate_back(grad_keys.astype(F32), cosine, sine).astype(BF),
            grad_values,
        ],
        axis=1,
    ).reshape(length, -1)
    grad_qkv = matmul(normed_one.T, grad_mixed)
    grad_norm_one, gain_one = norm_backward(
        matmul(grad_mixed, qkv_w.T), norm_one, inverse_one, gain[0]
    )
    grad_start = grad_middle + grad_norm_one

    grads_in = []
    for grad, shard in zip((grad_qkv, grad_mix, grad_expand, grad_shrink), layers):
        grads_in.append(grad.astype(BF).reshape(dims + (2,) + block_form(*shard.shape)))
    small = jnp.stack([grad_start[0], gain_one, gain_two, gain_top])
    small = small.reshape(4, chips * 2, gain_columns).transpose(1, 0, 2)
    small = jnp.pad(small, ((0, 0), (0, 4), (0, 128 - gain_columns))).reshape(dims + (2, 8, 128))
    behind = (z + nz - jnp.arange(nz)) % nz
    same = (all_labels[:, None] == all_labels[None, :]).astype(F32)
    partial = pad_rows(jnp.stack([jnp.zeros(()), loss_local, count_local]), 8)
    *layer_shares, code_share, smalls, sums = scatter_all(
        dims,
        grads_in,
        FIRST_AXES,
        grad_start.astype(BF),
        before[behind].reshape(-1, 128),
        grad_head,
        small,
        same,
        partial,
        device_codes,
        4,
    )
    small_mine = smalls.reshape(chips * 2, 8, 128)[:, :4, :gain_columns]
    class_pick = all_labels[:, None] == jnp.arange(class_table.shape[0])[None, :]
    class_share = jnp.dot(
        class_pick.astype(F32).T,
        small_mine[:, 0],
        precision=lax.Precision.HIGHEST,
        preferred_element_type=F32,
    )
    gain_share = jnp.sum(small_mine[:, 1:], axis=0)
    layer_shares = [g.reshape(v.shape) for g, v in zip(layer_shares, layers)]
    shares = (class_share, code_share, *layer_shares, grad_head.astype(F32), gain_share)
    total_square, loss_sum, loss_count = (sums[0, 0], sums[0, 1], sums[0, 2])
    grad_norm = jnp.sqrt(total_square) / loss_count
    factor = CLIP_NORM / jnp.maximum(grad_norm, CLIP_NORM) / loss_count
    news, firsts, seconds = ([], [], [])
    for member in range(8):
        fresh, moment, second = adam_update(
            masters[member],
            drifts[member],
            squares[member],
            shares[member] * factor,
            RATES[member],
            DECAYS[member],
        )
        news.append(fresh)
        firsts.append(moment)
        seconds.append(second)
    return tuple(news) + tuple(firsts) + tuple(seconds) + (grad_norm, loss_sum, loss_count)


def solution(mesh):
    rows, columns = (P(("dp", "seq"), None), P(None, ("dp", "seq")))
    eight = (columns, rows, rows, rows, rows, rows, columns, columns)
    return jax.shard_map(
        functools.partial(on_device, dims_of(mesh.shape["dp"])),
        mesh=mesh,
        in_specs=(P("dp"), P("dp", "seq"), P("dp"), P("dp", "seq")) + eight * 3,
        out_specs=eight * 3 + (P(), P(), P()),
        check_vma=False,
    )
```

```python
import functools

import jax
import jax.numpy as jnp
from jax import lax
from jax.experimental import pallas as pl
from jax.experimental.pallas import tpu as pltpu
from jax.sharding import PartitionSpec as P

HD = 64
GRID = 16
STEP = 10

EPS_NORM = 1e-05
BETA_ONE = 0.9
BETA_TWO = 0.95
ADAM_EPS = 1e-08
CLIP_NORM = 0.01
NEGATIVE_FILL = -1000000000.0
RATES = (0.8, 0.8, 0.08, 0.08, 0.08, 0.08, 0.08, 0.8)
DECAYS = (0.1, 0.1, 0.1, 0.1, 0.1, 0.1, 0.1, 0.0)

MESH = pl.DeviceIdType.MESH
ANY = pl.BlockSpec(memory_space=pl.ANY)
VMEM = pl.BlockSpec(memory_space=pltpu.VMEM)
BF = jnp.bfloat16
F32 = jnp.float32


def dims_of(dp):
    bits = dp.bit_length() - 1
    nz = 1 << (bits // 2)
    rest = dp // nz
    ny = 1 << ((rest.bit_length() - 1) // 2)
    return (nz, ny, rest // ny)


class Place:
    def __init__(self, dims):
        self.dims = dims
        nz, ny, nx = dims
        chip = lax.axis_index("dp")
        self.c = lax.axis_index("seq")
        self.z = chip // (ny * nx)
        self.y = (chip // nx) % ny
        self.x = chip % nx

    def zs(self, back):
        return (self.z + self.dims[0] - back) % self.dims[0]

    def ys(self, back):
        return (self.y + self.dims[1] - back) % self.dims[1]

    def xs(self, back):
        return (self.x + self.dims[2] - back) % self.dims[2]

    def dev(self, z=0, y=0, x=0, c=0):
        nz, ny, nx = self.dims
        z, y, x = ((self.z + z) % nz, (self.y + y) % ny, (self.x + x) % nx)
        return ((z * ny + y) * nx + x, (self.c + c) % 2)


def line_offsets(dims):
    nz, ny, nx = dims
    return (
        [(s, 0, 0, 0) for s in range(1, nz)]
        + [(0, s, 0, 0) for s in range(1, ny)]
        + [(0, 0, s, 0) for s in range(1, nx)]
        + [(0, 0, 0, 1)]
    )


def plane_offsets(dims):
    return [(0, v, u, 0) for v in range(dims[1]) for u in range(dims[2]) if v or u]


def greet(place, offsets):
    offsets = sorted(set(offsets))
    sem = pltpu.get_barrier_semaphore()
    for off in offsets:
        pl.semaphore_signal(sem, inc=1, device_id=place.dev(*off), device_id_type=MESH)
    pl.semaphore_wait(sem, len(offsets))


class Comm:
    def __init__(self, send_sems, recv_sems, local_sems):
        self.send_sems, self.recv_sems, self.local_sems = (send_sems, recv_sems, local_sems)
        self.sent, self.held, self.count, self.locals = ([], [], 0, 0)

    def send(self, src, dst, device):
        k = self.count
        self.count += 1
        copy = pltpu.make_async_remote_copy(
            src_ref=src,
            dst_ref=dst,
            send_sem=self.send_sems.at[k],
            recv_sem=self.recv_sems.at[k],
            device_id=device,
            device_id_type=MESH,
        )
        copy.start()
        self.sent.append(copy)
        return copy

    def keep(self, src, dst):
        copy = pltpu.make_async_copy(src, dst, self.local_sems.at[self.locals])
        self.locals += 1
        copy.start()
        self.held.append(copy)
        return copy

    def done(self, copy):
        copy.wait()
        self.held = [other for other in self.held if other is not copy]

    def finish(self):
        for copy in self.sent:
            copy.wait_send()
        for copy in self.held:
            copy.wait()


def all_offsets(dims):
    nz, ny, nx = dims
    spots = [(k, j, i, core) for k in range(nz) for j in range(ny) for i in range(nx) for core in range(2)]
    return spots[1:]


def small_exchange(comm, place, src, out, own):
    z, y, x, c = (place.z, place.y, place.x, place.c)
    nz, ny, nx = place.dims
    if own:
        comm.keep(src(z, y, x, c), out.at[z, y, x, c])
    got = []
    for off in all_offsets(place.dims):
        there = (place.zs(nz - off[0]), place.ys(ny - off[1]), place.xs(nx - off[2]), (c + off[3]) % 2)
        got.append(comm.send(src(*there), out.at[z, y, x, c], place.dev(*off)))
    return got


class PlaneGather:
    def __init__(self, comm, place):
        self.comm, self.place = (comm, place)
        self.firsts, self.seconds, self.mates = ([], [], [])

    def ways(self, axis):
        _, ny, nx = self.place.dims
        return range(1, ny if axis == "y" else nx)

    def back(self, axis, t, yy, xx):
        return (self.place.ys(t), xx) if axis == "y" else (yy, self.place.xs(t))

    def spread(self, block, first, src=None):
        place, second = (self.place, "y" if first == "x" else "x")
        dst = block(place.y, place.x)
        src = dst if src is None else src
        for t in self.ways(first):
            copy = self.comm.send(src, dst, place.dev(**{first: t}))
            self.firsts.append((block, first, second, t, copy))
        for t in self.ways(second):
            copy = self.comm.send(src, dst, place.dev(**{second: t}))
            self.seconds.append((block(*self.back(second, t, place.y, place.x)), copy))
        self.mates.append(self.comm.send(src, dst, place.dev(c=1)))

    def forward(self):
        place = self.place
        for block, first, second, t, copy in self.firsts:
            copy.wait_recv()
            yy, xx = self.back(first, t, place.y, place.x)
            held = block(yy, xx)
            for u in self.ways(second):
                copy = self.comm.send(held, held, place.dev(**{second: u}))
                self.seconds.append((block(*self.back(second, u, yy, xx)), copy))
            self.mates.append(self.comm.send(held, held, place.dev(c=1)))
        self.firsts = []

    def settle(self):
        for held, copy in self.seconds:
            copy.wait_recv()
            self.mates.append(self.comm.send(held, held, self.place.dev(c=1)))
        self.seconds = []

    def forward_some(self, count):
        rest = self.firsts[count:]
        self.firsts = self.firsts[:count]
        self.forward()
        self.firsts = rest

    def arrive(self):
        for copy in self.mates:
            copy.wait_recv()
        self.mates = []


def sems(count):
    return pltpu.SemaphoreType.DMA((count,))


def shape(dims, dtype):
    return jax.ShapeDtypeStruct(tuple(dims), dtype)


def call(kernel, outs, in_specs, out_specs, scratch, cid, name, args, vmem=None):
    return pl.pallas_call(
        kernel,
        out_shape=outs,
        in_specs=in_specs,
        out_specs=out_specs,
        scratch_shapes=scratch,
        compiler_params=pltpu.CompilerParams(
            collective_id=cid, has_side_effects=True, vmem_limit_bytes=vmem
        ),
        name=name,
    )(*args)


def small_sends(dims):
    return dims[0] * dims[1] * dims[2] * 2 - 1


def gather_all(dims, layers, first_axes, table, classes, gains, meta, images, cid):
    nz, ny, nx = dims
    n = len(layers)
    rows, width = table.shape
    length = meta.shape[1] * 2
    count_images = nz * ny * nx * images
    label_rows = -(-count_images // 128)
    groups = [(k,) for k in range(nz)] if nz <= 4 else [tuple(range(nz))]

    def kernel(*refs):
        ins, rest = (refs[:n], refs[n:])
        table_in, class_in, gain_in, meta_in, *rest = rest
        outs, rest = (rest[:n], rest[n:])
        parts_out, meta_out, small_out, *rest = rest
        low, rest = (rest[:n], rest[n:])
        whole, found, total, class_low, gain_row, small_in, ssem, rsem, lsem = rest
        place = Place(dims)
        z, y, x, c = (place.z, place.y, place.x, place.c)
        greet(place, all_offsets(dims))
        comm = Comm(ssem, rsem, lsem)
        metas = small_exchange(comm, place, lambda *spot: meta_in, meta_out, False)
        meta_out[z, y, x, c] = meta_in[...]
        waits = []
        whole[y, x, c] = table_in[...].astype(BF)
        tables, blocks = (PlaneGather(comm, place), PlaneGather(comm, place))
        for first, start in (("x", 0), ("y", rows // 2)):
            half = pl.ds(start, rows // 2)
            tables.spread(lambda yy, xx, half=half: whole.at[yy, xx, c, half], first)
        for a in range(n):
            low[a][...] = ins[a][...].astype(BF)
        along = {}
        for s in range(1, nz):
            for a in range(n):
                along[s, a] = comm.send(low[a], outs[a].at[z, y, x, c], place.dev(z=s))
        kept = [comm.keep(low[a], outs[a].at[z, y, x, c]) for a in range(n)]

        def spread(group):
            for a in range(n):
                for k in group:
                    if k:
                        along[k, a].wait_recv()
                if len(group) > 1:
                    comm.done(kept[a])
                    at = pl.ds(0, nz)
                else:
                    at = place.zs(group[0])
                blocks.spread(
                    lambda yy, xx, a=a, at=at: outs[a].at[at, yy, xx, c],
                    first_axes[a],
                    low[a] if group == (0,) else None,
                )

        for copy in metas:
            copy.wait_recv()

        class_low[...] = jnp.zeros_like(class_low)
        class_low[0 : class_in.shape[0], 0 : class_in.shape[1]] = class_in[...]
        small_in[...] = jnp.zeros_like(small_in)
        for r in range(label_rows):
            labels = jnp.zeros((1, 128), jnp.int32)
            for k in range(nz * ny * nx):
                labels = labels + meta_out[k // (ny * nx), k // nx % ny, k % nx, 0, 5 + r : 6 + r, :]
            pick = lax.broadcasted_iota(jnp.int32, (class_low.shape[0], 128), 0) == labels
            picked = lax.dot_general(
                jnp.where(pick, 1.0, 0.0).astype(BF),
                class_low[...].astype(BF),
                (((0,), (0,)), ((), ())),
                preferred_element_type=F32,
            )
            for i in range(min(128, count_images - 128 * r)):
                k, core = divmod(128 * r + i, 2)
                small_in[k // (ny * nx), k // nx % ny, k % nx, core, 0:1, :] = picked[i : i + 1]
        gain_row[...] = jnp.zeros_like(gain_row)
        gain_row[0:3, 0 : gain_in.shape[1]] = gain_in[...].astype(BF).astype(F32)

        @pl.loop(0, nz)
        def _(k):
            for j in range(ny):
                for i in range(nx):
                    for core in range(2):
                        small_in[k, j, i, core, 1:4, :] = gain_row[0:3]

        waits += small_exchange(comm, place, lambda *spot: small_in.at[spot], small_out, True)

        size = len(layers)
        steps = [lambda group=group: spread(group) for group in groups]
        steps.pop(0)()
        tables.forward()
        if steps:
            steps.pop(0)()
        blocks.forward_some(size)
        if steps:
            steps.pop(0)()
        tables.settle()
        blocks.forward_some(size)
        for step in steps:
            step()
        tables.arrive()

        for s in range(1, nz + 1):
            zz = place.zs(s % nz)
            columns = []
            for half in range(2):
                codes = meta_out[zz, y, x, half, pl.ds(c, 1), :].astype(F32)
                columns.append(jnp.broadcast_to(codes, (128, meta.shape[1])).T)
            column = jnp.concatenate(columns, axis=0)
            column = column - (z * ny * nx * 2 * rows).astype(F32)
            total[...] = jnp.zeros_like(total)

            @pl.loop(0, ny * nx * 2)
            def _(j):
                base = (j * rows).astype(F32)
                lane = lax.broadcasted_iota(jnp.int32, (length, 128), 1).astype(F32) + base
                picks = [
                    jnp.where(column == lane + float(128 * q), 1.0, 0.0).astype(BF)
                    for q in range(-(-rows // 128))
                ]
                pick = jnp.concatenate(picks, axis=1)[:, :rows]
                total[...] += matmul(pick, whole[j // (2 * nx), j // 2 % nx, j % 2])

            found[s % nz] = total[...].astype(BF)
            if s < nz:
                waits.append(comm.send(found.at[s], parts_out.at[nz - s], place.dev(z=nz - s)))
            blocks.forward_some(size)
        comm.keep(found.at[0], parts_out.at[0])
        blocks.forward()
        blocks.settle()
        blocks.arrive()
        for copy in waits:
            copy.wait_recv()
        comm.finish()

    count = n * (nz - 1) + (n * len(groups) + 2) * (2 * ny * nx - 1) + nz + 2 * small_sends(dims)
    small = dims + (2, 8, 128)
    outs = [shape(dims + (2,) + v.shape, BF) for v in layers]
    outs += [
        shape((nz, length, width), BF),
        shape(dims + (2,) + meta.shape, meta.dtype),
        shape(small, F32),
    ]
    scratch = [pltpu.VMEM(v.shape, BF) for v in layers]
    scratch += [
        pltpu.VMEM((ny, nx, 2) + table.shape, BF),
        pltpu.VMEM((nz, length, width), BF),
        pltpu.VMEM((length, width), F32),
        pltpu.VMEM((-(-classes.shape[0] // 128) * 128, 128), F32),
        pltpu.VMEM((8, 128), F32),
        pltpu.VMEM(small, F32),
        sems(count),
        sems(count),
        sems(n + 3),
    ]
    return call(
        kernel, outs, [VMEM] * (n + 4), [ANY] * (n + 1) + [VMEM] * 2, scratch,
        cid, "gather_all", (*layers, table, classes, gains, meta), 60 * 2**20,
    )


def add_blocks(out, terms):
    lead = out.shape[:-2]

    def visit(index):
        if len(index) < len(lead):

            @pl.loop(0, lead[len(index)])
            def _(i):
                visit(index + (i,))

        else:
            if len(terms) == 2 and out.dtype == BF:
                out[index] = terms[0][index] + terms[1][index]
                return
            total = terms[0][index].astype(F32)
            for term in terms[1:]:
                total = total + term[index].astype(F32)
            out[index] = total.astype(out.dtype)

    visit(())


def scatter_all(dims, grads, first_axes, rows, codes, head, small, same, partial, device_codes, cid):
    nz, ny, nx = dims
    n = len(grads)
    length, width = rows.shape
    block = (device_codes, width)
    parts = 2 if nz <= 4 else 1
    step = nz // parts
    items = [(a, g) for g in range(parts) for a in range(n)]

    def kernel(*refs):
        ins, rest = (refs[:n], refs[n:])
        rows_in, codes_in, head_in, small_in, same_in, partial_in, *rest = rest
        outs, rest = (rest[:n], rest[n:])
        table_out, small_out, sums, *rest = rest
        halves, ones, twos, threes, rest = (
            rest[:n], rest[n : 2 * n], rest[2 * n : 3 * n], rest[3 * n : 4 * n], rest[4 * n :]
        )
        lined, given, own, half, near, tops, mixed, mine, every, ssem, rsem, lsem = rest
        place = Place(dims)
        z, y, x, c = (place.z, place.y, place.x, place.c)
        offsets = plane_offsets(dims)
        greet(place, all_offsets(dims))
        comm = Comm(ssem, rsem, lsem)
        pair, got_one, got_two = ({}, {}, {})
        waits = small_exchange(comm, place, lambda *spot: small_in.at[spot], small_out, True)
        for a, g in items:
            span = pl.ds(g * step, step)
            pair[a, g] = comm.send(ins[a].at[span, :, :, 1 - c], halves[a].at[span], place.dev(c=1))
        lines = [comm.send(rows_in, lined.at[s], place.dev(z=s)) for s in range(1, nz)]
        lined[0] = rows_in[...]

        def first_step(a, g):
            span = pl.ds(g * step, step)
            pair[a, g].wait_recv()
            add_blocks(halves[a].at[span], [halves[a].at[span], ins[a].at[span, :, :, c]])
            if first_axes[a] == "y":
                got_one[a, g] = [
                    comm.send(halves[a].at[span, place.ys(ny - t)], ones[a].at[t - 1, span], place.dev(y=t))
                    for t in range(1, ny)
                ]
            else:
                got_one[a, g] = [
                    comm.send(halves[a].at[span, :, place.xs(nx - t)], ones[a].at[t - 1, span], place.dev(x=t))
                    for t in range(1, nx)
                ]

        def second_step(a, g):
            span = pl.ds(g * step, step)
            for copy in got_one[a, g]:
                copy.wait_recv()
            if first_axes[a] == "y":
                held = halves[a].at[span, y]
                add_blocks(held, [held] + [ones[a].at[t, span] for t in range(ny - 1)])
                got_two[a, g] = [
                    comm.send(halves[a].at[span, y, place.xs(nx - t)], twos[a].at[t - 1, span], place.dev(x=t))
                    for t in range(1, nx)
                ]
            else:
                held = halves[a].at[span, :, x]
                add_blocks(held, [held] + [ones[a].at[t, span] for t in range(nx - 1)])
                got_two[a, g] = [
                    comm.send(halves[a].at[span, place.ys(ny - t), x], twos[a].at[t - 1, span], place.dev(y=t))
                    for t in range(1, ny)
                ]

        for a, g in items:
            first_step(a, g)
        for a, g in items[: len(items) // 2]:
            second_step(a, g)

        for copy in lines:
            copy.wait_recv()
        held_codes = codes_in[...]
        flat = jnp.concatenate([held_codes[k : k + 1] for k in range(nz * length // 128)], axis=1)

        def product(into, core):
            @pl.loop(0, ny * nx)
            def _(j):
                code = lax.broadcasted_iota(jnp.int32, (device_codes, nz * length), 0)
                pick = code + (j * 2 + core) * device_codes == flat
                pick = jnp.where(pick, 1.0, 0.0).astype(BF)
                value = matmul(pick, lined[...].reshape(nz * length, width))
                into[j // nx, j % nx] = value.astype(BF)

        product(given, 1 - c)
        table_pair = comm.send(given, half, place.dev(c=1))
        product(own, c)
        for a, g in items[len(items) // 2 :]:
            second_step(a, g)
        table_pair.wait_recv()
        add_blocks(half, [half, own])
        arriving = [
            comm.send(half.at[place.ys(ny - off[1]), place.xs(nx - off[2])], near.at[k], place.dev(*off))
            for k, off in enumerate(offsets)
        ]

        third = {}
        for a in range(n):
            for g in range(parts):
                span = pl.ds(g * step, step)
                for copy in got_two[a, g]:
                    copy.wait_recv()
                held = halves[a].at[span, y, x]
                add_blocks(held, [held] + [twos[a].at[t, span] for t in range(twos[a].shape[0])])
            third[a] = [
                comm.send(halves[a].at[place.zs(nz - s), y, x], threes[a].at[s - 1], place.dev(z=s))
                for s in range(1, nz)
            ]
        for copy in waits:
            copy.wait_recv()
        comm.done(comm.held[0])
        mixed[...] = jnp.zeros_like(mixed)

        @pl.loop(0, nz)
        def _(k):
            for j in range(ny):
                for i in range(nx):
                    for core in range(2):
                        at = ((k * ny + j) * nx + i) * 2 + core
                        tops[pl.ds(at, 1), :] = small_out[k, j, i, core, 0:1, :]
                        mixed[...] += small_out[k, j, i, core]

        summed = jnp.dot(
            same_in[...], tops[...], precision=lax.Precision.HIGHEST, preferred_element_type=F32
        )
        row = lax.broadcasted_iota(jnp.int32, mixed.shape, 0)
        gained = jnp.where((row >= 1) & (row < 4), mixed[...], 0.0)
        square = jnp.sum(summed * tops[...]) + jnp.sum(gained * gained)
        share = head_in[...].astype(F32)
        square = square + jnp.sum(share * share)
        for a in range(n):
            for copy in third[a]:
                copy.wait_recv()
            add_blocks(outs[a], [halves[a].at[z, y, x]] + [threes[a].at[s] for s in range(nz - 1)])
            square = square + jnp.sum(outs[a][...] * outs[a][...])
        for copy in arriving:
            copy.wait_recv()
        add_blocks(table_out, [half.at[y, x]] + [near.at[k] for k in range(len(offsets))])
        square = square + jnp.sum(table_out[...] * table_out[...])
        first = (lax.broadcasted_iota(jnp.int32, mine.shape, 0) == 0) & (
            lax.broadcasted_iota(jnp.int32, mine.shape, 1) == 0
        )
        mine[...] = partial_in[...] + jnp.where(first, square, 0.0)
        for copy in small_exchange(comm, place, lambda *spot: mine, every, False):
            copy.wait_recv()
        every[z, y, x, c] = mine[...]
        sums[...] = jnp.zeros_like(sums)

        @pl.loop(0, nz)
        def _(k):
            for j in range(ny):
                for i in range(nx):
                    sums[...] += every[k, j, i, 0] + every[k, j, i, 1]

        comm.finish()

    count = n * (parts * (ny + nx - 1) + nz - 1) + nz + ny * nx + 2 * small_sends(dims)
    trail = [g.shape[4:] for g in grads]
    near_far = [(ny, nx) if axis == "y" else (nx, ny) for axis in first_axes]
    scratch = [pltpu.VMEM((nz, ny, nx) + t, BF) for t in trail]
    scratch += [pltpu.VMEM((u - 1, nz, v) + t, BF) for t, (u, v) in zip(trail, near_far)]
    scratch += [pltpu.VMEM((v - 1, nz) + t, BF) for t, (u, v) in zip(trail, near_far)]
    scratch += [pltpu.VMEM((nz - 1,) + t, BF) for t in trail]
    scratch += [
        pltpu.VMEM((nz, length, width), BF),
        pltpu.VMEM((ny, nx) + block, BF),
        pltpu.VMEM((ny, nx) + block, BF),
        pltpu.VMEM((ny, nx) + block, BF),
        pltpu.VMEM((ny * nx - 1,) + block, BF),
        pltpu.VMEM((same.shape[0], 128), F32),
        pltpu.VMEM((8, 128), F32),
        pltpu.VMEM(partial.shape, F32),
        pltpu.VMEM(dims + (2,) + partial.shape, F32),
        sems(count),
        sems(count),
        sems(2),
    ]
    outs = [shape(t, F32) for t in trail]
    outs += [shape(block, F32), shape(small.shape, F32), shape(partial.shape, F32)]
    return call(
        kernel, outs, [VMEM] * (n + 6), [VMEM] * (n + 3), scratch,
        cid, "scatter_all", (*grads, rows, codes, head, small, same, partial), 62 * 2**20,
    )


def head_all(dims, rows, head, marks, counted, cid):
    nz, ny, nx = dims
    length, width = rows.shape
    columns = head.shape[1]
    lanes = min(columns, 128)
    groups = columns // lanes
    plane = ny * nx
    blocks = 2 * plane
    keep = columns >= 128

    def kernel(*refs):
        rows_in, head_in, marks_in, counted_in, top_out, head_out, loss_out, *rest = refs
        whole, lined, turned, peaks, totals, picks, exps, grads, *rest = rest
        columned, partial, back, coming, mine, every, given, half, ssem, rsem, lsem = rest
        place = Place(dims)
        z, y, x, c = (place.z, place.y, place.x, place.c)
        greet(place, line_offsets(dims))
        comm = Comm(ssem, rsem, lsem)
        whole[c, y, x] = head_in[...].astype(BF)
        lined[0] = rows_in[...]
        arriving = [comm.send(lined.at[0], lined.at[s], place.dev(z=s)) for s in range(1, nz)]
        gather = PlaneGather(comm, place)
        for first, start in (("x", 0), ("y", width // 2)):
            part = pl.ds(start, width // 2)
            gather.spread(lambda yy, xx, part=part: whole.at[c, yy, xx, part], first)
        turned[:, 0:length] = lined[0].T
        gather.forward()
        gather.settle()
        gather.arrive()

        def block(k):
            return whole[k // plane, k // nx % ny, k % nx]

        def split(value):
            return [value[:, lanes * q : lanes * (q + 1)] for q in range(groups)]

        def hits(s, k):
            base = (k % plane * 2 + k // plane) * columns
            lane = lax.broadcasted_iota(jnp.int32, (length, lanes), 1) + base
            return [lane + lanes * q == marks_in[s] for q in range(groups)]

        def logits_of(s, k):
            return matmul(lined[s], block(k))

        def forward(s):
            at = pl.ds(s * length, length)
            peaks[...] = jnp.full_like(peaks, -jnp.inf)
            totals[...] = jnp.zeros_like(totals)
            picks[...] = jnp.zeros_like(picks)

            @pl.loop(0, blocks)
            def _(k):
                logits = logits_of(s, k)
                if keep:
                    exps[k, at] = logits
                high, found = (peaks[...], picks[...])
                for piece, hit in zip(split(logits), hits(s, k)):
                    high = jnp.maximum(high, piece)
                    found = found + jnp.where(hit, piece, 0.0)
                peaks[...] = high
                picks[...] = found

            peak = jnp.max(peaks[...], axis=1, keepdims=True)
            peaks[...] = jnp.broadcast_to(peak, (length, lanes))

            @pl.loop(0, blocks)
            def _(k):
                logits = exps[k, at] if keep else logits_of(s, k)
                total = totals[...]
                for q, piece in enumerate(split(logits)):
                    power = jnp.exp(piece - peaks[...])
                    if keep:
                        exps[k, at, lanes * q : lanes * (q + 1)] = power
                    total = total + power
                totals[...] = total

            if not keep:
                exps[s] = peaks[...]
            lane = lax.broadcasted_iota(jnp.int32, (length, 128), 1)
            total = jnp.sum(totals[...], axis=1, keepdims=True)
            found = jnp.sum(picks[...], axis=1, keepdims=True)
            table = jnp.where(lane == 0, peak, jnp.where(lane == 1, total, found))
            mine[place.zs(s)] = table.T[:8]

        forward(0)
        for s in range(1, nz):
            arriving[s - 1].wait_recv()
            turned[:, s * length : (s + 1) * length] = lined[s].T
            forward(s)
        stats = [comm.send(mine, every.at[s], place.dev(z=s)) for s in range(1, nz)]
        every[0] = mine[...]
        for copy in stats:
            copy.wait_recv()

        def backward(s):
            at = pl.ds(s * length, length)
            held = [every[q, place.zs(s)] for q in range(nz)]
            peak = held[0][0:1]
            for other in held[1:]:
                peak = jnp.maximum(peak, other[0:1])
            total = sum(other[1:2] * jnp.exp(other[0:1] - peak) for other in held)
            weight = counted_in[s : s + 1]
            if s == 0:
                found = sum(other[2:3] for other in held)
                loss = (peak + jnp.log(total) - found) * weight
                loss_out[...] = jnp.concatenate([loss, jnp.zeros((7, length), F32)], axis=0)
            scale = weight / total * jnp.exp(held[0][0:1] - peak)
            tall = jnp.concatenate([scale, weight, jnp.zeros((126, length), F32)], axis=0).T
            columned[0] = jnp.broadcast_to(tall[:, 0:1], (length, lanes))
            columned[1] = jnp.broadcast_to(tall[:, 1:2], (length, lanes))
            partial[...] = jnp.zeros_like(partial)

            @pl.loop(0, blocks)
            def _(k):
                if keep:
                    powers = split(exps[k, at])
                else:
                    powers = [jnp.exp(piece - exps[s]) for piece in split(logits_of(s, k))]
                pieces = []
                for power, hit in zip(powers, hits(s, k)):
                    grad = power * columned[0] - jnp.where(hit, columned[1], 0.0)
                    pieces.append(grad.astype(BF))
                grad = jnp.concatenate(pieces, axis=1) if groups > 1 else pieces[0]
                grads[k, at] = grad
                partial[...] += lax.dot_general(
                    grad, block(k), (((1,), (1,)), ((), ())), preferred_element_type=F32
                )

        coming_in = []
        for s in range(1, nz):
            backward(s)
            back[s - 1] = partial[...].astype(BF)
            coming_in.append(comm.send(back.at[s - 1], coming.at[s - 1], place.dev(z=nz - s)))
        backward(0)

        def weights(into, core):
            @pl.loop(0, plane)
            def _(j):
                into[j // nx, j % nx] = matmul(turned[...], grads[core * plane + j]).astype(BF)

        weights(given, 1 - c)
        pair = comm.send(given, half, place.dev(c=1))
        weights(head_out, c)
        pair.wait_recv()
        add_blocks(head_out, [head_out, half])
        for copy in coming_in:
            copy.wait_recv()
        total = partial[...]
        for s in range(nz - 1):
            total = total + coming[s].astype(F32)
        top_out[...] = total
        comm.finish()

    count = 3 * (nz - 1) + 2 * (2 * plane - 1) + 1
    scratch = [
        pltpu.VMEM((2, ny, nx) + head.shape, BF),
        pltpu.VMEM((nz, length, width), BF),
        pltpu.VMEM((width, nz * length), BF),
        pltpu.VMEM((length, lanes), F32),
        pltpu.VMEM((length, lanes), F32),
        pltpu.VMEM((length, lanes), F32),
        pltpu.VMEM((blocks, nz * length, columns) if keep else (nz, length, lanes), F32),
        pltpu.VMEM((blocks, nz * length, columns), BF),
        pltpu.VMEM((2, length, lanes), F32),
        pltpu.VMEM((length, width), F32),
        pltpu.VMEM((nz - 1, length, width), BF),
        pltpu.VMEM((nz - 1, length, width), BF),
        pltpu.VMEM((nz, 8, length), F32),
        pltpu.VMEM((nz, nz, 8, length), F32),
        pltpu.VMEM((ny, nx) + head.shape, BF),
        pltpu.VMEM((ny, nx) + head.shape, BF),
        sems(count),
        sems(count),
        sems(1),
    ]
    return call(
        kernel,
        [shape((length, width), F32), shape((ny, nx) + head.shape, BF), shape((8, length), F32)],
        [VMEM] * 4, [VMEM] * 3, scratch, cid, "head_all", (rows, head, marks, counted), 62 * 2**20,
    )


def matmul(left, right):
    return jnp.dot(left, right, preferred_element_type=F32)


def norm_forward(values, gain):
    inverse = lax.rsqrt(jnp.mean(values * values, axis=-1, keepdims=True) + EPS_NORM)
    normed = values * inverse
    return (normed * gain, normed, inverse)


def norm_backward(grad, normed, inverse, gain):
    scaled = grad * gain
    inner = jnp.mean(scaled * normed, axis=-1, keepdims=True)
    return (inverse * (scaled - normed * inner), jnp.sum(grad * normed, axis=0))


def turn_half(tensor):
    quarter = tensor.shape[-1] // 4
    return jnp.concatenate(
        [
            -tensor[..., quarter : 2 * quarter],
            tensor[..., :quarter],
            -tensor[..., 3 * quarter :],
            tensor[..., 2 * quarter : 3 * quarter],
        ],
        axis=-1,
    )


def rope_tables(positions, width):
    quarter = width // 4
    freq = 10000.0 ** (-jnp.arange(quarter, dtype=F32) / quarter)
    row_angle = (positions // GRID).astype(F32)[:, None] * freq
    col_angle = (positions % GRID).astype(F32)[:, None] * freq
    angles = jnp.concatenate([row_angle, row_angle, col_angle, col_angle], axis=-1)
    return (jnp.cos(angles)[:, None, :], jnp.sin(angles)[:, None, :])


def rotate(tensor, cosine, sine):
    return tensor * cosine + turn_half(tensor) * sine


def rotate_back(grad, cosine, sine):
    return grad * cosine - turn_half(grad * sine)


def masked_scores(query, keys, height):
    scores = jnp.einsum("qhd,khd->hqk", query, keys, preferred_element_type=F32) * HD ** (-0.5)
    places = jnp.arange(query.shape[0])
    allowed = (places[None, :] <= places[:, None]) & (places[None, :] < GRID * height)
    return jnp.where(allowed[None], scores, NEGATIVE_FILL)


def attend(query, keys, values, height):
    scores = masked_scores(query, keys, height)
    score_peak = jnp.max(scores, axis=-1, keepdims=True)
    exponent = jnp.exp(scores - score_peak)
    score_total = jnp.sum(exponent, axis=-1, keepdims=True)
    probs = exponent / score_total
    output = jnp.einsum("hqk,khd->qhd", probs.astype(BF), values, preferred_element_type=F32)
    return (output.astype(BF).reshape(query.shape[0], -1), probs)


def attend_back(query, keys, values, probs, grad_out):
    grad_heads = grad_out.reshape(query.shape)
    grad_probs = jnp.einsum("qhd,khd->hqk", grad_heads, values, preferred_element_type=F32)
    grad_scores = probs * (grad_probs - jnp.sum(probs * grad_probs, axis=-1, keepdims=True))
    grad_scores = grad_scores.astype(BF)
    scale = HD ** (-0.5)
    grad_query = jnp.einsum("hqk,khd->qhd", grad_scores, keys, preferred_element_type=F32) * scale
    grad_keys = jnp.einsum("hqk,qhd->khd", grad_scores, query, preferred_element_type=F32) * scale
    grad_values = jnp.einsum(
        "hqk,qhd->khd", probs.astype(BF), grad_heads, preferred_element_type=F32
    )
    return (grad_query.astype(BF), grad_keys.astype(BF), grad_values.astype(BF))


def adam_update(master, drift, square, grad, rate, decay):
    moment = BETA_ONE * drift + (1.0 - BETA_ONE) * grad
    second = BETA_TWO * square + (1.0 - BETA_TWO) * grad * grad
    stride = (
        moment / (1.0 - BETA_ONE**STEP) / (jnp.sqrt(second / (1.0 - BETA_TWO**STEP)) + ADAM_EPS)
    )
    return (master - rate * (stride + decay * master), moment, second)


def pad_rows(value, rows):
    flat = value.reshape(-1)
    return jnp.pad(flat, (0, rows * 128 - flat.shape[0])).reshape(rows, 128)


def block_form(rows, columns):
    return (rows, columns) if rows % 8 == 0 else (rows * columns // 128, 128)


FIRST_AXES = ("x", "x", "y", "x")


def on_device(dims, *args):
    labels, targets, heights, loss_mask = args[:4]
    masters, drifts, squares = (args[4:12], args[12:20], args[20:28])
    class_table, code_table, attend_in, attend_mix, expand_in, shrink_out, head_weight, norm_gains = masters
    nz, ny, nx = dims
    plane = ny * nx
    chips = nz * plane
    images, local_len = targets.shape
    length = local_len * 2
    width = code_table.shape[1]
    device_codes = code_table.shape[0]
    line_codes = device_codes * plane * 2
    gain_columns = norm_gains.shape[1]
    chip, core = (lax.axis_index("dp"), lax.axis_index("seq"))
    z, y, x = (chip // plane, (chip // nx) % ny, chip % nx)
    plane_groups = [[k * plane + i for i in range(plane)] for k in range(nz)]

    layers = (attend_in, attend_mix, expand_in, shrink_out)
    tail = pad_rows(jnp.concatenate([labels, heights]), 1)
    label_rows = -(-chips * images // 128)
    spread = lax.dynamic_update_slice(jnp.zeros((label_rows * 128,), jnp.int32), labels, (chip * images,))
    spread = jnp.pad(spread.reshape(label_rows, 128), ((0, 3 - label_rows), (0, 0)))
    meta = jnp.concatenate([targets, loss_mask, tail, spread], axis=0)
    *weights, row_parts, metas, smalls = gather_all(
        dims, layers, FIRST_AXES, code_table, class_table, norm_gains, meta, images, 0
    )

    own_tokens = lax.dynamic_slice_in_dim(metas, core, 1, axis=4)[:, :, :, :, 0]
    own_masks = lax.dynamic_slice_in_dim(metas, 2 + core, 1, axis=4)[:, :, :, :, 0]

    def of_line(value):
        value = lax.dynamic_slice_in_dim(value, y, 1, axis=1)
        return lax.dynamic_slice_in_dim(value, x, 1, axis=2).reshape(nz, -1)

    line_targets = of_line(own_tokens)
    line_heights = of_line(lax.dynamic_slice_in_dim(metas[:, :, :, 0, 4], images + core, 1, axis=3))
    places = jnp.arange(length)
    line_counted = (of_line(own_masks) * (places[None, :] < GRID * line_heights)).astype(F32)
    all_labels = metas[:, :, :, 0, 4, :images].reshape(-1)
    before = jnp.concatenate(
        [jnp.full((nz, 1), -1, jnp.int32), line_targets[:, :-1] - z * line_codes], axis=1
    )
    qkv_w, mix_w, expand_w, shrink_w = (v.reshape(-1, v.shape[-1]) for v in weights)

    smalls = smalls.reshape(chips * 2, 8, 128)[:, :, :gain_columns]
    class_row = smalls[:, 0].reshape(1, -1)
    gain = smalls[:, 1:4].transpose(1, 0, 2).reshape(3, -1)
    start = jnp.sum(row_parts.astype(F32), axis=0)
    start = jnp.concatenate([class_row, start[:-1]], axis=0)
    height = lax.dynamic_slice_in_dim(line_heights, z, 1, axis=0).reshape(())

    cosine, sine = rope_tables(places, HD)
    normed_one, norm_one, inverse_one = norm_forward(start, gain[0])
    normed_one = normed_one.astype(BF)
    mixed = matmul(normed_one, qkv_w).reshape(length, 3, -1, HD)
    query = rotate(mixed[:, 0], cosine, sine).astype(BF)
    keys = rotate(mixed[:, 1], cosine, sine).astype(BF)
    values = mixed[:, 2].astype(BF)
    attended, probs = attend(query, keys, values, height)
    middle = start + matmul(attended, mix_w)
    normed_two, norm_two, inverse_two = norm_forward(middle, gain[1])
    normed_two = normed_two.astype(BF)
    both = matmul(normed_two, expand_w)
    inner = both.shape[1] // 2
    gate_part, up_part = (both[:, :inner], both[:, inner:])
    hidden = (jax.nn.silu(gate_part) * up_part).astype(BF)
    final = middle + matmul(hidden, shrink_w)
    normed_top, norm_top, inverse_top = norm_forward(final, gain[2])
    normed_top = normed_top.astype(BF)

    behind = (z + nz - jnp.arange(nz)) % nz
    marks = (line_targets - z * line_codes)[behind]
    lanes = min(head_weight.shape[1], 128)
    marks = jnp.broadcast_to(marks[:, :, None], (nz, length, lanes))
    grad_top, grad_head, losses = head_all(
        dims, normed_top, head_weight, marks, line_counted[behind], 2
    )
    loss_local = jnp.sum(losses[0])
    count_local = jnp.sum(lax.dynamic_slice_in_dim(line_counted, z, 1, axis=0))
    grad_head = grad_head.reshape((plane,) + head_weight.shape)
    grad_head = lax.psum_scatter(grad_head, "dp", axis_index_groups=plane_groups)

    grad_final, gain_top = norm_backward(grad_top, norm_top, inverse_top, gain[2])
    back_down = grad_final.astype(BF)
    grad_shrink = matmul(hidden.T, back_down)
    grad_hidden = matmul(back_down, shrink_w.T)
    sigma = jax.nn.sigmoid(gate_part)
    grad_gate = grad_hidden * up_part * sigma * (1.0 + gate_part * (1.0 - sigma))
    grad_up = grad_hidden * gate_part * sigma
    grad_both = jnp.concatenate([grad_gate, grad_up], axis=1).astype(BF)
    grad_expand = matmul(normed_two.T, grad_both)
    grad_norm_two, gain_two = norm_backward(
        matmul(grad_both, expand_w.T), norm_two, inverse_two, gain[1]
    )
    grad_middle = grad_final + grad_norm_two
    back_mix = grad_middle.astype(BF)
    grad_mix = matmul(attended.T, back_mix)
    grad_attended = matmul(back_mix, mix_w.T).astype(BF)
    grad_query, grad_keys, grad_values = attend_back(query, keys, values, probs, grad_attended)
    grad_mixed = jnp.stack(
        [
            rotate_back(grad_query.astype(F32), cosine, sine).astype(BF),
            rotate_back(grad_keys.astype(F32), cosine, sine).astype(BF),
            grad_values,
        ],
        axis=1,
    ).reshape(length, -1)
    grad_qkv = matmul(normed_one.T, grad_mixed)
    grad_norm_one, gain_one = norm_backward(
        matmul(grad_mixed, qkv_w.T), norm_one, inverse_one, gain[0]
    )
    grad_start = grad_middle + grad_norm_one

    grads_in = []
    for grad, shard in zip((grad_qkv, grad_mix, grad_expand, grad_shrink), layers):
        grads_in.append(grad.astype(BF).reshape(dims + (2,) + block_form(*shard.shape)))
    small = jnp.stack([grad_start[0], gain_one, gain_two, gain_top])
    small = small.reshape(4, chips * 2, gain_columns).transpose(1, 0, 2)
    small = jnp.pad(small, ((0, 0), (0, 4), (0, 128 - gain_columns))).reshape(dims + (2, 8, 128))
    same = (all_labels[:, None] == all_labels[None, :]).astype(F32)
    partial = pad_rows(jnp.stack([jnp.zeros(()), loss_local, count_local]), 8)
    *layer_shares, code_share, smalls, sums = scatter_all(
        dims,
        grads_in,
        FIRST_AXES,
        grad_start.astype(BF),
        before[behind].reshape(-1, 128),
        grad_head,
        small,
        same,
        partial,
        device_codes,
        4,
    )
    small_mine = smalls.reshape(chips * 2, 8, 128)[:, :4, :gain_columns]
    class_pick = all_labels[:, None] == jnp.arange(class_table.shape[0])[None, :]
    class_share = jnp.dot(
        class_pick.astype(F32).T,
        small_mine[:, 0],
        precision=lax.Precision.HIGHEST,
        preferred_element_type=F32,
    )
    gain_share = jnp.sum(small_mine[:, 1:], axis=0)
    layer_shares = [g.reshape(v.shape) for g, v in zip(layer_shares, layers)]
    shares = (class_share, code_share, *layer_shares, grad_head.astype(F32), gain_share)
    total_square, loss_sum, loss_count = (sums[0, 0], sums[0, 1], sums[0, 2])
    grad_norm = jnp.sqrt(total_square) / loss_count
    factor = CLIP_NORM / jnp.maximum(grad_norm, CLIP_NORM) / loss_count
    news, firsts, seconds = ([], [], [])
    for member in range(8):
        fresh, moment, second = adam_update(
            masters[member],
            drifts[member],
            squares[member],
            shares[member] * factor,
            RATES[member],
            DECAYS[member],
        )
        news.append(fresh)
        firsts.append(moment)
        seconds.append(second)
    return tuple(news) + tuple(firsts) + tuple(seconds) + (grad_norm, loss_sum, loss_count)


def solution(mesh):
    rows, columns = (P(("dp", "seq"), None), P(None, ("dp", "seq")))
    eight = (columns, rows, rows, rows, rows, rows, columns, columns)
    return jax.shard_map(
        functools.partial(on_device, dims_of(mesh.shape["dp"])),
        mesh=mesh,
        in_specs=(P("dp"), P("dp", "seq"), P("dp"), P("dp", "seq")) + eight * 3,
        out_specs=eight * 3 + (P(), P(), P()),
        check_vma=False,
    )
```

```python
import functools

import jax
import jax.numpy as jnp
from jax import lax
from jax.experimental import pallas as pl
from jax.experimental.pallas import tpu as pltpu
from jax.sharding import PartitionSpec as P

HD = 64
GRID = 16
STEP = 10

EPS_NORM = 1e-05
BETA_ONE = 0.9
BETA_TWO = 0.95
ADAM_EPS = 1e-08
CLIP_NORM = 0.01
NEGATIVE_FILL = -1000000000.0
RATES = (0.8, 0.8, 0.08, 0.08, 0.08, 0.08, 0.08, 0.8)
DECAYS = (0.1, 0.1, 0.1, 0.1, 0.1, 0.1, 0.1, 0.0)

MESH = pl.DeviceIdType.MESH
ANY = pl.BlockSpec(memory_space=pl.ANY)
VMEM = pl.BlockSpec(memory_space=pltpu.VMEM)
BF = jnp.bfloat16
F32 = jnp.float32


def dims_of(dp):
    bits = dp.bit_length() - 1
    nz = 1 << (bits // 2)
    rest = dp // nz
    ny = 1 << ((rest.bit_length() - 1) // 2)
    return (nz, ny, rest // ny)


class Place:
    def __init__(self, dims):
        self.dims = dims
        nz, ny, nx = dims
        chip = lax.axis_index("dp")
        self.c = lax.axis_index("seq")
        self.z = chip // (ny * nx)
        self.y = (chip // nx) % ny
        self.x = chip % nx

    def zs(self, back):
        return (self.z + self.dims[0] - back) % self.dims[0]

    def ys(self, back):
        return (self.y + self.dims[1] - back) % self.dims[1]

    def xs(self, back):
        return (self.x + self.dims[2] - back) % self.dims[2]

    def dev(self, z=0, y=0, x=0, c=0):
        nz, ny, nx = self.dims
        z, y, x = ((self.z + z) % nz, (self.y + y) % ny, (self.x + x) % nx)
        return ((z * ny + y) * nx + x, (self.c + c) % 2)


def line_offsets(dims):
    nz, ny, nx = dims
    return (
        [(s, 0, 0, 0) for s in range(1, nz)]
        + [(0, s, 0, 0) for s in range(1, ny)]
        + [(0, 0, s, 0) for s in range(1, nx)]
        + [(0, 0, 0, 1)]
    )


def plane_offsets(dims):
    return [(0, v, u, 0) for v in range(dims[1]) for u in range(dims[2]) if v or u]


def greet(place, offsets):
    offsets = sorted(set(offsets))
    sem = pltpu.get_barrier_semaphore()
    for off in offsets:
        pl.semaphore_signal(sem, inc=1, device_id=place.dev(*off), device_id_type=MESH)
    pl.semaphore_wait(sem, len(offsets))


class Comm:
    def __init__(self, send_sems, recv_sems, local_sems):
        self.send_sems, self.recv_sems, self.local_sems = (send_sems, recv_sems, local_sems)
        self.sent, self.held, self.count, self.locals = ([], [], 0, 0)

    def send(self, src, dst, device):
        k = self.count
        self.count += 1
        copy = pltpu.make_async_remote_copy(
            src_ref=src,
            dst_ref=dst,
            send_sem=self.send_sems.at[k],
            recv_sem=self.recv_sems.at[k],
            device_id=device,
            device_id_type=MESH,
        )
        copy.start()
        self.sent.append(copy)
        return copy

    def keep(self, src, dst):
        copy = pltpu.make_async_copy(src, dst, self.local_sems.at[self.locals])
        self.locals += 1
        copy.start()
        self.held.append(copy)
        return copy

    def done(self, copy):
        copy.wait()
        self.held = [other for other in self.held if other is not copy]

    def finish(self):
        for copy in self.sent:
            copy.wait_send()
        for copy in self.held:
            copy.wait()


def drain(steps):
    for _ in steps:
        pass


def all_offsets(dims):
    nz, ny, nx = dims
    spots = [(k, j, i, core) for k in range(nz) for j in range(ny) for i in range(nx) for core in range(2)]
    return spots[1:]


def small_exchange(comm, place, src, out, own):
    z, y, x, c = (place.z, place.y, place.x, place.c)
    nz, ny, nx = place.dims
    if own:
        comm.keep(src(z, y, x, c), out.at[z, y, x, c])
    got = []
    for off in all_offsets(place.dims):
        there = (place.zs(nz - off[0]), place.ys(ny - off[1]), place.xs(nx - off[2]), (c + off[3]) % 2)
        got.append(comm.send(src(*there), out.at[z, y, x, c], place.dev(*off)))
    return got


class PlaneGather:
    def __init__(self, comm, place):
        self.comm, self.place = (comm, place)
        self.firsts, self.seconds, self.mates = ([], [], [])

    def ways(self, axis):
        _, ny, nx = self.place.dims
        return range(1, ny if axis == "y" else nx)

    def back(self, axis, t, yy, xx):
        return (self.place.ys(t), xx) if axis == "y" else (yy, self.place.xs(t))

    def spread(self, block, first, src=None):
        place, second = (self.place, "y" if first == "x" else "x")
        dst = block(place.y, place.x)
        src = dst if src is None else src
        for t in self.ways(first):
            copy = self.comm.send(src, dst, place.dev(**{first: t}))
            self.firsts.append((block, first, second, t, copy))
        for t in self.ways(second):
            copy = self.comm.send(src, dst, place.dev(**{second: t}))
            self.seconds.append((block(*self.back(second, t, place.y, place.x)), copy))
        self.mates.append(self.comm.send(src, dst, place.dev(c=1)))

    def forward(self):
        place = self.place
        for block, first, second, t, copy in self.firsts:
            copy.wait_recv()
            yy, xx = self.back(first, t, place.y, place.x)
            held = block(yy, xx)
            for u in self.ways(second):
                copy = self.comm.send(held, held, place.dev(**{second: u}))
                self.seconds.append((block(*self.back(second, u, yy, xx)), copy))
            self.mates.append(self.comm.send(held, held, place.dev(c=1)))
        self.firsts = []

    def settle(self):
        for held, copy in self.seconds:
            copy.wait_recv()
            self.mates.append(self.comm.send(held, held, self.place.dev(c=1)))
        self.seconds = []

    def forward_some(self, count):
        rest = self.firsts[count:]
        self.firsts = self.firsts[:count]
        self.forward()
        self.firsts = rest

    def arrive(self):
        for copy in self.mates:
            copy.wait_recv()
        self.mates = []


def sems(count):
    return pltpu.SemaphoreType.DMA((count,))


def shape(dims, dtype):
    return jax.ShapeDtypeStruct(tuple(dims), dtype)


def call(kernel, outs, in_specs, out_specs, scratch, cid, name, args, vmem=None):
    return pl.pallas_call(
        kernel,
        out_shape=outs,
        in_specs=in_specs,
        out_specs=out_specs,
        scratch_shapes=scratch,
        compiler_params=pltpu.CompilerParams(
            collective_id=cid, has_side_effects=True, vmem_limit_bytes=vmem
        ),
        name=name,
    )(*args)


def small_sends(dims):
    return dims[0] * dims[1] * dims[2] * 2 - 1


def gather_all(dims, layers, first_axes, table, classes, gains, meta, images, cid):
    nz, ny, nx = dims
    n = len(layers)
    rows, width = table.shape
    length = meta.shape[1] * 2
    count_images = nz * ny * nx * images
    label_rows = -(-count_images // 128)
    groups = [(k,) for k in range(nz)] if nz <= 4 else [tuple(range(nz))]

    def kernel(*refs):
        ins, rest = (refs[:n], refs[n:])
        table_in, class_in, gain_in, meta_in, *rest = rest
        outs, rest = (rest[:n], rest[n:])
        parts_out, meta_out, small_out, *rest = rest
        low, rest = (rest[:n], rest[n:])
        whole, found, total, class_low, gain_row, small_in, ssem, rsem, lsem = rest
        place = Place(dims)
        z, y, x, c = (place.z, place.y, place.x, place.c)
        greet(place, all_offsets(dims))
        comm = Comm(ssem, rsem, lsem)
        metas = small_exchange(comm, place, lambda *spot: meta_in, meta_out, False)
        meta_out[z, y, x, c] = meta_in[...]
        waits = []
        whole[y, x, c] = table_in[...].astype(BF)
        tables, blocks = (PlaneGather(comm, place), PlaneGather(comm, place))
        for first, start in (("x", 0), ("y", rows // 2)):
            half = pl.ds(start, rows // 2)
            tables.spread(lambda yy, xx, half=half: whole.at[yy, xx, c, half], first)
        for a in range(n):
            low[a][...] = ins[a][...].astype(BF)
        along = {}
        for s in range(1, nz):
            for a in range(n):
                along[s, a] = comm.send(low[a], outs[a].at[z, y, x, c], place.dev(z=s))
        kept = [comm.keep(low[a], outs[a].at[z, y, x, c]) for a in range(n)]

        def spread(group):
            for a in range(n):
                for k in group:
                    if k:
                        along[k, a].wait_recv()
                if len(group) > 1:
                    comm.done(kept[a])
                    at = pl.ds(0, nz)
                else:
                    at = place.zs(group[0])
                blocks.spread(
                    lambda yy, xx, a=a, at=at: outs[a].at[at, yy, xx, c],
                    first_axes[a],
                    low[a] if group == (0,) else None,
                )

        for copy in metas:
            copy.wait_recv()

        class_low[...] = jnp.zeros_like(class_low)
        class_low[0 : class_in.shape[0], 0 : class_in.shape[1]] = class_in[...]
        small_in[...] = jnp.zeros_like(small_in)
        for r in range(label_rows):
            labels = jnp.zeros((1, 128), jnp.int32)
            for k in range(nz * ny * nx):
                labels = labels + meta_out[k // (ny * nx), k // nx % ny, k % nx, 0, 5 + r : 6 + r, :]
            pick = lax.broadcasted_iota(jnp.int32, (class_low.shape[0], 128), 0) == labels
            picked = lax.dot_general(
                jnp.where(pick, 1.0, 0.0).astype(BF),
                class_low[...].astype(BF),
                (((0,), (0,)), ((), ())),
                preferred_element_type=F32,
            )
            for i in range(min(128, count_images - 128 * r)):
                k, core = divmod(128 * r + i, 2)
                small_in[k // (ny * nx), k // nx % ny, k % nx, core, 0:1, :] = picked[i : i + 1]
        gain_row[...] = jnp.zeros_like(gain_row)
        gain_row[0:3, 0 : gain_in.shape[1]] = gain_in[...].astype(BF).astype(F32)

        @pl.loop(0, nz)
        def _(k):
            for j in range(ny):
                for i in range(nx):
                    for core in range(2):
                        small_in[k, j, i, core, 1:4, :] = gain_row[0:3]

        waits += small_exchange(comm, place, lambda *spot: small_in.at[spot], small_out, True)

        size = len(layers)
        steps = [lambda group=group: spread(group) for group in groups]
        steps.pop(0)()
        tables.forward()
        if steps:
            steps.pop(0)()
        blocks.forward_some(size)
        if steps:
            steps.pop(0)()
        tables.settle()
        blocks.forward_some(size)
        for step in steps:
            step()
        tables.arrive()

        for s in range(1, nz + 1):
            zz = place.zs(s % nz)
            columns = []
            for half in range(2):
                codes = meta_out[zz, y, x, half, pl.ds(c, 1), :].astype(F32)
                columns.append(jnp.broadcast_to(codes, (128, meta.shape[1])).T)
            column = jnp.concatenate(columns, axis=0)
            column = column - (z * ny * nx * 2 * rows).astype(F32)
            total[...] = jnp.zeros_like(total)

            @pl.loop(0, ny * nx * 2)
            def _(j):
                base = (j * rows).astype(F32)
                lane = lax.broadcasted_iota(jnp.int32, (length, 128), 1).astype(F32) + base
                picks = [
                    jnp.where(column == lane + float(128 * q), 1.0, 0.0).astype(BF)
                    for q in range(-(-rows // 128))
                ]
                pick = jnp.concatenate(picks, axis=1)[:, :rows]
                total[...] += matmul(pick, whole[j // (2 * nx), j // 2 % nx, j % 2])

            found[s % nz] = total[...].astype(BF)
            if s < nz:
                waits.append(comm.send(found.at[s], parts_out.at[nz - s], place.dev(z=nz - s)))
            blocks.forward_some(size)
        comm.keep(found.at[0], parts_out.at[0])
        blocks.forward()
        blocks.settle()
        blocks.arrive()
        for copy in waits:
            copy.wait_recv()
        comm.finish()

    count = n * (nz - 1) + (n * len(groups) + 2) * (2 * ny * nx - 1) + nz + 2 * small_sends(dims)
    small = dims + (2, 8, 128)
    outs = [shape(dims + (2,) + v.shape, BF) for v in layers]
    outs += [
        shape((nz, length, width), BF),
        shape(dims + (2,) + meta.shape, meta.dtype),
        shape(small, F32),
    ]
    scratch = [pltpu.VMEM(v.shape, BF) for v in layers]
    scratch += [
        pltpu.VMEM((ny, nx, 2) + table.shape, BF),
        pltpu.VMEM((nz, length, width), BF),
        pltpu.VMEM((length, width), F32),
        pltpu.VMEM((-(-classes.shape[0] // 128) * 128, 128), F32),
        pltpu.VMEM((8, 128), F32),
        pltpu.VMEM(small, F32),
        sems(count),
        sems(count),
        sems(n + 3),
    ]
    return call(
        kernel, outs, [VMEM] * (n + 4), [ANY] * (n + 1) + [VMEM] * 2, scratch,
        cid, "gather_all", (*layers, table, classes, gains, meta), 60 * 2**20,
    )


def add_blocks(out, terms):
    lead = out.shape[:-2]

    def visit(index):
        if len(index) < len(lead):

            @pl.loop(0, lead[len(index)])
            def _(i):
                visit(index + (i,))

        else:
            if len(terms) == 2 and out.dtype == BF:
                out[index] = terms[0][index] + terms[1][index]
                return
            total = terms[0][index].astype(F32)
            for term in terms[1:]:
                total = total + term[index].astype(F32)
            out[index] = total.astype(out.dtype)

    visit(())


def items_of(shapes, axes):
    if shapes[0][0] % 8:
        return [[(a, slice(0, shapes[a][0]), slice(0, shapes[a][1]), axes[a]) for a in pair] for pair in ((2, 3), (0, 1))]
    (rows, qkv), (_, mix), (_, both), (deep, width) = shapes
    every, piece = (slice(0, rows), both // 4)
    return [
        [(3, slice(0, deep // 2), slice(0, width), "x"), (3, slice(deep // 2, deep), slice(0, width), "y")],
        [(2, every, slice(0, piece), "x"), (2, every, slice(2 * piece, 3 * piece), "y")],
        [(0, every, slice(0, 2 * mix), "x"), (0, every, slice(2 * mix, qkv), "y"), (1, every, slice(0, mix), "y")],
        [(2, every, slice(piece, 2 * piece), "x"), (2, every, slice(3 * piece, both), "y")],
    ]


def scatter_all(dims, grads, axes, rows, codes, head, small, same, partial, device_codes, cid):
    nz, ny, nx = dims
    plane = ny * nx
    n = len(grads)
    shapes = [g.shape[4:] for g in grads]
    steps = items_of(shapes, axes)
    items = [item for step in steps for item in step]
    order, at = ([], 0)
    for step in steps:
        order.append(list(range(at, at + len(step))))
        at += len(step)
    length, width = rows.shape
    block = (device_codes, width)
    sizes = {"x": nx, "y": ny}

    def kernel(*refs):
        parts, rest = (refs[:n], list(refs[n:]))
        rows_in, codes_in, head_in, small_in, same_in, partial_in = (rest.pop(0) for _ in range(6))
        outs = [rest.pop(0) for _ in range(n)]
        table_out, small_out, sums = (rest.pop(0) for _ in range(3))
        owns, halves, ones, twos, threes = ([rest.pop(0) for _ in items] for _ in range(5))
        near, far = ([rest.pop(0), rest.pop(0)] for _ in range(2))
        lined, given, own, half, tops, mixed, mine, every, ssem, rsem, lsem = rest
        place = Place(dims)
        z, y, x, c = (place.z, place.y, place.x, place.c)
        comm = Comm(ssem, rsem, lsem)
        kept = []
        for i, (a, span, cols, _) in enumerate(items):
            kept.append(comm.keep(parts[a].at[:, :, :, c, span, cols], owns[i]))
        greet(place, all_offsets(dims))
        waits = small_exchange(comm, place, lambda *spot: small_in.at[spot], small_out, False)
        small_out[z, y, x, c] = small_in[z, y, x, c]
        pair, got_one, got_two, third = ({}, {}, {}, {})

        def set_out(g):
            for i in order[g] if g < len(order) else []:
                a, span, cols, _ = items[i]
                pair[i] = comm.send(parts[a].at[:, :, :, 1 - c, span, cols], halves[i], place.dev(c=1))

        def back(axis, t):
            return place.ys(ny - t) if axis == "y" else place.xs(nx - t)

        def first_add(g):
            for i in order[g]:
                pair[i].wait_recv()
                comm.done(kept[i])
                add_blocks(halves[i], [halves[i], owns[i]])

        def first_send(g):
            for i in order[g]:
                axis = items[i][3]
                got_one[i] = [
                    comm.send(
                        halves[i].at[:, back(axis, t)] if axis == "y" else halves[i].at[:, :, back(axis, t)],
                        ones[i].at[t - 1],
                        place.dev(**{axis: t}),
                    )
                    for t in range(1, sizes[axis])
                ]

        def second_step(g):
            for i in order[g]:
                axis = items[i][3]
                other = "x" if axis == "y" else "y"
                for copy in got_one[i]:
                    copy.wait_recv()
                held = halves[i].at[:, y] if axis == "y" else halves[i].at[:, :, x]
                add_blocks(held, [held] + [ones[i].at[t] for t in range(ones[i].shape[0])])
                got_two[i] = [
                    comm.send(
                        halves[i].at[:, y, back("x", t)] if other == "x" else halves[i].at[:, back("y", t), x],
                        twos[i].at[t - 1],
                        place.dev(**{other: t}),
                    )
                    for t in range(1, sizes[other])
                ]

        def third_step(g):
            for i in order[g]:
                for copy in got_two[i]:
                    copy.wait_recv()
                held = halves[i].at[:, y, x]
                add_blocks(held, [held] + [twos[i].at[t] for t in range(twos[i].shape[0])])
                third[i] = [
                    comm.send(halves[i].at[place.zs(nz - s), y, x], threes[i].at[s - 1], place.dev(z=s))
                    for s in range(1, nz)
                ]

        def last_step(g):
            for i in order[g]:
                a, span, cols, _ = items[i]
                for copy in third[i]:
                    copy.wait_recv()
                terms = [halves[i].at[z, y, x]] + [threes[i].at[s] for s in range(nz - 1)]
                add_blocks(outs[a].at[span, cols], terms)

        held_codes = codes_in[...]
        flat = jnp.concatenate([held_codes[k : k + 1] for k in range(nz * length // 128)], axis=1)

        def product(into, core):
            @pl.loop(0, plane)
            def _(j):
                code = lax.broadcasted_iota(jnp.int32, (device_codes, nz * length), 0)
                pick = code + (j * 2 + core) * device_codes == flat
                pick = jnp.where(pick, 1.0, 0.0).astype(BF)
                value = matmul(pick, lined[...].reshape(nz * length, width))
                into[j // nx, j % nx] = value.astype(BF)

        set_out(0)
        set_out(1)
        lined[0] = rows_in[...]
        lines = [comm.send(lined.at[0], lined.at[s], place.dev(z=s)) for s in range(1, nz)]
        count = len(order)
        for g in range(count):
            first_add(g)
            set_out(g + 2)
            if g >= 2:
                second_step(g - 2)
            first_send(g)
            if g >= 3:
                third_step(g - 3)
        for copy in lines:
            copy.wait_recv()
        product(given, 1 - c)
        table_pair = comm.send(given, half, place.dev(c=1))
        second_step(count - 2)
        product(own, c)
        if count > 2:
            third_step(count - 3)
        second_step(count - 1)
        table_pair.wait_recv()
        add_blocks(half, [half, own])
        parts_of = [pl.ds(0, device_codes // 2), pl.ds(device_codes // 2, device_codes // 2)]
        came = [
            [
                comm.send(half.at[:, back("x", t), parts_of[0]], near[0].at[t - 1], place.dev(x=t))
                for t in range(1, nx)
            ],
            [
                comm.send(half.at[back("y", t), :, parts_of[1]], near[1].at[t - 1], place.dev(y=t))
                for t in range(1, ny)
            ],
        ]
        third_step(count - 2)
        third_step(count - 1)

        for copy in waits:
            copy.wait_recv()
        mixed[...] = jnp.zeros_like(mixed)

        @pl.loop(0, nz)
        def _(k):
            for j in range(ny):
                for i in range(nx):
                    for core in range(2):
                        at = ((k * ny + j) * nx + i) * 2 + core
                        tops[pl.ds(at, 1), :] = small_out[k, j, i, core, 0:1, :]
                        mixed[...] += small_out[k, j, i, core]

        summed = jnp.dot(
            same_in[...], tops[...], precision=lax.Precision.HIGHEST, preferred_element_type=F32
        )
        row = lax.broadcasted_iota(jnp.int32, mixed.shape, 0)
        gained = jnp.where((row >= 1) & (row < 4), mixed[...], 0.0)
        square = jnp.sum(summed * tops[...]) + jnp.sum(gained * gained)
        share = head_in[...].astype(F32)
        square = square + jnp.sum(share * share)
        for g in range(count - 1):
            last_step(g)

        for copy in came[0] + came[1]:
            copy.wait_recv()
        for h, held in ((0, half.at[:, x, parts_of[0]]), (1, half.at[y, :, parts_of[1]])):
            add_blocks(held, [held] + [near[h].at[t] for t in range(near[h].shape[0])])
        came = [
            comm.send(half.at[back("y", t), x, parts_of[0]], far[0].at[t - 1], place.dev(y=t))
            for t in range(1, ny)
        ]
        came += [
            comm.send(half.at[y, back("x", t), parts_of[1]], far[1].at[t - 1], place.dev(x=t))
            for t in range(1, nx)
        ]
        last_step(count - 1)
        for a in range(n):
            square = square + jnp.sum(outs[a][...] * outs[a][...])
        for copy in came:
            copy.wait_recv()
        for h in range(2):
            terms = [half.at[y, x, parts_of[h]]] + [far[h].at[t] for t in range(far[h].shape[0])]
            add_blocks(table_out.at[parts_of[h]], terms)
        square = square + jnp.sum(table_out[...] * table_out[...])
        first = (lax.broadcasted_iota(jnp.int32, mine.shape, 0) == 0) & (
            lax.broadcasted_iota(jnp.int32, mine.shape, 1) == 0
        )
        mine[...] = partial_in[...] + jnp.where(first, square, 0.0)
        for copy in small_exchange(comm, place, lambda *spot: mine, every, False):
            copy.wait_recv()
        every[z, y, x, c] = mine[...]
        sums[...] = jnp.zeros_like(sums)

        @pl.loop(0, nz)
        def _(k):
            for j in range(ny):
                for i in range(nx):
                    sums[...] += every[k, j, i, 0] + every[k, j, i, 1]

        comm.finish()

    total = len(items) * (ny + nx - 1 + nz - 1) + nz + 2 * (ny + nx) + 2 * small_sends(dims)
    cuts = [(span.stop - span.start, cols.stop - cols.start) for _, span, cols, _ in items]
    near_far = [(ny, nx) if item[3] == "y" else (nx, ny) for item in items]
    part = (device_codes // 2, width)
    scratch = [pltpu.VMEM((nz, ny, nx) + t, BF) for t in cuts] * 2
    scratch += [pltpu.VMEM((u - 1, nz, v) + t, BF) for t, (u, v) in zip(cuts, near_far)]
    scratch += [pltpu.VMEM((v - 1, nz) + t, BF) for t, (u, v) in zip(cuts, near_far)]
    scratch += [pltpu.VMEM((nz - 1,) + t, BF) for t in cuts]
    scratch += [
        pltpu.VMEM((nx - 1, ny) + part, BF),
        pltpu.VMEM((ny - 1, nx) + part, BF),
        pltpu.VMEM((ny - 1,) + part, BF),
        pltpu.VMEM((nx - 1,) + part, BF),
        pltpu.VMEM((nz, length, width), BF),
        pltpu.VMEM((ny, nx) + block, BF),
        pltpu.VMEM((ny, nx) + block, BF),
        pltpu.VMEM((ny, nx) + block, BF),
        pltpu.VMEM((same.shape[0], 128), F32),
        pltpu.VMEM((8, 128), F32),
        pltpu.VMEM(partial.shape, F32),
        pltpu.VMEM(dims + (2,) + partial.shape, F32),
        sems(total),
        sems(total),
        sems(len(items)),
    ]
    outs = [shape(t, F32) for t in shapes]
    outs += [shape(block, F32), shape(dims + (2, 8, 128), F32), shape(partial.shape, F32)]
    return call(
        kernel, outs, [ANY] * n + [VMEM] * 6, [VMEM] * (n + 3), scratch,
        cid, "scatter_all", (*grads, rows, codes, head, small, same, partial), 60 * 2**20,
    )


def head_all(dims, rows, head, marks, counted, cid):
    nz, ny, nx = dims
    length, width = rows.shape
    columns = head.shape[1]
    lanes = min(columns, 128)
    groups = columns // lanes
    plane = ny * nx
    blocks = 2 * plane
    keep = columns >= 128

    def kernel(*refs):
        rows_in, head_in, marks_in, counted_in, top_out, head_out, loss_out, *rest = refs
        whole, lined, turned, peaks, totals, picks, exps, grads, *rest = rest
        columned, partial, back, coming, mine, every, given, half, ssem, rsem, lsem = rest
        place = Place(dims)
        z, y, x, c = (place.z, place.y, place.x, place.c)
        greet(place, line_offsets(dims))
        comm = Comm(ssem, rsem, lsem)
        whole[c, y, x] = head_in[...].astype(BF)
        lined[0] = rows_in[...]
        arriving = [comm.send(lined.at[0], lined.at[s], place.dev(z=s)) for s in range(1, nz)]
        gather = PlaneGather(comm, place)
        for first, start in (("x", 0), ("y", width // 2)):
            part = pl.ds(start, width // 2)
            gather.spread(lambda yy, xx, part=part: whole.at[c, yy, xx, part], first)
        turned[:, 0:length] = lined[0].T
        gather.forward()
        gather.settle()
        gather.arrive()

        def block(k):
            return whole[k // plane, k // nx % ny, k % nx]

        def split(value):
            return [value[:, lanes * q : lanes * (q + 1)] for q in range(groups)]

        def hits(s, k):
            base = (k % plane * 2 + k // plane) * columns
            lane = lax.broadcasted_iota(jnp.int32, (length, lanes), 1) + base
            return [lane + lanes * q == marks_in[s] for q in range(groups)]

        def logits_of(s, k):
            return matmul(lined[s], block(k))

        def forward(s):
            at = pl.ds(s * length, length)
            peaks[...] = jnp.full_like(peaks, -jnp.inf)
            totals[...] = jnp.zeros_like(totals)
            picks[...] = jnp.zeros_like(picks)

            @pl.loop(0, blocks)
            def _(k):
                logits = logits_of(s, k)
                if keep:
                    exps[k, at] = logits
                high, found = (peaks[...], picks[...])
                for piece, hit in zip(split(logits), hits(s, k)):
                    high = jnp.maximum(high, piece)
                    found = found + jnp.where(hit, piece, 0.0)
                peaks[...] = high
                picks[...] = found

            peak = jnp.max(peaks[...], axis=1, keepdims=True)
            peaks[...] = jnp.broadcast_to(peak, (length, lanes))

            @pl.loop(0, blocks)
            def _(k):
                logits = exps[k, at] if keep else logits_of(s, k)
                total = totals[...]
                for q, piece in enumerate(split(logits)):
                    power = jnp.exp(piece - peaks[...])
                    if keep:
                        exps[k, at, lanes * q : lanes * (q + 1)] = power
                    total = total + power
                totals[...] = total

            if not keep:
                exps[s] = peaks[...]
            lane = lax.broadcasted_iota(jnp.int32, (length, 128), 1)
            total = jnp.sum(totals[...], axis=1, keepdims=True)
            found = jnp.sum(picks[...], axis=1, keepdims=True)
            table = jnp.where(lane == 0, peak, jnp.where(lane == 1, total, found))
            mine[place.zs(s)] = table.T[:8]

        forward(0)
        for s in range(1, nz):
            arriving[s - 1].wait_recv()
            turned[:, s * length : (s + 1) * length] = lined[s].T
            forward(s)
        stats = [comm.send(mine, every.at[s], place.dev(z=s)) for s in range(1, nz)]
        every[0] = mine[...]
        for copy in stats:
            copy.wait_recv()

        def backward(s):
            at = pl.ds(s * length, length)
            held = [every[q, place.zs(s)] for q in range(nz)]
            peak = held[0][0:1]
            for other in held[1:]:
                peak = jnp.maximum(peak, other[0:1])
            total = sum(other[1:2] * jnp.exp(other[0:1] - peak) for other in held)
            weight = counted_in[s : s + 1]
            if s == 0:
                found = sum(other[2:3] for other in held)
                loss = (peak + jnp.log(total) - found) * weight
                loss_out[...] = jnp.concatenate([loss, jnp.zeros((7, length), F32)], axis=0)
            scale = weight / total * jnp.exp(held[0][0:1] - peak)
            tall = jnp.concatenate([scale, weight, jnp.zeros((126, length), F32)], axis=0).T
            columned[0] = jnp.broadcast_to(tall[:, 0:1], (length, lanes))
            columned[1] = jnp.broadcast_to(tall[:, 1:2], (length, lanes))
            partial[...] = jnp.zeros_like(partial)

            @pl.loop(0, blocks)
            def _(k):
                if keep:
                    powers = split(exps[k, at])
                else:
                    powers = [jnp.exp(piece - exps[s]) for piece in split(logits_of(s, k))]
                pieces = []
                for power, hit in zip(powers, hits(s, k)):
                    grad = power * columned[0] - jnp.where(hit, columned[1], 0.0)
                    pieces.append(grad.astype(BF))
                grad = jnp.concatenate(pieces, axis=1) if groups > 1 else pieces[0]
                grads[k, at] = grad
                partial[...] += lax.dot_general(
                    grad, block(k), (((1,), (1,)), ((), ())), preferred_element_type=F32
                )

        coming_in = []
        for s in range(1, nz):
            backward(s)
            back[s - 1] = partial[...].astype(BF)
            coming_in.append(comm.send(back.at[s - 1], coming.at[s - 1], place.dev(z=nz - s)))
        backward(0)

        def weights(into, core):
            @pl.loop(0, plane)
            def _(j):
                into[j // nx, j % nx] = matmul(turned[...], grads[core * plane + j]).astype(BF)

        weights(given, 1 - c)
        pair = comm.send(given, half, place.dev(c=1))
        weights(head_out, c)
        pair.wait_recv()
        add_blocks(head_out, [head_out, half])
        for copy in coming_in:
            copy.wait_recv()
        total = partial[...]
        for s in range(nz - 1):
            total = total + coming[s].astype(F32)
        top_out[...] = total
        comm.finish()

    count = 3 * (nz - 1) + 2 * (2 * plane - 1) + 1
    scratch = [
        pltpu.VMEM((2, ny, nx) + head.shape, BF),
        pltpu.VMEM((nz, length, width), BF),
        pltpu.VMEM((width, nz * length), BF),
        pltpu.VMEM((length, lanes), F32),
        pltpu.VMEM((length, lanes), F32),
        pltpu.VMEM((length, lanes), F32),
        pltpu.VMEM((blocks, nz * length, columns) if keep else (nz, length, lanes), F32),
        pltpu.VMEM((blocks, nz * length, columns), BF),
        pltpu.VMEM((2, length, lanes), F32),
        pltpu.VMEM((length, width), F32),
        pltpu.VMEM((nz - 1, length, width), BF),
        pltpu.VMEM((nz - 1, length, width), BF),
        pltpu.VMEM((nz, 8, length), F32),
        pltpu.VMEM((nz, nz, 8, length), F32),
        pltpu.VMEM((ny, nx) + head.shape, BF),
        pltpu.VMEM((ny, nx) + head.shape, BF),
        sems(count),
        sems(count),
        sems(1),
    ]
    return call(
        kernel,
        [shape((length, width), F32), shape((ny, nx) + head.shape, BF), shape((8, length), F32)],
        [VMEM] * 4, [VMEM] * 3, scratch, cid, "head_all", (rows, head, marks, counted), 62 * 2**20,
    )


def matmul(left, right):
    return jnp.dot(left, right, preferred_element_type=F32)


def norm_forward(values, gain):
    inverse = lax.rsqrt(jnp.mean(values * values, axis=-1, keepdims=True) + EPS_NORM)
    normed = values * inverse
    return (normed * gain, normed, inverse)


def norm_backward(grad, normed, inverse, gain):
    scaled = grad * gain
    inner = jnp.mean(scaled * normed, axis=-1, keepdims=True)
    return (inverse * (scaled - normed * inner), jnp.sum(grad * normed, axis=0))


def turned(value, low):
    return jnp.where(low, -pltpu.roll(value, 112, 1), pltpu.roll(value, 16, 1))


def low_quarters(rows):
    return lax.broadcasted_iota(jnp.int32, (rows, 128), 1) % 32 < 16


def left_half(rows):
    return lax.broadcasted_iota(jnp.int32, (rows, 128), 1) < HD


def times_turned(left, right):
    return lax.dot_general(left, right, (((1,), (1,)), ((), ())), preferred_element_type=F32)


def turned_times(left, right):
    return lax.dot_general(left, right, (((0,), (0,)), ((), ())), preferred_element_type=F32)


def attention_steps(start, gain, angles, allowed, weights, mix, held, probs, out):
    length, width = start.shape
    normed = norm_forward(start[...], gain[0:1])[0].astype(BF)
    low, left = (low_quarters(length), left_half(length))
    for k in range(3):
        value = matmul(normed, weights(k))
        for p in range(width // 128):
            piece = value[:, 128 * p : 128 * p + 128]
            if k < 2:
                piece = piece * angles[0] + turned(piece, low) * angles[1]
            held[k, :, 128 * p : 128 * p + 128] = piece.astype(BF)
        yield
    for p in range(width // 128):
        at = slice(128 * p, 128 * p + 128)
        query, keys, values = (held[0, :, at], held[1, :, at], held[2, :, at])
        parts = []
        for side in range(2):
            own = jnp.where(left == (side == 0), query, jnp.zeros_like(query))
            scores = times_turned(own, keys) * HD ** (-0.5)
            scores = jnp.where(allowed[...] > 0, scores, NEGATIVE_FILL)
            power = jnp.exp(scores - jnp.max(scores, axis=1, keepdims=True))
            power = power / jnp.sum(power, axis=1, keepdims=True)
            probs[2 * p + side] = power
            parts.append(matmul(power.astype(BF), values))
        held[3, :, at] = jnp.where(left, parts[0], parts[1]).astype(BF)
        yield
    out[...] = start[...] + matmul(held[3], mix())
    yield


def attention_back_steps(start, gain, angles, weights, mix, held, probs, grad_mid, put, out, gains):
    length, width = start.shape
    low, left = (low_quarters(length), left_half(length))
    back = grad_mid[...].astype(BF)
    put(3, turned_times(held[3], back))
    grad_out = times_turned(back, mix()).astype(BF)
    yield
    grads = [[], [], []]
    for p in range(width // 128):
        at = slice(128 * p, 128 * p + 128)
        query, keys, values, grad = (held[0, :, at], held[1, :, at], held[2, :, at], grad_out[:, at])
        parts = []
        for side in range(2):
            own = jnp.where(left == (side == 0), grad, jnp.zeros_like(grad))
            grad_probs = times_turned(own, values)
            power = probs[2 * p + side]
            inner = jnp.sum(power * grad_probs, axis=1, keepdims=True)
            score = (power * (grad_probs - inner)).astype(BF)
            parts.append(
                (
                    matmul(score, keys) * HD ** (-0.5),
                    turned_times(score, query) * HD ** (-0.5),
                    turned_times(power.astype(BF), grad),
                )
            )
        for k in range(3):
            value = jnp.where(left, parts[0][k], parts[1][k]).astype(BF)
            if k < 2:
                value = value.astype(F32)
                value = (value * angles[0] - turned(value * angles[1], low)).astype(BF)
            grads[k].append(value)
        yield
    gain_row = gain[0:1]
    normed_gain, normed, inverse = norm_forward(start[...], gain_row)
    normed_gain = normed_gain.astype(BF)
    total = jnp.zeros((length, width), F32)
    for k in range(3):
        grad = jnp.concatenate(grads[k], axis=1)
        put(k, turned_times(normed_gain, grad))
        total = total + times_turned(grad, weights(k))
        yield
    grad, gain_grad = norm_backward(total, normed, inverse, gain_row)
    gains[0:1] = gain_grad.reshape(1, width)
    out[...] = grad_mid[...] + grad
    yield


def local_call(kernel, outs, args, scratch, name, flops, spaces=None):
    spaces = [VMEM] * len(args) if spaces is None else spaces
    return pl.pallas_call(
        kernel,
        out_shape=outs,
        in_specs=spaces,
        out_specs=[VMEM] * len(outs),
        scratch_shapes=scratch,
        compiler_params=pltpu.CompilerParams(vmem_limit_bytes=60 * 2**20),
        cost_estimate=pl.CostEstimate(flops=flops, bytes_accessed=2**24, transcendentals=0),
        name=name,
    )(*args)


def attention_forward(start, gain, angles, allowed, qkv_w, mix_w):
    length, width = start.shape

    def kernel(start, gain, angles, allowed, qkv, mix, held, probs, out):
        def weights(k):
            return qkv[:, width * k : width * (k + 1)]

        drain(attention_steps(start, gain, angles, allowed, weights, lambda: mix[...], held, probs, out))

    outs = [
        shape((4, length, width), BF),
        shape((width // HD, length, length), F32),
        shape((length, width), F32),
    ]
    args = (start, gain, angles, allowed, qkv_w, mix_w)
    return local_call(kernel, outs, args, [], "attention_forward", 2**31)


def attention_backward(start, gain, angles, qkv_w, mix_w, held, probs, grad_mid):
    length, width = start.shape

    def kernel(start, gain, angles, qkv, mix, held, probs, grad_mid, grad_qkv, grad_mix, out, gains):
        def weights(k):
            return qkv[:, width * k : width * (k + 1)]

        def put(k, value):
            if k == 3:
                grad_mix[...] = value.astype(BF)
            else:
                grad_qkv[:, width * k : width * (k + 1)] = value.astype(BF)

        gains[...] = jnp.zeros_like(gains)
        drain(
            attention_back_steps(
                start, gain, angles, weights, lambda: mix[...], held, probs, grad_mid, put, out, gains
            )
        )

    outs = [
        shape(qkv_w.shape, BF),
        shape(mix_w.shape, BF),
        shape((length, width), F32),
        shape((8, width), F32),
    ]
    args = (start, gain, angles, qkv_w, mix_w, held, probs, grad_mid)
    return local_call(kernel, outs, args, [], "attention_backward", 2**32)


PIECE = 512


def feed_forward(middle, gain, expand_w, shrink_w):
    length, width = middle.shape
    inner = shrink_w.shape[0]

    def kernel(middle, gain, expand, shrink, both, final, top):
        normed = norm_forward(middle[...], gain[1:2])[0].astype(BF)
        total = middle[...]
        for k in range(inner // PIECE):
            at = slice(PIECE * k, PIECE * (k + 1))
            up_at = slice(inner + PIECE * k, inner + PIECE * (k + 1))
            gate, up = (matmul(normed, expand[:, at]), matmul(normed, expand[:, up_at]))
            both[:, at] = gate
            both[:, up_at] = up
            hidden = (gate * jax.nn.sigmoid(gate) * up).astype(BF)
            total = total + matmul(hidden, shrink[at])
        final[...] = total
        top[...] = norm_forward(total, gain[2:3])[0].astype(BF)

    outs = [shape((length, 2 * inner), F32), shape((length, width), F32), shape((length, width), BF)]
    args = (middle, gain, expand_w, shrink_w)
    return local_call(kernel, outs, args, [], "feed_forward", 2**32)


def feed_backward(grad_top, final, middle, both, gain, expand_w, shrink_w):
    length, width = middle.shape
    inner = shrink_w.shape[0]

    def kernel(grad_top, final, middle, both, gain, expand, shrink, grad_expand, grad_shrink, out, gains):
        _, normed, inverse = norm_forward(final[...], gain[2:3])
        grad_final, gain_top = norm_backward(grad_top[...], normed, inverse, gain[2:3])
        back = grad_final.astype(BF)
        low, normed, inverse = norm_forward(middle[...], gain[1:2])
        low = low.astype(BF)
        total = jnp.zeros((length, width), F32)
        for k in range(inner // PIECE):
            at = slice(PIECE * k, PIECE * (k + 1))
            up_at = slice(inner + PIECE * k, inner + PIECE * (k + 1))
            gate, up = (both[:, at], both[:, up_at])
            sigma = jax.nn.sigmoid(gate)
            hidden = (gate * sigma * up).astype(BF)
            grad_shrink[at] = turned_times(hidden, back).astype(BF)
            grad = times_turned(back, shrink[at])
            grad_gate = (grad * up * sigma * (1.0 + gate * (1.0 - sigma))).astype(BF)
            grad_up = (grad * gate * sigma).astype(BF)
            grad_expand[:, at] = turned_times(low, grad_gate).astype(BF)
            grad_expand[:, up_at] = turned_times(low, grad_up).astype(BF)
            total = total + times_turned(grad_gate, expand[:, at])
            total = total + times_turned(grad_up, expand[:, up_at])
        grad_middle, gain_two = norm_backward(total, normed, inverse, gain[1:2])
        out[...] = grad_final + grad_middle
        gains[...] = jnp.zeros_like(gains)
        gains[1:2] = gain_two.reshape(1, width)
        gains[2:3] = gain_top.reshape(1, width)

    outs = [
        shape(expand_w.shape, BF),
        shape(shrink_w.shape, BF),
        shape((length, width), F32),
        shape((8, width), F32),
    ]
    args = (grad_top, final, middle, both, gain, expand_w, shrink_w)
    return local_call(kernel, outs, args, [], "feed_backward", 2**33)


def rope_tables(positions, width):
    quarter = width // 4
    freq = 10000.0 ** (-jnp.arange(quarter, dtype=F32) / quarter)
    row_angle = (positions // GRID).astype(F32)[:, None] * freq
    col_angle = (positions % GRID).astype(F32)[:, None] * freq
    angles = jnp.concatenate([row_angle, row_angle, col_angle, col_angle] * (128 // width), axis=-1)
    return jnp.stack([jnp.cos(angles), jnp.sin(angles)])


def adam_update(master, drift, square, grad, rate, decay):
    moment = BETA_ONE * drift + (1.0 - BETA_ONE) * grad
    second = BETA_TWO * square + (1.0 - BETA_TWO) * grad * grad
    stride = (
        moment / (1.0 - BETA_ONE**STEP) / (jnp.sqrt(second / (1.0 - BETA_TWO**STEP)) + ADAM_EPS)
    )
    return (master - rate * (stride + decay * master), moment, second)


def pad_rows(value, rows):
    flat = value.reshape(-1)
    return jnp.pad(flat, (0, rows * 128 - flat.shape[0])).reshape(rows, 128)


def block_form(rows, columns):
    return (rows, columns) if rows % 8 == 0 else (rows * columns // 128, 128)


FIRST_AXES = ("x", "x", "y", "x")


def on_device(dims, *args):
    labels, targets, heights, loss_mask = args[:4]
    masters, drifts, squares = (args[4:12], args[12:20], args[20:28])
    class_table, code_table, attend_in, attend_mix, expand_in, shrink_out, head_weight, norm_gains = masters
    nz, ny, nx = dims
    plane = ny * nx
    chips = nz * plane
    images, local_len = targets.shape
    length = local_len * 2
    width = code_table.shape[1]
    device_codes = code_table.shape[0]
    line_codes = device_codes * plane * 2
    gain_columns = norm_gains.shape[1]
    chip, core = (lax.axis_index("dp"), lax.axis_index("seq"))
    z, y, x = (chip // plane, (chip // nx) % ny, chip % nx)
    plane_groups = [[k * plane + i for i in range(plane)] for k in range(nz)]

    layers = (attend_in, attend_mix, expand_in, shrink_out)
    tail = pad_rows(jnp.concatenate([labels, heights]), 1)
    label_rows = -(-chips * images // 128)
    spread = lax.dynamic_update_slice(jnp.zeros((label_rows * 128,), jnp.int32), labels, (chip * images,))
    spread = jnp.pad(spread.reshape(label_rows, 128), ((0, 3 - label_rows), (0, 0)))
    meta = jnp.concatenate([targets, loss_mask, tail, spread], axis=0)
    *weights, row_parts, metas, smalls = gather_all(
        dims, layers, FIRST_AXES, code_table, class_table, norm_gains, meta, images, 0
    )

    own_tokens = lax.dynamic_slice_in_dim(metas, core, 1, axis=4)[:, :, :, :, 0]
    own_masks = lax.dynamic_slice_in_dim(metas, 2 + core, 1, axis=4)[:, :, :, :, 0]

    def of_line(value):
        value = lax.dynamic_slice_in_dim(value, y, 1, axis=1)
        return lax.dynamic_slice_in_dim(value, x, 1, axis=2).reshape(nz, -1)

    line_targets = of_line(own_tokens)
    line_heights = of_line(lax.dynamic_slice_in_dim(metas[:, :, :, 0, 4], images + core, 1, axis=3))
    places = jnp.arange(length)
    line_counted = (of_line(own_masks) * (places[None, :] < GRID * line_heights)).astype(F32)
    all_labels = metas[:, :, :, 0, 4, :images].reshape(-1)
    before = jnp.concatenate(
        [jnp.full((nz, 1), -1, jnp.int32), line_targets[:, :-1] - z * line_codes], axis=1
    )
    qkv_w, mix_w, expand_w, shrink_w = (v.reshape(-1, v.shape[-1]) for v in weights)

    smalls = smalls.reshape(chips * 2, 8, 128)[:, :, :gain_columns]
    class_row = smalls[:, 0].reshape(1, -1)
    gain = smalls[:, 1:4].transpose(1, 0, 2).reshape(3, -1)
    start = jnp.sum(row_parts.astype(F32), axis=0)
    start = jnp.concatenate([class_row, start[:-1]], axis=0)
    height = lax.dynamic_slice_in_dim(line_heights, z, 1, axis=0).reshape(())

    angles = rope_tables(places, HD)
    allowed = (places[None, :] <= places[:, None]) & (places[None, :] < GRID * height)
    gain = jnp.pad(gain, ((0, 5), (0, 0)))
    held, probs, middle = attention_forward(
        start, gain, angles, allowed.astype(F32), qkv_w, mix_w
    )
    both, final, normed_top = feed_forward(middle, gain, expand_w, shrink_w)

    behind = (z + nz - jnp.arange(nz)) % nz
    marks = (line_targets - z * line_codes)[behind]
    lanes = min(head_weight.shape[1], 128)
    marks = jnp.broadcast_to(marks[:, :, None], (nz, length, lanes))
    grad_top, grad_head, losses = head_all(
        dims, normed_top, head_weight, marks, line_counted[behind], 2
    )
    loss_local = jnp.sum(losses[0])
    count_local = jnp.sum(lax.dynamic_slice_in_dim(line_counted, z, 1, axis=0))
    grad_head = grad_head.reshape((plane,) + head_weight.shape)
    grad_head = lax.psum_scatter(grad_head, "dp", axis_index_groups=plane_groups)

    grad_expand, grad_shrink, grad_middle, gain_high = feed_backward(
        grad_top, final, middle, both, gain, expand_w, shrink_w
    )
    grad_qkv, grad_mix, grad_start, gain_low = attention_backward(
        start, gain, angles, qkv_w, mix_w, held, probs, grad_middle
    )
    gain_grads = (gain_high + gain_low)[:3]

    grads_in = []
    for grad, shard in zip((grad_qkv, grad_mix, grad_expand, grad_shrink), layers):
        grads_in.append(grad.astype(BF).reshape(dims + (2,) + block_form(*shard.shape)))
    small = jnp.concatenate([grad_start[:1], gain_grads], axis=0)
    small = small.reshape(4, chips * 2, gain_columns).transpose(1, 0, 2)
    small = jnp.pad(small, ((0, 0), (0, 4), (0, 128 - gain_columns))).reshape(dims + (2, 8, 128))
    same = (all_labels[:, None] == all_labels[None, :]).astype(F32)
    partial = pad_rows(jnp.stack([jnp.zeros(()), loss_local, count_local]), 8)
    *layer_shares, code_share, smalls, sums = scatter_all(
        dims,
        grads_in,
        FIRST_AXES,
        grad_start.astype(BF),
        before[behind].reshape(-1, 128),
        grad_head,
        small,
        same,
        partial,
        device_codes,
        4,
    )
    small_mine = smalls.reshape(chips * 2, 8, 128)[:, :4, :gain_columns]
    class_pick = all_labels[:, None] == jnp.arange(class_table.shape[0])[None, :]
    class_share = jnp.dot(
        class_pick.astype(F32).T,
        small_mine[:, 0],
        precision=lax.Precision.HIGHEST,
        preferred_element_type=F32,
    )
    gain_share = jnp.sum(small_mine[:, 1:], axis=0)
    layer_shares = [g.reshape(v.shape) for g, v in zip(layer_shares, layers)]
    shares = (class_share, code_share, *layer_shares, grad_head.astype(F32), gain_share)
    total_square, loss_sum, loss_count = (sums[0, 0], sums[0, 1], sums[0, 2])
    grad_norm = jnp.sqrt(total_square) / loss_count
    factor = CLIP_NORM / jnp.maximum(grad_norm, CLIP_NORM) / loss_count
    news, firsts, seconds = ([], [], [])
    for member in range(8):
        fresh, moment, second = adam_update(
            masters[member],
            drifts[member],
            squares[member],
            shares[member] * factor,
            RATES[member],
            DECAYS[member],
        )
        news.append(fresh)
        firsts.append(moment)
        seconds.append(second)
    return tuple(news) + tuple(firsts) + tuple(seconds) + (grad_norm, loss_sum, loss_count)


def solution(mesh):
    rows, columns = (P(("dp", "seq"), None), P(None, ("dp", "seq")))
    eight = (columns, rows, rows, rows, rows, rows, columns, columns)
    return jax.shard_map(
        functools.partial(on_device, dims_of(mesh.shape["dp"])),
        mesh=mesh,
        in_specs=(P("dp"), P("dp", "seq"), P("dp"), P("dp", "seq")) + eight * 3,
        out_specs=eight * 3 + (P(), P(), P()),
        check_vma=False,
    )
```

```python
import functools

import jax
import jax.numpy as jnp
import numpy as np
from jax import lax
from jax.experimental import pallas as pl
from jax.experimental.pallas import tpu as pltpu
from jax.sharding import PartitionSpec as P

HD = 64
GRID = 16
STEP = 10

EPS_NORM = 1e-05
BETA_ONE = 0.9
BETA_TWO = 0.95
ADAM_EPS = 1e-08
CLIP_NORM = 0.01
NEGATIVE_FILL = -1000000000.0
RATES = (0.8, 0.8, 0.08, 0.08, 0.08, 0.08, 0.08, 0.8)
DECAYS = (0.1, 0.1, 0.1, 0.1, 0.1, 0.1, 0.1, 0.0)

PIECE = 512

MESH = pl.DeviceIdType.MESH
ANY = pl.BlockSpec(memory_space=pl.ANY)
VMEM = pl.BlockSpec(memory_space=pltpu.VMEM)
SMEM = pl.BlockSpec(memory_space=pltpu.SMEM)
BF = jnp.bfloat16
F32 = jnp.float32


def dims_of(dp):
    bits = dp.bit_length() - 1
    nz = 1 << (bits // 2)
    rest = dp // nz
    ny = 1 << ((rest.bit_length() - 1) // 2)
    return (nz, ny, rest // ny)


class Place:
    def __init__(self, dims):
        self.dims = dims
        nz, ny, nx = dims
        chip = lax.axis_index("dp")
        self.c = lax.axis_index("seq")
        self.z = chip // (ny * nx)
        self.y = (chip // nx) % ny
        self.x = chip % nx

    def zs(self, back):
        return (self.z + self.dims[0] - back) % self.dims[0]

    def ys(self, back):
        return (self.y + self.dims[1] - back) % self.dims[1]

    def xs(self, back):
        return (self.x + self.dims[2] - back) % self.dims[2]

    def dev(self, z=0, y=0, x=0, c=0):
        nz, ny, nx = self.dims
        z, y, x = ((self.z + z) % nz, (self.y + y) % ny, (self.x + x) % nx)
        return ((z * ny + y) * nx + x, (self.c + c) % 2)


def line_offsets(dims):
    nz, ny, nx = dims
    return (
        [(s, 0, 0, 0) for s in range(1, nz)]
        + [(0, s, 0, 0) for s in range(1, ny)]
        + [(0, 0, s, 0) for s in range(1, nx)]
        + [(0, 0, 0, 1)]
    )


def plane_offsets(dims):
    return [(0, v, u, 0) for v in range(dims[1]) for u in range(dims[2]) if v or u]


def greet(place, offsets):
    offsets = sorted(set(offsets))
    sem = pltpu.get_barrier_semaphore()
    for off in offsets:
        pl.semaphore_signal(sem, inc=1, device_id=place.dev(*off), device_id_type=MESH)
    pl.semaphore_wait(sem, len(offsets))


class Comm:
    def __init__(self, send_sems, recv_sems, local_sems):
        self.send_sems, self.recv_sems, self.local_sems = (send_sems, recv_sems, local_sems)
        self.sent, self.held, self.count, self.locals = ([], [], 0, 0)

    def send(self, src, dst, device):
        k = self.count
        self.count += 1
        copy = pltpu.make_async_remote_copy(
            src_ref=src,
            dst_ref=dst,
            send_sem=self.send_sems.at[k],
            recv_sem=self.recv_sems.at[k],
            device_id=device,
            device_id_type=MESH,
        )
        copy.start()
        self.sent.append(copy)
        return copy

    def keep(self, src, dst):
        copy = pltpu.make_async_copy(src, dst, self.local_sems.at[self.locals])
        self.locals += 1
        copy.start()
        self.held.append(copy)
        return copy

    def gone(self, copy):
        copy.wait_send()
        self.sent = [other for other in self.sent if other is not copy]

    def done(self, copy):
        copy.wait()
        self.held = [other for other in self.held if other is not copy]

    def finish(self):
        for copy in self.sent:
            copy.wait_send()
        for copy in self.held:
            copy.wait()


def drain(steps):
    for _ in steps:
        pass


def all_offsets(dims):
    nz, ny, nx = dims
    spots = [(k, j, i, core) for k in range(nz) for j in range(ny) for i in range(nx) for core in range(2)]
    return spots[1:]


def small_exchange(comm, place, src, out, own):
    z, y, x, c = (place.z, place.y, place.x, place.c)
    nz, ny, nx = place.dims
    if own:
        comm.keep(src(z, y, x, c), out.at[z, y, x, c])
    got = []
    for off in all_offsets(place.dims):
        there = (place.zs(nz - off[0]), place.ys(ny - off[1]), place.xs(nx - off[2]), (c + off[3]) % 2)
        got.append(comm.send(src(*there), out.at[z, y, x, c], place.dev(*off)))
    return got


class PlaneGather:
    def __init__(self, comm, place):
        self.comm, self.place = (comm, place)
        self.firsts, self.seconds, self.mates = ([], [], [])

    def ways(self, axis):
        _, ny, nx = self.place.dims
        return range(1, ny if axis == "y" else nx)

    def back(self, axis, t, yy, xx):
        return (self.place.ys(t), xx) if axis == "y" else (yy, self.place.xs(t))

    def spread(self, block, first, src=None):
        place, second = (self.place, "y" if first == "x" else "x")
        dst = block(place.y, place.x)
        src = dst if src is None else src
        for t in self.ways(first):
            copy = self.comm.send(src, dst, place.dev(**{first: t}))
            self.firsts.append((block, first, second, t, copy))
        for t in self.ways(second):
            copy = self.comm.send(src, dst, place.dev(**{second: t}))
            self.seconds.append((block(*self.back(second, t, place.y, place.x)), copy))
        self.mates.append(self.comm.send(src, dst, place.dev(c=1)))

    def forward(self):
        place = self.place
        for block, first, second, t, copy in self.firsts:
            copy.wait_recv()
            yy, xx = self.back(first, t, place.y, place.x)
            held = block(yy, xx)
            for u in self.ways(second):
                copy = self.comm.send(held, held, place.dev(**{second: u}))
                self.seconds.append((block(*self.back(second, u, yy, xx)), copy))
            self.mates.append(self.comm.send(held, held, place.dev(c=1)))
        self.firsts = []

    def settle(self):
        for held, copy in self.seconds:
            copy.wait_recv()
            self.mates.append(self.comm.send(held, held, self.place.dev(c=1)))
        self.seconds = []

    def forward_some(self, count):
        rest = self.firsts[count:]
        self.firsts = self.firsts[:count]
        self.forward()
        self.firsts = rest

    def arrive(self):
        for copy in self.mates:
            copy.wait_recv()
        self.mates = []


def sems(count):
    return pltpu.SemaphoreType.DMA((count,))


def shape(dims, dtype):
    return jax.ShapeDtypeStruct(tuple(dims), dtype)


def call(kernel, outs, in_specs, out_specs, scratch, cid, name, args, vmem=None):
    return pl.pallas_call(
        kernel,
        out_shape=outs,
        in_specs=in_specs,
        out_specs=out_specs,
        scratch_shapes=scratch,
        compiler_params=pltpu.CompilerParams(
            collective_id=cid, has_side_effects=True, vmem_limit_bytes=vmem
        ),
        name=name,
    )(*args)


def small_sends(dims):
    return dims[0] * dims[1] * dims[2] * 2 - 1


def gather_all(dims, layers, first_axes, table, classes, gains, labels, targets, heights, masks, cid):
    nz, ny, nx = dims
    n = len(layers)
    rows, width = table.shape
    images, local_len = targets.shape
    length = local_len * 2
    columns = gains.shape[1]
    meta = (8, 128)
    count_images = nz * ny * nx * images
    label_rows = -(-count_images // 128)
    groups = [(k,) for k in range(nz)] if nz <= 4 else [tuple(range(nz))]

    def kernel(*refs):
        ins, rest = (refs[:n], refs[n:])
        table_in, class_in, gain_in, labels_in, targets_in, heights_in, masks_in, *rest = rest
        outs, rest = (rest[:n], rest[n:])
        start_out, gain_out, meta_out, allowed_out, *rest = rest
        low, rest = (rest[:n], rest[n:])
        whole, found, total, class_low, gain_row, meta_in, parts_out, small_out, small_in, *rest = rest
        ssem, rsem, lsem = rest
        place = Place(dims)
        z, y, x, c = (place.z, place.y, place.x, place.c)
        chip = (z * ny + y) * nx + x
        meta_in[...] = jnp.zeros_like(meta_in)
        meta_in[0:images] = targets_in[...]
        meta_in[images : 2 * images] = masks_in[...]
        lane = lax.broadcasted_iota(jnp.int32, (1, 128), 1)
        for i in range(images):
            meta_in[4:5] += jnp.where(lane == i, labels_in[i], 0)
            meta_in[4:5] += jnp.where(lane == images + i, heights_in[i], 0)
            for r in range(label_rows):
                meta_in[5 + r : 6 + r] += jnp.where(lane == chip * images + i - 128 * r, labels_in[i], 0)
        greet(place, all_offsets(dims))
        comm = Comm(ssem, rsem, lsem)
        metas = small_exchange(comm, place, lambda *spot: meta_in, meta_out, False)
        meta_out[z, y, x, c] = meta_in[...]
        waits = []
        whole[y, x, c] = table_in[...].astype(BF)
        tables, blocks = (PlaneGather(comm, place), PlaneGather(comm, place))
        for first, start in (("x", 0), ("y", rows // 2)):
            half = pl.ds(start, rows // 2)
            tables.spread(lambda yy, xx, half=half: whole.at[yy, xx, c, half], first)
        for a in range(n):
            low[a][...] = ins[a][...].astype(BF)
        along = {}
        for s in range(1, nz):
            for a in range(n):
                along[s, a] = comm.send(low[a], outs[a].at[z, y, x, c], place.dev(z=s))
        kept = [comm.keep(low[a], outs[a].at[z, y, x, c]) for a in range(n)]

        def spread(group):
            for a in range(n):
                for k in group:
                    if k:
                        along[k, a].wait_recv()
                if len(group) > 1:
                    comm.done(kept[a])
                    at = pl.ds(0, nz)
                else:
                    at = place.zs(group[0])
                blocks.spread(
                    lambda yy, xx, a=a, at=at: outs[a].at[at, yy, xx, c],
                    first_axes[a],
                    low[a] if group == (0,) else None,
                )

        for copy in metas:
            copy.wait_recv()

        class_low[...] = jnp.zeros_like(class_low)
        class_low[0:columns, 0 : class_in.shape[1]] = class_in[...]
        small_in[...] = jnp.zeros_like(small_in)
        for r in range(label_rows):
            labels = jnp.zeros((1, 128), jnp.int32)
            for k in range(nz * ny * nx):
                labels = labels + meta_out[k // (ny * nx), k // nx % ny, k % nx, 0, 5 + r : 6 + r, :]
            pick = lax.broadcasted_iota(jnp.int32, (class_low.shape[1], 128), 0) == labels
            picked = lax.dot_general(
                jnp.where(pick, 1.0, 0.0).astype(BF),
                class_low[...].astype(BF),
                (((0,), (1,)), ((), ())),
                preferred_element_type=F32,
            )
            for i in range(min(128, count_images - 128 * r)):
                k, core = divmod(128 * r + i, 2)
                small_in[k // (ny * nx), k // nx % ny, k % nx, core, 0:1, 0 : class_low.shape[0]] = picked[
                    i : i + 1
                ]
        gain_row[...] = jnp.zeros_like(gain_row)
        gain_row[0:3, 0:columns] = gain_in[...].astype(BF).astype(F32)

        @pl.loop(0, nz)
        def _(k):
            for j in range(ny):
                for i in range(nx):
                    for core in range(2):
                        small_in[k, j, i, core, 1:4, :] = gain_row[0:3]

        smalls = small_exchange(comm, place, lambda *spot: small_in.at[spot], small_out, False)
        small_out[z, y, x, c] = small_in[z, y, x, c]

        size = len(layers)
        steps = [lambda group=group: spread(group) for group in groups]
        steps.pop(0)()
        tables.forward()
        if steps:
            steps.pop(0)()
        blocks.forward_some(size)
        if steps:
            steps.pop(0)()
        tables.settle()
        blocks.forward_some(size)
        for step in steps:
            step()
        tables.arrive()

        for s in range(1, nz + 1):
            zz = place.zs(s % nz)
            halves = []
            for half in range(2):
                codes = meta_out[zz, y, x, half, pl.ds(c, 1), :].astype(F32)
                halves.append(jnp.broadcast_to(codes, (128, local_len)).T)
            column = jnp.concatenate(halves, axis=0)
            column = column - (z * ny * nx * 2 * rows).astype(F32)
            total[...] = jnp.zeros_like(total)

            @pl.loop(0, ny * nx * 2)
            def _(j):
                base = (j * rows).astype(F32)
                lane = lax.broadcasted_iota(jnp.int32, (length, 128), 1).astype(F32) + base
                picks = [
                    jnp.where(column == lane + float(128 * q), 1.0, 0.0).astype(BF)
                    for q in range(-(-rows // 128))
                ]
                pick = jnp.concatenate(picks, axis=1)[:, :rows]
                total[...] += matmul(pick, whole[j // (2 * nx), j // 2 % nx, j % 2])

            found[s % nz] = total[...].astype(BF)
            if s < nz:
                waits.append(comm.send(found.at[s], parts_out.at[nz - s - 1], place.dev(z=nz - s)))
            blocks.forward_some(size)
        blocks.forward()
        height = jnp.where(c == 0, heights_in[0], heights_in[images - 1])
        query = lax.broadcasted_iota(jnp.int32, (length, length), 0)
        key = lax.broadcasted_iota(jnp.int32, (length, length), 1)
        allowed_out[...] = jnp.where((key <= query) & (key < GRID * height), 1.0, 0.0)
        for copy in smalls:
            copy.wait_recv()
        joined = jnp.zeros((8, width), F32)
        blank = jnp.zeros((8, width - 128), F32)
        for d in range(2 * nz * ny * nx):
            k, core = divmod(d, 2)
            piece = small_out[k // (ny * nx), k // nx % ny, k % nx, core]
            joined = joined + pltpu.roll(jnp.concatenate([piece, blank], axis=1), columns * d, 1)
        gain_out[...] = jnp.concatenate([joined[1:4], jnp.zeros((5, width), F32)], axis=0)
        blocks.settle()
        for copy in waits:
            copy.wait_recv()
        added = found[0].astype(F32)
        for s in range(1, nz):
            added = added + parts_out[s - 1].astype(F32)
        first = lax.broadcasted_iota(jnp.int32, (length, 128), 0) == 0
        for k in range(width // 128):
            at = slice(128 * k, 128 * k + 128)
            start_out[:, at] = jnp.where(first, joined[0:1, at], pltpu.roll(added[:, at], 1, 0))
        blocks.arrive()
        comm.finish()

    count = n * (nz - 1) + (n * len(groups) + 2) * (2 * ny * nx - 1) + nz + 2 * small_sends(dims)
    small = dims + (2, 8, 128)
    outs = [shape(dims + (2,) + v.shape, BF) for v in layers]
    outs += [
        shape((length, width), F32),
        shape((8, width), F32),
        shape(dims + (2,) + meta, jnp.int32),
        shape((length, length), F32),
    ]
    scratch = [pltpu.VMEM(v.shape, BF) for v in layers]
    scratch += [
        pltpu.VMEM((ny, nx, 2) + table.shape, BF),
        pltpu.VMEM((nz, length, width), BF),
        pltpu.VMEM((length, width), F32),
        pltpu.VMEM((-(-columns // 16) * 16, -(-classes.shape[1] // 128) * 128), F32),
        pltpu.VMEM((8, 128), F32),
        pltpu.VMEM(meta, jnp.int32),
        pltpu.VMEM((nz - 1, length, width), BF),
        pltpu.VMEM(small, F32),
        pltpu.VMEM(small, F32),
        sems(count),
        sems(count),
        sems(n),
    ]
    return call(
        kernel, outs, [VMEM] * (n + 3) + [SMEM, VMEM, SMEM, VMEM], [ANY] * n + [VMEM] * 4, scratch,
        cid, "gather_all", (*layers, table, classes, gains, labels, targets, heights, masks), 60 * 2**20,
    )


def add_blocks(out, terms):
    lead = out.shape[:-2]

    def visit(index):
        if len(index) < len(lead):

            @pl.loop(0, lead[len(index)])
            def _(i):
                visit(index + (i,))

        else:
            if len(terms) == 2 and out.dtype == BF:
                out[index] = terms[0][index] + terms[1][index]
                return
            total = terms[0][index].astype(F32)
            for term in terms[1:]:
                total = total + term[index].astype(F32)
            out[index] = total.astype(out.dtype)

    visit(())


def items_of(shapes, axes):
    if shapes[0][0] % 8:
        return [[(a, slice(0, shapes[a][0]), slice(0, shapes[a][1]), axes[a]) for a in pair] for pair in ((2, 3), (0, 1))]
    (rows, qkv), (_, mix), (_, both), (deep, width) = shapes
    every, piece = (slice(0, rows), both // 4)
    return [
        [(3, slice(0, deep // 2), slice(0, width), "x"), (3, slice(deep // 2, deep), slice(0, width), "y")],
        [(2, every, slice(0, piece), "x"), (2, every, slice(2 * piece, 3 * piece), "y")],
        [(0, every, slice(0, 2 * mix), "x"), (0, every, slice(2 * mix, qkv), "y"), (1, every, slice(0, mix), "y")],
        [(2, every, slice(piece, 2 * piece), "x"), (2, every, slice(3 * piece, both), "y")],
    ]


def scatter_all(dims, grads, axes, rows, gains, metas, head, partial, device_codes, classes, cid):
    nz, ny, nx = dims
    plane = ny * nx
    n = len(grads)
    shapes = [g.shape[4:] for g in grads]
    steps = items_of(shapes, axes)
    items = [item for step in steps for item in step]
    order, at = ([], 0)
    for step in steps:
        order.append(list(range(at, at + len(step))))
        at += len(step)
    length, width = rows.shape
    block = (device_codes, width)
    sizes = {"x": nx, "y": ny}
    columns = width // (2 * nz * plane)
    label_rows = -(-2 * nz * plane // 128)

    def kernel(*refs):
        parts, rest = (refs[:n], list(refs[n:]))
        rows_in, gains_in, meta_in, head_in, partial_in = (rest.pop(0) for _ in range(5))
        outs = [rest.pop(0) for _ in range(n)]
        table_out, class_out, gain_out, sums = (rest.pop(0) for _ in range(4))
        owns, halves, ones, twos, threes = ([rest.pop(0) for _ in items] for _ in range(5))
        near, far = ([rest.pop(0), rest.pop(0)] for _ in range(2))
        lined, given, own, half, small_in, small_out, tops, mine, every, ssem, rsem, lsem = rest
        place = Place(dims)
        z, y, x, c = (place.z, place.y, place.x, place.c)
        comm = Comm(ssem, rsem, lsem)
        kept = []
        for i, (a, span, cols, _) in enumerate(items):
            kept.append(comm.keep(parts[a].at[:, :, :, c, span, cols], owns[i]))
        lane = lax.broadcasted_iota(jnp.int32, (8, 128), 1)
        top = jnp.concatenate([rows_in[0:1], gains_in[0:3], jnp.zeros((4, width), F32)], axis=0)
        for d in range(2 * nz * plane):
            k, core = divmod(d, 2)
            piece = pltpu.roll(top, (width - columns * d) % width, 1)[:, :128]
            small_in[k // plane, k // nx % ny, k % nx, core] = jnp.where(lane < columns, piece, 0.0)
        greet(place, all_offsets(dims))
        waits = small_exchange(comm, place, lambda *spot: small_in.at[spot], small_out, False)
        small_out[z, y, x, c] = small_in[z, y, x, c]
        pair, got_one, got_two, third = ({}, {}, {}, {})

        def set_out(g):
            for i in order[g] if g < len(order) else []:
                a, span, cols, _ = items[i]
                pair[i] = comm.send(parts[a].at[:, :, :, 1 - c, span, cols], halves[i], place.dev(c=1))

        def back(axis, t):
            return place.ys(ny - t) if axis == "y" else place.xs(nx - t)

        def first_add(g):
            for i in order[g]:
                pair[i].wait_recv()
                comm.done(kept[i])
                add_blocks(halves[i], [halves[i], owns[i]])

        def first_send(g):
            for i in order[g]:
                axis = items[i][3]
                got_one[i] = [
                    comm.send(
                        halves[i].at[:, back(axis, t)] if axis == "y" else halves[i].at[:, :, back(axis, t)],
                        ones[i].at[t - 1],
                        place.dev(**{axis: t}),
                    )
                    for t in range(1, sizes[axis])
                ]

        def second_step(g):
            for i in order[g]:
                axis = items[i][3]
                other = "x" if axis == "y" else "y"
                for copy in got_one[i]:
                    copy.wait_recv()
                held = halves[i].at[:, y] if axis == "y" else halves[i].at[:, :, x]
                add_blocks(held, [held] + [ones[i].at[t] for t in range(ones[i].shape[0])])
                got_two[i] = [
                    comm.send(
                        halves[i].at[:, y, back("x", t)] if other == "x" else halves[i].at[:, back("y", t), x],
                        twos[i].at[t - 1],
                        place.dev(**{other: t}),
                    )
                    for t in range(1, sizes[other])
                ]

        def third_step(g):
            for i in order[g]:
                for copy in got_two[i]:
                    copy.wait_recv()
                held = halves[i].at[:, y, x]
                add_blocks(held, [held] + [twos[i].at[t] for t in range(twos[i].shape[0])])
                third[i] = [
                    comm.send(halves[i].at[place.zs(nz - s), y, x], threes[i].at[s - 1], place.dev(z=s))
                    for s in range(1, nz)
                ]

        def last_step(g):
            for i in order[g]:
                a, span, cols, _ = items[i]
                for copy in third[i]:
                    copy.wait_recv()
                terms = [halves[i].at[z, y, x]] + [threes[i].at[s] for s in range(nz - 1)]
                add_blocks(outs[a].at[span, cols], terms)

        flat = []
        first = lax.broadcasted_iota(jnp.int32, (1, length), 1) == 0
        for s in range(nz):
            codes = [meta_in[place.zs(s), y, x, part, pl.ds(c, 1), :] for part in range(2)]
            codes = pltpu.roll(jnp.concatenate(codes, axis=1) - z * (2 * plane * device_codes), 1, 1)
            flat.append(jnp.where(first, -1, codes))
        flat = jnp.concatenate(flat, axis=1)

        def product(into, core):
            @pl.loop(0, plane)
            def _(j):
                code = lax.broadcasted_iota(jnp.int32, (device_codes, nz * length), 0)
                pick = code + (j * 2 + core) * device_codes == flat
                pick = jnp.where(pick, 1.0, 0.0).astype(BF)
                value = matmul(pick, lined[...].reshape(nz * length, width))
                into[j // nx, j % nx] = value.astype(BF)

        set_out(0)
        set_out(1)
        lined[0] = rows_in[...].astype(BF)
        lines = [comm.send(lined.at[0], lined.at[s], place.dev(z=s)) for s in range(1, nz)]
        count = len(order)
        for g in range(count):
            first_add(g)
            set_out(g + 2)
            if g >= 2:
                second_step(g - 2)
            first_send(g)
            if g >= 3:
                third_step(g - 3)
        for copy in lines:
            copy.wait_recv()
        product(given, 1 - c)
        table_pair = comm.send(given, half, place.dev(c=1))
        second_step(count - 2)
        product(own, c)
        if count > 2:
            third_step(count - 3)
        second_step(count - 1)
        table_pair.wait_recv()
        add_blocks(half, [half, own])
        parts_of = [pl.ds(0, device_codes // 2), pl.ds(device_codes // 2, device_codes // 2)]
        came = [
            [
                comm.send(half.at[:, back("x", t), parts_of[0]], near[0].at[t - 1], place.dev(x=t))
                for t in range(1, nx)
            ],
            [
                comm.send(half.at[back("y", t), :, parts_of[1]], near[1].at[t - 1], place.dev(y=t))
                for t in range(1, ny)
            ],
        ]
        third_step(count - 2)
        third_step(count - 1)

        for copy in waits:
            copy.wait_recv()
        gain_out[...] = jnp.zeros_like(gain_out)
        tops[...] = jnp.zeros_like(tops)

        @pl.loop(0, nz)
        def _(k):
            for j in range(ny):
                for i in range(nx):
                    for core in range(2):
                        at = ((k * ny + j) * nx + i) * 2 + core
                        tops[pl.ds(at, 1), :] = small_out[k, j, i, core, 0:1, :]
                        gain_out[...] += small_out[k, j, i, core]

        value = jnp.zeros(class_out.shape, F32)
        for r in range(label_rows):
            labels = jnp.zeros((1, 128), jnp.int32)
            for k in range(nz * plane):
                labels = labels + meta_in[k // plane, k // nx % ny, k % nx, 0, 5 + r : 6 + r, :]
            at = lax.broadcasted_iota(jnp.int32, class_out.shape, 1) + 128 * r
            pick = lax.broadcasted_iota(jnp.int32, class_out.shape, 0) == labels
            pick = jnp.where(pick & (at < 2 * nz * plane), 1.0, 0.0)
            value = value + jnp.dot(
                pick,
                tops[128 * r : 128 * r + 128],
                precision=lax.Precision.HIGHEST,
                preferred_element_type=F32,
            )
        class_out[...] = value
        row = lax.broadcasted_iota(jnp.int32, gain_out.shape, 0)
        gained = jnp.where((row >= 1) & (row < 4), gain_out[...], 0.0)
        square = jnp.sum(value * value) + jnp.sum(gained * gained)
        share = head_in[...].astype(F32)
        square = square + jnp.sum(share * share)
        for g in range(count - 1):
            last_step(g)

        for copy in came[0] + came[1]:
            copy.wait_recv()
        for h, held in ((0, half.at[:, x, parts_of[0]]), (1, half.at[y, :, parts_of[1]])):
            add_blocks(held, [held] + [near[h].at[t] for t in range(near[h].shape[0])])
        came = [
            comm.send(half.at[back("y", t), x, parts_of[0]], far[0].at[t - 1], place.dev(y=t))
            for t in range(1, ny)
        ]
        came += [
            comm.send(half.at[y, back("x", t), parts_of[1]], far[1].at[t - 1], place.dev(x=t))
            for t in range(1, nx)
        ]
        last_step(count - 1)
        for a in range(n):
            square = square + jnp.sum(outs[a][...] * outs[a][...])
        for copy in came:
            copy.wait_recv()
        for h in range(2):
            terms = [half.at[y, x, parts_of[h]]] + [far[h].at[t] for t in range(far[h].shape[0])]
            add_blocks(table_out.at[parts_of[h]], terms)
        square = square + jnp.sum(table_out[...] * table_out[...])
        first = (lax.broadcasted_iota(jnp.int32, mine.shape, 0) == 0) & (
            lax.broadcasted_iota(jnp.int32, mine.shape, 1) == 0
        )
        mine[...] = partial_in[...] + jnp.where(first, square, 0.0)
        for copy in small_exchange(comm, place, lambda *spot: mine, every, False):
            copy.wait_recv()
        every[z, y, x, c] = mine[...]
        sums[...] = jnp.zeros_like(sums)

        @pl.loop(0, nz)
        def _(k):
            for j in range(ny):
                for i in range(nx):
                    sums[...] += every[k, j, i, 0] + every[k, j, i, 1]

        comm.finish()

    total = len(items) * (ny + nx - 1 + nz - 1) + nz + 2 * (ny + nx) + 2 * small_sends(dims)
    cuts = [(span.stop - span.start, cols.stop - cols.start) for _, span, cols, _ in items]
    near_far = [(ny, nx) if item[3] == "y" else (nx, ny) for item in items]
    part = (device_codes // 2, width)
    scratch = [pltpu.VMEM((nz, ny, nx) + t, BF) for t in cuts] * 2
    scratch += [pltpu.VMEM((u - 1, nz, v) + t, BF) for t, (u, v) in zip(cuts, near_far)]
    scratch += [pltpu.VMEM((v - 1, nz) + t, BF) for t, (u, v) in zip(cuts, near_far)]
    scratch += [pltpu.VMEM((nz - 1,) + t, BF) for t in cuts]
    scratch += [
        pltpu.VMEM((nx - 1, ny) + part, BF),
        pltpu.VMEM((ny - 1, nx) + part, BF),
        pltpu.VMEM((ny - 1,) + part, BF),
        pltpu.VMEM((nx - 1,) + part, BF),
        pltpu.VMEM((nz, length, width), BF),
        pltpu.VMEM((ny, nx) + block, BF),
        pltpu.VMEM((ny, nx) + block, BF),
        pltpu.VMEM((ny, nx) + block, BF),
        pltpu.VMEM(dims + (2, 8, 128), F32),
        pltpu.VMEM(dims + (2, 8, 128), F32),
        pltpu.VMEM((128 * label_rows, 128), F32),
        pltpu.VMEM(partial.shape, F32),
        pltpu.VMEM(dims + (2,) + partial.shape, F32),
        sems(total),
        sems(total),
        sems(len(items)),
    ]
    outs = [shape(t, F32) for t in shapes]
    deep = -(-classes // 8) * 8
    outs += [shape(block, F32), shape((deep, 128), F32), shape((8, 128), F32), shape(partial.shape, F32)]
    return call(
        kernel, outs, [ANY] * n + [VMEM] * 5, [VMEM] * (n + 4), scratch,
        cid, "scatter_all", (*grads, rows, gains, metas, head, partial), 60 * 2**20,
    )


def head_all(dims, middle, gain, metas, head, expand_w, shrink_w, images, cid):
    nz, ny, nx = dims
    length, width = middle.shape
    inner = shrink_w.shape[0]
    pieces = inner // PIECE
    columns = head.shape[1]
    lanes = min(columns, 128)
    groups = columns // lanes
    plane = ny * nx
    blocks = 2 * plane
    keep = columns >= 128
    shared = columns == PIECE and nz * length >= width and blocks >= 2 * pieces

    def kernel(*refs):
        middle_in, gain_in, meta_in, head_in, expand_in, shrink_in, *rest = refs
        top_out, head_out, loss_out, both_out, final_out, *rest = rest
        whole, marks_in, wide, lined, turned, peaks, totals, picks, exps, grads, *rest = rest
        columned, partial, back, coming, mine, every, given, half, ssem, rsem, lsem = rest
        place = Place(dims)
        z, y, x, c = (place.z, place.y, place.x, place.c)
        greet(place, line_offsets(dims))
        comm = Comm(ssem, rsem, lsem)
        room, loads = ({}, {})

        def load(j):
            room[j] = grads.at[j, pl.ds(0, width)] if shared else wide.at[j // pieces]
            loads[j] = comm.keep(expand_in.at[:, pl.ds(PIECE * j, PIECE)], room[j])

        for j in range(2 * pieces) if shared else []:
            load(j)
        whole[c, y, x] = head_in[...].astype(BF)
        gather = PlaneGather(comm, place)
        for first, start in (("x", 0), ("y", width // 2)):
            part = pl.ds(start, width // 2)
            gather.spread(lambda yy, xx, part=part: whole.at[c, yy, xx, part], first)
        normed = norm_forward(middle_in[...], gain_in[1:2])[0].astype(BF)
        total = middle_in[...]
        for j in range(pieces):
            at = slice(PIECE * j, PIECE * (j + 1))
            for k in (j, pieces + j):
                if not shared:
                    load(k)
                comm.done(loads[k])
            gate, up = (matmul(normed, room[j][...]), matmul(normed, room[pieces + j][...]))
            both_out[:, at] = gate
            both_out[:, inner + PIECE * j : inner + PIECE * (j + 1)] = up
            hidden = (gate * jax.nn.sigmoid(gate) * up).astype(BF)
            total = total + matmul(hidden, shrink_in[at])
        final_out[...] = total
        lined[0] = norm_forward(total, gain_in[2:3])[0].astype(BF)
        turns = sorted(range(1, nz), key=lambda s: min(s, nz - s))
        arriving = {s: comm.send(lined.at[0], lined.at[s], place.dev(z=s)) for s in turns[:2]}
        turned[:, 0:length] = lined[0].T
        for s in range(nz):
            for part in range(2):
                codes = meta_in[place.zs(s), y, x, part, pl.ds(c, 1), :].astype(F32)
                tall = jnp.broadcast_to(codes, (128, 128)).T.astype(jnp.int32)
                marks_in[s, 128 * part : 128 * part + 128] = tall[:, :lanes] - z * (blocks * columns)
        gather.forward()
        gather.settle()
        for s in turns[:2]:
            comm.gone(arriving[s])
        for s in turns[2:]:
            arriving[s] = comm.send(lined.at[0], lined.at[s], place.dev(z=s))
        gather.arrive()

        def block(k):
            return whole[k // plane, k // nx % ny, k % nx]

        def split(value):
            return [value[:, lanes * q : lanes * (q + 1)] for q in range(groups)]

        def hits(s, k):
            base = (k % plane * 2 + k // plane) * columns
            lane = lax.broadcasted_iota(jnp.int32, (length, lanes), 1) + base
            return [lane + lanes * q == marks_in[s] for q in range(groups)]

        def logits_of(s, k):
            return matmul(lined[s], block(k))

        def forward(s):
            at = pl.ds(s * length, length)
            peaks[...] = jnp.full_like(peaks, -jnp.inf)
            totals[...] = jnp.zeros_like(totals)
            picks[...] = jnp.zeros_like(picks)

            @pl.loop(0, blocks)
            def _(k):
                logits = logits_of(s, k)
                if keep:
                    exps[k, at] = logits
                high, found = (peaks[...], picks[...])
                for piece, hit in zip(split(logits), hits(s, k)):
                    high = jnp.maximum(high, piece)
                    found = found + jnp.where(hit, piece, 0.0)
                peaks[...] = high
                picks[...] = found

            peak = jnp.max(peaks[...], axis=1, keepdims=True)
            peaks[...] = jnp.broadcast_to(peak, (length, lanes))

            @pl.loop(0, blocks)
            def _(k):
                logits = exps[k, at] if keep else logits_of(s, k)
                total = totals[...]
                for q, piece in enumerate(split(logits)):
                    power = jnp.exp(piece - peaks[...])
                    if keep:
                        exps[k, at, lanes * q : lanes * (q + 1)] = power
                    total = total + power
                totals[...] = total

            if not keep:
                exps[s] = peaks[...]
            lane = lax.broadcasted_iota(jnp.int32, (length, 128), 1)
            total = jnp.sum(totals[...], axis=1, keepdims=True)
            found = jnp.sum(picks[...], axis=1, keepdims=True)
            table = jnp.where(lane == 0, peak, jnp.where(lane == 1, total, found))
            mine[place.zs(s)] = table.T[:8]

        forward(0)
        for s in turns:
            arriving[s].wait_recv()
            turned[:, s * length : (s + 1) * length] = lined[s].T
            forward(s)
        stats = [comm.send(mine, every.at[s], place.dev(z=s)) for s in range(1, nz)]
        every[0] = mine[...]
        for copy in stats:
            copy.wait_recv()

        def backward(s):
            at = pl.ds(s * length, length)
            held = [every[q, place.zs(s)] for q in range(nz)]
            peak = held[0][0:1]
            for other in held[1:]:
                peak = jnp.maximum(peak, other[0:1])
            total = sum(other[1:2] * jnp.exp(other[0:1] - peak) for other in held)
            zz = place.zs(s)
            mask = [meta_in[zz, y, x, part, pl.ds(images + c, 1), :] for part in range(2)]
            mask = jnp.concatenate(mask, axis=1).astype(F32)
            tail = meta_in[zz, y, x, 0, 4:5, :]
            lane = lax.broadcasted_iota(jnp.int32, (1, 128), 1)
            tall = jnp.sum(jnp.where(lane == images + c, tail, 0).astype(F32), axis=1, keepdims=True)
            place_of = lax.broadcasted_iota(jnp.int32, (1, length), 1).astype(F32)
            weight = jnp.where(place_of < GRID * tall, mask, 0.0)
            if s == 0:
                found = sum(other[2:3] for other in held)
                loss = (peak + jnp.log(total) - found) * weight
                lane = lax.broadcasted_iota(jnp.int32, (8, 128), 1)
                row = lax.broadcasted_iota(jnp.int32, (8, 128), 0)
                sums = jnp.where(lane == 1, jnp.sum(loss, axis=1, keepdims=True), 0.0)
                sums = sums + jnp.where(lane == 2, jnp.sum(weight, axis=1, keepdims=True), 0.0)
                loss_out[...] = jnp.where(row == 0, sums, 0.0)
            scale = weight / total * jnp.exp(held[0][0:1] - peak)
            tall = jnp.concatenate([scale, weight, jnp.zeros((126, length), F32)], axis=0).T
            columned[0] = jnp.broadcast_to(tall[:, 0:1], (length, lanes))
            columned[1] = jnp.broadcast_to(tall[:, 1:2], (length, lanes))
            partial[...] = jnp.zeros_like(partial)

            @pl.loop(0, blocks)
            def _(k):
                if keep:
                    powers = split(exps[k, at])
                else:
                    powers = [jnp.exp(piece - exps[s]) for piece in split(logits_of(s, k))]
                pieces = []
                for power, hit in zip(powers, hits(s, k)):
                    grad = power * columned[0] - jnp.where(hit, columned[1], 0.0)
                    pieces.append(grad.astype(BF))
                grad = jnp.concatenate(pieces, axis=1) if groups > 1 else pieces[0]
                grads[k, at] = grad
                partial[...] += lax.dot_general(
                    grad, block(k), (((1,), (1,)), ((), ())), preferred_element_type=F32
                )

        coming_in = []
        for s in range(1, nz):
            backward(s)
            back[s - 1] = partial[...].astype(BF)
            coming_in.append(comm.send(back.at[s - 1], coming.at[s - 1], place.dev(z=nz - s)))
        backward(0)

        def weights(into, core):
            @pl.loop(0, plane)
            def _(j):
                into[j // nx, j % nx] = matmul(turned[...], grads[core * plane + j]).astype(BF)

        weights(given, 1 - c)
        pair = comm.send(given, half, place.dev(c=1))
        weights(head_out, c)
        pair.wait_recv()
        add_blocks(head_out, [head_out, half])
        for copy in coming_in:
            copy.wait_recv()
        total = partial[...]
        for s in range(nz - 1):
            total = total + coming[s].astype(F32)
        top_out[...] = total
        comm.finish()

    count = 3 * (nz - 1) + 2 * (2 * plane - 1) + 1
    scratch = [
        pltpu.VMEM((2, ny, nx) + head.shape, BF),
        pltpu.VMEM((nz, length, lanes), jnp.int32),
        pltpu.VMEM((16, 128) if shared else (2, width, PIECE), BF),
        pltpu.VMEM((nz, length, width), BF),
        pltpu.VMEM((width, nz * length), BF),
        pltpu.VMEM((length, lanes), F32),
        pltpu.VMEM((length, lanes), F32),
        pltpu.VMEM((length, lanes), F32),
        pltpu.VMEM((blocks, nz * length, columns) if keep else (nz, length, lanes), F32),
        pltpu.VMEM((blocks, nz * length, columns), BF),
        pltpu.VMEM((2, length, lanes), F32),
        pltpu.VMEM((length, width), F32),
        pltpu.VMEM((nz - 1, length, width), BF),
        pltpu.VMEM((nz - 1, length, width), BF),
        pltpu.VMEM((nz, 8, length), F32),
        pltpu.VMEM((nz, nz, 8, length), F32),
        pltpu.VMEM((ny, nx) + head.shape, BF),
        pltpu.VMEM((ny, nx) + head.shape, BF),
        sems(count),
        sems(count),
        sems(2 * pieces),
    ]
    outs = [
        shape((length, width), F32),
        shape((ny, nx) + head.shape, BF),
        shape((8, 128), F32),
        shape((length, 2 * inner), F32),
        shape((length, width), F32),
    ]
    return call(
        kernel, outs, [VMEM] * 4 + [ANY, VMEM], [VMEM] * 5, scratch,
        cid, "head_all", (middle, gain, metas, head, expand_w, shrink_w), 63 * 2**20,
    )


def matmul(left, right):
    return jnp.dot(left, right, preferred_element_type=F32)


def norm_forward(values, gain):
    inverse = lax.rsqrt(jnp.mean(values * values, axis=-1, keepdims=True) + EPS_NORM)
    normed = values * inverse
    return (normed * gain, normed, inverse)


def norm_backward(grad, normed, inverse, gain):
    scaled = grad * gain
    inner = jnp.mean(scaled * normed, axis=-1, keepdims=True)
    return (inverse * (scaled - normed * inner), jnp.sum(grad * normed, axis=0))


def turned(value, low):
    return jnp.where(low, -pltpu.roll(value, 112, 1), pltpu.roll(value, 16, 1))


def low_quarters(rows):
    return lax.broadcasted_iota(jnp.int32, (rows, 128), 1) % 32 < 16


def left_half(rows):
    return lax.broadcasted_iota(jnp.int32, (rows, 128), 1) < HD


def times_turned(left, right):
    return lax.dot_general(left, right, (((1,), (1,)), ((), ())), preferred_element_type=F32)


def turned_times(left, right):
    return lax.dot_general(left, right, (((0,), (0,)), ((), ())), preferred_element_type=F32)


def attention_steps(start, gain, angles, allowed, weights, mix, held, probs, out):
    length, width = start.shape
    normed = norm_forward(start[...], gain[0:1])[0].astype(BF)
    low, left = (low_quarters(length), left_half(length))
    for k in range(3):
        value = matmul(normed, weights(k))
        for p in range(width // 128):
            piece = value[:, 128 * p : 128 * p + 128]
            if k < 2:
                piece = piece * angles[0] + turned(piece, low) * angles[1]
            held[k, :, 128 * p : 128 * p + 128] = piece.astype(BF)
        yield
    for p in range(width // 128):
        at = slice(128 * p, 128 * p + 128)
        query, keys, values = (held[0, :, at], held[1, :, at], held[2, :, at])
        parts = []
        for side in range(2):
            own = jnp.where(left == (side == 0), query, jnp.zeros_like(query))
            scores = times_turned(own, keys) * HD ** (-0.5)
            scores = jnp.where(allowed[...] > 0, scores, NEGATIVE_FILL)
            power = jnp.exp(scores - jnp.max(scores, axis=1, keepdims=True))
            power = power / jnp.sum(power, axis=1, keepdims=True)
            probs[2 * p + side] = power
            parts.append(matmul(power.astype(BF), values))
        held[3, :, at] = jnp.where(left, parts[0], parts[1]).astype(BF)
        yield
    out[...] = start[...] + matmul(held[3], mix())
    yield


def attention_back_steps(start, gain, angles, weights, mix, held, probs, grad_mid, put, out, gains):
    length, width = start.shape
    low, left = (low_quarters(length), left_half(length))
    back = grad_mid[...].astype(BF)
    put(3, turned_times(held[3], back))
    grad_out = times_turned(back, mix()).astype(BF)
    yield
    grads = [[], [], []]
    for p in range(width // 128):
        at = slice(128 * p, 128 * p + 128)
        query, keys, values, grad = (held[0, :, at], held[1, :, at], held[2, :, at], grad_out[:, at])
        parts = []
        for side in range(2):
            own = jnp.where(left == (side == 0), grad, jnp.zeros_like(grad))
            grad_probs = times_turned(own, values)
            power = probs[2 * p + side]
            inner = jnp.sum(power * grad_probs, axis=1, keepdims=True)
            score = (power * (grad_probs - inner)).astype(BF)
            parts.append(
                (
                    matmul(score, keys) * HD ** (-0.5),
                    turned_times(score, query) * HD ** (-0.5),
                    turned_times(power.astype(BF), grad),
                )
            )
        for k in range(3):
            value = jnp.where(left, parts[0][k], parts[1][k]).astype(BF)
            if k < 2:
                value = value.astype(F32)
                value = (value * angles[0] - turned(value * angles[1], low)).astype(BF)
            grads[k].append(value)
        yield
    gain_row = gain[0:1]
    normed_gain, normed, inverse = norm_forward(start[...], gain_row)
    normed_gain = normed_gain.astype(BF)
    total = jnp.zeros((length, width), F32)
    for k in range(3):
        grad = jnp.concatenate(grads[k], axis=1)
        put(k, turned_times(normed_gain, grad))
        total = total + times_turned(grad, weights(k))
        yield
    grad, gain_grad = norm_backward(total, normed, inverse, gain_row)
    gains[0:1] = gain_grad.reshape(1, width)
    out[...] = grad_mid[...] + grad
    yield


def local_call(kernel, outs, args, scratch, name, flops, spaces=None):
    spaces = [VMEM] * len(args) if spaces is None else spaces
    return pl.pallas_call(
        kernel,
        out_shape=outs,
        in_specs=spaces,
        out_specs=[VMEM] * len(outs),
        scratch_shapes=scratch,
        compiler_params=pltpu.CompilerParams(vmem_limit_bytes=60 * 2**20),
        cost_estimate=pl.CostEstimate(flops=flops, bytes_accessed=2**24, transcendentals=0),
        name=name,
    )(*args)


def attention_forward(start, gain, angles, allowed, qkv_w, mix_w):
    length, width = start.shape

    def kernel(start, gain, angles, allowed, qkv, mix, held, probs, out):
        def weights(k):
            return qkv[:, width * k : width * (k + 1)]

        drain(attention_steps(start, gain, angles, allowed, weights, lambda: mix[...], held, probs, out))

    outs = [
        shape((4, length, width), BF),
        shape((width // HD, length, length), F32),
        shape((length, width), F32),
    ]
    args = (start, gain, angles, allowed, qkv_w, mix_w)
    return local_call(kernel, outs, args, [], "attention_forward", 2**31)


def attention_backward(start, gain, angles, qkv_w, mix_w, held, probs, grad_mid, gain_high):
    length, width = start.shape

    def kernel(*refs):
        start, gain, angles, qkv, mix, held, probs, grad_mid, high, grad_qkv, grad_mix, out, gains = refs

        def weights(k):
            return qkv[:, width * k : width * (k + 1)]

        def put(k, value):
            if k == 3:
                grad_mix[...] = value.astype(BF)
            else:
                grad_qkv[:, width * k : width * (k + 1)] = value.astype(BF)

        gains[...] = high[...]
        drain(
            attention_back_steps(
                start, gain, angles, weights, lambda: mix[...], held, probs, grad_mid, put, out, gains
            )
        )

    outs = [
        shape(qkv_w.shape, BF),
        shape(mix_w.shape, BF),
        shape((length, width), F32),
        shape((8, width), F32),
    ]
    args = (start, gain, angles, qkv_w, mix_w, held, probs, grad_mid, gain_high)
    return local_call(kernel, outs, args, [], "attention_backward", 2**32)


def feed_backward(grad_top, final, middle, both, gain, expand_w, shrink_w):
    length, width = middle.shape
    inner = shrink_w.shape[0]

    def kernel(grad_top, final, middle, both, gain, expand, shrink, grad_expand, grad_shrink, out, gains):
        _, normed, inverse = norm_forward(final[...], gain[2:3])
        grad_final, gain_top = norm_backward(grad_top[...], normed, inverse, gain[2:3])
        back = grad_final.astype(BF)
        low, normed, inverse = norm_forward(middle[...], gain[1:2])
        low = low.astype(BF)
        total = jnp.zeros((length, width), F32)
        for k in range(inner // PIECE):
            at = slice(PIECE * k, PIECE * (k + 1))
            up_at = slice(inner + PIECE * k, inner + PIECE * (k + 1))
            gate, up = (both[:, at], both[:, up_at])
            sigma = jax.nn.sigmoid(gate)
            hidden = (gate * sigma * up).astype(BF)
            grad_shrink[at] = turned_times(hidden, back).astype(BF)
            grad = times_turned(back, shrink[at])
            grad_gate = (grad * up * sigma * (1.0 + gate * (1.0 - sigma))).astype(BF)
            grad_up = (grad * gate * sigma).astype(BF)
            grad_expand[:, at] = turned_times(low, grad_gate).astype(BF)
            grad_expand[:, up_at] = turned_times(low, grad_up).astype(BF)
            total = total + times_turned(grad_gate, expand[:, at])
            total = total + times_turned(grad_up, expand[:, up_at])
        grad_middle, gain_two = norm_backward(total, normed, inverse, gain[1:2])
        out[...] = grad_final + grad_middle
        gains[...] = jnp.zeros_like(gains)
        gains[1:2] = gain_two.reshape(1, width)
        gains[2:3] = gain_top.reshape(1, width)

    outs = [
        shape(expand_w.shape, BF),
        shape(shrink_w.shape, BF),
        shape((length, width), F32),
        shape((8, width), F32),
    ]
    args = (grad_top, final, middle, both, gain, expand_w, shrink_w)
    return local_call(kernel, outs, args, [], "feed_backward", 2**33)


def rope_tables(length, width):
    quarter = width // 4
    places = np.arange(length)
    freq = np.float32(10000.0) ** (-np.arange(quarter, dtype=np.float32) / np.float32(quarter))
    row_angle = (places // GRID).astype(np.float32)[:, None] * freq
    col_angle = (places % GRID).astype(np.float32)[:, None] * freq
    angles = np.concatenate([row_angle, row_angle, col_angle, col_angle] * (128 // width), axis=-1)
    return jnp.asarray(np.stack([np.cos(angles), np.sin(angles)]).astype(np.float32))


def adam_update(master, drift, square, grad, rate, decay):
    moment = BETA_ONE * drift + (1.0 - BETA_ONE) * grad
    second = BETA_TWO * square + (1.0 - BETA_TWO) * grad * grad
    stride = (
        moment / (1.0 - BETA_ONE**STEP) / (jnp.sqrt(second / (1.0 - BETA_TWO**STEP)) + ADAM_EPS)
    )
    return (master - rate * (stride + decay * master), moment, second)


def block_form(rows, columns):
    return (rows, columns) if rows % 8 == 0 else (rows * columns // 128, 128)


FIRST_AXES = ("x", "x", "y", "x")


def on_device(dims, *args):
    labels, targets, heights, loss_mask = args[:4]
    masters, drifts, squares = (args[4:12], args[12:20], args[20:28])
    class_table, code_table, attend_in, attend_mix, expand_in, shrink_out, head_weight, norm_gains = masters
    nz, ny, nx = dims
    plane = ny * nx
    images, local_len = targets.shape
    length = local_len * 2
    plane_groups = [[k * plane + i for i in range(plane)] for k in range(nz)]

    layers = (attend_in, attend_mix, expand_in, shrink_out)
    *weights, start, gain, metas, allowed = gather_all(
        dims, layers, FIRST_AXES, code_table, class_table.T, norm_gains, labels, targets, heights, loss_mask, 0
    )
    qkv_w, mix_w, expand_w, shrink_w = (v.reshape(-1, v.shape[-1]) for v in weights)

    angles = rope_tables(length, HD)
    held, probs, middle = attention_forward(start, gain, angles, allowed, qkv_w, mix_w)
    grad_top, grad_head, partial, both, final = head_all(
        dims, middle, gain, metas, head_weight, expand_w, shrink_w, images, 2
    )
    grad_head = grad_head.reshape((plane,) + head_weight.shape)
    grad_head = lax.psum_scatter(grad_head, "dp", axis_index_groups=plane_groups)
    grad_expand, grad_shrink, grad_middle, gain_high = feed_backward(
        grad_top, final, middle, both, gain, expand_w, shrink_w
    )
    grad_qkv, grad_mix, grad_start, gain_grads = attention_backward(
        start, gain, angles, qkv_w, mix_w, held, probs, grad_middle, gain_high
    )

    grads_in = []
    for grad, shard in zip((grad_qkv, grad_mix, grad_expand, grad_shrink), layers):
        grads_in.append(grad.reshape(dims + (2,) + block_form(*shard.shape)))
    *layer_shares, code_share, class_share, gain_share, sums = scatter_all(
        dims,
        grads_in,
        FIRST_AXES,
        grad_start,
        gain_grads,
        metas,
        grad_head,
        partial,
        code_table.shape[0],
        class_table.shape[0],
        4,
    )
    layer_shares = [g.reshape(v.shape) for g, v in zip(layer_shares, layers)]
    class_share = class_share[: class_table.shape[0], : class_table.shape[1]]
    gain_share = gain_share[1:4, : norm_gains.shape[1]]
    shares = (class_share, code_share, *layer_shares, grad_head.astype(F32), gain_share)
    total_square, loss_sum, loss_count = (sums[0, 0], sums[0, 1], sums[0, 2])
    grad_norm = jnp.sqrt(total_square) / loss_count
    factor = CLIP_NORM / jnp.maximum(grad_norm, CLIP_NORM) / loss_count
    news, firsts, seconds = ([], [], [])
    for member in range(8):
        fresh, moment, second = adam_update(
            masters[member],
            drifts[member],
            squares[member],
            shares[member] * factor,
            RATES[member],
            DECAYS[member],
        )
        news.append(fresh)
        firsts.append(moment)
        seconds.append(second)
    return tuple(news) + tuple(firsts) + tuple(seconds) + (grad_norm, loss_sum, loss_count)


def solution(mesh):
    rows, columns = (P(("dp", "seq"), None), P(None, ("dp", "seq")))
    eight = (columns, rows, rows, rows, rows, rows, columns, columns)
    return jax.shard_map(
        functools.partial(on_device, dims_of(mesh.shape["dp"])),
        mesh=mesh,
        in_specs=(P("dp"), P("dp", "seq"), P("dp"), P("dp", "seq")) + eight * 3,
        out_specs=eight * 3 + (P(), P(), P()),
        check_vma=False,
    )
```

```python
import functools

import jax
import jax.numpy as jnp
import numpy as np
from jax import lax
from jax.experimental import pallas as pl
from jax.experimental.pallas import tpu as pltpu
from jax.sharding import PartitionSpec as P

HD = 64
GRID = 16
STEP = 10

EPS_NORM = 1e-05
BETA_ONE = 0.9
BETA_TWO = 0.95
ADAM_EPS = 1e-08
CLIP_NORM = 0.01
NEGATIVE_FILL = -1000000000.0
RATES = (0.8, 0.8, 0.08, 0.08, 0.08, 0.08, 0.08, 0.8)
DECAYS = (0.1, 0.1, 0.1, 0.1, 0.1, 0.1, 0.1, 0.0)

PIECE = 512

MESH = pl.DeviceIdType.MESH
ANY = pl.BlockSpec(memory_space=pl.ANY)
VMEM = pl.BlockSpec(memory_space=pltpu.VMEM)
SMEM = pl.BlockSpec(memory_space=pltpu.SMEM)
BF = jnp.bfloat16
F32 = jnp.float32


def dims_of(dp):
    bits = dp.bit_length() - 1
    nz = 1 << (bits // 2)
    rest = dp // nz
    ny = 1 << ((rest.bit_length() - 1) // 2)
    return (nz, ny, rest // ny)


class Place:
    def __init__(self, dims):
        self.dims = dims
        nz, ny, nx = dims
        chip = lax.axis_index("dp")
        self.c = lax.axis_index("seq")
        self.z = chip // (ny * nx)
        self.y = (chip // nx) % ny
        self.x = chip % nx

    def zs(self, back):
        return (self.z + self.dims[0] - back) % self.dims[0]

    def ys(self, back):
        return (self.y + self.dims[1] - back) % self.dims[1]

    def xs(self, back):
        return (self.x + self.dims[2] - back) % self.dims[2]

    def dev(self, z=0, y=0, x=0, c=0):
        nz, ny, nx = self.dims
        z, y, x = ((self.z + z) % nz, (self.y + y) % ny, (self.x + x) % nx)
        return ((z * ny + y) * nx + x, (self.c + c) % 2)


def line_offsets(dims):
    nz, ny, nx = dims
    return (
        [(s, 0, 0, 0) for s in range(1, nz)]
        + [(0, s, 0, 0) for s in range(1, ny)]
        + [(0, 0, s, 0) for s in range(1, nx)]
        + [(0, 0, 0, 1)]
    )


def plane_offsets(dims):
    return [(0, v, u, 0) for v in range(dims[1]) for u in range(dims[2]) if v or u]


def greet(place, offsets):
    offsets = sorted(set(offsets))
    sem = pltpu.get_barrier_semaphore()
    for off in offsets:
        pl.semaphore_signal(sem, inc=1, device_id=place.dev(*off), device_id_type=MESH)
    pl.semaphore_wait(sem, len(offsets))


class Comm:
    def __init__(self, send_sems, recv_sems, local_sems):
        self.send_sems, self.recv_sems, self.local_sems = (send_sems, recv_sems, local_sems)
        self.sent, self.held, self.count, self.locals = ([], [], 0, 0)

    def send(self, src, dst, device):
        k = self.count
        self.count += 1
        copy = pltpu.make_async_remote_copy(
            src_ref=src,
            dst_ref=dst,
            send_sem=self.send_sems.at[k],
            recv_sem=self.recv_sems.at[k],
            device_id=device,
            device_id_type=MESH,
        )
        copy.start()
        self.sent.append(copy)
        return copy

    def keep(self, src, dst):
        copy = pltpu.make_async_copy(src, dst, self.local_sems.at[self.locals])
        self.locals += 1
        copy.start()
        self.held.append(copy)
        return copy

    def gone(self, copy):
        copy.wait_send()
        self.sent = [other for other in self.sent if other is not copy]

    def done(self, copy):
        copy.wait()
        self.held = [other for other in self.held if other is not copy]

    def finish(self):
        for copy in self.sent:
            copy.wait_send()
        for copy in self.held:
            copy.wait()


def drain(steps):
    for _ in steps:
        pass


def all_offsets(dims):
    nz, ny, nx = dims
    spots = [(k, j, i, core) for k in range(nz) for j in range(ny) for i in range(nx) for core in range(2)]
    return spots[1:]


def small_exchange(comm, place, src, out, own):
    z, y, x, c = (place.z, place.y, place.x, place.c)
    nz, ny, nx = place.dims
    if own:
        comm.keep(src(z, y, x, c), out.at[z, y, x, c])
    got = []
    for off in all_offsets(place.dims):
        there = (place.zs(nz - off[0]), place.ys(ny - off[1]), place.xs(nx - off[2]), (c + off[3]) % 2)
        got.append(comm.send(src(*there), out.at[z, y, x, c], place.dev(*off)))
    return got


class PlaneGather:
    def __init__(self, comm, place):
        self.comm, self.place = (comm, place)
        self.firsts, self.seconds, self.mates = ([], [], [])

    def ways(self, axis):
        _, ny, nx = self.place.dims
        return range(1, ny if axis == "y" else nx)

    def back(self, axis, t, yy, xx):
        return (self.place.ys(t), xx) if axis == "y" else (yy, self.place.xs(t))

    def spread(self, block, first, src=None):
        place, second = (self.place, "y" if first == "x" else "x")
        dst = block(place.y, place.x)
        src = dst if src is None else src
        for t in self.ways(first):
            copy = self.comm.send(src, dst, place.dev(**{first: t}))
            self.firsts.append((block, first, second, t, copy))
        for t in self.ways(second):
            copy = self.comm.send(src, dst, place.dev(**{second: t}))
            self.seconds.append((block(*self.back(second, t, place.y, place.x)), copy))
        self.mates.append(self.comm.send(src, dst, place.dev(c=1)))

    def forward(self):
        place = self.place
        for block, first, second, t, copy in self.firsts:
            copy.wait_recv()
            yy, xx = self.back(first, t, place.y, place.x)
            held = block(yy, xx)
            for u in self.ways(second):
                copy = self.comm.send(held, held, place.dev(**{second: u}))
                self.seconds.append((block(*self.back(second, u, yy, xx)), copy))
            self.mates.append(self.comm.send(held, held, place.dev(c=1)))
        self.firsts = []

    def settle(self):
        for held, copy in self.seconds:
            copy.wait_recv()
            self.mates.append(self.comm.send(held, held, self.place.dev(c=1)))
        self.seconds = []

    def forward_some(self, count):
        rest = self.firsts[count:]
        self.firsts = self.firsts[:count]
        self.forward()
        self.firsts = rest

    def arrive(self):
        for copy in self.mates:
            copy.wait_recv()
        self.mates = []


def sems(count):
    return pltpu.SemaphoreType.DMA((count,))


def shape(dims, dtype):
    return jax.ShapeDtypeStruct(tuple(dims), dtype)


def call(kernel, outs, in_specs, out_specs, scratch, cid, name, args, vmem=None):
    return pl.pallas_call(
        kernel,
        out_shape=outs,
        in_specs=in_specs,
        out_specs=out_specs,
        scratch_shapes=scratch,
        compiler_params=pltpu.CompilerParams(
            collective_id=cid, has_side_effects=True, vmem_limit_bytes=vmem
        ),
        name=name,
    )(*args)


def small_sends(dims):
    return dims[0] * dims[1] * dims[2] * 2 - 1


def gather_all(dims, layers, first_axes, table, classes, gains, labels, targets, heights, masks, cid):
    nz, ny, nx = dims
    n = len(layers)
    rows, width = table.shape
    images, local_len = targets.shape
    length = local_len * 2
    columns = gains.shape[1]
    meta = (8, 128)
    count_images = nz * ny * nx * images
    label_rows = -(-count_images // 128)
    groups = [(k,) for k in range(nz)] if nz <= 4 else [tuple(range(nz))]

    def kernel(*refs):
        ins, rest = (refs[:n], refs[n:])
        table_in, class_in, gain_in, labels_in, targets_in, heights_in, masks_in, *rest = rest
        outs, rest = (rest[:n], rest[n:])
        start_out, gain_out, meta_out, allowed_out, *rest = rest
        low, rest = (rest[:n], rest[n:])
        whole, found, total, class_low, gain_row, meta_in, parts_out, small_out, small_in, *rest = rest
        ssem, rsem, lsem = rest
        place = Place(dims)
        z, y, x, c = (place.z, place.y, place.x, place.c)
        chip = (z * ny + y) * nx + x
        meta_in[...] = jnp.zeros_like(meta_in)
        meta_in[0:images] = targets_in[...]
        meta_in[images : 2 * images] = masks_in[...]
        lane = lax.broadcasted_iota(jnp.int32, (1, 128), 1)
        for i in range(images):
            meta_in[4:5] += jnp.where(lane == i, labels_in[i], 0)
            meta_in[4:5] += jnp.where(lane == images + i, heights_in[i], 0)
            for r in range(label_rows):
                meta_in[5 + r : 6 + r] += jnp.where(lane == chip * images + i - 128 * r, labels_in[i], 0)
        greet(place, all_offsets(dims))
        comm = Comm(ssem, rsem, lsem)
        metas = small_exchange(comm, place, lambda *spot: meta_in, meta_out, False)
        meta_out[z, y, x, c] = meta_in[...]
        waits = []
        whole[y, x, c] = table_in[...].astype(BF)
        tables, blocks = (PlaneGather(comm, place), PlaneGather(comm, place))
        for first, start in (("x", 0), ("y", rows // 2)):
            half = pl.ds(start, rows // 2)
            tables.spread(lambda yy, xx, half=half: whole.at[yy, xx, c, half], first)
        for a in range(n):
            low[a][...] = ins[a][...].astype(BF)
        along = {}
        for s in range(1, nz):
            for a in range(n):
                along[s, a] = comm.send(low[a], outs[a].at[z, y, x, c], place.dev(z=s))
        kept = [comm.keep(low[a], outs[a].at[z, y, x, c]) for a in range(n)]

        def spread(group):
            for a in range(n):
                for k in group:
                    if k:
                        along[k, a].wait_recv()
                if len(group) > 1:
                    comm.done(kept[a])
                    at = pl.ds(0, nz)
                else:
                    at = place.zs(group[0])
                blocks.spread(
                    lambda yy, xx, a=a, at=at: outs[a].at[at, yy, xx, c],
                    first_axes[a],
                    low[a] if group == (0,) else None,
                )

        for copy in metas:
            copy.wait_recv()

        class_low[...] = jnp.zeros_like(class_low)
        class_low[0:columns, 0 : class_in.shape[1]] = class_in[...]
        small_in[...] = jnp.zeros_like(small_in)
        for r in range(label_rows):
            labels = jnp.zeros((1, 128), jnp.int32)
            for k in range(nz * ny * nx):
                labels = labels + meta_out[k // (ny * nx), k // nx % ny, k % nx, 0, 5 + r : 6 + r, :]
            pick = lax.broadcasted_iota(jnp.int32, (class_low.shape[1], 128), 0) == labels
            picked = lax.dot_general(
                jnp.where(pick, 1.0, 0.0).astype(BF),
                class_low[...].astype(BF),
                (((0,), (1,)), ((), ())),
                preferred_element_type=F32,
            )
            for i in range(min(128, count_images - 128 * r)):
                k, core = divmod(128 * r + i, 2)
                small_in[k // (ny * nx), k // nx % ny, k % nx, core, 0:1, 0 : class_low.shape[0]] = picked[
                    i : i + 1
                ]
        gain_row[...] = jnp.zeros_like(gain_row)
        gain_row[0:3, 0:columns] = gain_in[...].astype(BF).astype(F32)

        @pl.loop(0, nz)
        def _(k):
            for j in range(ny):
                for i in range(nx):
                    for core in range(2):
                        small_in[k, j, i, core, 1:4, :] = gain_row[0:3]

        smalls = small_exchange(comm, place, lambda *spot: small_in.at[spot], small_out, False)
        small_out[z, y, x, c] = small_in[z, y, x, c]

        size = len(layers)
        steps = [lambda group=group: spread(group) for group in groups]
        steps.pop(0)()
        tables.forward()
        if steps:
            steps.pop(0)()
        blocks.forward_some(size)
        if steps:
            steps.pop(0)()
        tables.settle()
        blocks.forward_some(size)
        for step in steps:
            step()
        tables.arrive()

        for s in range(1, nz + 1):
            zz = place.zs(s % nz)
            halves = []
            for half in range(2):
                codes = meta_out[zz, y, x, half, pl.ds(c, 1), :].astype(F32)
                halves.append(jnp.broadcast_to(codes, (128, local_len)).T)
            column = jnp.concatenate(halves, axis=0)
            column = column - (z * ny * nx * 2 * rows).astype(F32)
            total[...] = jnp.zeros_like(total)

            @pl.loop(0, ny * nx * 2)
            def _(j):
                base = (j * rows).astype(F32)
                lane = lax.broadcasted_iota(jnp.int32, (length, 128), 1).astype(F32) + base
                picks = [
                    jnp.where(column == lane + float(128 * q), 1.0, 0.0).astype(BF)
                    for q in range(-(-rows // 128))
                ]
                pick = jnp.concatenate(picks, axis=1)[:, :rows]
                total[...] += matmul(pick, whole[j // (2 * nx), j // 2 % nx, j % 2])

            found[s % nz] = total[...].astype(BF)
            if s < nz:
                waits.append(comm.send(found.at[s], parts_out.at[nz - s - 1], place.dev(z=nz - s)))
            blocks.forward_some(size)
        blocks.forward()
        height = jnp.where(c == 0, heights_in[0], heights_in[images - 1])
        query = lax.broadcasted_iota(jnp.int32, (length, length), 0)
        key = lax.broadcasted_iota(jnp.int32, (length, length), 1)
        allowed_out[...] = jnp.where((key <= query) & (key < GRID * height), 1.0, 0.0)
        for copy in smalls:
            copy.wait_recv()
        joined = jnp.zeros((8, width), F32)
        blank = jnp.zeros((8, width - 128), F32)
        for d in range(2 * nz * ny * nx):
            k, core = divmod(d, 2)
            piece = small_out[k // (ny * nx), k // nx % ny, k % nx, core]
            joined = joined + pltpu.roll(jnp.concatenate([piece, blank], axis=1), columns * d, 1)
        gain_out[...] = jnp.concatenate([joined[1:4], jnp.zeros((5, width), F32)], axis=0)
        blocks.settle()
        for copy in waits:
            copy.wait_recv()
        added = found[0].astype(F32)
        for s in range(1, nz):
            added = added + parts_out[s - 1].astype(F32)
        first = lax.broadcasted_iota(jnp.int32, (length, 128), 0) == 0
        for k in range(width // 128):
            at = slice(128 * k, 128 * k + 128)
            start_out[:, at] = jnp.where(first, joined[0:1, at], pltpu.roll(added[:, at], 1, 0))
        blocks.arrive()
        comm.finish()

    count = n * (nz - 1) + (n * len(groups) + 2) * (2 * ny * nx - 1) + nz + 2 * small_sends(dims)
    small = dims + (2, 8, 128)
    outs = [shape(dims + (2,) + v.shape, BF) for v in layers]
    outs += [
        shape((length, width), F32),
        shape((8, width), F32),
        shape(dims + (2,) + meta, jnp.int32),
        shape((length, length), F32),
    ]
    scratch = [pltpu.VMEM(v.shape, BF) for v in layers]
    scratch += [
        pltpu.VMEM((ny, nx, 2) + table.shape, BF),
        pltpu.VMEM((nz, length, width), BF),
        pltpu.VMEM((length, width), F32),
        pltpu.VMEM((-(-columns // 16) * 16, -(-classes.shape[1] // 128) * 128), F32),
        pltpu.VMEM((8, 128), F32),
        pltpu.VMEM(meta, jnp.int32),
        pltpu.VMEM((nz - 1, length, width), BF),
        pltpu.VMEM(small, F32),
        pltpu.VMEM(small, F32),
        sems(count),
        sems(count),
        sems(n),
    ]
    return call(
        kernel, outs, [VMEM] * (n + 3) + [SMEM, VMEM, SMEM, VMEM], [ANY] * n + [VMEM] * 4, scratch,
        cid, "gather_all", (*layers, table, classes, gains, labels, targets, heights, masks), 60 * 2**20,
    )


def add_blocks(out, terms):
    lead = out.shape[:-2]

    def visit(index):
        if len(index) < len(lead):

            @pl.loop(0, lead[len(index)])
            def _(i):
                visit(index + (i,))

        else:
            if len(terms) == 2 and out.dtype == BF:
                out[index] = terms[0][index] + terms[1][index]
                return
            total = terms[0][index].astype(F32)
            for term in terms[1:]:
                total = total + term[index].astype(F32)
            out[index] = total.astype(out.dtype)

    visit(())


def items_of(shapes, axes):
    if shapes[0][0] % 8:
        return [[(a, slice(0, shapes[a][0]), slice(0, shapes[a][1]), axes[a]) for a in pair] for pair in ((2, 3), (0, 1))]
    (rows, qkv), (_, mix), (_, both), (deep, width) = shapes
    every, piece = (slice(0, rows), both // 4)
    return [
        [(3, slice(0, deep // 2), slice(0, width), "x"), (3, slice(deep // 2, deep), slice(0, width), "y")],
        [(2, every, slice(0, piece), "x"), (2, every, slice(2 * piece, 3 * piece), "y")],
        [(0, every, slice(0, 2 * mix), "x"), (0, every, slice(2 * mix, qkv), "y"), (1, every, slice(0, mix), "y")],
        [(2, every, slice(piece, 2 * piece), "x"), (2, every, slice(3 * piece, both), "y")],
    ]


def scatter_all(dims, grads, axes, rows, gains, metas, head, partial, device_codes, classes, cid):
    nz, ny, nx = dims
    plane = ny * nx
    n = len(grads)
    shapes = [g.shape[4:] for g in grads]
    steps = items_of(shapes, axes)
    items = [item for step in steps for item in step]
    order, at = ([], 0)
    for step in steps:
        order.append(list(range(at, at + len(step))))
        at += len(step)
    length, width = rows.shape
    block = (device_codes, width)
    sizes = {"x": nx, "y": ny}
    columns = width // (2 * nz * plane)
    label_rows = -(-2 * nz * plane // 128)

    def kernel(*refs):
        parts, rest = (refs[:n], list(refs[n:]))
        rows_in, gains_in, meta_in, head_in, partial_in = (rest.pop(0) for _ in range(5))
        outs = [rest.pop(0) for _ in range(n)]
        table_out, class_out, gain_out, sums = (rest.pop(0) for _ in range(4))
        owns, halves, ones, twos, threes = ([rest.pop(0) for _ in items] for _ in range(5))
        near, far = ([rest.pop(0), rest.pop(0)] for _ in range(2))
        lined, given, own, half, small_in, small_out, tops, mine, every, ssem, rsem, lsem = rest
        place = Place(dims)
        z, y, x, c = (place.z, place.y, place.x, place.c)
        comm = Comm(ssem, rsem, lsem)
        kept = []
        for i, (a, span, cols, _) in enumerate(items):
            kept.append(comm.keep(parts[a].at[:, :, :, c, span, cols], owns[i]))
        lane = lax.broadcasted_iota(jnp.int32, (8, 128), 1)
        top = jnp.concatenate([rows_in[0:1], gains_in[0:3], jnp.zeros((4, width), F32)], axis=0)
        for d in range(2 * nz * plane):
            k, core = divmod(d, 2)
            piece = pltpu.roll(top, (width - columns * d) % width, 1)[:, :128]
            small_in[k // plane, k // nx % ny, k % nx, core] = jnp.where(lane < columns, piece, 0.0)
        greet(place, all_offsets(dims))
        waits = small_exchange(comm, place, lambda *spot: small_in.at[spot], small_out, False)
        small_out[z, y, x, c] = small_in[z, y, x, c]
        pair, got_one, got_two, third = ({}, {}, {}, {})

        def set_out(g):
            for i in order[g] if g < len(order) else []:
                a, span, cols, _ = items[i]
                pair[i] = comm.send(parts[a].at[:, :, :, 1 - c, span, cols], halves[i], place.dev(c=1))

        def back(axis, t):
            return place.ys(ny - t) if axis == "y" else place.xs(nx - t)

        def first_add(g):
            for i in order[g]:
                pair[i].wait_recv()
                comm.done(kept[i])
                add_blocks(halves[i], [halves[i], owns[i]])

        def first_send(g):
            for i in order[g]:
                axis = items[i][3]
                got_one[i] = [
                    comm.send(
                        halves[i].at[:, back(axis, t)] if axis == "y" else halves[i].at[:, :, back(axis, t)],
                        ones[i].at[t - 1],
                        place.dev(**{axis: t}),
                    )
                    for t in range(1, sizes[axis])
                ]

        def second_step(g):
            for i in order[g]:
                axis = items[i][3]
                other = "x" if axis == "y" else "y"
                for copy in got_one[i]:
                    copy.wait_recv()
                held = halves[i].at[:, y] if axis == "y" else halves[i].at[:, :, x]
                add_blocks(held, [held] + [ones[i].at[t] for t in range(ones[i].shape[0])])
                got_two[i] = [
                    comm.send(
                        halves[i].at[:, y, back("x", t)] if other == "x" else halves[i].at[:, back("y", t), x],
                        twos[i].at[t - 1],
                        place.dev(**{other: t}),
                    )
                    for t in range(1, sizes[other])
                ]

        def third_step(g):
            for i in order[g]:
                for copy in got_two[i]:
                    copy.wait_recv()
                held = halves[i].at[:, y, x]
                add_blocks(held, [held] + [twos[i].at[t] for t in range(twos[i].shape[0])])
                third[i] = [
                    comm.send(halves[i].at[place.zs(nz - s), y, x], threes[i].at[s - 1], place.dev(z=s))
                    for s in range(1, nz)
                ]

        def last_step(g):
            for i in order[g]:
                a, span, cols, _ = items[i]
                for copy in third[i]:
                    copy.wait_recv()
                terms = [halves[i].at[z, y, x]] + [threes[i].at[s] for s in range(nz - 1)]
                add_blocks(outs[a].at[span, cols], terms)

        flat = []
        first = lax.broadcasted_iota(jnp.int32, (1, length), 1) == 0
        for s in range(nz):
            codes = [meta_in[place.zs(s), y, x, part, pl.ds(c, 1), :] for part in range(2)]
            codes = pltpu.roll(jnp.concatenate(codes, axis=1) - z * (2 * plane * device_codes), 1, 1)
            flat.append(jnp.where(first, -1, codes))
        flat = jnp.concatenate(flat, axis=1)

        def product(into, core):
            @pl.loop(0, plane)
            def _(j):
                code = lax.broadcasted_iota(jnp.int32, (device_codes, nz * length), 0)
                pick = code + (j * 2 + core) * device_codes == flat
                pick = jnp.where(pick, 1.0, 0.0).astype(BF)
                value = matmul(pick, lined[...].reshape(nz * length, width))
                into[j // nx, j % nx] = value.astype(BF)

        set_out(0)
        set_out(1)
        lined[0] = rows_in[...].astype(BF)
        lines = [comm.send(lined.at[0], lined.at[s], place.dev(z=s)) for s in range(1, nz)]
        count = len(order)
        for g in range(count):
            first_add(g)
            set_out(g + 2)
            if g >= 2:
                second_step(g - 2)
            first_send(g)
            if g >= 3:
                third_step(g - 3)
        for copy in lines:
            copy.wait_recv()
        product(given, 1 - c)
        table_pair = comm.send(given, half, place.dev(c=1))
        second_step(count - 2)
        product(own, c)
        if count > 2:
            third_step(count - 3)
        second_step(count - 1)
        table_pair.wait_recv()
        add_blocks(half, [half, own])
        parts_of = [pl.ds(0, device_codes // 2), pl.ds(device_codes // 2, device_codes // 2)]
        came = [
            [
                comm.send(half.at[:, back("x", t), parts_of[0]], near[0].at[t - 1], place.dev(x=t))
                for t in range(1, nx)
            ],
            [
                comm.send(half.at[back("y", t), :, parts_of[1]], near[1].at[t - 1], place.dev(y=t))
                for t in range(1, ny)
            ],
        ]
        third_step(count - 2)
        third_step(count - 1)

        for copy in waits:
            copy.wait_recv()
        gain_out[...] = jnp.zeros_like(gain_out)
        tops[...] = jnp.zeros_like(tops)

        @pl.loop(0, nz)
        def _(k):
            for j in range(ny):
                for i in range(nx):
                    for core in range(2):
                        at = ((k * ny + j) * nx + i) * 2 + core
                        tops[pl.ds(at, 1), :] = small_out[k, j, i, core, 0:1, :]
                        gain_out[...] += small_out[k, j, i, core]

        value = jnp.zeros(class_out.shape, F32)
        high = class_out.shape[1]
        for r in range(label_rows):
            labels = jnp.zeros((1, 128), jnp.int32)
            for k in range(nz * plane):
                labels = labels + meta_in[k // plane, k // nx % ny, k % nx, 0, 5 + r : 6 + r, :]
            at = lax.broadcasted_iota(jnp.int32, (high, 128), 1) + 128 * r
            pick = lax.broadcasted_iota(jnp.int32, (high, 128), 0) == labels
            pick = jnp.where(pick & (at < 2 * nz * plane), 1.0, 0.0)
            value = value + lax.dot_general(
                tops[128 * r : 128 * r + 128],
                pick,
                (((0,), (1,)), ((), ())),
                precision=lax.Precision.HIGHEST,
                preferred_element_type=F32,
            )
        class_out[...] = value
        row = lax.broadcasted_iota(jnp.int32, gain_out.shape, 0)
        gained = jnp.where((row >= 1) & (row < 4), gain_out[...], 0.0)
        square = jnp.sum(value * value) + jnp.sum(gained * gained)
        share = head_in[...].astype(F32)
        square = square + jnp.sum(share * share)
        for g in range(count - 1):
            last_step(g)

        for copy in came[0] + came[1]:
            copy.wait_recv()
        for h, held in ((0, half.at[:, x, parts_of[0]]), (1, half.at[y, :, parts_of[1]])):
            add_blocks(held, [held] + [near[h].at[t] for t in range(near[h].shape[0])])
        came = [
            comm.send(half.at[back("y", t), x, parts_of[0]], far[0].at[t - 1], place.dev(y=t))
            for t in range(1, ny)
        ]
        came += [
            comm.send(half.at[y, back("x", t), parts_of[1]], far[1].at[t - 1], place.dev(x=t))
            for t in range(1, nx)
        ]
        last_step(count - 1)
        for a in range(n):
            square = square + jnp.sum(outs[a][...] * outs[a][...])
        for copy in came:
            copy.wait_recv()
        for h in range(2):
            terms = [half.at[y, x, parts_of[h]]] + [far[h].at[t] for t in range(far[h].shape[0])]
            add_blocks(table_out.at[parts_of[h]], terms)
        square = square + jnp.sum(table_out[...] * table_out[...])
        first = (lax.broadcasted_iota(jnp.int32, mine.shape, 0) == 0) & (
            lax.broadcasted_iota(jnp.int32, mine.shape, 1) == 0
        )
        mine[...] = partial_in[...] + jnp.where(first, square, 0.0)
        for copy in small_exchange(comm, place, lambda *spot: mine, every, False):
            copy.wait_recv()
        every[z, y, x, c] = mine[...]
        sums[...] = jnp.zeros_like(sums)

        @pl.loop(0, nz)
        def _(k):
            for j in range(ny):
                for i in range(nx):
                    sums[...] += every[k, j, i, 0] + every[k, j, i, 1]

        comm.finish()

    total = len(items) * (ny + nx - 1 + nz - 1) + nz + 2 * (ny + nx) + 2 * small_sends(dims)
    cuts = [(span.stop - span.start, cols.stop - cols.start) for _, span, cols, _ in items]
    near_far = [(ny, nx) if item[3] == "y" else (nx, ny) for item in items]
    part = (device_codes // 2, width)
    scratch = [pltpu.VMEM((nz, ny, nx) + t, BF) for t in cuts] * 2
    scratch += [pltpu.VMEM((u - 1, nz, v) + t, BF) for t, (u, v) in zip(cuts, near_far)]
    scratch += [pltpu.VMEM((v - 1, nz) + t, BF) for t, (u, v) in zip(cuts, near_far)]
    scratch += [pltpu.VMEM((nz - 1,) + t, BF) for t in cuts]
    scratch += [
        pltpu.VMEM((nx - 1, ny) + part, BF),
        pltpu.VMEM((ny - 1, nx) + part, BF),
        pltpu.VMEM((ny - 1,) + part, BF),
        pltpu.VMEM((nx - 1,) + part, BF),
        pltpu.VMEM((nz, length, width), BF),
        pltpu.VMEM((ny, nx) + block, BF),
        pltpu.VMEM((ny, nx) + block, BF),
        pltpu.VMEM((ny, nx) + block, BF),
        pltpu.VMEM(dims + (2, 8, 128), F32),
        pltpu.VMEM(dims + (2, 8, 128), F32),
        pltpu.VMEM((128 * label_rows, 128), F32),
        pltpu.VMEM(partial.shape, F32),
        pltpu.VMEM(dims + (2,) + partial.shape, F32),
        sems(total),
        sems(total),
        sems(len(items)),
    ]
    outs = [shape(t, F32) for t in shapes]
    high = -(-classes // 128) * 128
    outs += [shape(block, F32), shape((128, high), F32), shape((8, 128), F32), shape(partial.shape, F32)]
    return call(
        kernel, outs, [ANY] * n + [VMEM] * 5, [VMEM] * (n + 4), scratch,
        cid, "scatter_all", (*grads, rows, gains, metas, head, partial), 60 * 2**20,
    )


def head_all(dims, middle, gain, metas, head, expand_w, shrink_w, images, cid):
    nz, ny, nx = dims
    length, width = middle.shape
    inner = shrink_w.shape[0]
    pieces = inner // PIECE
    columns = head.shape[1]
    lanes = min(columns, 128)
    groups = columns // lanes
    plane = ny * nx
    blocks = 2 * plane
    keep = columns >= 128
    shared = columns == PIECE and nz * length >= width and blocks >= 2 * pieces

    def kernel(*refs):
        middle_in, gain_in, meta_in, head_in, expand_in, shrink_in, *rest = refs
        top_out, head_out, loss_out, both_out, final_out, *rest = rest
        whole, marks_in, wide, lined, turned, peaks, totals, picks, exps, grads, *rest = rest
        columned, partial, back, coming, mine, every, given, half, ssem, rsem, lsem = rest
        place = Place(dims)
        z, y, x, c = (place.z, place.y, place.x, place.c)
        greet(place, line_offsets(dims))
        comm = Comm(ssem, rsem, lsem)
        room, loads = ({}, {})

        def load(j):
            room[j] = grads.at[j, pl.ds(0, width)] if shared else wide.at[j // pieces]
            loads[j] = comm.keep(expand_in.at[:, pl.ds(PIECE * j, PIECE)], room[j])

        for j in range(2 * pieces) if shared else []:
            load(j)
        whole[c, y, x] = head_in[...].astype(BF)
        gather = PlaneGather(comm, place)
        for first, start in (("x", 0), ("y", width // 2)):
            part = pl.ds(start, width // 2)
            gather.spread(lambda yy, xx, part=part: whole.at[c, yy, xx, part], first)
        normed = norm_forward(middle_in[...], gain_in[1:2])[0].astype(BF)
        total = middle_in[...]
        for j in range(pieces):
            at = slice(PIECE * j, PIECE * (j + 1))
            for k in (j, pieces + j):
                if not shared:
                    load(k)
                comm.done(loads[k])
            gate, up = (matmul(normed, room[j][...]), matmul(normed, room[pieces + j][...]))
            both_out[:, at] = gate
            both_out[:, inner + PIECE * j : inner + PIECE * (j + 1)] = up
            hidden = (gate * jax.nn.sigmoid(gate) * up).astype(BF)
            total = total + matmul(hidden, shrink_in[at])
        final_out[...] = total
        lined[0] = norm_forward(total, gain_in[2:3])[0].astype(BF)
        turns = sorted(range(1, nz), key=lambda s: min(s, nz - s))
        arriving = {s: comm.send(lined.at[0], lined.at[s], place.dev(z=s)) for s in turns[:2]}
        turned[:, 0:length] = lined[0].T
        for s in range(nz):
            for part in range(2):
                codes = meta_in[place.zs(s), y, x, part, pl.ds(c, 1), :].astype(F32)
                tall = jnp.broadcast_to(codes, (128, 128)).T.astype(jnp.int32)
                marks_in[s, 128 * part : 128 * part + 128] = tall[:, :lanes] - z * (blocks * columns)
        gather.forward()
        gather.settle()
        for s in turns[:2]:
            comm.gone(arriving[s])
        for s in turns[2:]:
            arriving[s] = comm.send(lined.at[0], lined.at[s], place.dev(z=s))
        gather.arrive()

        def block(k):
            return whole[k // plane, k // nx % ny, k % nx]

        def split(value):
            return [value[:, lanes * q : lanes * (q + 1)] for q in range(groups)]

        def hits(s, k):
            base = (k % plane * 2 + k // plane) * columns
            lane = lax.broadcasted_iota(jnp.int32, (length, lanes), 1) + base
            return [lane + lanes * q == marks_in[s] for q in range(groups)]

        def logits_of(s, k):
            return matmul(lined[s], block(k))

        def forward(s):
            at = pl.ds(s * length, length)
            peaks[...] = jnp.full_like(peaks, -jnp.inf)
            totals[...] = jnp.zeros_like(totals)
            picks[...] = jnp.zeros_like(picks)

            @pl.loop(0, blocks)
            def _(k):
                logits = logits_of(s, k)
                if keep:
                    exps[k, at] = logits
                high, found = (peaks[...], picks[...])
                for piece, hit in zip(split(logits), hits(s, k)):
                    high = jnp.maximum(high, piece)
                    found = found + jnp.where(hit, piece, 0.0)
                peaks[...] = high
                picks[...] = found

            peak = jnp.max(peaks[...], axis=1, keepdims=True)
            peaks[...] = jnp.broadcast_to(peak, (length, lanes))

            @pl.loop(0, blocks)
            def _(k):
                logits = exps[k, at] if keep else logits_of(s, k)
                total = totals[...]
                for q, piece in enumerate(split(logits)):
                    power = jnp.exp(piece - peaks[...])
                    if keep:
                        exps[k, at, lanes * q : lanes * (q + 1)] = power
                    total = total + power
                totals[...] = total

            if not keep:
                exps[s] = peaks[...]
            lane = lax.broadcasted_iota(jnp.int32, (length, 128), 1)
            total = jnp.sum(totals[...], axis=1, keepdims=True)
            found = jnp.sum(picks[...], axis=1, keepdims=True)
            table = jnp.where(lane == 0, peak, jnp.where(lane == 1, total, found))
            mine[place.zs(s)] = table.T[:8]

        forward(0)
        for s in turns:
            arriving[s].wait_recv()
            turned[:, s * length : (s + 1) * length] = lined[s].T
            forward(s)
        stats = [comm.send(mine, every.at[s], place.dev(z=s)) for s in range(1, nz)]
        every[0] = mine[...]
        for copy in stats:
            copy.wait_recv()

        def backward(s):
            at = pl.ds(s * length, length)
            held = [every[q, place.zs(s)] for q in range(nz)]
            peak = held[0][0:1]
            for other in held[1:]:
                peak = jnp.maximum(peak, other[0:1])
            total = sum(other[1:2] * jnp.exp(other[0:1] - peak) for other in held)
            zz = place.zs(s)
            mask = [meta_in[zz, y, x, part, pl.ds(images + c, 1), :] for part in range(2)]
            mask = jnp.concatenate(mask, axis=1).astype(F32)
            tail = meta_in[zz, y, x, 0, 4:5, :]
            lane = lax.broadcasted_iota(jnp.int32, (1, 128), 1)
            tall = jnp.sum(jnp.where(lane == images + c, tail, 0).astype(F32), axis=1, keepdims=True)
            place_of = lax.broadcasted_iota(jnp.int32, (1, length), 1).astype(F32)
            weight = jnp.where(place_of < GRID * tall, mask, 0.0)
            if s == 0:
                found = sum(other[2:3] for other in held)
                loss = (peak + jnp.log(total) - found) * weight
                lane = lax.broadcasted_iota(jnp.int32, (8, 128), 1)
                row = lax.broadcasted_iota(jnp.int32, (8, 128), 0)
                sums = jnp.where(lane == 1, jnp.sum(loss, axis=1, keepdims=True), 0.0)
                sums = sums + jnp.where(lane == 2, jnp.sum(weight, axis=1, keepdims=True), 0.0)
                loss_out[...] = jnp.where(row == 0, sums, 0.0)
            scale = weight / total * jnp.exp(held[0][0:1] - peak)
            tall = jnp.concatenate([scale, weight, jnp.zeros((126, length), F32)], axis=0).T
            columned[0] = jnp.broadcast_to(tall[:, 0:1], (length, lanes))
            columned[1] = jnp.broadcast_to(tall[:, 1:2], (length, lanes))
            partial[...] = jnp.zeros_like(partial)

            @pl.loop(0, blocks)
            def _(k):
                if keep:
                    powers = split(exps[k, at])
                else:
                    powers = [jnp.exp(piece - exps[s]) for piece in split(logits_of(s, k))]
                pieces = []
                for power, hit in zip(powers, hits(s, k)):
                    grad = power * columned[0] - jnp.where(hit, columned[1], 0.0)
                    pieces.append(grad.astype(BF))
                grad = jnp.concatenate(pieces, axis=1) if groups > 1 else pieces[0]
                grads[k, at] = grad
                partial[...] += lax.dot_general(
                    grad, block(k), (((1,), (1,)), ((), ())), preferred_element_type=F32
                )

        coming_in = []
        for s in range(1, nz):
            backward(s)
            back[s - 1] = partial[...].astype(BF)
            coming_in.append(comm.send(back.at[s - 1], coming.at[s - 1], place.dev(z=nz - s)))
        backward(0)

        def weights(into, core):
            @pl.loop(0, plane)
            def _(j):
                into[j // nx, j % nx] = matmul(turned[...], grads[core * plane + j]).astype(BF)

        weights(given, 1 - c)
        pair = comm.send(given, half, place.dev(c=1))
        weights(head_out, c)
        pair.wait_recv()
        add_blocks(head_out, [head_out, half])
        for copy in coming_in:
            copy.wait_recv()
        total = partial[...]
        for s in range(nz - 1):
            total = total + coming[s].astype(F32)
        top_out[...] = total
        comm.finish()

    count = 3 * (nz - 1) + 2 * (2 * plane - 1) + 1
    scratch = [
        pltpu.VMEM((2, ny, nx) + head.shape, BF),
        pltpu.VMEM((nz, length, lanes), jnp.int32),
        pltpu.VMEM((16, 128) if shared else (2, width, PIECE), BF),
        pltpu.VMEM((nz, length, width), BF),
        pltpu.VMEM((width, nz * length), BF),
        pltpu.VMEM((length, lanes), F32),
        pltpu.VMEM((length, lanes), F32),
        pltpu.VMEM((length, lanes), F32),
        pltpu.VMEM((blocks, nz * length, columns) if keep else (nz, length, lanes), F32),
        pltpu.VMEM((blocks, nz * length, columns), BF),
        pltpu.VMEM((2, length, lanes), F32),
        pltpu.VMEM((length, width), F32),
        pltpu.VMEM((nz - 1, length, width), BF),
        pltpu.VMEM((nz - 1, length, width), BF),
        pltpu.VMEM((nz, 8, length), F32),
        pltpu.VMEM((nz, nz, 8, length), F32),
        pltpu.VMEM((ny, nx) + head.shape, BF),
        pltpu.VMEM((ny, nx) + head.shape, BF),
        sems(count),
        sems(count),
        sems(2 * pieces),
    ]
    outs = [
        shape((length, width), F32),
        shape((ny, nx) + head.shape, BF),
        shape((8, 128), F32),
        shape((length, 2 * inner), F32),
        shape((length, width), F32),
    ]
    return call(
        kernel, outs, [VMEM] * 4 + [ANY, VMEM], [VMEM] * 5, scratch,
        cid, "head_all", (middle, gain, metas, head, expand_w, shrink_w), 63 * 2**20,
    )


def matmul(left, right):
    return jnp.dot(left, right, preferred_element_type=F32)


def norm_forward(values, gain):
    inverse = lax.rsqrt(jnp.mean(values * values, axis=-1, keepdims=True) + EPS_NORM)
    normed = values * inverse
    return (normed * gain, normed, inverse)


def norm_backward(grad, normed, inverse, gain):
    scaled = grad * gain
    inner = jnp.mean(scaled * normed, axis=-1, keepdims=True)
    return (inverse * (scaled - normed * inner), jnp.sum(grad * normed, axis=0))


def turned(value, low):
    return jnp.where(low, -pltpu.roll(value, 112, 1), pltpu.roll(value, 16, 1))


def low_quarters(rows):
    return lax.broadcasted_iota(jnp.int32, (rows, 128), 1) % 32 < 16


def left_half(rows):
    return lax.broadcasted_iota(jnp.int32, (rows, 128), 1) < HD


def times_turned(left, right):
    return lax.dot_general(left, right, (((1,), (1,)), ((), ())), preferred_element_type=F32)


def turned_times(left, right):
    return lax.dot_general(left, right, (((0,), (0,)), ((), ())), preferred_element_type=F32)


def attention_steps(start, gain, angles, allowed, weights, mix, held, probs, out):
    length, width = start.shape
    normed = norm_forward(start[...], gain[0:1])[0].astype(BF)
    low, left = (low_quarters(length), left_half(length))
    for k in range(3):
        value = matmul(normed, weights(k))
        for p in range(width // 128):
            piece = value[:, 128 * p : 128 * p + 128]
            if k < 2:
                piece = piece * angles[0] + turned(piece, low) * angles[1]
            held[k, :, 128 * p : 128 * p + 128] = piece.astype(BF)
        yield
    for p in range(width // 128):
        at = slice(128 * p, 128 * p + 128)
        query, keys, values = (held[0, :, at], held[1, :, at], held[2, :, at])
        parts = []
        for side in range(2):
            own = jnp.where(left == (side == 0), query, jnp.zeros_like(query))
            scores = times_turned(own, keys) * HD ** (-0.5)
            scores = jnp.where(allowed[...] > 0, scores, NEGATIVE_FILL)
            power = jnp.exp(scores - jnp.max(scores, axis=1, keepdims=True))
            power = power / jnp.sum(power, axis=1, keepdims=True)
            probs[2 * p + side] = power
            parts.append(matmul(power.astype(BF), values))
        held[3, :, at] = jnp.where(left, parts[0], parts[1]).astype(BF)
        yield
    out[...] = start[...] + matmul(held[3], mix())
    yield


def attention_back_steps(start, gain, angles, weights, mix, held, probs, grad_mid, put, out, gains):
    length, width = start.shape
    low, left = (low_quarters(length), left_half(length))
    back = grad_mid[...].astype(BF)
    put(3, turned_times(held[3], back))
    grad_out = times_turned(back, mix()).astype(BF)
    yield
    grads = [[], [], []]
    for p in range(width // 128):
        at = slice(128 * p, 128 * p + 128)
        query, keys, values, grad = (held[0, :, at], held[1, :, at], held[2, :, at], grad_out[:, at])
        parts = []
        for side in range(2):
            own = jnp.where(left == (side == 0), grad, jnp.zeros_like(grad))
            grad_probs = times_turned(own, values)
            power = probs[2 * p + side]
            inner = jnp.sum(power * grad_probs, axis=1, keepdims=True)
            score = (power * (grad_probs - inner)).astype(BF)
            parts.append(
                (
                    matmul(score, keys) * HD ** (-0.5),
                    turned_times(score, query) * HD ** (-0.5),
                    turned_times(power.astype(BF), grad),
                )
            )
        for k in range(3):
            value = jnp.where(left, parts[0][k], parts[1][k]).astype(BF)
            if k < 2:
                value = value.astype(F32)
                value = (value * angles[0] - turned(value * angles[1], low)).astype(BF)
            grads[k].append(value)
        yield
    gain_row = gain[0:1]
    normed_gain, normed, inverse = norm_forward(start[...], gain_row)
    normed_gain = normed_gain.astype(BF)
    total = jnp.zeros((length, width), F32)
    for k in range(3):
        grad = jnp.concatenate(grads[k], axis=1)
        put(k, turned_times(normed_gain, grad))
        total = total + times_turned(grad, weights(k))
        yield
    grad, gain_grad = norm_backward(total, normed, inverse, gain_row)
    gains[0:1] = gain_grad.reshape(1, width)
    out[...] = grad_mid[...] + grad
    yield


def local_call(kernel, outs, args, scratch, name, flops, spaces=None):
    spaces = [VMEM] * len(args) if spaces is None else spaces
    return pl.pallas_call(
        kernel,
        out_shape=outs,
        in_specs=spaces,
        out_specs=[VMEM] * len(outs),
        scratch_shapes=scratch,
        compiler_params=pltpu.CompilerParams(vmem_limit_bytes=60 * 2**20),
        cost_estimate=pl.CostEstimate(flops=flops, bytes_accessed=2**24, transcendentals=0),
        name=name,
    )(*args)


def attention_forward(start, gain, angles, allowed, qkv_w, mix_w):
    length, width = start.shape

    def kernel(start, gain, angles, allowed, qkv, mix, held, probs, out):
        def weights(k):
            return qkv[:, width * k : width * (k + 1)]

        drain(attention_steps(start, gain, angles, allowed, weights, lambda: mix[...], held, probs, out))

    outs = [
        shape((4, length, width), BF),
        shape((width // HD, length, length), F32),
        shape((length, width), F32),
    ]
    args = (start, gain, angles, allowed, qkv_w, mix_w)
    return local_call(kernel, outs, args, [], "attention_forward", 2**31)


def feed_back_steps(grad_top, final, middle, both, gain, expand, shrink, grad_expand, grad_shrink, out, gains):
    length, width = middle.shape
    inner = shrink.shape[0]
    _, normed, inverse = norm_forward(final[...], gain[2:3])
    grad_final, gain_top = norm_backward(grad_top[...], normed, inverse, gain[2:3])
    back = grad_final.astype(BF)
    low, normed, inverse = norm_forward(middle[...], gain[1:2])
    low = low.astype(BF)
    total = jnp.zeros((length, width), F32)
    for k in range(inner // PIECE):
        at = slice(PIECE * k, PIECE * (k + 1))
        up_at = slice(inner + PIECE * k, inner + PIECE * (k + 1))
        gate, up = (both[:, at], both[:, up_at])
        sigma = jax.nn.sigmoid(gate)
        hidden = (gate * sigma * up).astype(BF)
        grad_shrink[at] = turned_times(hidden, back).astype(BF)
        grad = times_turned(back, shrink[at])
        grad_gate = (grad * up * sigma * (1.0 + gate * (1.0 - sigma))).astype(BF)
        grad_up = (grad * gate * sigma).astype(BF)
        grad_expand[:, at] = turned_times(low, grad_gate).astype(BF)
        grad_expand[:, up_at] = turned_times(low, grad_up).astype(BF)
        total = total + times_turned(grad_gate, expand[:, at])
        total = total + times_turned(grad_up, expand[:, up_at])
        yield
    grad_middle, gain_two = norm_backward(total, normed, inverse, gain[1:2])
    out[...] = grad_final + grad_middle
    gains[...] = jnp.zeros_like(gains)
    gains[1:2] = gain_two.reshape(1, width)
    gains[2:3] = gain_top.reshape(1, width)
    yield


def layer_backward(dims, grad_top, final, middle, both, gain, expand_w, shrink_w, start, angles, attention, head, cid):
    nz, ny, nx = dims
    length, width = middle.shape
    deep, columns = head.shape[2:]
    later = len(attention)

    def kernel(*refs):
        grad_top, final, middle, both, gain, expand, shrink, start, angles, head_in, *rest = refs
        sources, rest = (rest[:later], rest[later:])
        expand_out, shrink_out, grad_qkv, grad_mix, start_out, gains, head_out, *rest = rest
        qkv, mix, held, probs, *rest = rest
        grad_expand, grad_shrink, grad_mid, *rest = rest
        near, mids, fars, (ssem, rsem, lsem) = (rest[0:2], rest[2:4], rest[4:6], rest[6:])
        place = Place(dims)
        y, x = (place.y, place.x)
        comm = Comm(ssem, rsem, lsem)
        loads = [comm.keep(src, dst) for src, dst in zip(sources, (qkv, mix, held, probs))]
        greet(place, [off for off in line_offsets(dims) if off[1] or off[2]])
        parts = (pl.ds(0, deep // 2), pl.ds(deep // 2, deep // 2))
        by_x = [(t, place.xs(nx - t), place.dev(x=t)) for t in range(1, nx)]
        by_y = [(t, place.ys(ny - t), place.dev(y=t)) for t in range(1, ny)]
        came = [comm.send(head_in.at[:, to, parts[0]], near[0].at[t - 1], dev) for t, to, dev in by_x]
        came += [comm.send(head_in.at[to, :, parts[1]], near[1].at[t - 1], dev) for t, to, dev in by_y]
        drain(
            feed_back_steps(
                grad_top, final, middle, both, gain, expand, shrink, grad_expand, grad_shrink, grad_mid, gains
            )
        )
        comm.keep(grad_expand, expand_out)
        comm.keep(grad_shrink, shrink_out)
        for copy in came:
            copy.wait_recv()
        add_blocks(mids[0], [head_in.at[:, x, parts[0]]] + [near[0].at[t] for t in range(nx - 1)])
        add_blocks(mids[1], [head_in.at[y, :, parts[1]]] + [near[1].at[t] for t in range(ny - 1)])
        came = [comm.send(mids[0].at[to], fars[0].at[t - 1], dev) for t, to, dev in by_y]
        came += [comm.send(mids[1].at[to], fars[1].at[t - 1], dev) for t, to, dev in by_x]
        for copy in loads:
            comm.done(copy)

        def weights(k):
            return qkv[:, width * k : width * (k + 1)]

        def put(k, value):
            if k == 3:
                grad_mix[...] = value.astype(BF)
            else:
                grad_qkv[:, width * k : width * (k + 1)] = value.astype(BF)

        drain(
            attention_back_steps(
                start, gain, angles, weights, lambda: mix[...], held, probs, grad_mid, put, start_out, gains
            )
        )
        for copy in came:
            copy.wait_recv()
        for part, mid, far in ((parts[0], mids[0].at[y], fars[0]), (parts[1], mids[1].at[x], fars[1])):
            add_blocks(head_out.at[part], [mid] + [far.at[t] for t in range(far.shape[0])])
        comm.finish()

    count = 2 * (ny + nx)
    half = (deep // 2, columns)
    outs = [
        shape(expand_w.shape, BF),
        shape(shrink_w.shape, BF),
        shape(attention[0].shape, BF),
        shape(attention[1].shape, BF),
        shape((length, width), F32),
        shape((8, width), F32),
        shape(head.shape[2:], F32),
    ]
    scratch = [pltpu.VMEM(v.shape, v.dtype) for v in attention]
    scratch += [pltpu.VMEM(expand_w.shape, BF), pltpu.VMEM(shrink_w.shape, BF)]
    scratch += [
        pltpu.VMEM((length, width), F32),
        pltpu.VMEM((nx - 1, ny) + half, BF),
        pltpu.VMEM((ny - 1, nx) + half, BF),
        pltpu.VMEM((ny,) + half, BF),
        pltpu.VMEM((nx,) + half, BF),
        pltpu.VMEM((ny - 1,) + half, BF),
        pltpu.VMEM((nx - 1,) + half, BF),
        sems(count),
        sems(count),
        sems(later + 2),
    ]
    args = (grad_top, final, middle, both, gain, expand_w, shrink_w, start, angles, head, *attention)
    return call(
        kernel, outs, [VMEM] * 10 + [ANY] * later, [ANY] * 2 + [VMEM] * 5, scratch,
        cid, "layer_backward", args, 60 * 2**20,
    )


def rope_tables(length, width):
    quarter = width // 4
    places = np.arange(length)
    freq = np.float32(10000.0) ** (-np.arange(quarter, dtype=np.float32) / np.float32(quarter))
    row_angle = (places // GRID).astype(np.float32)[:, None] * freq
    col_angle = (places % GRID).astype(np.float32)[:, None] * freq
    angles = np.concatenate([row_angle, row_angle, col_angle, col_angle] * (128 // width), axis=-1)
    return jnp.asarray(np.stack([np.cos(angles), np.sin(angles)]).astype(np.float32))


def adam_update(master, drift, square, grad, rate, decay):
    moment = BETA_ONE * drift + (1.0 - BETA_ONE) * grad
    second = BETA_TWO * square + (1.0 - BETA_TWO) * grad * grad
    stride = (
        moment / (1.0 - BETA_ONE**STEP) / (jnp.sqrt(second / (1.0 - BETA_TWO**STEP)) + ADAM_EPS)
    )
    return (master - rate * (stride + decay * master), moment, second)


def block_form(rows, columns):
    return (rows, columns) if rows % 8 == 0 else (rows * columns // 128, 128)


FIRST_AXES = ("x", "x", "y", "x")


def on_device(dims, *args):
    labels, targets, heights, loss_mask = args[:4]
    masters, drifts, squares = (args[4:12], args[12:20], args[20:28])
    class_table, code_table, attend_in, attend_mix, expand_in, shrink_out, head_weight, norm_gains = masters
    images, local_len = targets.shape
    length = local_len * 2

    layers = (attend_in, attend_mix, expand_in, shrink_out)
    *weights, start, gain, metas, allowed = gather_all(
        dims, layers, FIRST_AXES, code_table, class_table.T, norm_gains, labels, targets, heights, loss_mask, 0
    )
    qkv_w, mix_w, expand_w, shrink_w = (v.reshape(-1, v.shape[-1]) for v in weights)

    angles = rope_tables(length, HD)
    held, probs, middle = attention_forward(start, gain, angles, allowed, qkv_w, mix_w)
    grad_top, grad_head, partial, both, final = head_all(
        dims, middle, gain, metas, head_weight, expand_w, shrink_w, images, 2
    )
    grad_expand, grad_shrink, grad_qkv, grad_mix, grad_start, gain_grads, grad_head = layer_backward(
        dims, grad_top, final, middle, both, gain, expand_w, shrink_w, start, angles,
        (qkv_w, mix_w, held, probs), grad_head, 3,
    )

    grads_in = []
    for grad, shard in zip((grad_qkv, grad_mix, grad_expand, grad_shrink), layers):
        grads_in.append(grad.reshape(dims + (2,) + block_form(*shard.shape)))
    *layer_shares, code_share, class_share, gain_share, sums = scatter_all(
        dims,
        grads_in,
        FIRST_AXES,
        grad_start,
        gain_grads,
        metas,
        grad_head,
        partial,
        code_table.shape[0],
        class_table.shape[0],
        4,
    )
    layer_shares = [g.reshape(v.shape) for g, v in zip(layer_shares, layers)]
    class_share = class_share[: class_table.shape[1], : class_table.shape[0]].T
    gain_share = gain_share[1:4, : norm_gains.shape[1]]
    shares = (class_share, code_share, *layer_shares, grad_head, gain_share)
    total_square, loss_sum, loss_count = (sums[0, 0], sums[0, 1], sums[0, 2])
    grad_norm = jnp.sqrt(total_square) / loss_count
    factor = CLIP_NORM / jnp.maximum(grad_norm, CLIP_NORM) / loss_count
    news, firsts, seconds = ([], [], [])
    for member in range(8):
        fresh, moment, second = adam_update(
            masters[member],
            drifts[member],
            squares[member],
            shares[member] * factor,
            RATES[member],
            DECAYS[member],
        )
        news.append(fresh)
        firsts.append(moment)
        seconds.append(second)
    return tuple(news) + tuple(firsts) + tuple(seconds) + (grad_norm, loss_sum, loss_count)


def solution(mesh):
    rows, columns = (P(("dp", "seq"), None), P(None, ("dp", "seq")))
    eight = (columns, rows, rows, rows, rows, rows, columns, columns)
    return jax.shard_map(
        functools.partial(on_device, dims_of(mesh.shape["dp"])),
        mesh=mesh,
        in_specs=(P("dp"), P("dp", "seq"), P("dp"), P("dp", "seq")) + eight * 3,
        out_specs=eight * 3 + (P(), P(), P()),
        check_vma=False,
    )
```

```python
import functools

import jax
import jax.numpy as jnp
import numpy as np
from jax import lax
from jax.experimental import pallas as pl
from jax.experimental.pallas import tpu as pltpu
from jax.sharding import PartitionSpec as P

HD = 64
GRID = 16
STEP = 10

EPS_NORM = 1e-05
BETA_ONE = 0.9
BETA_TWO = 0.95
ADAM_EPS = 1e-08
CLIP_NORM = 0.01
NEGATIVE_FILL = -1000000000.0
RATES = (0.8, 0.8, 0.08, 0.08, 0.08, 0.08, 0.08, 0.8)
DECAYS = (0.1, 0.1, 0.1, 0.1, 0.1, 0.1, 0.1, 0.0)

PIECE = 512

MESH = pl.DeviceIdType.MESH
ANY = pl.BlockSpec(memory_space=pl.ANY)
VMEM = pl.BlockSpec(memory_space=pltpu.VMEM)
SMEM = pl.BlockSpec(memory_space=pltpu.SMEM)
BF = jnp.bfloat16
F32 = jnp.float32


def dims_of(dp):
    bits = dp.bit_length() - 1
    nz = 1 << (bits // 2)
    rest = dp // nz
    ny = 1 << ((rest.bit_length() - 1) // 2)
    return (nz, ny, rest // ny)


class Place:
    def __init__(self, dims):
        self.dims = dims
        nz, ny, nx = dims
        chip = lax.axis_index("dp")
        self.c = lax.axis_index("seq")
        self.z = chip // (ny * nx)
        self.y = (chip // nx) % ny
        self.x = chip % nx

    def zs(self, back):
        return (self.z + self.dims[0] - back) % self.dims[0]

    def ys(self, back):
        return (self.y + self.dims[1] - back) % self.dims[1]

    def xs(self, back):
        return (self.x + self.dims[2] - back) % self.dims[2]

    def dev(self, z=0, y=0, x=0, c=0):
        nz, ny, nx = self.dims
        z, y, x = ((self.z + z) % nz, (self.y + y) % ny, (self.x + x) % nx)
        return ((z * ny + y) * nx + x, (self.c + c) % 2)


def line_offsets(dims):
    nz, ny, nx = dims
    return (
        [(s, 0, 0, 0) for s in range(1, nz)]
        + [(0, s, 0, 0) for s in range(1, ny)]
        + [(0, 0, s, 0) for s in range(1, nx)]
        + [(0, 0, 0, 1)]
    )


def plane_offsets(dims):
    return [(0, v, u, 0) for v in range(dims[1]) for u in range(dims[2]) if v or u]


def greet(place, offsets):
    offsets = sorted(set(offsets))
    sem = pltpu.get_barrier_semaphore()
    for off in offsets:
        pl.semaphore_signal(sem, inc=1, device_id=place.dev(*off), device_id_type=MESH)
    pl.semaphore_wait(sem, len(offsets))


class Comm:
    def __init__(self, send_sems, recv_sems, local_sems):
        self.send_sems, self.recv_sems, self.local_sems = (send_sems, recv_sems, local_sems)
        self.sent, self.held, self.count, self.locals = ([], [], 0, 0)

    def send(self, src, dst, device):
        k = self.count
        self.count += 1
        copy = pltpu.make_async_remote_copy(
            src_ref=src,
            dst_ref=dst,
            send_sem=self.send_sems.at[k],
            recv_sem=self.recv_sems.at[k],
            device_id=device,
            device_id_type=MESH,
        )
        copy.start()
        self.sent.append(copy)
        return copy

    def keep(self, src, dst):
        copy = pltpu.make_async_copy(src, dst, self.local_sems.at[self.locals])
        self.locals += 1
        copy.start()
        self.held.append(copy)
        return copy

    def gone(self, copy):
        copy.wait_send()
        self.sent = [other for other in self.sent if other is not copy]

    def done(self, copy):
        copy.wait()
        self.held = [other for other in self.held if other is not copy]

    def finish(self):
        for copy in self.sent:
            copy.wait_send()
        for copy in self.held:
            copy.wait()


def drain(steps):
    for _ in steps:
        pass


def all_offsets(dims):
    nz, ny, nx = dims
    spots = [(k, j, i, core) for k in range(nz) for j in range(ny) for i in range(nx) for core in range(2)]
    return spots[1:]


def small_exchange(comm, place, src, out, own):
    z, y, x, c = (place.z, place.y, place.x, place.c)
    nz, ny, nx = place.dims
    if own:
        comm.keep(src(z, y, x, c), out.at[z, y, x, c])
    got = []
    for off in all_offsets(place.dims):
        there = (place.zs(nz - off[0]), place.ys(ny - off[1]), place.xs(nx - off[2]), (c + off[3]) % 2)
        got.append(comm.send(src(*there), out.at[z, y, x, c], place.dev(*off)))
    return got


class PlaneGather:
    def __init__(self, comm, place):
        self.comm, self.place = (comm, place)
        self.firsts, self.seconds, self.mates = ([], [], [])

    def ways(self, axis):
        _, ny, nx = self.place.dims
        return range(1, ny if axis == "y" else nx)

    def back(self, axis, t, yy, xx):
        return (self.place.ys(t), xx) if axis == "y" else (yy, self.place.xs(t))

    def spread(self, block, first, src=None):
        place, second = (self.place, "y" if first == "x" else "x")
        dst = block(place.y, place.x)
        src = dst if src is None else src
        for t in self.ways(first):
            copy = self.comm.send(src, dst, place.dev(**{first: t}))
            self.firsts.append((block, first, second, t, copy))
        for t in self.ways(second):
            copy = self.comm.send(src, dst, place.dev(**{second: t}))
            self.seconds.append((block(*self.back(second, t, place.y, place.x)), copy))
        self.mates.append(self.comm.send(src, dst, place.dev(c=1)))

    def forward(self):
        place = self.place
        for block, first, second, t, copy in self.firsts:
            copy.wait_recv()
            yy, xx = self.back(first, t, place.y, place.x)
            held = block(yy, xx)
            for u in self.ways(second):
                copy = self.comm.send(held, held, place.dev(**{second: u}))
                self.seconds.append((block(*self.back(second, u, yy, xx)), copy))
            self.mates.append(self.comm.send(held, held, place.dev(c=1)))
        self.firsts = []

    def settle(self):
        for held, copy in self.seconds:
            copy.wait_recv()
            self.mates.append(self.comm.send(held, held, self.place.dev(c=1)))
        self.seconds = []

    def forward_some(self, count):
        rest = self.firsts[count:]
        self.firsts = self.firsts[:count]
        self.forward()
        self.firsts = rest

    def arrive(self):
        for copy in self.mates:
            copy.wait_recv()
        self.mates = []


def sems(count):
    return pltpu.SemaphoreType.DMA((count,))


def shape(dims, dtype):
    return jax.ShapeDtypeStruct(tuple(dims), dtype)


def call(kernel, outs, in_specs, out_specs, scratch, cid, name, args, vmem=None):
    return pl.pallas_call(
        kernel,
        out_shape=outs,
        in_specs=in_specs,
        out_specs=out_specs,
        scratch_shapes=scratch,
        compiler_params=pltpu.CompilerParams(
            collective_id=cid, has_side_effects=True, vmem_limit_bytes=vmem
        ),
        name=name,
    )(*args)


def small_sends(dims):
    return dims[0] * dims[1] * dims[2] * 2 - 1


def gather_all(dims, layers, first_axes, table, classes, gains, labels, targets, heights, masks, cid):
    nz, ny, nx = dims
    n = len(layers)
    rows, width = table.shape
    images, local_len = targets.shape
    length = local_len * 2
    columns = gains.shape[1]
    meta = (8, 128)
    count_images = nz * ny * nx * images
    label_rows = -(-count_images // 128)
    groups = [(k,) for k in range(nz)] if nz <= 4 else [tuple(range(nz))]

    def kernel(*refs):
        ins, rest = (refs[:n], refs[n:])
        table_in, class_in, gain_in, labels_in, targets_in, heights_in, masks_in, *rest = rest
        outs, rest = (rest[:n], rest[n:])
        start_out, gain_out, meta_out, allowed_out, *rest = rest
        low, rest = (rest[:n], rest[n:])
        whole, found, total, class_low, gain_row, meta_in, parts_out, small_out, small_in, *rest = rest
        ssem, rsem, lsem = rest
        place = Place(dims)
        z, y, x, c = (place.z, place.y, place.x, place.c)
        chip = (z * ny + y) * nx + x
        meta_in[...] = jnp.zeros_like(meta_in)
        meta_in[0:images] = targets_in[...]
        meta_in[images : 2 * images] = masks_in[...]
        lane = lax.broadcasted_iota(jnp.int32, (1, 128), 1)
        for i in range(images):
            meta_in[4:5] += jnp.where(lane == i, labels_in[i], 0)
            meta_in[4:5] += jnp.where(lane == images + i, heights_in[i], 0)
            for r in range(label_rows):
                meta_in[5 + r : 6 + r] += jnp.where(lane == chip * images + i - 128 * r, labels_in[i], 0)
        greet(place, all_offsets(dims))
        comm = Comm(ssem, rsem, lsem)
        metas = small_exchange(comm, place, lambda *spot: meta_in, meta_out, False)
        meta_out[z, y, x, c] = meta_in[...]
        waits = []
        whole[y, x, c] = table_in[...].astype(BF)
        tables, blocks = (PlaneGather(comm, place), PlaneGather(comm, place))
        for first, start in (("x", 0), ("y", rows // 2)):
            half = pl.ds(start, rows // 2)
            tables.spread(lambda yy, xx, half=half: whole.at[yy, xx, c, half], first)
        for a in range(n):
            low[a][...] = ins[a][...].astype(BF)
        along = {}
        for s in range(1, nz):
            for a in range(n):
                along[s, a] = comm.send(low[a], outs[a].at[z, y, x, c], place.dev(z=s))
        kept = [comm.keep(low[a], outs[a].at[z, y, x, c]) for a in range(n)]

        def spread(group):
            for a in range(n):
                for k in group:
                    if k:
                        along[k, a].wait_recv()
                if len(group) > 1:
                    comm.done(kept[a])
                    at = pl.ds(0, nz)
                else:
                    at = place.zs(group[0])
                blocks.spread(
                    lambda yy, xx, a=a, at=at: outs[a].at[at, yy, xx, c],
                    first_axes[a],
                    low[a] if group == (0,) else None,
                )

        for copy in metas:
            copy.wait_recv()

        class_low[...] = jnp.zeros_like(class_low)
        class_low[0:columns, 0 : class_in.shape[1]] = class_in[...]
        small_in[...] = jnp.zeros_like(small_in)
        for r in range(label_rows):
            labels = jnp.zeros((1, 128), jnp.int32)
            for k in range(nz * ny * nx):
                labels = labels + meta_out[k // (ny * nx), k // nx % ny, k % nx, 0, 5 + r : 6 + r, :]
            pick = lax.broadcasted_iota(jnp.int32, (class_low.shape[1], 128), 0) == labels
            picked = lax.dot_general(
                jnp.where(pick, 1.0, 0.0).astype(BF),
                class_low[...].astype(BF),
                (((0,), (1,)), ((), ())),
                preferred_element_type=F32,
            )
            for i in range(min(128, count_images - 128 * r)):
                k, core = divmod(128 * r + i, 2)
                small_in[k // (ny * nx), k // nx % ny, k % nx, core, 0:1, 0 : class_low.shape[0]] = picked[
                    i : i + 1
                ]
        gain_row[...] = jnp.zeros_like(gain_row)
        gain_row[0:3, 0:columns] = gain_in[...].astype(BF).astype(F32)

        @pl.loop(0, nz)
        def _(k):
            for j in range(ny):
                for i in range(nx):
                    for core in range(2):
                        small_in[k, j, i, core, 1:4, :] = gain_row[0:3]

        smalls = small_exchange(comm, place, lambda *spot: small_in.at[spot], small_out, False)
        small_out[z, y, x, c] = small_in[z, y, x, c]

        size = len(layers)
        steps = [lambda group=group: spread(group) for group in groups]
        steps.pop(0)()
        tables.forward()
        if steps:
            steps.pop(0)()
        blocks.forward_some(size)
        if steps:
            steps.pop(0)()
        tables.settle()
        blocks.forward_some(size)
        for step in steps:
            step()
        tables.arrive()

        for s in range(1, nz + 1):
            zz = place.zs(s % nz)
            halves = []
            for half in range(2):
                codes = meta_out[zz, y, x, half, pl.ds(c, 1), :].astype(F32)
                halves.append(jnp.broadcast_to(codes, (128, local_len)).T)
            column = jnp.concatenate(halves, axis=0)
            column = column - (z * ny * nx * 2 * rows).astype(F32)
            total[...] = jnp.zeros_like(total)

            @pl.loop(0, ny * nx * 2)
            def _(j):
                base = (j * rows).astype(F32)
                lane = lax.broadcasted_iota(jnp.int32, (length, 128), 1).astype(F32) + base
                picks = [
                    jnp.where(column == lane + float(128 * q), 1.0, 0.0).astype(BF)
                    for q in range(-(-rows // 128))
                ]
                pick = jnp.concatenate(picks, axis=1)[:, :rows]
                total[...] += matmul(pick, whole[j // (2 * nx), j // 2 % nx, j % 2])

            found[s % nz] = total[...].astype(BF)
            if s < nz:
                waits.append(comm.send(found.at[s], parts_out.at[nz - s - 1], place.dev(z=nz - s)))
            blocks.forward_some(size)
        blocks.forward()
        height = jnp.where(c == 0, heights_in[0], heights_in[images - 1])
        query = lax.broadcasted_iota(jnp.int32, (length, length), 0)
        key = lax.broadcasted_iota(jnp.int32, (length, length), 1)
        allowed_out[...] = jnp.where((key <= query) & (key < GRID * height), 1.0, 0.0)
        for copy in smalls:
            copy.wait_recv()
        joined = jnp.zeros((8, width), F32)
        blank = jnp.zeros((8, width - 128), F32)
        for d in range(2 * nz * ny * nx):
            k, core = divmod(d, 2)
            piece = small_out[k // (ny * nx), k // nx % ny, k % nx, core]
            joined = joined + pltpu.roll(jnp.concatenate([piece, blank], axis=1), columns * d, 1)
        gain_out[...] = jnp.concatenate([joined[1:4], jnp.zeros((5, width), F32)], axis=0)
        blocks.settle()
        for copy in waits:
            copy.wait_recv()
        added = found[0].astype(F32)
        for s in range(1, nz):
            added = added + parts_out[s - 1].astype(F32)
        first = lax.broadcasted_iota(jnp.int32, (length, 128), 0) == 0
        for k in range(width // 128):
            at = slice(128 * k, 128 * k + 128)
            start_out[:, at] = jnp.where(first, joined[0:1, at], pltpu.roll(added[:, at], 1, 0))
        blocks.arrive()
        comm.finish()

    count = n * (nz - 1) + (n * len(groups) + 2) * (2 * ny * nx - 1) + nz + 2 * small_sends(dims)
    small = dims + (2, 8, 128)
    outs = [shape(dims + (2,) + v.shape, BF) for v in layers]
    outs += [
        shape((length, width), F32),
        shape((8, width), F32),
        shape(dims + (2,) + meta, jnp.int32),
        shape((length, length), F32),
    ]
    scratch = [pltpu.VMEM(v.shape, BF) for v in layers]
    scratch += [
        pltpu.VMEM((ny, nx, 2) + table.shape, BF),
        pltpu.VMEM((nz, length, width), BF),
        pltpu.VMEM((length, width), F32),
        pltpu.VMEM((-(-columns // 16) * 16, -(-classes.shape[1] // 128) * 128), F32),
        pltpu.VMEM((8, 128), F32),
        pltpu.VMEM(meta, jnp.int32),
        pltpu.VMEM((nz - 1, length, width), BF),
        pltpu.VMEM(small, F32),
        pltpu.VMEM(small, F32),
        sems(count),
        sems(count),
        sems(n),
    ]
    return call(
        kernel, outs, [VMEM] * (n + 3) + [SMEM, VMEM, SMEM, VMEM], [ANY] * n + [VMEM] * 4, scratch,
        cid, "gather_all", (*layers, table, classes, gains, labels, targets, heights, masks), 60 * 2**20,
    )


def add_blocks(out, terms):
    lead = out.shape[:-2]

    def visit(index):
        if len(index) < len(lead):

            @pl.loop(0, lead[len(index)])
            def _(i):
                visit(index + (i,))

        else:
            if len(terms) == 2 and out.dtype == BF:
                out[index] = terms[0][index] + terms[1][index]
                return
            total = terms[0][index].astype(F32)
            for term in terms[1:]:
                total = total + term[index].astype(F32)
            out[index] = total.astype(out.dtype)

    visit(())


def items_of(shapes, axes):
    if shapes[0][0] % 8:
        return [[(a, slice(0, shapes[a][0]), slice(0, shapes[a][1]), axes[a]) for a in pair] for pair in ((2, 3), (0, 1))]
    (rows, qkv), (_, mix), (_, both), (deep, width) = shapes
    every, piece = (slice(0, rows), both // 4)
    return [
        [(3, slice(0, deep // 2), slice(0, width), "x"), (3, slice(deep // 2, deep), slice(0, width), "y")],
        [(2, every, slice(0, piece), "x"), (2, every, slice(2 * piece, 3 * piece), "y")],
        [(0, every, slice(0, 2 * mix), "x"), (0, every, slice(2 * mix, qkv), "y"), (1, every, slice(0, mix), "y")],
        [(2, every, slice(piece, 2 * piece), "x"), (2, every, slice(3 * piece, both), "y")],
    ]


def scatter_all(dims, grads, axes, rows, gains, metas, head, partial, device_codes, classes, cid):
    nz, ny, nx = dims
    plane = ny * nx
    n = len(grads)
    shapes = [g.shape[4:] for g in grads]
    steps = items_of(shapes, axes)
    items = [item for step in steps for item in step]
    order, at = ([], 0)
    for step in steps:
        order.append(list(range(at, at + len(step))))
        at += len(step)
    length, width = rows.shape
    block = (device_codes, width)
    sizes = {"x": nx, "y": ny}
    columns = width // (2 * nz * plane)
    label_rows = -(-2 * nz * plane // 128)

    def kernel(*refs):
        parts, rest = (refs[:n], list(refs[n:]))
        rows_in, gains_in, meta_in, head_in, partial_in = (rest.pop(0) for _ in range(5))
        outs = [rest.pop(0) for _ in range(n)]
        table_out, class_out, gain_out, sums = (rest.pop(0) for _ in range(4))
        owns, halves, ones, twos, threes = ([rest.pop(0) for _ in items] for _ in range(5))
        near, far = ([rest.pop(0), rest.pop(0)] for _ in range(2))
        lined, given, own, half, small_in, small_out, tops, mine, every, ssem, rsem, lsem = rest
        place = Place(dims)
        z, y, x, c = (place.z, place.y, place.x, place.c)
        comm = Comm(ssem, rsem, lsem)
        kept = []
        for i, (a, span, cols, _) in enumerate(items):
            kept.append(comm.keep(parts[a].at[:, :, :, c, span, cols], owns[i]))
        lane = lax.broadcasted_iota(jnp.int32, (8, 128), 1)
        top = jnp.concatenate([rows_in[0:1], gains_in[0:3], jnp.zeros((4, width), F32)], axis=0)
        for d in range(2 * nz * plane):
            k, core = divmod(d, 2)
            piece = pltpu.roll(top, (width - columns * d) % width, 1)[:, :128]
            small_in[k // plane, k // nx % ny, k % nx, core] = jnp.where(lane < columns, piece, 0.0)
        greet(place, all_offsets(dims))
        waits = small_exchange(comm, place, lambda *spot: small_in.at[spot], small_out, False)
        small_out[z, y, x, c] = small_in[z, y, x, c]
        pair, got_one, got_two, third = ({}, {}, {}, {})

        def set_out(g):
            for i in order[g] if g < len(order) else []:
                a, span, cols, _ = items[i]
                pair[i] = comm.send(parts[a].at[:, :, :, 1 - c, span, cols], halves[i], place.dev(c=1))

        def back(axis, t):
            return place.ys(ny - t) if axis == "y" else place.xs(nx - t)

        def first_add(g):
            for i in order[g]:
                pair[i].wait_recv()
                comm.done(kept[i])
                add_blocks(halves[i], [halves[i], owns[i]])

        def first_send(g):
            for i in order[g]:
                axis = items[i][3]
                got_one[i] = [
                    comm.send(
                        halves[i].at[:, back(axis, t)] if axis == "y" else halves[i].at[:, :, back(axis, t)],
                        ones[i].at[t - 1],
                        place.dev(**{axis: t}),
                    )
                    for t in range(1, sizes[axis])
                ]

        def second_step(g):
            for i in order[g]:
                axis = items[i][3]
                other = "x" if axis == "y" else "y"
                for copy in got_one[i]:
                    copy.wait_recv()
                held = halves[i].at[:, y] if axis == "y" else halves[i].at[:, :, x]
                add_blocks(held, [held] + [ones[i].at[t] for t in range(ones[i].shape[0])])
                got_two[i] = [
                    comm.send(
                        halves[i].at[:, y, back("x", t)] if other == "x" else halves[i].at[:, back("y", t), x],
                        twos[i].at[t - 1],
                        place.dev(**{other: t}),
                    )
                    for t in range(1, sizes[other])
                ]

        def third_step(g):
            for i in order[g]:
                for copy in got_two[i]:
                    copy.wait_recv()
                held = halves[i].at[:, y, x]
                add_blocks(held, [held] + [twos[i].at[t] for t in range(twos[i].shape[0])])
                third[i] = [
                    comm.send(halves[i].at[place.zs(nz - s), y, x], threes[i].at[s - 1], place.dev(z=s))
                    for s in range(1, nz)
                ]

        def last_step(g):
            for i in order[g]:
                a, span, cols, _ = items[i]
                for copy in third[i]:
                    copy.wait_recv()
                terms = [halves[i].at[z, y, x]] + [threes[i].at[s] for s in range(nz - 1)]
                add_blocks(outs[a].at[span, cols], terms)

        flat = []
        first = lax.broadcasted_iota(jnp.int32, (1, length), 1) == 0
        for s in range(nz):
            codes = [meta_in[place.zs(s), y, x, part, pl.ds(c, 1), :] for part in range(2)]
            codes = pltpu.roll(jnp.concatenate(codes, axis=1) - z * (2 * plane * device_codes), 1, 1)
            flat.append(jnp.where(first, -1, codes))
        flat = jnp.concatenate(flat, axis=1)

        def product(into, core):
            @pl.loop(0, plane)
            def _(j):
                code = lax.broadcasted_iota(jnp.int32, (device_codes, nz * length), 0)
                pick = code + (j * 2 + core) * device_codes == flat
                pick = jnp.where(pick, 1.0, 0.0).astype(BF)
                value = matmul(pick, lined[...].reshape(nz * length, width))
                into[j // nx, j % nx] = value.astype(BF)

        set_out(0)
        set_out(1)
        lined[0] = rows_in[...].astype(BF)
        lines = [comm.send(lined.at[0], lined.at[s], place.dev(z=s)) for s in range(1, nz)]
        count = len(order)
        for g in range(count):
            first_add(g)
            set_out(g + 2)
            if g >= 2:
                second_step(g - 2)
            first_send(g)
            if g >= 3:
                third_step(g - 3)
        for copy in lines:
            copy.wait_recv()
        product(given, 1 - c)
        table_pair = comm.send(given, half, place.dev(c=1))
        second_step(count - 2)
        product(own, c)
        if count > 2:
            third_step(count - 3)
        second_step(count - 1)
        table_pair.wait_recv()
        add_blocks(half, [half, own])
        parts_of = [pl.ds(0, device_codes // 2), pl.ds(device_codes // 2, device_codes // 2)]
        came = [
            [
                comm.send(half.at[:, back("x", t), parts_of[0]], near[0].at[t - 1], place.dev(x=t))
                for t in range(1, nx)
            ],
            [
                comm.send(half.at[back("y", t), :, parts_of[1]], near[1].at[t - 1], place.dev(y=t))
                for t in range(1, ny)
            ],
        ]
        third_step(count - 2)
        third_step(count - 1)

        for copy in waits:
            copy.wait_recv()
        gain_out[...] = jnp.zeros_like(gain_out)
        tops[...] = jnp.zeros_like(tops)

        @pl.loop(0, nz)
        def _(k):
            for j in range(ny):
                for i in range(nx):
                    for core in range(2):
                        at = ((k * ny + j) * nx + i) * 2 + core
                        tops[pl.ds(at, 1), :] = small_out[k, j, i, core, 0:1, :]
                        gain_out[...] += small_out[k, j, i, core]

        value = jnp.zeros(class_out.shape, F32)
        high = class_out.shape[1]
        for r in range(label_rows):
            labels = jnp.zeros((1, 128), jnp.int32)
            for k in range(nz * plane):
                labels = labels + meta_in[k // plane, k // nx % ny, k % nx, 0, 5 + r : 6 + r, :]
            at = lax.broadcasted_iota(jnp.int32, (high, 128), 1) + 128 * r
            pick = lax.broadcasted_iota(jnp.int32, (high, 128), 0) == labels
            pick = jnp.where(pick & (at < 2 * nz * plane), 1.0, 0.0)
            value = value + lax.dot_general(
                tops[128 * r : 128 * r + 128],
                pick,
                (((0,), (1,)), ((), ())),
                precision=lax.Precision.HIGHEST,
                preferred_element_type=F32,
            )
        class_out[...] = value
        row = lax.broadcasted_iota(jnp.int32, gain_out.shape, 0)
        gained = jnp.where((row >= 1) & (row < 4), gain_out[...], 0.0)
        square = jnp.sum(value * value) + jnp.sum(gained * gained)
        share = head_in[...].astype(F32)
        square = square + jnp.sum(share * share)
        for g in range(count - 1):
            last_step(g)

        for copy in came[0] + came[1]:
            copy.wait_recv()
        for h, held in ((0, half.at[:, x, parts_of[0]]), (1, half.at[y, :, parts_of[1]])):
            add_blocks(held, [held] + [near[h].at[t] for t in range(near[h].shape[0])])
        came = [
            comm.send(half.at[back("y", t), x, parts_of[0]], far[0].at[t - 1], place.dev(y=t))
            for t in range(1, ny)
        ]
        came += [
            comm.send(half.at[y, back("x", t), parts_of[1]], far[1].at[t - 1], place.dev(x=t))
            for t in range(1, nx)
        ]
        last_step(count - 1)
        for a in range(n):
            square = square + jnp.sum(outs[a][...] * outs[a][...])
        for copy in came:
            copy.wait_recv()
        for h in range(2):
            terms = [half.at[y, x, parts_of[h]]] + [far[h].at[t] for t in range(far[h].shape[0])]
            add_blocks(table_out.at[parts_of[h]], terms)
        square = square + jnp.sum(table_out[...] * table_out[...])
        first = (lax.broadcasted_iota(jnp.int32, mine.shape, 0) == 0) & (
            lax.broadcasted_iota(jnp.int32, mine.shape, 1) == 0
        )
        mine[...] = partial_in[...] + jnp.where(first, square, 0.0)
        for copy in small_exchange(comm, place, lambda *spot: mine, every, False):
            copy.wait_recv()
        every[z, y, x, c] = mine[...]
        sums[...] = jnp.zeros_like(sums)

        @pl.loop(0, nz)
        def _(k):
            for j in range(ny):
                for i in range(nx):
                    sums[...] += every[k, j, i, 0] + every[k, j, i, 1]

        comm.finish()

    total = len(items) * (ny + nx - 1 + nz - 1) + nz + 2 * (ny + nx) + 2 * small_sends(dims)
    cuts = [(span.stop - span.start, cols.stop - cols.start) for _, span, cols, _ in items]
    near_far = [(ny, nx) if item[3] == "y" else (nx, ny) for item in items]
    part = (device_codes // 2, width)
    scratch = [pltpu.VMEM((nz, ny, nx) + t, BF) for t in cuts] * 2
    scratch += [pltpu.VMEM((u - 1, nz, v) + t, BF) for t, (u, v) in zip(cuts, near_far)]
    scratch += [pltpu.VMEM((v - 1, nz) + t, BF) for t, (u, v) in zip(cuts, near_far)]
    scratch += [pltpu.VMEM((nz - 1,) + t, BF) for t in cuts]
    scratch += [
        pltpu.VMEM((nx - 1, ny) + part, BF),
        pltpu.VMEM((ny - 1, nx) + part, BF),
        pltpu.VMEM((ny - 1,) + part, BF),
        pltpu.VMEM((nx - 1,) + part, BF),
        pltpu.VMEM((nz, length, width), BF),
        pltpu.VMEM((ny, nx) + block, BF),
        pltpu.VMEM((ny, nx) + block, BF),
        pltpu.VMEM((ny, nx) + block, BF),
        pltpu.VMEM(dims + (2, 8, 128), F32),
        pltpu.VMEM(dims + (2, 8, 128), F32),
        pltpu.VMEM((128 * label_rows, 128), F32),
        pltpu.VMEM(partial.shape, F32),
        pltpu.VMEM(dims + (2,) + partial.shape, F32),
        sems(total),
        sems(total),
        sems(len(items)),
    ]
    outs = [shape(t, F32) for t in shapes]
    high = -(-classes // 128) * 128
    outs += [shape(block, F32), shape((128, high), F32), shape((8, 128), F32), shape(partial.shape, F32)]
    return call(
        kernel, outs, [ANY] * n + [VMEM] * 5, [VMEM] * (n + 4), scratch,
        cid, "scatter_all", (*grads, rows, gains, metas, head, partial), 60 * 2**20,
    )


def head_all(dims, middle, gain, metas, head, expand_w, shrink_w, images, cid):
    nz, ny, nx = dims
    length, width = middle.shape
    inner = shrink_w.shape[0]
    pieces = inner // PIECE
    columns = head.shape[1]
    lanes = min(columns, 128)
    groups = columns // lanes
    plane = ny * nx
    blocks = 2 * plane
    keep = columns >= 128
    shared = columns == PIECE and nz * length >= width and blocks >= 2 * pieces

    def kernel(*refs):
        middle_in, gain_in, meta_in, head_in, expand_in, shrink_in, *rest = refs
        top_out, head_out, loss_out, both_out, final_out, *rest = rest
        whole, marks_in, wide, lined, turned, peaks, totals, picks, exps, grads, *rest = rest
        columned, partial, back, coming, mine, every, given, half, ssem, rsem, lsem = rest
        place = Place(dims)
        z, y, x, c = (place.z, place.y, place.x, place.c)
        greet(place, line_offsets(dims))
        comm = Comm(ssem, rsem, lsem)
        room, loads = ({}, {})

        def load(j):
            room[j] = grads.at[j, pl.ds(0, width)] if shared else wide.at[j // pieces]
            loads[j] = comm.keep(expand_in.at[:, pl.ds(PIECE * j, PIECE)], room[j])

        for j in range(2 * pieces) if shared else []:
            load(j)
        whole[c, y, x] = head_in[...].astype(BF)
        gather = PlaneGather(comm, place)
        for first, start in (("x", 0), ("y", width // 2)):
            part = pl.ds(start, width // 2)
            gather.spread(lambda yy, xx, part=part: whole.at[c, yy, xx, part], first)
        normed = norm_forward(middle_in[...], gain_in[1:2])[0].astype(BF)
        total = middle_in[...]
        for j in range(pieces):
            at = slice(PIECE * j, PIECE * (j + 1))
            for k in (j, pieces + j):
                if not shared:
                    load(k)
                comm.done(loads[k])
            gate, up = (matmul(normed, room[j][...]), matmul(normed, room[pieces + j][...]))
            both_out[:, at] = gate
            both_out[:, inner + PIECE * j : inner + PIECE * (j + 1)] = up
            hidden = (gate * jax.nn.sigmoid(gate) * up).astype(BF)
            total = total + matmul(hidden, shrink_in[at])
        final_out[...] = total
        lined[0] = norm_forward(total, gain_in[2:3])[0].astype(BF)
        turns = sorted(range(1, nz), key=lambda s: min(s, nz - s))
        arriving = {s: comm.send(lined.at[0], lined.at[s], place.dev(z=s)) for s in turns[:2]}
        turned[:, 0:length] = lined[0].T
        for s in range(nz):
            for part in range(2):
                codes = meta_in[place.zs(s), y, x, part, pl.ds(c, 1), :].astype(F32)
                tall = jnp.broadcast_to(codes, (128, 128)).T.astype(jnp.int32)
                marks_in[s, 128 * part : 128 * part + 128] = tall[:, :lanes] - z * (blocks * columns)
        gather.forward()
        gather.settle()
        for s in turns[:2]:
            comm.gone(arriving[s])
        for s in turns[2:]:
            arriving[s] = comm.send(lined.at[0], lined.at[s], place.dev(z=s))
        gather.arrive()

        def block(k):
            return whole[k // plane, k // nx % ny, k % nx]

        def split(value):
            return [value[:, lanes * q : lanes * (q + 1)] for q in range(groups)]

        def hits(s, k):
            base = (k % plane * 2 + k // plane) * columns
            lane = lax.broadcasted_iota(jnp.int32, (length, lanes), 1) + base
            return [lane + lanes * q == marks_in[s] for q in range(groups)]

        def logits_of(s, k):
            return matmul(lined[s], block(k))

        def forward(s):
            at = pl.ds(s * length, length)
            peaks[...] = jnp.full_like(peaks, -jnp.inf)
            totals[...] = jnp.zeros_like(totals)
            picks[...] = jnp.zeros_like(picks)

            @pl.loop(0, blocks)
            def _(k):
                logits = logits_of(s, k)
                if keep:
                    exps[k, at] = logits
                high, found = (peaks[...], picks[...])
                for piece, hit in zip(split(logits), hits(s, k)):
                    high = jnp.maximum(high, piece)
                    found = found + jnp.where(hit, piece, 0.0)
                peaks[...] = high
                picks[...] = found

            peak = jnp.max(peaks[...], axis=1, keepdims=True)
            peaks[...] = jnp.broadcast_to(peak, (length, lanes))

            @pl.loop(0, blocks)
            def _(k):
                logits = exps[k, at] if keep else logits_of(s, k)
                total = totals[...]
                for q, piece in enumerate(split(logits)):
                    power = jnp.exp(piece - peaks[...])
                    if keep:
                        exps[k, at, lanes * q : lanes * (q + 1)] = power
                    total = total + power
                totals[...] = total

            if not keep:
                exps[s] = peaks[...]
            lane = lax.broadcasted_iota(jnp.int32, (length, 128), 1)
            total = jnp.sum(totals[...], axis=1, keepdims=True)
            found = jnp.sum(picks[...], axis=1, keepdims=True)
            table = jnp.where(lane == 0, peak, jnp.where(lane == 1, total, found))
            mine[place.zs(s)] = table.T[:8]

        forward(0)
        for s in turns:
            arriving[s].wait_recv()
            turned[:, s * length : (s + 1) * length] = lined[s].T
            forward(s)
        stats = [comm.send(mine, every.at[s], place.dev(z=s)) for s in range(1, nz)]
        every[0] = mine[...]
        for copy in stats:
            copy.wait_recv()

        def backward(s):
            at = pl.ds(s * length, length)
            held = [every[q, place.zs(s)] for q in range(nz)]
            peak = held[0][0:1]
            for other in held[1:]:
                peak = jnp.maximum(peak, other[0:1])
            total = sum(other[1:2] * jnp.exp(other[0:1] - peak) for other in held)
            zz = place.zs(s)
            mask = [meta_in[zz, y, x, part, pl.ds(images + c, 1), :] for part in range(2)]
            mask = jnp.concatenate(mask, axis=1).astype(F32)
            tail = meta_in[zz, y, x, 0, 4:5, :]
            lane = lax.broadcasted_iota(jnp.int32, (1, 128), 1)
            tall = jnp.sum(jnp.where(lane == images + c, tail, 0).astype(F32), axis=1, keepdims=True)
            place_of = lax.broadcasted_iota(jnp.int32, (1, length), 1).astype(F32)
            weight = jnp.where(place_of < GRID * tall, mask, 0.0)
            if s == 0:
                found = sum(other[2:3] for other in held)
                loss = (peak + jnp.log(total) - found) * weight
                lane = lax.broadcasted_iota(jnp.int32, (8, 128), 1)
                row = lax.broadcasted_iota(jnp.int32, (8, 128), 0)
                sums = jnp.where(lane == 1, jnp.sum(loss, axis=1, keepdims=True), 0.0)
                sums = sums + jnp.where(lane == 2, jnp.sum(weight, axis=1, keepdims=True), 0.0)
                loss_out[...] = jnp.where(row == 0, sums, 0.0)
            scale = weight / total * jnp.exp(held[0][0:1] - peak)
            tall = jnp.concatenate([scale, weight, jnp.zeros((126, length), F32)], axis=0).T
            columned[0] = jnp.broadcast_to(tall[:, 0:1], (length, lanes))
            columned[1] = jnp.broadcast_to(tall[:, 1:2], (length, lanes))
            partial[...] = jnp.zeros_like(partial)

            @pl.loop(0, blocks)
            def _(k):
                if keep:
                    powers = split(exps[k, at])
                else:
                    powers = [jnp.exp(piece - exps[s]) for piece in split(logits_of(s, k))]
                pieces = []
                for power, hit in zip(powers, hits(s, k)):
                    grad = power * columned[0] - jnp.where(hit, columned[1], 0.0)
                    pieces.append(grad.astype(BF))
                grad = jnp.concatenate(pieces, axis=1) if groups > 1 else pieces[0]
                grads[k, at] = grad
                partial[...] += lax.dot_general(
                    grad, block(k), (((1,), (1,)), ((), ())), preferred_element_type=F32
                )

        coming_in = []
        for s in range(1, nz):
            backward(s)
            back[s - 1] = partial[...].astype(BF)
            coming_in.append(comm.send(back.at[s - 1], coming.at[s - 1], place.dev(z=nz - s)))
        backward(0)

        def weights(into, core):
            @pl.loop(0, plane)
            def _(j):
                into[j // nx, j % nx] = matmul(turned[...], grads[core * plane + j]).astype(BF)

        weights(given, 1 - c)
        pair = comm.send(given, half, place.dev(c=1))
        weights(head_out, c)
        pair.wait_recv()
        add_blocks(head_out, [head_out, half])
        for copy in coming_in:
            copy.wait_recv()
        total = partial[...]
        for s in range(nz - 1):
            total = total + coming[s].astype(F32)
        top_out[...] = total
        comm.finish()

    count = 3 * (nz - 1) + 2 * (2 * plane - 1) + 1
    scratch = [
        pltpu.VMEM((2, ny, nx) + head.shape, BF),
        pltpu.VMEM((nz, length, lanes), jnp.int32),
        pltpu.VMEM((16, 128) if shared else (2, width, PIECE), BF),
        pltpu.VMEM((nz, length, width), BF),
        pltpu.VMEM((width, nz * length), BF),
        pltpu.VMEM((length, lanes), F32),
        pltpu.VMEM((length, lanes), F32),
        pltpu.VMEM((length, lanes), F32),
        pltpu.VMEM((blocks, nz * length, columns) if keep else (nz, length, lanes), F32),
        pltpu.VMEM((blocks, nz * length, columns), BF),
        pltpu.VMEM((2, length, lanes), F32),
        pltpu.VMEM((length, width), F32),
        pltpu.VMEM((nz - 1, length, width), BF),
        pltpu.VMEM((nz - 1, length, width), BF),
        pltpu.VMEM((nz, 8, length), F32),
        pltpu.VMEM((nz, nz, 8, length), F32),
        pltpu.VMEM((ny, nx) + head.shape, BF),
        pltpu.VMEM((ny, nx) + head.shape, BF),
        sems(count),
        sems(count),
        sems(2 * pieces),
    ]
    outs = [
        shape((length, width), F32),
        shape((ny, nx) + head.shape, BF),
        shape((8, 128), F32),
        shape((length, 2 * inner), F32),
        shape((length, width), F32),
    ]
    return call(
        kernel, outs, [VMEM] * 4 + [ANY, VMEM], [VMEM] * 5, scratch,
        cid, "head_all", (middle, gain, metas, head, expand_w, shrink_w), 63 * 2**20,
    )


def matmul(left, right):
    return jnp.dot(left, right, preferred_element_type=F32)


def norm_forward(values, gain):
    inverse = lax.rsqrt(jnp.mean(values * values, axis=-1, keepdims=True) + EPS_NORM)
    normed = values * inverse
    return (normed * gain, normed, inverse)


def norm_backward(grad, normed, inverse, gain):
    scaled = grad * gain
    inner = jnp.mean(scaled * normed, axis=-1, keepdims=True)
    return (inverse * (scaled - normed * inner), jnp.sum(grad * normed, axis=0))


def turned(value, low):
    return jnp.where(low, -pltpu.roll(value, 112, 1), pltpu.roll(value, 16, 1))


def low_quarters(rows):
    return lax.broadcasted_iota(jnp.int32, (rows, 128), 1) % 32 < 16


def left_half(rows):
    return lax.broadcasted_iota(jnp.int32, (rows, 128), 1) < HD


def times_turned(left, right):
    return lax.dot_general(left, right, (((1,), (1,)), ((), ())), preferred_element_type=F32)


def turned_times(left, right):
    return lax.dot_general(left, right, (((0,), (0,)), ((), ())), preferred_element_type=F32)


def attention_steps(start, gain, angles, allowed, weights, mix, held, probs, out):
    length, width = start.shape
    normed = norm_forward(start[...], gain[0:1])[0].astype(BF)
    low, left = (low_quarters(length), left_half(length))
    for k in range(3):
        value = matmul(normed, weights(k))
        for p in range(width // 128):
            piece = value[:, 128 * p : 128 * p + 128]
            if k < 2:
                piece = piece * angles[0] + turned(piece, low) * angles[1]
            held[k, :, 128 * p : 128 * p + 128] = piece.astype(BF)
        yield
    for p in range(width // 128):
        at = slice(128 * p, 128 * p + 128)
        query, keys, values = (held[0, :, at], held[1, :, at], held[2, :, at])
        parts = []
        for side in range(2):
            own = jnp.where(left == (side == 0), query, jnp.zeros_like(query))
            scores = times_turned(own, keys) * HD ** (-0.5)
            scores = jnp.where(allowed[...] > 0, scores, NEGATIVE_FILL)
            power = jnp.exp(scores - jnp.max(scores, axis=1, keepdims=True))
            power = power / jnp.sum(power, axis=1, keepdims=True)
            probs[2 * p + side] = power
            parts.append(matmul(power.astype(BF), values))
        held[3, :, at] = jnp.where(left, parts[0], parts[1]).astype(BF)
        yield
    out[...] = start[...] + matmul(held[3], mix())
    yield


def attention_back_steps(start, gain, angles, weights, mix, held, probs, grad_mid, put, out, gains):
    length, width = start.shape
    low, left = (low_quarters(length), left_half(length))
    back = grad_mid[...].astype(BF)
    put(3, turned_times(held[3], back))
    grad_out = times_turned(back, mix()).astype(BF)
    yield
    grads = [[], [], []]
    for p in range(width // 128):
        at = slice(128 * p, 128 * p + 128)
        query, keys, values, grad = (held[0, :, at], held[1, :, at], held[2, :, at], grad_out[:, at])
        parts = []
        for side in range(2):
            own = jnp.where(left == (side == 0), grad, jnp.zeros_like(grad))
            grad_probs = times_turned(own, values)
            power = probs[2 * p + side]
            inner = jnp.sum(power * grad_probs, axis=1, keepdims=True)
            score = (power * (grad_probs - inner)).astype(BF)
            parts.append(
                (
                    matmul(score, keys) * HD ** (-0.5),
                    turned_times(score, query) * HD ** (-0.5),
                    turned_times(power.astype(BF), grad),
                )
            )
        for k in range(3):
            value = jnp.where(left, parts[0][k], parts[1][k]).astype(BF)
            if k < 2:
                value = value.astype(F32)
                value = (value * angles[0] - turned(value * angles[1], low)).astype(BF)
            grads[k].append(value)
        yield
    gain_row = gain[0:1]
    normed_gain, normed, inverse = norm_forward(start[...], gain_row)
    normed_gain = normed_gain.astype(BF)
    total = jnp.zeros((length, width), F32)
    for k in range(3):
        grad = jnp.concatenate(grads[k], axis=1)
        put(k, turned_times(normed_gain, grad))
        total = total + times_turned(grad, weights(k))
        yield
    grad, gain_grad = norm_backward(total, normed, inverse, gain_row)
    gains[0:1] = gain_grad.reshape(1, width)
    out[...] = grad_mid[...] + grad
    yield


def local_call(kernel, outs, args, scratch, name, flops, spaces=None):
    spaces = [VMEM] * len(args) if spaces is None else spaces
    return pl.pallas_call(
        kernel,
        out_shape=outs,
        in_specs=spaces,
        out_specs=[VMEM] * len(outs),
        scratch_shapes=scratch,
        compiler_params=pltpu.CompilerParams(vmem_limit_bytes=60 * 2**20),
        cost_estimate=pl.CostEstimate(flops=flops, bytes_accessed=2**24, transcendentals=0),
        name=name,
    )(*args)


def attention_forward(start, gain, angles, allowed, qkv_w, mix_w):
    length, width = start.shape

    def kernel(start, gain, angles, allowed, qkv, mix, held, probs, out):
        def weights(k):
            return qkv[:, width * k : width * (k + 1)]

        drain(attention_steps(start, gain, angles, allowed, weights, lambda: mix[...], held, probs, out))

    outs = [
        shape((4, length, width), BF),
        shape((width // HD, length, length), F32),
        shape((length, width), F32),
    ]
    args = (start, gain, angles, allowed, qkv_w, mix_w)
    return local_call(kernel, outs, args, [], "attention_forward", 2**31)


def feed_back_steps(grad_top, final, middle, both, gain, expand, shrink, grad_expand, grad_shrink, out, gains):
    length, width = middle.shape
    inner = shrink.shape[0]
    _, normed, inverse = norm_forward(final[...], gain[2:3])
    grad_final, gain_top = norm_backward(grad_top[...], normed, inverse, gain[2:3])
    back = grad_final.astype(BF)
    low, normed, inverse = norm_forward(middle[...], gain[1:2])
    low = low.astype(BF)
    total = jnp.zeros((length, width), F32)
    for k in range(inner // PIECE):
        at = slice(PIECE * k, PIECE * (k + 1))
        up_at = slice(inner + PIECE * k, inner + PIECE * (k + 1))
        gate, up = (both[:, at], both[:, up_at])
        sigma = jax.nn.sigmoid(gate)
        hidden = (gate * sigma * up).astype(BF)
        grad_shrink[at] = turned_times(hidden, back).astype(BF)
        grad = times_turned(back, shrink[at])
        grad_gate = (grad * up * sigma * (1.0 + gate * (1.0 - sigma))).astype(BF)
        grad_up = (grad * gate * sigma).astype(BF)
        grad_expand[:, at] = turned_times(low, grad_gate).astype(BF)
        grad_expand[:, up_at] = turned_times(low, grad_up).astype(BF)
        total = total + times_turned(grad_gate, expand[:, at])
        total = total + times_turned(grad_up, expand[:, up_at])
        yield
    grad_middle, gain_two = norm_backward(total, normed, inverse, gain[1:2])
    out[...] = grad_final + grad_middle
    gains[...] = jnp.zeros_like(gains)
    gains[1:2] = gain_two.reshape(1, width)
    gains[2:3] = gain_top.reshape(1, width)
    yield


def layer_backward(dims, grad_top, final, middle, both, gain, expand_w, shrink_w, start, angles, attention, head, cid):
    nz, ny, nx = dims
    length, width = middle.shape
    deep, columns = head.shape[2:]
    later = len(attention)

    def kernel(*refs):
        grad_top, final, middle, both, gain, expand, shrink, start, angles, head_in, *rest = refs
        sources, rest = (rest[:later], rest[later:])
        expand_out, shrink_out, grad_qkv, grad_mix, start_out, gains, head_out, *rest = rest
        qkv, mix, held, probs, *rest = rest
        grad_expand, grad_shrink, grad_mid, *rest = rest
        near, mids, fars, (ssem, rsem, lsem) = (rest[0:2], rest[2:4], rest[4:6], rest[6:])
        place = Place(dims)
        y, x = (place.y, place.x)
        comm = Comm(ssem, rsem, lsem)
        loads = [comm.keep(src, dst) for src, dst in zip(sources, (qkv, mix, held, probs))]
        greet(place, [off for off in line_offsets(dims) if off[1] or off[2]])
        parts = (pl.ds(0, deep // 2), pl.ds(deep // 2, deep // 2))
        by_x = [(t, place.xs(nx - t), place.dev(x=t)) for t in range(1, nx)]
        by_y = [(t, place.ys(ny - t), place.dev(y=t)) for t in range(1, ny)]
        came = [comm.send(head_in.at[:, to, parts[0]], near[0].at[t - 1], dev) for t, to, dev in by_x]
        came += [comm.send(head_in.at[to, :, parts[1]], near[1].at[t - 1], dev) for t, to, dev in by_y]
        drain(
            feed_back_steps(
                grad_top, final, middle, both, gain, expand, shrink, grad_expand, grad_shrink, grad_mid, gains
            )
        )
        comm.keep(grad_expand, expand_out)
        comm.keep(grad_shrink, shrink_out)
        for copy in came:
            copy.wait_recv()
        add_blocks(mids[0], [head_in.at[:, x, parts[0]]] + [near[0].at[t] for t in range(nx - 1)])
        add_blocks(mids[1], [head_in.at[y, :, parts[1]]] + [near[1].at[t] for t in range(ny - 1)])
        came = [comm.send(mids[0].at[to], fars[0].at[t - 1], dev) for t, to, dev in by_y]
        came += [comm.send(mids[1].at[to], fars[1].at[t - 1], dev) for t, to, dev in by_x]
        for copy in loads:
            comm.done(copy)

        def weights(k):
            return qkv[:, width * k : width * (k + 1)]

        def put(k, value):
            if k == 3:
                grad_mix[...] = value.astype(BF)
            else:
                grad_qkv[:, width * k : width * (k + 1)] = value.astype(BF)

        drain(
            attention_back_steps(
                start, gain, angles, weights, lambda: mix[...], held, probs, grad_mid, put, start_out, gains
            )
        )
        for copy in came:
            copy.wait_recv()
        for part, mid, far in ((parts[0], mids[0].at[y], fars[0]), (parts[1], mids[1].at[x], fars[1])):
            add_blocks(head_out.at[part], [mid] + [far.at[t] for t in range(far.shape[0])])
        comm.finish()

    count = 2 * (ny + nx)
    half = (deep // 2, columns)
    outs = [
        shape(expand_w.shape, BF),
        shape(shrink_w.shape, BF),
        shape(attention[0].shape, BF),
        shape(attention[1].shape, BF),
        shape((length, width), F32),
        shape((8, width), F32),
        shape(head.shape[2:], F32),
    ]
    scratch = [pltpu.VMEM(v.shape, v.dtype) for v in attention]
    scratch += [pltpu.VMEM(expand_w.shape, BF), pltpu.VMEM(shrink_w.shape, BF)]
    scratch += [
        pltpu.VMEM((length, width), F32),
        pltpu.VMEM((nx - 1, ny) + half, BF),
        pltpu.VMEM((ny - 1, nx) + half, BF),
        pltpu.VMEM((ny,) + half, BF),
        pltpu.VMEM((nx,) + half, BF),
        pltpu.VMEM((ny - 1,) + half, BF),
        pltpu.VMEM((nx - 1,) + half, BF),
        sems(count),
        sems(count),
        sems(later + 2),
    ]
    args = (grad_top, final, middle, both, gain, expand_w, shrink_w, start, angles, head, *attention)
    return call(
        kernel, outs, [VMEM] * 10 + [ANY] * later, [ANY] * 2 + [VMEM] * 5, scratch,
        cid, "layer_backward", args, 60 * 2**20,
    )


def rope_tables(length, width):
    quarter = width // 4
    places = np.arange(length)
    freq = np.float32(10000.0) ** (-np.arange(quarter, dtype=np.float32) / np.float32(quarter))
    row_angle = (places // GRID).astype(np.float32)[:, None] * freq
    col_angle = (places % GRID).astype(np.float32)[:, None] * freq
    angles = np.concatenate([row_angle, row_angle, col_angle, col_angle] * (128 // width), axis=-1)
    return jnp.asarray(np.stack([np.cos(angles), np.sin(angles)]).astype(np.float32))


def adam_update(master, drift, square, grad, rate, decay):
    moment = BETA_ONE * drift + (1.0 - BETA_ONE) * grad
    second = BETA_TWO * square + (1.0 - BETA_TWO) * grad * grad
    stride = (
        moment / (1.0 - BETA_ONE**STEP) / (jnp.sqrt(second / (1.0 - BETA_TWO**STEP)) + ADAM_EPS)
    )
    return (master - rate * (stride + decay * master), moment, second)


def adam_all(masters, drifts, squares, grads, sums, rates, decays):
    n = len(masters)
    pieces = []
    for i, master in enumerate(masters):
        rows = master.shape[0]
        cut = rows // 4 if rows % 32 == 0 and rows >= 256 else rows
        pieces += [(i, k, min(cut, rows)) for k in range(0, rows, cut)]

    def kernel(*refs):
        ins = [refs[n * k : n * (k + 1)] for k in range(4)]
        sums_in = refs[4 * n]
        outs = [refs[4 * n + 1 + n * k : 4 * n + 1 + n * (k + 1)] for k in range(3)]
        sums_out = refs[7 * n + 1]
        rest = refs[7 * n + 2 :]
        held = [rest[n * k : n * (k + 1)] for k in range(4)]
        in_sems, out_sems = rest[4 * n :]
        loads, stores = ([], [])
        for p, (i, at, size) in enumerate(pieces):
            span = pl.ds(at, size)
            loads.append(
                [
                    pltpu.make_async_copy(ins[k][i].at[span], held[k][i].at[span], in_sems.at[p, k])
                    for k in range(4)
                ]
            )
            for copy in loads[-1]:
                copy.start()
        row = sums_in[0:1]
        norm = jnp.sqrt(row[:, 0:1]) / row[:, 2:3]
        factor = CLIP_NORM / jnp.maximum(norm, CLIP_NORM) / row[:, 2:3]
        lane = lax.broadcasted_iota(jnp.int32, (8, 128), 1)
        sums_out[...] = jnp.where(lane == 0, norm, sums_in[...])

        def update(i, span):
            fresh, moment, second = adam_update(
                held[0][i][span],
                held[1][i][span],
                held[2][i][span],
                held[3][i][span] * factor,
                rates[i],
                decays[i],
            )
            held[0][i][span], held[1][i][span], held[2][i][span] = (fresh, moment, second)

        for p, (i, at, size) in enumerate(pieces):
            for copy in loads[p]:
                copy.wait()
            if size % 8:
                update(i, slice(at, at + size))
            else:

                @pl.loop(0, size // 8)
                def _(k, i=i, at=at):
                    update(i, pl.ds(pl.multiple_of(at + 8 * k, 8), 8))

            span = pl.ds(at, size)
            for k in range(3):
                copy = pltpu.make_async_copy(held[k][i].at[span], outs[k][i].at[span], out_sems.at[p, k])
                copy.start()
                stores.append(copy)
        for copy in stores:
            copy.wait()

    return pl.pallas_call(
        kernel,
        out_shape=[shape(v.shape, F32) for v in masters] * 3 + [shape((8, 128), F32)],
        in_specs=[ANY] * (4 * n) + [VMEM],
        out_specs=[ANY] * (3 * n) + [VMEM],
        scratch_shapes=[pltpu.VMEM(v.shape, F32) for v in masters] * 4
        + [pltpu.SemaphoreType.DMA((len(pieces), 4)), pltpu.SemaphoreType.DMA((len(pieces), 3))],
        compiler_params=pltpu.CompilerParams(vmem_limit_bytes=62 * 2**20),
        name="adam_all",
    )(*masters, *drifts, *squares, *grads, sums)


def block_form(rows, columns):
    return (rows, columns) if rows % 8 == 0 else (rows * columns // 128, 128)


FIRST_AXES = ("x", "x", "y", "x")


def on_device(dims, *args):
    labels, targets, heights, loss_mask = args[:4]
    masters, drifts, squares = (args[4:12], args[12:20], args[20:28])
    class_table, code_table, attend_in, attend_mix, expand_in, shrink_out, head_weight, norm_gains = masters
    images, local_len = targets.shape
    length = local_len * 2

    layers = (attend_in, attend_mix, expand_in, shrink_out)
    *weights, start, gain, metas, allowed = gather_all(
        dims, layers, FIRST_AXES, code_table, class_table.T, norm_gains, labels, targets, heights, loss_mask, 0
    )
    qkv_w, mix_w, expand_w, shrink_w = (v.reshape(-1, v.shape[-1]) for v in weights)

    angles = rope_tables(length, HD)
    held, probs, middle = attention_forward(start, gain, angles, allowed, qkv_w, mix_w)
    grad_top, grad_head, partial, both, final = head_all(
        dims, middle, gain, metas, head_weight, expand_w, shrink_w, images, 2
    )
    grad_expand, grad_shrink, grad_qkv, grad_mix, grad_start, gain_grads, grad_head = layer_backward(
        dims, grad_top, final, middle, both, gain, expand_w, shrink_w, start, angles,
        (qkv_w, mix_w, held, probs), grad_head, 3,
    )

    grads_in = []
    for grad, shard in zip((grad_qkv, grad_mix, grad_expand, grad_shrink), layers):
        grads_in.append(grad.reshape(dims + (2,) + block_form(*shard.shape)))
    *layer_shares, code_share, class_share, gain_share, sums = scatter_all(
        dims,
        grads_in,
        FIRST_AXES,
        grad_start,
        gain_grads,
        metas,
        grad_head,
        partial,
        code_table.shape[0],
        class_table.shape[0],
        4,
    )
    layer_shares = [g.reshape(v.shape) for g, v in zip(layer_shares, layers)]
    class_share = class_share[: class_table.shape[1], : class_table.shape[0]]
    gain_share = gain_share[1:4, : norm_gains.shape[1]]
    shares = (class_share, code_share, *layer_shares, grad_head, gain_share)

    def laid(members):
        return (members[0].T, *members[1:])

    *updated, sums = adam_all(
        laid(masters), laid(drifts), laid(squares), shares, sums, RATES, DECAYS
    )
    updated = tuple(member for k in range(3) for member in laid(updated[8 * k : 8 * k + 8]))
    return updated + (sums[0, 0], sums[0, 1], sums[0, 2])


def solution(mesh):
    rows, columns = (P(("dp", "seq"), None), P(None, ("dp", "seq")))
    eight = (columns, rows, rows, rows, rows, rows, columns, columns)
    return jax.shard_map(
        functools.partial(on_device, dims_of(mesh.shape["dp"])),
        mesh=mesh,
        in_specs=(P("dp"), P("dp", "seq"), P("dp"), P("dp", "seq")) + eight * 3,
        out_specs=eight * 3 + (P(), P(), P()),
        check_vma=False,
    )
```

```python
import functools

import jax
import jax.numpy as jnp
import numpy as np
from jax import lax
from jax.experimental import pallas as pl
from jax.experimental.pallas import tpu as pltpu
from jax.sharding import PartitionSpec as P

HD = 64
GRID = 16
STEP = 10

EPS_NORM = 1e-05
BETA_ONE = 0.9
BETA_TWO = 0.95
ADAM_EPS = 1e-08
CLIP_NORM = 0.01
NEGATIVE_FILL = -1000000000.0
RATES = (0.8, 0.8, 0.08, 0.08, 0.08, 0.08, 0.08, 0.8)
DECAYS = (0.1, 0.1, 0.1, 0.1, 0.1, 0.1, 0.1, 0.0)

PIECE = 512

MESH = pl.DeviceIdType.MESH
ANY = pl.BlockSpec(memory_space=pl.ANY)
VMEM = pl.BlockSpec(memory_space=pltpu.VMEM)
SMEM = pl.BlockSpec(memory_space=pltpu.SMEM)
BF = jnp.bfloat16
F32 = jnp.float32


def dims_of(dp):
    bits = dp.bit_length() - 1
    nz = 1 << (bits // 2)
    rest = dp // nz
    ny = 1 << ((rest.bit_length() - 1) // 2)
    return (nz, ny, rest // ny)


class Place:
    def __init__(self, dims):
        self.dims = dims
        nz, ny, nx = dims
        chip = lax.axis_index("dp")
        self.c = lax.axis_index("seq")
        self.z = chip // (ny * nx)
        self.y = (chip // nx) % ny
        self.x = chip % nx

    def zs(self, back):
        return (self.z + self.dims[0] - back) % self.dims[0]

    def ys(self, back):
        return (self.y + self.dims[1] - back) % self.dims[1]

    def xs(self, back):
        return (self.x + self.dims[2] - back) % self.dims[2]

    def dev(self, z=0, y=0, x=0, c=0):
        nz, ny, nx = self.dims
        z, y, x = ((self.z + z) % nz, (self.y + y) % ny, (self.x + x) % nx)
        return ((z * ny + y) * nx + x, (self.c + c) % 2)


def line_offsets(dims):
    nz, ny, nx = dims
    return (
        [(s, 0, 0, 0) for s in range(1, nz)]
        + [(0, s, 0, 0) for s in range(1, ny)]
        + [(0, 0, s, 0) for s in range(1, nx)]
        + [(0, 0, 0, 1)]
    )


def plane_offsets(dims):
    return [(0, v, u, 0) for v in range(dims[1]) for u in range(dims[2]) if v or u]


def greet(place, offsets):
    offsets = sorted(set(offsets))
    sem = pltpu.get_barrier_semaphore()
    for off in offsets:
        pl.semaphore_signal(sem, inc=1, device_id=place.dev(*off), device_id_type=MESH)
    pl.semaphore_wait(sem, len(offsets))


class Comm:
    def __init__(self, send_sems, recv_sems, local_sems):
        self.send_sems, self.recv_sems, self.local_sems = (send_sems, recv_sems, local_sems)
        self.sent, self.held, self.count, self.locals = ([], [], 0, 0)

    def send(self, src, dst, device):
        k = self.count
        self.count += 1
        copy = pltpu.make_async_remote_copy(
            src_ref=src,
            dst_ref=dst,
            send_sem=self.send_sems.at[k],
            recv_sem=self.recv_sems.at[k],
            device_id=device,
            device_id_type=MESH,
        )
        copy.start()
        self.sent.append(copy)
        return copy

    def keep(self, src, dst):
        copy = pltpu.make_async_copy(src, dst, self.local_sems.at[self.locals])
        self.locals += 1
        copy.start()
        self.held.append(copy)
        return copy

    def gone(self, copy):
        copy.wait_send()
        self.sent = [other for other in self.sent if other is not copy]

    def done(self, copy):
        copy.wait()
        self.held = [other for other in self.held if other is not copy]

    def finish(self):
        for copy in self.sent:
            copy.wait_send()
        for copy in self.held:
            copy.wait()


def drain(steps):
    for _ in steps:
        pass


def all_offsets(dims):
    nz, ny, nx = dims
    spots = [(k, j, i, core) for k in range(nz) for j in range(ny) for i in range(nx) for core in range(2)]
    return spots[1:]


def small_exchange(comm, place, src, out, own):
    z, y, x, c = (place.z, place.y, place.x, place.c)
    nz, ny, nx = place.dims
    if own:
        comm.keep(src(z, y, x, c), out.at[z, y, x, c])
    got = []
    for off in all_offsets(place.dims):
        there = (place.zs(nz - off[0]), place.ys(ny - off[1]), place.xs(nx - off[2]), (c + off[3]) % 2)
        got.append(comm.send(src(*there), out.at[z, y, x, c], place.dev(*off)))
    return got


class PlaneGather:
    def __init__(self, comm, place):
        self.comm, self.place = (comm, place)
        self.firsts, self.seconds, self.mates = ([], [], [])

    def ways(self, axis):
        _, ny, nx = self.place.dims
        return range(1, ny if axis == "y" else nx)

    def back(self, axis, t, yy, xx):
        return (self.place.ys(t), xx) if axis == "y" else (yy, self.place.xs(t))

    def spread(self, block, first, src=None):
        place, second = (self.place, "y" if first == "x" else "x")
        dst = block(place.y, place.x)
        src = dst if src is None else src
        for t in self.ways(first):
            copy = self.comm.send(src, dst, place.dev(**{first: t}))
            self.firsts.append((block, first, second, t, copy))
        for t in self.ways(second):
            copy = self.comm.send(src, dst, place.dev(**{second: t}))
            self.seconds.append((block(*self.back(second, t, place.y, place.x)), copy))
        self.mates.append(self.comm.send(src, dst, place.dev(c=1)))

    def forward(self):
        place = self.place
        for block, first, second, t, copy in self.firsts:
            copy.wait_recv()
            yy, xx = self.back(first, t, place.y, place.x)
            held = block(yy, xx)
            for u in self.ways(second):
                copy = self.comm.send(held, held, place.dev(**{second: u}))
                self.seconds.append((block(*self.back(second, u, yy, xx)), copy))
            self.mates.append(self.comm.send(held, held, place.dev(c=1)))
        self.firsts = []

    def settle(self):
        for held, copy in self.seconds:
            copy.wait_recv()
            self.mates.append(self.comm.send(held, held, self.place.dev(c=1)))
        self.seconds = []

    def forward_some(self, count):
        rest = self.firsts[count:]
        self.firsts = self.firsts[:count]
        self.forward()
        self.firsts = rest

    def arrive(self):
        for copy in self.mates:
            copy.wait_recv()
        self.mates = []


def sems(count):
    return pltpu.SemaphoreType.DMA((count,))


def shape(dims, dtype):
    return jax.ShapeDtypeStruct(tuple(dims), dtype)


def call(kernel, outs, in_specs, out_specs, scratch, cid, name, args, vmem=None):
    return pl.pallas_call(
        kernel,
        out_shape=outs,
        in_specs=in_specs,
        out_specs=out_specs,
        scratch_shapes=scratch,
        compiler_params=pltpu.CompilerParams(
            collective_id=cid, has_side_effects=True, vmem_limit_bytes=vmem
        ),
        name=name,
    )(*args)


def small_sends(dims):
    return dims[0] * dims[1] * dims[2] * 2 - 1


def gather_all(dims, layers, first_axes, table, classes, gains, labels, targets, heights, masks, cid):
    nz, ny, nx = dims
    n = len(layers)
    rows, width = table.shape
    images, local_len = targets.shape
    length = local_len * 2
    columns = gains.shape[1]
    meta = (8, 128)
    count_images = nz * ny * nx * images
    label_rows = -(-count_images // 128)
    groups = [(k,) for k in range(nz)] if nz <= 4 else [tuple(range(nz))]

    def kernel(*refs):
        ins, rest = (refs[:n], refs[n:])
        table_in, class_in, gain_in, labels_in, targets_in, heights_in, masks_in, *rest = rest
        outs, rest = (rest[:n], rest[n:])
        start_out, gain_out, meta_out, allowed_out, *rest = rest
        low, rest = (rest[:n], rest[n:])
        whole, found, total, class_low, gain_row, meta_in, parts_out, small_out, small_in, *rest = rest
        ssem, rsem, lsem = rest
        place = Place(dims)
        z, y, x, c = (place.z, place.y, place.x, place.c)
        chip = (z * ny + y) * nx + x
        meta_in[...] = jnp.zeros_like(meta_in)
        meta_in[0:images] = targets_in[...]
        meta_in[images : 2 * images] = masks_in[...]
        lane = lax.broadcasted_iota(jnp.int32, (1, 128), 1)
        for i in range(images):
            meta_in[4:5] += jnp.where(lane == i, labels_in[i], 0)
            meta_in[4:5] += jnp.where(lane == images + i, heights_in[i], 0)
            for r in range(label_rows):
                meta_in[5 + r : 6 + r] += jnp.where(lane == chip * images + i - 128 * r, labels_in[i], 0)
        greet(place, all_offsets(dims))
        comm = Comm(ssem, rsem, lsem)
        metas = small_exchange(comm, place, lambda *spot: meta_in, meta_out, False)
        meta_out[z, y, x, c] = meta_in[...]
        waits = []
        whole[y, x, c] = table_in[...].astype(BF)
        tables, blocks = (PlaneGather(comm, place), PlaneGather(comm, place))
        for first, start in (("x", 0), ("y", rows // 2)):
            half = pl.ds(start, rows // 2)
            tables.spread(lambda yy, xx, half=half: whole.at[yy, xx, c, half], first)
        for a in range(n):
            low[a][...] = ins[a][...].astype(BF)
        along = {}
        for s in range(1, nz):
            for a in range(n):
                along[s, a] = comm.send(low[a], outs[a].at[z, y, x, c], place.dev(z=s))
        kept = [comm.keep(low[a], outs[a].at[z, y, x, c]) for a in range(n)]

        def spread(group):
            for a in range(n):
                for k in group:
                    if k:
                        along[k, a].wait_recv()
                if len(group) > 1:
                    comm.done(kept[a])
                    at = pl.ds(0, nz)
                else:
                    at = place.zs(group[0])
                blocks.spread(
                    lambda yy, xx, a=a, at=at: outs[a].at[at, yy, xx, c],
                    first_axes[a],
                    low[a] if group == (0,) else None,
                )

        for copy in metas:
            copy.wait_recv()

        class_low[...] = jnp.zeros_like(class_low)
        class_low[0:columns, 0 : class_in.shape[1]] = class_in[...]
        small_in[...] = jnp.zeros_like(small_in)
        for r in range(label_rows):
            labels = jnp.zeros((1, 128), jnp.int32)
            for k in range(nz * ny * nx):
                labels = labels + meta_out[k // (ny * nx), k // nx % ny, k % nx, 0, 5 + r : 6 + r, :]
            pick = lax.broadcasted_iota(jnp.int32, (class_low.shape[1], 128), 0) == labels
            picked = lax.dot_general(
                jnp.where(pick, 1.0, 0.0).astype(BF),
                class_low[...].astype(BF),
                (((0,), (1,)), ((), ())),
                preferred_element_type=F32,
            )
            for i in range(min(128, count_images - 128 * r)):
                k, core = divmod(128 * r + i, 2)
                small_in[k // (ny * nx), k // nx % ny, k % nx, core, 0:1, 0 : class_low.shape[0]] = picked[
                    i : i + 1
                ]
        gain_row[...] = jnp.zeros_like(gain_row)
        gain_row[0:3, 0:columns] = gain_in[...].astype(BF).astype(F32)

        @pl.loop(0, nz)
        def _(k):
            for j in range(ny):
                for i in range(nx):
                    for core in range(2):
                        small_in[k, j, i, core, 1:4, :] = gain_row[0:3]

        smalls = small_exchange(comm, place, lambda *spot: small_in.at[spot], small_out, False)
        small_out[z, y, x, c] = small_in[z, y, x, c]

        size = len(layers)
        steps = [lambda group=group: spread(group) for group in groups]
        steps.pop(0)()
        tables.forward()
        if steps:
            steps.pop(0)()
        blocks.forward_some(size)
        if steps:
            steps.pop(0)()
        tables.settle()
        blocks.forward_some(size)
        for step in steps:
            step()
        tables.arrive()

        for s in range(1, nz + 1):
            zz = place.zs(s % nz)
            halves = []
            for half in range(2):
                codes = meta_out[zz, y, x, half, pl.ds(c, 1), :].astype(F32)
                halves.append(jnp.broadcast_to(codes, (128, local_len)).T)
            column = jnp.concatenate(halves, axis=0)
            column = column - (z * ny * nx * 2 * rows).astype(F32)
            total[...] = jnp.zeros_like(total)

            @pl.loop(0, ny * nx * 2)
            def _(j):
                base = (j * rows).astype(F32)
                lane = lax.broadcasted_iota(jnp.int32, (length, 128), 1).astype(F32) + base
                picks = [
                    jnp.where(column == lane + float(128 * q), 1.0, 0.0).astype(BF)
                    for q in range(-(-rows // 128))
                ]
                pick = jnp.concatenate(picks, axis=1)[:, :rows]
                total[...] += matmul(pick, whole[j // (2 * nx), j // 2 % nx, j % 2])

            found[s % nz] = total[...].astype(BF)
            if s < nz:
                waits.append(comm.send(found.at[s], parts_out.at[nz - s - 1], place.dev(z=nz - s)))
            blocks.forward_some(size)
        blocks.forward()
        height = jnp.where(c == 0, heights_in[0], heights_in[images - 1])
        query = lax.broadcasted_iota(jnp.int32, (length, length), 0)
        key = lax.broadcasted_iota(jnp.int32, (length, length), 1)
        allowed_out[...] = jnp.where((key <= query) & (key < GRID * height), 1.0, 0.0)
        for copy in smalls:
            copy.wait_recv()
        joined = jnp.zeros((8, width), F32)
        blank = jnp.zeros((8, width - 128), F32)
        for d in range(2 * nz * ny * nx):
            k, core = divmod(d, 2)
            piece = small_out[k // (ny * nx), k // nx % ny, k % nx, core]
            joined = joined + pltpu.roll(jnp.concatenate([piece, blank], axis=1), columns * d, 1)
        gain_out[...] = jnp.concatenate([joined[1:4], jnp.zeros((5, width), F32)], axis=0)
        blocks.settle()
        for copy in waits:
            copy.wait_recv()
        added = found[0].astype(F32)
        for s in range(1, nz):
            added = added + parts_out[s - 1].astype(F32)
        first = lax.broadcasted_iota(jnp.int32, (length, 128), 0) == 0
        for k in range(width // 128):
            at = slice(128 * k, 128 * k + 128)
            start_out[:, at] = jnp.where(first, joined[0:1, at], pltpu.roll(added[:, at], 1, 0))
        blocks.arrive()
        comm.finish()

    count = n * (nz - 1) + (n * len(groups) + 2) * (2 * ny * nx - 1) + nz + 2 * small_sends(dims)
    small = dims + (2, 8, 128)
    outs = [shape(dims + (2,) + v.shape, BF) for v in layers]
    outs += [
        shape((length, width), F32),
        shape((8, width), F32),
        shape(dims + (2,) + meta, jnp.int32),
        shape((length, length), F32),
    ]
    scratch = [pltpu.VMEM(v.shape, BF) for v in layers]
    scratch += [
        pltpu.VMEM((ny, nx, 2) + table.shape, BF),
        pltpu.VMEM((nz, length, width), BF),
        pltpu.VMEM((length, width), F32),
        pltpu.VMEM((-(-columns // 16) * 16, -(-classes.shape[1] // 128) * 128), F32),
        pltpu.VMEM((8, 128), F32),
        pltpu.VMEM(meta, jnp.int32),
        pltpu.VMEM((nz - 1, length, width), BF),
        pltpu.VMEM(small, F32),
        pltpu.VMEM(small, F32),
        sems(count),
        sems(count),
        sems(n),
    ]
    return call(
        kernel, outs, [VMEM] * (n + 3) + [SMEM, VMEM, SMEM, VMEM], [ANY] * n + [VMEM] * 4, scratch,
        cid, "gather_all", (*layers, table, classes, gains, labels, targets, heights, masks), 60 * 2**20,
    )


def add_blocks(out, terms):
    lead = out.shape[:-2]

    def visit(index):
        if len(index) < len(lead):

            @pl.loop(0, lead[len(index)])
            def _(i):
                visit(index + (i,))

        else:
            if len(terms) == 2 and out.dtype == BF:
                out[index] = terms[0][index] + terms[1][index]
                return
            total = terms[0][index].astype(F32)
            for term in terms[1:]:
                total = total + term[index].astype(F32)
            out[index] = total.astype(out.dtype)

    visit(())


def items_of(shapes, axes):
    if shapes[0][0] % 8:
        return [[(a, slice(0, shapes[a][0]), slice(0, shapes[a][1]), axes[a]) for a in pair] for pair in ((2, 3), (0, 1))]
    (rows, qkv), (_, mix), (_, both), (deep, width) = shapes
    every, piece = (slice(0, rows), both // 4)
    return [
        [(3, slice(0, deep // 2), slice(0, width), "x"), (3, slice(deep // 2, deep), slice(0, width), "y")],
        [(2, every, slice(0, piece), "x"), (2, every, slice(2 * piece, 3 * piece), "y")],
        [(0, every, slice(0, 2 * mix), "x"), (0, every, slice(2 * mix, qkv), "y"), (1, every, slice(0, mix), "y")],
        [(2, every, slice(piece, 2 * piece), "x"), (2, every, slice(3 * piece, both), "y")],
    ]


def scatter_all(dims, grads, axes, rows, gains, metas, head, partial, device_codes, classes, cid):
    nz, ny, nx = dims
    plane = ny * nx
    n = len(grads)
    shapes = [g.shape[4:] for g in grads]
    steps = items_of(shapes, axes)
    items = [item for step in steps for item in step]
    order, at = ([], 0)
    for step in steps:
        order.append(list(range(at, at + len(step))))
        at += len(step)
    length, width = rows.shape
    block = (device_codes, width)
    sizes = {"x": nx, "y": ny}
    columns = width // (2 * nz * plane)
    label_rows = -(-2 * nz * plane // 128)

    def kernel(*refs):
        parts, rest = (refs[:n], list(refs[n:]))
        rows_in, gains_in, meta_in, head_in, partial_in = (rest.pop(0) for _ in range(5))
        outs = [rest.pop(0) for _ in range(n)]
        table_out, class_out, gain_out, sums = (rest.pop(0) for _ in range(4))
        owns, halves, ones, twos, threes = ([rest.pop(0) for _ in items] for _ in range(5))
        near, far = ([rest.pop(0), rest.pop(0)] for _ in range(2))
        lined, given, own, half, small_in, small_out, tops, gained_all, mine, every, *rest = rest
        ssem, rsem, lsem = rest
        place = Place(dims)
        z, y, x, c = (place.z, place.y, place.x, place.c)
        comm = Comm(ssem, rsem, lsem)
        kept = []
        for i, (a, span, cols, _) in enumerate(items):
            kept.append(comm.keep(parts[a].at[:, :, :, c, span, cols], owns[i]))
        lane = lax.broadcasted_iota(jnp.int32, (8, 128), 1)
        top = jnp.concatenate([rows_in[0:1], gains_in[0:3], jnp.zeros((4, width), F32)], axis=0)
        for d in range(2 * nz * plane):
            k, core = divmod(d, 2)
            piece = pltpu.roll(top, (width - columns * d) % width, 1)[:, :128]
            small_in[k // plane, k // nx % ny, k % nx, core] = jnp.where(lane < columns, piece, 0.0)
        greet(place, all_offsets(dims))
        waits = small_exchange(comm, place, lambda *spot: small_in.at[spot], small_out, False)
        small_out[z, y, x, c] = small_in[z, y, x, c]
        pair, got_one, got_two, third = ({}, {}, {}, {})

        def set_out(g):
            for i in order[g] if g < len(order) else []:
                a, span, cols, _ = items[i]
                pair[i] = comm.send(parts[a].at[:, :, :, 1 - c, span, cols], halves[i], place.dev(c=1))

        def back(axis, t):
            return place.ys(ny - t) if axis == "y" else place.xs(nx - t)

        def first_add(g):
            for i in order[g]:
                pair[i].wait_recv()
                comm.done(kept[i])
                add_blocks(halves[i], [halves[i], owns[i]])

        def first_send(g):
            for i in order[g]:
                axis = items[i][3]
                got_one[i] = [
                    comm.send(
                        halves[i].at[:, back(axis, t)] if axis == "y" else halves[i].at[:, :, back(axis, t)],
                        ones[i].at[t - 1],
                        place.dev(**{axis: t}),
                    )
                    for t in range(1, sizes[axis])
                ]

        def second_step(g):
            for i in order[g]:
                axis = items[i][3]
                other = "x" if axis == "y" else "y"
                for copy in got_one[i]:
                    copy.wait_recv()
                held = halves[i].at[:, y] if axis == "y" else halves[i].at[:, :, x]
                add_blocks(held, [held] + [ones[i].at[t] for t in range(ones[i].shape[0])])
                got_two[i] = [
                    comm.send(
                        halves[i].at[:, y, back("x", t)] if other == "x" else halves[i].at[:, back("y", t), x],
                        twos[i].at[t - 1],
                        place.dev(**{other: t}),
                    )
                    for t in range(1, sizes[other])
                ]

        def third_step(g):
            for i in order[g]:
                for copy in got_two[i]:
                    copy.wait_recv()
                held = halves[i].at[:, y, x]
                add_blocks(held, [held] + [twos[i].at[t] for t in range(twos[i].shape[0])])
                third[i] = [
                    comm.send(halves[i].at[place.zs(nz - s), y, x], threes[i].at[s - 1], place.dev(z=s))
                    for s in range(1, nz)
                ]

        def last_step(g):
            for i in order[g]:
                a, span, cols, _ = items[i]
                for copy in third[i]:
                    copy.wait_recv()
                terms = [halves[i].at[z, y, x]] + [threes[i].at[s] for s in range(nz - 1)]
                add_blocks(outs[a].at[span, cols], terms)

        flat = []
        first = lax.broadcasted_iota(jnp.int32, (1, length), 1) == 0
        for s in range(nz):
            codes = [meta_in[place.zs(s), y, x, part, pl.ds(c, 1), :] for part in range(2)]
            codes = pltpu.roll(jnp.concatenate(codes, axis=1) - z * (2 * plane * device_codes), 1, 1)
            flat.append(jnp.where(first, -1, codes))
        flat = jnp.concatenate(flat, axis=1)

        def product(into, core):
            @pl.loop(0, plane)
            def _(j):
                code = lax.broadcasted_iota(jnp.int32, (device_codes, nz * length), 0)
                pick = code + (j * 2 + core) * device_codes == flat
                pick = jnp.where(pick, 1.0, 0.0).astype(BF)
                value = matmul(pick, lined[...].reshape(nz * length, width))
                into[j // nx, j % nx] = value.astype(BF)

        set_out(0)
        set_out(1)
        lined[0] = rows_in[...].astype(BF)
        lines = [comm.send(lined.at[0], lined.at[s], place.dev(z=s)) for s in range(1, nz)]
        count = len(order)
        for g in range(count):
            first_add(g)
            set_out(g + 2)
            if g >= 2:
                second_step(g - 2)
            first_send(g)
            if g >= 3:
                third_step(g - 3)
        for copy in lines:
            copy.wait_recv()
        product(given, 1 - c)
        table_pair = comm.send(given, half, place.dev(c=1))
        second_step(count - 2)
        product(own, c)
        if count > 2:
            third_step(count - 3)
        second_step(count - 1)
        table_pair.wait_recv()
        add_blocks(half, [half, own])
        parts_of = [pl.ds(0, device_codes // 2), pl.ds(device_codes // 2, device_codes // 2)]
        came = [
            [
                comm.send(half.at[:, back("x", t), parts_of[0]], near[0].at[t - 1], place.dev(x=t))
                for t in range(1, nx)
            ],
            [
                comm.send(half.at[back("y", t), :, parts_of[1]], near[1].at[t - 1], place.dev(y=t))
                for t in range(1, ny)
            ],
        ]
        third_step(count - 2)
        third_step(count - 1)

        for copy in waits:
            copy.wait_recv()
        gained_all[...] = jnp.zeros_like(gained_all)
        tops[...] = jnp.zeros_like(tops)

        @pl.loop(0, nz)
        def _(k):
            for j in range(ny):
                for i in range(nx):
                    for core in range(2):
                        at = ((k * ny + j) * nx + i) * 2 + core
                        tops[pl.ds(at, 1), :] = small_out[k, j, i, core, 0:1, :]
                        gained_all[...] += small_out[k, j, i, core]

        high = -(-classes // 128) * 128
        value = jnp.zeros((128, high), F32)
        for r in range(label_rows):
            labels = jnp.zeros((1, 128), jnp.int32)
            for k in range(nz * plane):
                labels = labels + meta_in[k // plane, k // nx % ny, k % nx, 0, 5 + r : 6 + r, :]
            at = lax.broadcasted_iota(jnp.int32, (high, 128), 1) + 128 * r
            pick = lax.broadcasted_iota(jnp.int32, (high, 128), 0) == labels
            pick = jnp.where(pick & (at < 2 * nz * plane), 1.0, 0.0)
            value = value + lax.dot_general(
                tops[128 * r : 128 * r + 128],
                pick,
                (((0,), (1,)), ((), ())),
                precision=lax.Precision.HIGHEST,
                preferred_element_type=F32,
            )
        class_out[...] = value[:columns, :classes]
        gain_out[...] = gained_all[1:4, :columns]
        row = lax.broadcasted_iota(jnp.int32, gained_all.shape, 0)
        gained = jnp.where((row >= 1) & (row < 4), gained_all[...], 0.0)
        square = jnp.sum(value * value) + jnp.sum(gained * gained)
        share = head_in[...].astype(F32)
        square = square + jnp.sum(share * share)
        for g in range(count - 1):
            last_step(g)

        for copy in came[0] + came[1]:
            copy.wait_recv()
        for h, held in ((0, half.at[:, x, parts_of[0]]), (1, half.at[y, :, parts_of[1]])):
            add_blocks(held, [held] + [near[h].at[t] for t in range(near[h].shape[0])])
        came = [
            comm.send(half.at[back("y", t), x, parts_of[0]], far[0].at[t - 1], place.dev(y=t))
            for t in range(1, ny)
        ]
        came += [
            comm.send(half.at[y, back("x", t), parts_of[1]], far[1].at[t - 1], place.dev(x=t))
            for t in range(1, nx)
        ]
        last_step(count - 1)
        for a in range(n):
            square = square + jnp.sum(outs[a][...] * outs[a][...])
        for copy in came:
            copy.wait_recv()
        for h in range(2):
            terms = [half.at[y, x, parts_of[h]]] + [far[h].at[t] for t in range(far[h].shape[0])]
            add_blocks(table_out.at[parts_of[h]], terms)
        square = square + jnp.sum(table_out[...] * table_out[...])
        first = (lax.broadcasted_iota(jnp.int32, mine.shape, 0) == 0) & (
            lax.broadcasted_iota(jnp.int32, mine.shape, 1) == 0
        )
        mine[...] = partial_in[...] + jnp.where(first, square, 0.0)
        for copy in small_exchange(comm, place, lambda *spot: mine, every, False):
            copy.wait_recv()
        every[z, y, x, c] = mine[...]
        sums[...] = jnp.zeros_like(sums)

        @pl.loop(0, nz)
        def _(k):
            for j in range(ny):
                for i in range(nx):
                    sums[...] += every[k, j, i, 0] + every[k, j, i, 1]

        comm.finish()

    total = len(items) * (ny + nx - 1 + nz - 1) + nz + 2 * (ny + nx) + 2 * small_sends(dims)
    cuts = [(span.stop - span.start, cols.stop - cols.start) for _, span, cols, _ in items]
    near_far = [(ny, nx) if item[3] == "y" else (nx, ny) for item in items]
    part = (device_codes // 2, width)
    scratch = [pltpu.VMEM((nz, ny, nx) + t, BF) for t in cuts] * 2
    scratch += [pltpu.VMEM((u - 1, nz, v) + t, BF) for t, (u, v) in zip(cuts, near_far)]
    scratch += [pltpu.VMEM((v - 1, nz) + t, BF) for t, (u, v) in zip(cuts, near_far)]
    scratch += [pltpu.VMEM((nz - 1,) + t, BF) for t in cuts]
    scratch += [
        pltpu.VMEM((nx - 1, ny) + part, BF),
        pltpu.VMEM((ny - 1, nx) + part, BF),
        pltpu.VMEM((ny - 1,) + part, BF),
        pltpu.VMEM((nx - 1,) + part, BF),
        pltpu.VMEM((nz, length, width), BF),
        pltpu.VMEM((ny, nx) + block, BF),
        pltpu.VMEM((ny, nx) + block, BF),
        pltpu.VMEM((ny, nx) + block, BF),
        pltpu.VMEM(dims + (2, 8, 128), F32),
        pltpu.VMEM(dims + (2, 8, 128), F32),
        pltpu.VMEM((128 * label_rows, 128), F32),
        pltpu.VMEM((8, 128), F32),
        pltpu.VMEM(partial.shape, F32),
        pltpu.VMEM(dims + (2,) + partial.shape, F32),
        sems(total),
        sems(total),
        sems(len(items)),
    ]
    outs = [shape(t, F32) for t in shapes]
    outs += [shape(block, F32), shape((columns, classes), F32), shape((3, columns), F32)]
    outs += [shape(partial.shape, F32)]
    return call(
        kernel, outs, [ANY] * n + [VMEM] * 5, [VMEM] * (n + 4), scratch,
        cid, "scatter_all", (*grads, rows, gains, metas, head, partial), 60 * 2**20,
    )


def head_all(dims, middle, gain, metas, head, expand_w, shrink_w, images, cid):
    nz, ny, nx = dims
    length, width = middle.shape
    inner = shrink_w.shape[0]
    pieces = inner // PIECE
    columns = head.shape[1]
    lanes = min(columns, 128)
    groups = columns // lanes
    plane = ny * nx
    blocks = 2 * plane
    keep = columns >= 128
    shared = columns == PIECE and nz * length >= width and blocks >= 2 * pieces

    def kernel(*refs):
        middle_in, gain_in, meta_in, head_in, expand_in, shrink_in, *rest = refs
        top_out, head_out, loss_out, both_out, final_out, *rest = rest
        whole, marks_in, wide, lined, turned, peaks, totals, picks, exps, grads, *rest = rest
        columned, partial, back, coming, mine, every, given, half, ssem, rsem, lsem = rest
        place = Place(dims)
        z, y, x, c = (place.z, place.y, place.x, place.c)
        greet(place, line_offsets(dims))
        comm = Comm(ssem, rsem, lsem)
        room, loads = ({}, {})

        def load(j):
            room[j] = grads.at[j, pl.ds(0, width)] if shared else wide.at[j // pieces]
            loads[j] = comm.keep(expand_in.at[:, pl.ds(PIECE * j, PIECE)], room[j])

        for j in range(2 * pieces) if shared else []:
            load(j)
        whole[c, y, x] = head_in[...].astype(BF)
        gather = PlaneGather(comm, place)
        for first, start in (("x", 0), ("y", width // 2)):
            part = pl.ds(start, width // 2)
            gather.spread(lambda yy, xx, part=part: whole.at[c, yy, xx, part], first)
        normed = norm_forward(middle_in[...], gain_in[1:2])[0].astype(BF)
        total = middle_in[...]
        for j in range(pieces):
            at = slice(PIECE * j, PIECE * (j + 1))
            for k in (j, pieces + j):
                if not shared:
                    load(k)
                comm.done(loads[k])
            gate, up = (matmul(normed, room[j][...]), matmul(normed, room[pieces + j][...]))
            both_out[:, at] = gate
            both_out[:, inner + PIECE * j : inner + PIECE * (j + 1)] = up
            hidden = (gate * jax.nn.sigmoid(gate) * up).astype(BF)
            total = total + matmul(hidden, shrink_in[at])
        final_out[...] = total
        lined[0] = norm_forward(total, gain_in[2:3])[0].astype(BF)
        turns = sorted(range(1, nz), key=lambda s: min(s, nz - s))
        arriving = {s: comm.send(lined.at[0], lined.at[s], place.dev(z=s)) for s in turns[:2]}
        turned[:, 0:length] = lined[0].T
        for s in range(nz):
            for part in range(2):
                codes = meta_in[place.zs(s), y, x, part, pl.ds(c, 1), :].astype(F32)
                tall = jnp.broadcast_to(codes, (128, 128)).T.astype(jnp.int32)
                marks_in[s, 128 * part : 128 * part + 128] = tall[:, :lanes] - z * (blocks * columns)
        gather.forward()
        for s in turns[:2]:
            comm.gone(arriving[s])
        for s in turns[2:]:
            arriving[s] = comm.send(lined.at[0], lined.at[s], place.dev(z=s))
        gather.settle()
        gather.arrive()

        def block(k):
            return whole[k // plane, k // nx % ny, k % nx]

        def split(value):
            return [value[:, lanes * q : lanes * (q + 1)] for q in range(groups)]

        def hits(s, k):
            base = (k % plane * 2 + k // plane) * columns
            lane = lax.broadcasted_iota(jnp.int32, (length, lanes), 1) + base
            return [lane + lanes * q == marks_in[s] for q in range(groups)]

        def logits_of(s, k):
            return matmul(lined[s], block(k))

        def forward(s):
            at = pl.ds(s * length, length)
            peaks[...] = jnp.full_like(peaks, -jnp.inf)
            totals[...] = jnp.zeros_like(totals)
            picks[...] = jnp.zeros_like(picks)

            @pl.loop(0, blocks // 2)
            def _(pair):
                high, found = (peaks[...], picks[...])
                for k in (2 * pair, 2 * pair + 1):
                    logits = logits_of(s, k)
                    if keep:
                        exps[k, at] = logits
                    for piece, hit in zip(split(logits), hits(s, k)):
                        high = jnp.maximum(high, piece)
                        found = found + jnp.where(hit, piece, 0.0)
                peaks[...] = high
                picks[...] = found

            peak = jnp.max(peaks[...], axis=1, keepdims=True)
            peaks[...] = jnp.broadcast_to(peak, (length, lanes))

            @pl.loop(0, blocks // 2)
            def _(pair):
                total = totals[...]
                for k in (2 * pair, 2 * pair + 1):
                    logits = exps[k, at] if keep else logits_of(s, k)
                    for q, piece in enumerate(split(logits)):
                        power = jnp.exp(piece - peaks[...])
                        if keep:
                            exps[k, at, lanes * q : lanes * (q + 1)] = power
                        total = total + power
                totals[...] = total

            if not keep:
                exps[s] = peaks[...]
            lane = lax.broadcasted_iota(jnp.int32, (length, 128), 1)
            total = jnp.sum(totals[...], axis=1, keepdims=True)
            found = jnp.sum(picks[...], axis=1, keepdims=True)
            table = jnp.where(lane == 0, peak, jnp.where(lane == 1, total, found))
            mine[place.zs(s)] = table.T[:8]

        forward(0)
        for s in turns:
            arriving[s].wait_recv()
            turned[:, s * length : (s + 1) * length] = lined[s].T
            forward(s)
        stats = [comm.send(mine, every.at[s], place.dev(z=s)) for s in range(1, nz)]
        every[0] = mine[...]
        for copy in stats:
            copy.wait_recv()

        def backward(s):
            at = pl.ds(s * length, length)
            held = [every[q, place.zs(s)] for q in range(nz)]
            peak = held[0][0:1]
            for other in held[1:]:
                peak = jnp.maximum(peak, other[0:1])
            total = sum(other[1:2] * jnp.exp(other[0:1] - peak) for other in held)
            zz = place.zs(s)
            mask = [meta_in[zz, y, x, part, pl.ds(images + c, 1), :] for part in range(2)]
            mask = jnp.concatenate(mask, axis=1).astype(F32)
            tail = meta_in[zz, y, x, 0, 4:5, :]
            lane = lax.broadcasted_iota(jnp.int32, (1, 128), 1)
            tall = jnp.sum(jnp.where(lane == images + c, tail, 0).astype(F32), axis=1, keepdims=True)
            place_of = lax.broadcasted_iota(jnp.int32, (1, length), 1).astype(F32)
            weight = jnp.where(place_of < GRID * tall, mask, 0.0)
            if s == 0:
                found = sum(other[2:3] for other in held)
                loss = (peak + jnp.log(total) - found) * weight
                lane = lax.broadcasted_iota(jnp.int32, (8, 128), 1)
                row = lax.broadcasted_iota(jnp.int32, (8, 128), 0)
                sums = jnp.where(lane == 1, jnp.sum(loss, axis=1, keepdims=True), 0.0)
                sums = sums + jnp.where(lane == 2, jnp.sum(weight, axis=1, keepdims=True), 0.0)
                loss_out[...] = jnp.where(row == 0, sums, 0.0)
            scale = weight / total * jnp.exp(held[0][0:1] - peak)
            tall = jnp.concatenate([scale, weight, jnp.zeros((126, length), F32)], axis=0).T
            columned[0] = jnp.broadcast_to(tall[:, 0:1], (length, lanes))
            columned[1] = jnp.broadcast_to(tall[:, 1:2], (length, lanes))
            partial[...] = jnp.zeros_like(partial)

            @pl.loop(0, blocks // 2)
            def _(pair):
                added = partial[...]
                for k in (2 * pair, 2 * pair + 1):
                    if keep:
                        powers = split(exps[k, at])
                    else:
                        powers = [jnp.exp(piece - exps[s]) for piece in split(logits_of(s, k))]
                    parts = []
                    for power, hit in zip(powers, hits(s, k)):
                        grad = power * columned[0] - jnp.where(hit, columned[1], 0.0)
                        parts.append(grad.astype(BF))
                    grad = jnp.concatenate(parts, axis=1) if groups > 1 else parts[0]
                    grads[k, at] = grad
                    added = added + times_turned(grad, block(k))
                partial[...] = added

        coming_in = []
        for s in range(1, nz):
            backward(s)
            back[s - 1] = partial[...].astype(BF)
            coming_in.append(comm.send(back.at[s - 1], coming.at[s - 1], place.dev(z=nz - s)))
        backward(0)

        def weights(into, core):
            @pl.loop(0, plane)
            def _(j):
                into[j // nx, j % nx] = matmul(turned[...], grads[core * plane + j]).astype(BF)

        weights(given, 1 - c)
        pair = comm.send(given, half, place.dev(c=1))
        weights(head_out, c)
        pair.wait_recv()
        add_blocks(head_out, [head_out, half])
        for copy in coming_in:
            copy.wait_recv()
        total = partial[...]
        for s in range(nz - 1):
            total = total + coming[s].astype(F32)
        top_out[...] = total
        comm.finish()

    count = 3 * (nz - 1) + 2 * (2 * plane - 1) + 1
    scratch = [
        pltpu.VMEM((2, ny, nx) + head.shape, BF),
        pltpu.VMEM((nz, length, lanes), jnp.int32),
        pltpu.VMEM((16, 128) if shared else (2, width, PIECE), BF),
        pltpu.VMEM((nz, length, width), BF),
        pltpu.VMEM((width, nz * length), BF),
        pltpu.VMEM((length, lanes), F32),
        pltpu.VMEM((length, lanes), F32),
        pltpu.VMEM((length, lanes), F32),
        pltpu.VMEM((blocks, nz * length, columns) if keep else (nz, length, lanes), F32),
        pltpu.VMEM((blocks, nz * length, columns), BF),
        pltpu.VMEM((2, length, lanes), F32),
        pltpu.VMEM((length, width), F32),
        pltpu.VMEM((nz - 1, length, width), BF),
        pltpu.VMEM((nz - 1, length, width), BF),
        pltpu.VMEM((nz, 8, length), F32),
        pltpu.VMEM((nz, nz, 8, length), F32),
        pltpu.VMEM((ny, nx) + head.shape, BF),
        pltpu.VMEM((ny, nx) + head.shape, BF),
        sems(count),
        sems(count),
        sems(2 * pieces),
    ]
    outs = [
        shape((length, width), F32),
        shape((ny, nx) + head.shape, BF),
        shape((8, 128), F32),
        shape((length, 2 * inner), F32),
        shape((length, width), F32),
    ]
    return call(
        kernel, outs, [VMEM] * 4 + [ANY, VMEM], [VMEM] * 5, scratch,
        cid, "head_all", (middle, gain, metas, head, expand_w, shrink_w), 63 * 2**20,
    )


def matmul(left, right):
    return jnp.dot(left, right, preferred_element_type=F32)


def norm_forward(values, gain):
    inverse = lax.rsqrt(jnp.mean(values * values, axis=-1, keepdims=True) + EPS_NORM)
    normed = values * inverse
    return (normed * gain, normed, inverse)


def norm_backward(grad, normed, inverse, gain):
    scaled = grad * gain
    inner = jnp.mean(scaled * normed, axis=-1, keepdims=True)
    return (inverse * (scaled - normed * inner), jnp.sum(grad * normed, axis=0))


def turned(value, low):
    return jnp.where(low, -pltpu.roll(value, 112, 1), pltpu.roll(value, 16, 1))


def low_quarters(rows):
    return lax.broadcasted_iota(jnp.int32, (rows, 128), 1) % 32 < 16


def left_half(rows):
    return lax.broadcasted_iota(jnp.int32, (rows, 128), 1) < HD


def times_turned(left, right):
    return lax.dot_general(left, right, (((1,), (1,)), ((), ())), preferred_element_type=F32)


def turned_times(left, right):
    return lax.dot_general(left, right, (((0,), (0,)), ((), ())), preferred_element_type=F32)


def attention_steps(start, gain, angles, allowed, weights, mix, held, probs, out):
    length, width = start.shape
    normed = norm_forward(start[...], gain[0:1])[0].astype(BF)
    low, left = (low_quarters(length), left_half(length))
    for k in range(3):
        value = matmul(normed, weights(k))
        for p in range(width // 128):
            piece = value[:, 128 * p : 128 * p + 128]
            if k < 2:
                piece = piece * angles[0] + turned(piece, low) * angles[1]
            held[k, :, 128 * p : 128 * p + 128] = piece.astype(BF)
        yield
    for p in range(width // 128):
        at = slice(128 * p, 128 * p + 128)
        query, keys, values = (held[0, :, at], held[1, :, at], held[2, :, at])
        parts = []
        for side in range(2):
            own = jnp.where(left == (side == 0), query, jnp.zeros_like(query))
            scores = times_turned(own, keys) * HD ** (-0.5)
            scores = jnp.where(allowed[...] > 0, scores, NEGATIVE_FILL)
            power = jnp.exp(scores - jnp.max(scores, axis=1, keepdims=True))
            power = power / jnp.sum(power, axis=1, keepdims=True)
            probs[2 * p + side] = power
            parts.append(matmul(power.astype(BF), values))
        held[3, :, at] = jnp.where(left, parts[0], parts[1]).astype(BF)
        yield
    out[...] = start[...] + matmul(held[3], mix())
    yield


def attention_back_steps(start, gain, angles, weights, mix, held, probs, grad_mid, put, out, gains):
    length, width = start.shape
    low, left = (low_quarters(length), left_half(length))
    back = grad_mid[...].astype(BF)
    put(3, turned_times(held[3], back))
    grad_out = times_turned(back, mix()).astype(BF)
    yield
    grads = [[], [], []]
    for p in range(width // 128):
        at = slice(128 * p, 128 * p + 128)
        query, keys, values, grad = (held[0, :, at], held[1, :, at], held[2, :, at], grad_out[:, at])
        parts = []
        for side in range(2):
            own = jnp.where(left == (side == 0), grad, jnp.zeros_like(grad))
            grad_probs = times_turned(own, values)
            power = probs[2 * p + side]
            inner = jnp.sum(power * grad_probs, axis=1, keepdims=True)
            score = (power * (grad_probs - inner)).astype(BF)
            parts.append(
                (
                    matmul(score, keys) * HD ** (-0.5),
                    turned_times(score, query) * HD ** (-0.5),
                    turned_times(power.astype(BF), grad),
                )
            )
        for k in range(3):
            value = jnp.where(left, parts[0][k], parts[1][k]).astype(BF)
            if k < 2:
                value = value.astype(F32)
                value = (value * angles[0] - turned(value * angles[1], low)).astype(BF)
            grads[k].append(value)
        yield
    gain_row = gain[0:1]
    normed_gain, normed, inverse = norm_forward(start[...], gain_row)
    normed_gain = normed_gain.astype(BF)
    total = jnp.zeros((length, width), F32)
    for k in range(3):
        grad = jnp.concatenate(grads[k], axis=1)
        put(k, turned_times(normed_gain, grad))
        total = total + times_turned(grad, weights(k))
        yield
    grad, gain_grad = norm_backward(total, normed, inverse, gain_row)
    gains[0:1] = gain_grad.reshape(1, width)
    out[...] = grad_mid[...] + grad
    yield


def local_call(kernel, outs, args, scratch, name, flops, spaces=None):
    spaces = [VMEM] * len(args) if spaces is None else spaces
    return pl.pallas_call(
        kernel,
        out_shape=outs,
        in_specs=spaces,
        out_specs=[VMEM] * len(outs),
        scratch_shapes=scratch,
        compiler_params=pltpu.CompilerParams(vmem_limit_bytes=60 * 2**20),
        cost_estimate=pl.CostEstimate(flops=flops, bytes_accessed=2**24, transcendentals=0),
        name=name,
    )(*args)


def attention_forward(start, gain, angles, allowed, qkv_w, mix_w):
    length, width = start.shape

    def kernel(start, gain, angles, allowed, qkv, mix, held, probs, out):
        def weights(k):
            return qkv[:, width * k : width * (k + 1)]

        drain(attention_steps(start, gain, angles, allowed, weights, lambda: mix[...], held, probs, out))

    outs = [
        shape((4, length, width), BF),
        shape((width // HD, length, length), F32),
        shape((length, width), F32),
    ]
    args = (start, gain, angles, allowed, qkv_w, mix_w)
    return local_call(kernel, outs, args, [], "attention_forward", 2**31)


def feed_back_steps(grad_top, final, middle, both, gain, expand, shrink, grad_expand, grad_shrink, out, gains):
    length, width = middle.shape
    inner = shrink.shape[0]
    _, normed, inverse = norm_forward(final[...], gain[2:3])
    grad_final, gain_top = norm_backward(grad_top[...], normed, inverse, gain[2:3])
    back = grad_final.astype(BF)
    low, normed, inverse = norm_forward(middle[...], gain[1:2])
    low = low.astype(BF)
    total = jnp.zeros((length, width), F32)
    for k in range(inner // PIECE):
        at = slice(PIECE * k, PIECE * (k + 1))
        up_at = slice(inner + PIECE * k, inner + PIECE * (k + 1))
        gate, up = (both[:, at], both[:, up_at])
        sigma = jax.nn.sigmoid(gate)
        hidden = (gate * sigma * up).astype(BF)
        grad_shrink[at] = turned_times(hidden, back).astype(BF)
        grad = times_turned(back, shrink[at])
        grad_gate = (grad * up * sigma * (1.0 + gate * (1.0 - sigma))).astype(BF)
        grad_up = (grad * gate * sigma).astype(BF)
        grad_expand[:, at] = turned_times(low, grad_gate).astype(BF)
        grad_expand[:, up_at] = turned_times(low, grad_up).astype(BF)
        total = total + times_turned(grad_gate, expand[:, at])
        total = total + times_turned(grad_up, expand[:, up_at])
        yield
    grad_middle, gain_two = norm_backward(total, normed, inverse, gain[1:2])
    out[...] = grad_final + grad_middle
    gains[...] = jnp.zeros_like(gains)
    gains[1:2] = gain_two.reshape(1, width)
    gains[2:3] = gain_top.reshape(1, width)
    yield


def layer_backward(dims, grad_top, final, middle, both, gain, expand_w, shrink_w, start, angles, attention, head, cid):
    nz, ny, nx = dims
    length, width = middle.shape
    deep, columns = head.shape[2:]
    later = len(attention)

    def kernel(*refs):
        grad_top, final, middle, both, gain, expand, shrink, start, angles, head_in, *rest = refs
        sources, rest = (rest[:later], rest[later:])
        expand_out, shrink_out, grad_qkv, grad_mix, start_out, gains, head_out, *rest = rest
        qkv, mix, held, probs, *rest = rest
        grad_expand, grad_shrink, grad_mid, *rest = rest
        near, mids, fars, (ssem, rsem, lsem) = (rest[0:2], rest[2:4], rest[4:6], rest[6:])
        place = Place(dims)
        y, x = (place.y, place.x)
        comm = Comm(ssem, rsem, lsem)
        loads = [comm.keep(src, dst) for src, dst in zip(sources, (qkv, mix, held, probs))]
        greet(place, [off for off in line_offsets(dims) if off[1] or off[2]])
        parts = (pl.ds(0, deep // 2), pl.ds(deep // 2, deep // 2))
        by_x = [(t, place.xs(nx - t), place.dev(x=t)) for t in range(1, nx)]
        by_y = [(t, place.ys(ny - t), place.dev(y=t)) for t in range(1, ny)]
        came = [comm.send(head_in.at[:, to, parts[0]], near[0].at[t - 1], dev) for t, to, dev in by_x]
        came += [comm.send(head_in.at[to, :, parts[1]], near[1].at[t - 1], dev) for t, to, dev in by_y]
        drain(
            feed_back_steps(
                grad_top, final, middle, both, gain, expand, shrink, grad_expand, grad_shrink, grad_mid, gains
            )
        )
        comm.keep(grad_expand, expand_out)
        comm.keep(grad_shrink, shrink_out)
        for copy in came:
            copy.wait_recv()
        add_blocks(mids[0], [head_in.at[:, x, parts[0]]] + [near[0].at[t] for t in range(nx - 1)])
        add_blocks(mids[1], [head_in.at[y, :, parts[1]]] + [near[1].at[t] for t in range(ny - 1)])
        came = [comm.send(mids[0].at[to], fars[0].at[t - 1], dev) for t, to, dev in by_y]
        came += [comm.send(mids[1].at[to], fars[1].at[t - 1], dev) for t, to, dev in by_x]
        for copy in loads:
            comm.done(copy)

        def weights(k):
            return qkv[:, width * k : width * (k + 1)]

        def put(k, value):
            if k == 3:
                grad_mix[...] = value.astype(BF)
            else:
                grad_qkv[:, width * k : width * (k + 1)] = value.astype(BF)

        drain(
            attention_back_steps(
                start, gain, angles, weights, lambda: mix[...], held, probs, grad_mid, put, start_out, gains
            )
        )
        for copy in came:
            copy.wait_recv()
        for part, mid, far in ((parts[0], mids[0].at[y], fars[0]), (parts[1], mids[1].at[x], fars[1])):
            add_blocks(head_out.at[part], [mid] + [far.at[t] for t in range(far.shape[0])])
        comm.finish()

    count = 2 * (ny + nx)
    half = (deep // 2, columns)
    outs = [
        shape(expand_w.shape, BF),
        shape(shrink_w.shape, BF),
        shape(attention[0].shape, BF),
        shape(attention[1].shape, BF),
        shape((length, width), F32),
        shape((8, width), F32),
        shape(head.shape[2:], F32),
    ]
    scratch = [pltpu.VMEM(v.shape, v.dtype) for v in attention]
    scratch += [pltpu.VMEM(expand_w.shape, BF), pltpu.VMEM(shrink_w.shape, BF)]
    scratch += [
        pltpu.VMEM((length, width), F32),
        pltpu.VMEM((nx - 1, ny) + half, BF),
        pltpu.VMEM((ny - 1, nx) + half, BF),
        pltpu.VMEM((ny,) + half, BF),
        pltpu.VMEM((nx,) + half, BF),
        pltpu.VMEM((ny - 1,) + half, BF),
        pltpu.VMEM((nx - 1,) + half, BF),
        sems(count),
        sems(count),
        sems(later + 2),
    ]
    args = (grad_top, final, middle, both, gain, expand_w, shrink_w, start, angles, head, *attention)
    return call(
        kernel, outs, [VMEM] * 10 + [ANY] * later, [ANY] * 2 + [VMEM] * 5, scratch,
        cid, "layer_backward", args, 60 * 2**20,
    )


def rope_tables(length, width):
    quarter = width // 4
    places = np.arange(length)
    freq = np.float32(10000.0) ** (-np.arange(quarter, dtype=np.float32) / np.float32(quarter))
    row_angle = (places // GRID).astype(np.float32)[:, None] * freq
    col_angle = (places % GRID).astype(np.float32)[:, None] * freq
    angles = np.concatenate([row_angle, row_angle, col_angle, col_angle] * (128 // width), axis=-1)
    return jnp.asarray(np.stack([np.cos(angles), np.sin(angles)]).astype(np.float32))


def adam_update(master, drift, square, grad, rate, decay):
    moment = BETA_ONE * drift + (1.0 - BETA_ONE) * grad
    second = BETA_TWO * square + (1.0 - BETA_TWO) * grad * grad
    stride = (
        moment / (1.0 - BETA_ONE**STEP) / (jnp.sqrt(second / (1.0 - BETA_TWO**STEP)) + ADAM_EPS)
    )
    return (master - rate * (stride + decay * master), moment, second)


def adam_all(masters, drifts, squares, grads, sums, rates, decays):
    n = len(masters)
    pieces = []
    for i, master in enumerate(masters):
        rows = master.shape[0]
        cut = rows // 4 if rows % 32 == 0 and rows >= 256 else rows
        pieces += [(i, k, min(cut, rows)) for k in range(0, rows, cut)]

    def kernel(*refs):
        ins = [refs[n * k : n * (k + 1)] for k in range(4)]
        sums_in = refs[4 * n]
        outs = [refs[4 * n + 1 + n * k : 4 * n + 1 + n * (k + 1)] for k in range(3)]
        sums_out = refs[7 * n + 1 : 7 * n + 4]
        rest = refs[7 * n + 4 :]
        held = [rest[n * k : n * (k + 1)] for k in range(4)]
        in_sems, out_sems = rest[4 * n :]
        loads, stores = ([], [])
        for p, (i, at, size) in enumerate(pieces):
            span = pl.ds(at, size)
            loads.append(
                [
                    pltpu.make_async_copy(ins[k][i].at[span], held[k][i].at[span], in_sems.at[p, k])
                    for k in range(4)
                ]
            )
        ahead = 3
        for p in range(ahead):
            for copy in loads[p]:
                copy.start()
        row = sums_in[0:1]
        norm = jnp.sqrt(row[:, 0:1]) / row[:, 2:3]
        factor = CLIP_NORM / jnp.maximum(norm, CLIP_NORM) / row[:, 2:3]
        for out, value in zip(sums_out, (norm, row[:, 1:2], row[:, 2:3])):
            out[...] = value

        def update(i, span):
            fresh, moment, second = adam_update(
                held[0][i][span],
                held[1][i][span],
                held[2][i][span],
                held[3][i][span] * factor,
                rates[i],
                decays[i],
            )
            held[0][i][span], held[1][i][span], held[2][i][span] = (fresh, moment, second)

        for p, (i, at, size) in enumerate(pieces):
            for copy in loads[p]:
                copy.wait()
            if p + ahead < len(pieces):
                for copy in loads[p + ahead]:
                    copy.start()
            if size % 8:
                update(i, slice(at, at + size))
            else:

                @pl.loop(0, size // 8)
                def _(k, i=i, at=at):
                    update(i, pl.ds(pl.multiple_of(at + 8 * k, 8), 8))

            span = pl.ds(at, size)
            for k in range(3):
                copy = pltpu.make_async_copy(held[k][i].at[span], outs[k][i].at[span], out_sems.at[p, k])
                copy.start()
                stores.append(copy)
        for copy in stores:
            copy.wait()

    return pl.pallas_call(
        kernel,
        out_shape=[shape(v.shape, F32) for v in masters] * 3 + [shape((1, 1), F32)] * 3,
        in_specs=[ANY] * (4 * n) + [VMEM],
        out_specs=[ANY] * (3 * n) + [VMEM] * 3,
        scratch_shapes=[pltpu.VMEM(v.shape, F32) for v in masters] * 4
        + [pltpu.SemaphoreType.DMA((len(pieces), 4)), pltpu.SemaphoreType.DMA((len(pieces), 3))],
        compiler_params=pltpu.CompilerParams(vmem_limit_bytes=62 * 2**20),
        name="adam_all",
    )(*masters, *drifts, *squares, *grads, sums)


def block_form(rows, columns):
    return (rows, columns) if rows % 8 == 0 else (rows * columns // 128, 128)


FIRST_AXES = ("x", "x", "y", "x")


def on_device(dims, *args):
    labels, targets, heights, loss_mask = args[:4]
    masters, drifts, squares = (args[4:12], args[12:20], args[20:28])
    class_table, code_table, attend_in, attend_mix, expand_in, shrink_out, head_weight, norm_gains = masters
    images, local_len = targets.shape
    length = local_len * 2

    layers = (attend_in, attend_mix, expand_in, shrink_out)
    *weights, start, gain, metas, allowed = gather_all(
        dims, layers, FIRST_AXES, code_table, class_table.T, norm_gains, labels, targets, heights, loss_mask, 0
    )
    qkv_w, mix_w, expand_w, shrink_w = (v.reshape(-1, v.shape[-1]) for v in weights)

    angles = rope_tables(length, HD)
    held, probs, middle = attention_forward(start, gain, angles, allowed, qkv_w, mix_w)
    grad_top, grad_head, partial, both, final = head_all(
        dims, middle, gain, metas, head_weight, expand_w, shrink_w, images, 2
    )
    grad_expand, grad_shrink, grad_qkv, grad_mix, grad_start, gain_grads, grad_head = layer_backward(
        dims, grad_top, final, middle, both, gain, expand_w, shrink_w, start, angles,
        (qkv_w, mix_w, held, probs), grad_head, 3,
    )

    grads_in = []
    for grad, shard in zip((grad_qkv, grad_mix, grad_expand, grad_shrink), layers):
        grads_in.append(grad.reshape(dims + (2,) + block_form(*shard.shape)))
    *layer_shares, code_share, class_share, gain_share, sums = scatter_all(
        dims,
        grads_in,
        FIRST_AXES,
        grad_start,
        gain_grads,
        metas,
        grad_head,
        partial,
        code_table.shape[0],
        class_table.shape[0],
        4,
    )
    layer_shares = [g.reshape(v.shape) for g, v in zip(layer_shares, layers)]
    shares = (class_share, code_share, *layer_shares, grad_head, gain_share)

    def laid(members):
        return (members[0].T, *members[1:])

    updated = adam_all(laid(masters), laid(drifts), laid(squares), shares, sums, RATES, DECAYS)
    sums = updated[24:]
    updated = tuple(member for k in range(3) for member in laid(updated[8 * k : 8 * k + 8]))
    return updated + tuple(member.reshape(()) for member in sums)


def solution(mesh):
    rows, columns = (P(("dp", "seq"), None), P(None, ("dp", "seq")))
    eight = (columns, rows, rows, rows, rows, rows, columns, columns)
    return jax.shard_map(
        functools.partial(on_device, dims_of(mesh.shape["dp"])),
        mesh=mesh,
        in_specs=(P("dp"), P("dp", "seq"), P("dp"), P("dp", "seq")) + eight * 3,
        out_specs=eight * 3 + (P(), P(), P()),
        check_vma=False,
    )
```

```python
import functools

import jax
import jax.numpy as jnp
import numpy as np
from jax import lax
from jax.experimental import pallas as pl
from jax.experimental.pallas import tpu as pltpu
from jax.sharding import PartitionSpec as P

HD = 64
GRID = 16
STEP = 10

EPS_NORM = 1e-05
BETA_ONE = 0.9
BETA_TWO = 0.95
ADAM_EPS = 1e-08
CLIP_NORM = 0.01
NEGATIVE_FILL = -1000000000.0
RATES = (0.8, 0.8, 0.08, 0.08, 0.08, 0.08, 0.08, 0.8)
DECAYS = (0.1, 0.1, 0.1, 0.1, 0.1, 0.1, 0.1, 0.0)

PIECE = 512

MESH = pl.DeviceIdType.MESH
ANY = pl.BlockSpec(memory_space=pl.ANY)
VMEM = pl.BlockSpec(memory_space=pltpu.VMEM)
SMEM = pl.BlockSpec(memory_space=pltpu.SMEM)
BF = jnp.bfloat16
F32 = jnp.float32


def dims_of(dp):
    bits = dp.bit_length() - 1
    nz = 1 << (bits // 2)
    rest = dp // nz
    ny = 1 << ((rest.bit_length() - 1) // 2)
    return (nz, ny, rest // ny)


class Place:
    def __init__(self, dims):
        self.dims = dims
        nz, ny, nx = dims
        chip = lax.axis_index("dp")
        self.c = lax.axis_index("seq")
        self.z = chip // (ny * nx)
        self.y = (chip // nx) % ny
        self.x = chip % nx

    def zs(self, back):
        return (self.z + self.dims[0] - back) % self.dims[0]

    def ys(self, back):
        return (self.y + self.dims[1] - back) % self.dims[1]

    def xs(self, back):
        return (self.x + self.dims[2] - back) % self.dims[2]

    def dev(self, z=0, y=0, x=0, c=0):
        nz, ny, nx = self.dims
        z, y, x = ((self.z + z) % nz, (self.y + y) % ny, (self.x + x) % nx)
        return ((z * ny + y) * nx + x, (self.c + c) % 2)


def line_offsets(dims):
    nz, ny, nx = dims
    return (
        [(s, 0, 0, 0) for s in range(1, nz)]
        + [(0, s, 0, 0) for s in range(1, ny)]
        + [(0, 0, s, 0) for s in range(1, nx)]
        + [(0, 0, 0, 1)]
    )


def plane_offsets(dims):
    return [(0, v, u, 0) for v in range(dims[1]) for u in range(dims[2]) if v or u]


def greet(place, offsets):
    offsets = sorted(set(offsets))
    sem = pltpu.get_barrier_semaphore()
    for off in offsets:
        pl.semaphore_signal(sem, inc=1, device_id=place.dev(*off), device_id_type=MESH)
    pl.semaphore_wait(sem, len(offsets))


class Comm:
    def __init__(self, send_sems, recv_sems, local_sems):
        self.send_sems, self.recv_sems, self.local_sems = (send_sems, recv_sems, local_sems)
        self.sent, self.held, self.count, self.locals = ([], [], 0, 0)

    def send(self, src, dst, device):
        k = self.count
        self.count += 1
        copy = pltpu.make_async_remote_copy(
            src_ref=src,
            dst_ref=dst,
            send_sem=self.send_sems.at[k],
            recv_sem=self.recv_sems.at[k],
            device_id=device,
            device_id_type=MESH,
        )
        copy.start()
        self.sent.append(copy)
        return copy

    def keep(self, src, dst):
        copy = pltpu.make_async_copy(src, dst, self.local_sems.at[self.locals])
        self.locals += 1
        copy.start()
        self.held.append(copy)
        return copy

    def gone(self, copy):
        copy.wait_send()
        self.sent = [other for other in self.sent if other is not copy]

    def done(self, copy):
        copy.wait()
        self.held = [other for other in self.held if other is not copy]

    def finish(self):
        for copy in self.sent:
            copy.wait_send()
        for copy in self.held:
            copy.wait()


def drain(steps):
    for _ in steps:
        pass


def all_offsets(dims):
    nz, ny, nx = dims
    spots = [(k, j, i, core) for k in range(nz) for j in range(ny) for i in range(nx) for core in range(2)]
    return spots[1:]


def small_exchange(comm, place, src, out, own):
    z, y, x, c = (place.z, place.y, place.x, place.c)
    nz, ny, nx = place.dims
    if own:
        comm.keep(src(z, y, x, c), out.at[z, y, x, c])
    got = []
    for off in all_offsets(place.dims):
        there = (place.zs(nz - off[0]), place.ys(ny - off[1]), place.xs(nx - off[2]), (c + off[3]) % 2)
        got.append(comm.send(src(*there), out.at[z, y, x, c], place.dev(*off)))
    return got


class PlaneGather:
    def __init__(self, comm, place):
        self.comm, self.place = (comm, place)
        self.firsts, self.seconds, self.mates = ([], [], [])

    def ways(self, axis):
        _, ny, nx = self.place.dims
        return range(1, ny if axis == "y" else nx)

    def back(self, axis, t, yy, xx):
        return (self.place.ys(t), xx) if axis == "y" else (yy, self.place.xs(t))

    def spread(self, block, first, src=None):
        place, second = (self.place, "y" if first == "x" else "x")
        dst = block(place.y, place.x)
        src = dst if src is None else src
        for t in self.ways(first):
            copy = self.comm.send(src, dst, place.dev(**{first: t}))
            self.firsts.append((block, first, second, t, copy))
        for t in self.ways(second):
            copy = self.comm.send(src, dst, place.dev(**{second: t}))
            self.seconds.append((block(*self.back(second, t, place.y, place.x)), copy))
        self.mates.append(self.comm.send(src, dst, place.dev(c=1)))

    def forward(self):
        place = self.place
        for block, first, second, t, copy in self.firsts:
            copy.wait_recv()
            yy, xx = self.back(first, t, place.y, place.x)
            held = block(yy, xx)
            for u in self.ways(second):
                copy = self.comm.send(held, held, place.dev(**{second: u}))
                self.seconds.append((block(*self.back(second, u, yy, xx)), copy))
            self.mates.append(self.comm.send(held, held, place.dev(c=1)))
        self.firsts = []

    def settle(self):
        for held, copy in self.seconds:
            copy.wait_recv()
            self.mates.append(self.comm.send(held, held, self.place.dev(c=1)))
        self.seconds = []

    def forward_some(self, count):
        rest = self.firsts[count:]
        self.firsts = self.firsts[:count]
        self.forward()
        self.firsts = rest

    def arrive(self):
        for copy in self.mates:
            copy.wait_recv()
        self.mates = []


def sems(count):
    return pltpu.SemaphoreType.DMA((count,))


def shape(dims, dtype):
    return jax.ShapeDtypeStruct(tuple(dims), dtype)


def call(kernel, outs, in_specs, out_specs, scratch, cid, name, args, vmem=None):
    return pl.pallas_call(
        kernel,
        out_shape=outs,
        in_specs=in_specs,
        out_specs=out_specs,
        scratch_shapes=scratch,
        compiler_params=pltpu.CompilerParams(
            collective_id=cid, has_side_effects=True, vmem_limit_bytes=vmem
        ),
        name=name,
    )(*args)


def small_sends(dims):
    return dims[0] * dims[1] * dims[2] * 2 - 1


def gather_all(dims, layers, first_axes, table, classes, gains, labels, targets, heights, masks, cid):
    nz, ny, nx = dims
    n = len(layers)
    rows, width = table.shape
    images, local_len = targets.shape
    length = local_len * 2
    columns = gains.shape[1]
    meta = (8, 128)
    count_images = nz * ny * nx * images
    label_rows = -(-count_images // 128)
    groups = [(k,) for k in range(nz)] if nz <= 4 else [tuple(range(nz))]

    def kernel(*refs):
        ins, rest = (refs[:n], refs[n:])
        table_in, class_in, gain_in, labels_in, targets_in, heights_in, masks_in, *rest = rest
        outs, rest = (rest[:n], rest[n:])
        start_out, gain_out, meta_out, allowed_out, *rest = rest
        low, rest = (rest[:n], rest[n:])
        whole, found, total, class_low, gain_row, meta_in, parts_out, small_out, small_in, *rest = rest
        ssem, rsem, lsem = rest
        place = Place(dims)
        z, y, x, c = (place.z, place.y, place.x, place.c)
        chip = (z * ny + y) * nx + x
        meta_in[...] = jnp.zeros_like(meta_in)
        meta_in[0:images] = targets_in[...]
        meta_in[images : 2 * images] = masks_in[...]
        lane = lax.broadcasted_iota(jnp.int32, (1, 128), 1)
        for i in range(images):
            meta_in[4:5] += jnp.where(lane == i, labels_in[i], 0)
            meta_in[4:5] += jnp.where(lane == images + i, heights_in[i], 0)
            for r in range(label_rows):
                meta_in[5 + r : 6 + r] += jnp.where(lane == chip * images + i - 128 * r, labels_in[i], 0)
        greet(place, all_offsets(dims))
        comm = Comm(ssem, rsem, lsem)
        metas = small_exchange(comm, place, lambda *spot: meta_in, meta_out, False)
        meta_out[z, y, x, c] = meta_in[...]
        waits = []
        whole[y, x, c] = table_in[...].astype(BF)
        tables, blocks = (PlaneGather(comm, place), PlaneGather(comm, place))
        for first, start in (("x", 0), ("y", rows // 2)):
            half = pl.ds(start, rows // 2)
            tables.spread(lambda yy, xx, half=half: whole.at[yy, xx, c, half], first)
        for a in range(n):
            low[a][...] = ins[a][...].astype(BF)
        along = {}
        for s in range(1, nz):
            for a in range(n):
                along[s, a] = comm.send(low[a], outs[a].at[z, y, x, c], place.dev(z=s))
        kept = [comm.keep(low[a], outs[a].at[z, y, x, c]) for a in range(n)]

        def spread(group):
            for a in range(n):
                for k in group:
                    if k:
                        along[k, a].wait_recv()
                if len(group) > 1:
                    comm.done(kept[a])
                    at = pl.ds(0, nz)
                else:
                    at = place.zs(group[0])
                blocks.spread(
                    lambda yy, xx, a=a, at=at: outs[a].at[at, yy, xx, c],
                    first_axes[a],
                    low[a] if group == (0,) else None,
                )

        for copy in metas:
            copy.wait_recv()

        class_low[...] = jnp.zeros_like(class_low)
        class_low[0:columns, 0 : class_in.shape[1]] = class_in[...]
        small_in[...] = jnp.zeros_like(small_in)
        for r in range(label_rows):
            labels = jnp.zeros((1, 128), jnp.int32)
            for k in range(nz * ny * nx):
                labels = labels + meta_out[k // (ny * nx), k // nx % ny, k % nx, 0, 5 + r : 6 + r, :]
            pick = lax.broadcasted_iota(jnp.int32, (class_low.shape[1], 128), 0) == labels
            picked = lax.dot_general(
                jnp.where(pick, 1.0, 0.0).astype(BF),
                class_low[...].astype(BF),
                (((0,), (1,)), ((), ())),
                preferred_element_type=F32,
            )
            for i in range(min(128, count_images - 128 * r)):
                k, core = divmod(128 * r + i, 2)
                small_in[k // (ny * nx), k // nx % ny, k % nx, core, 0:1, 0 : class_low.shape[0]] = picked[
                    i : i + 1
                ]
        gain_row[...] = jnp.zeros_like(gain_row)
        gain_row[0:3, 0:columns] = gain_in[...].astype(BF).astype(F32)

        @pl.loop(0, nz)
        def _(k):
            for j in range(ny):
                for i in range(nx):
                    for core in range(2):
                        small_in[k, j, i, core, 1:4, :] = gain_row[0:3]

        smalls = small_exchange(comm, place, lambda *spot: small_in.at[spot], small_out, False)
        small_out[z, y, x, c] = small_in[z, y, x, c]

        size = len(layers)
        steps = [lambda group=group: spread(group) for group in groups]
        steps.pop(0)()
        tables.forward()
        if steps:
            steps.pop(0)()
        blocks.forward_some(size)
        if steps:
            steps.pop(0)()
        tables.settle()
        blocks.forward_some(size)
        for step in steps:
            step()
        tables.arrive()

        for s in range(1, nz + 1):
            zz = place.zs(s % nz)
            halves = []
            for half in range(2):
                codes = meta_out[zz, y, x, half, pl.ds(c, 1), :].astype(F32)
                halves.append(jnp.broadcast_to(codes, (128, local_len)).T)
            column = jnp.concatenate(halves, axis=0)
            column = column - (z * ny * nx * 2 * rows).astype(F32)
            total[...] = jnp.zeros_like(total)

            @pl.loop(0, ny * nx * 2)
            def _(j):
                base = (j * rows).astype(F32)
                lane = lax.broadcasted_iota(jnp.int32, (length, 128), 1).astype(F32) + base
                picks = [
                    jnp.where(column == lane + float(128 * q), 1.0, 0.0).astype(BF)
                    for q in range(-(-rows // 128))
                ]
                pick = jnp.concatenate(picks, axis=1)[:, :rows]
                total[...] += matmul(pick, whole[j // (2 * nx), j // 2 % nx, j % 2])

            found[s % nz] = total[...].astype(BF)
            if s < nz:
                waits.append(comm.send(found.at[s], parts_out.at[nz - s - 1], place.dev(z=nz - s)))
            blocks.forward_some(size)
        blocks.forward()
        height = jnp.where(c == 0, heights_in[0], heights_in[images - 1])
        query = lax.broadcasted_iota(jnp.int32, (length, length), 0)
        key = lax.broadcasted_iota(jnp.int32, (length, length), 1)
        allowed_out[...] = jnp.where((key <= query) & (key < GRID * height), 1.0, 0.0)
        for copy in smalls:
            copy.wait_recv()
        joined = jnp.zeros((8, width), F32)
        blank = jnp.zeros((8, width - 128), F32)
        for d in range(2 * nz * ny * nx):
            k, core = divmod(d, 2)
            piece = small_out[k // (ny * nx), k // nx % ny, k % nx, core]
            joined = joined + pltpu.roll(jnp.concatenate([piece, blank], axis=1), columns * d, 1)
        gain_out[...] = jnp.concatenate([joined[1:4], jnp.zeros((5, width), F32)], axis=0)
        blocks.settle()
        for copy in waits:
            copy.wait_recv()
        added = found[0].astype(F32)
        for s in range(1, nz):
            added = added + parts_out[s - 1].astype(F32)
        first = lax.broadcasted_iota(jnp.int32, (length, 128), 0) == 0
        for k in range(width // 128):
            at = slice(128 * k, 128 * k + 128)
            start_out[:, at] = jnp.where(first, joined[0:1, at], pltpu.roll(added[:, at], 1, 0))
        blocks.arrive()
        comm.finish()

    count = n * (nz - 1) + (n * len(groups) + 2) * (2 * ny * nx - 1) + nz + 2 * small_sends(dims)
    small = dims + (2, 8, 128)
    outs = [shape(dims + (2,) + v.shape, BF) for v in layers]
    outs += [
        shape((length, width), F32),
        shape((8, width), F32),
        shape(dims + (2,) + meta, jnp.int32),
        shape((length, length), F32),
    ]
    scratch = [pltpu.VMEM(v.shape, BF) for v in layers]
    scratch += [
        pltpu.VMEM((ny, nx, 2) + table.shape, BF),
        pltpu.VMEM((nz, length, width), BF),
        pltpu.VMEM((length, width), F32),
        pltpu.VMEM((-(-columns // 16) * 16, -(-classes.shape[1] // 128) * 128), F32),
        pltpu.VMEM((8, 128), F32),
        pltpu.VMEM(meta, jnp.int32),
        pltpu.VMEM((nz - 1, length, width), BF),
        pltpu.VMEM(small, F32),
        pltpu.VMEM(small, F32),
        sems(count),
        sems(count),
        sems(n),
    ]
    return call(
        kernel, outs, [VMEM] * (n + 3) + [SMEM, VMEM, SMEM, VMEM], [ANY] * n + [VMEM] * 4, scratch,
        cid, "gather_all", (*layers, table, classes, gains, labels, targets, heights, masks), 60 * 2**20,
    )


def add_blocks(out, terms):
    lead = out.shape[:-2]

    def visit(index):
        if len(index) < len(lead):

            @pl.loop(0, lead[len(index)])
            def _(i):
                visit(index + (i,))

        else:
            if len(terms) == 2 and out.dtype == BF:
                out[index] = terms[0][index] + terms[1][index]
                return
            total = terms[0][index].astype(F32)
            for term in terms[1:]:
                total = total + term[index].astype(F32)
            out[index] = total.astype(out.dtype)

    visit(())


def items_of(shapes, axes):
    if shapes[0][0] % 8:
        return [[(a, slice(0, shapes[a][0]), slice(0, shapes[a][1]), axes[a]) for a in pair] for pair in ((2, 3), (0, 1))]
    (rows, qkv), (_, mix), (_, both), (deep, width) = shapes
    every, piece = (slice(0, rows), both // 4)
    return [
        [(3, slice(0, deep // 2), slice(0, width), "x"), (3, slice(deep // 2, deep), slice(0, width), "y")],
        [(2, every, slice(0, piece), "x"), (2, every, slice(2 * piece, 3 * piece), "y")],
        [(0, every, slice(0, 2 * mix), "x"), (0, every, slice(2 * mix, qkv), "y"), (1, every, slice(0, mix), "y")],
        [(2, every, slice(piece, 2 * piece), "x"), (2, every, slice(3 * piece, both), "y")],
    ]


def scatter_all(dims, grads, axes, rows, gains, metas, head, partial, device_codes, classes, cid):
    nz, ny, nx = dims
    plane = ny * nx
    n = len(grads)
    shapes = [g.shape[4:] for g in grads]
    steps = items_of(shapes, axes)
    items = [item for step in steps for item in step]
    order, at = ([], 0)
    for step in steps:
        order.append(list(range(at, at + len(step))))
        at += len(step)
    length, width = rows.shape
    block = (device_codes, width)
    sizes = {"x": nx, "y": ny}
    columns = width // (2 * nz * plane)
    label_rows = -(-2 * nz * plane // 128)

    def kernel(*refs):
        parts, rest = (refs[:n], list(refs[n:]))
        rows_in, gains_in, meta_in, head_in, partial_in = (rest.pop(0) for _ in range(5))
        outs = [rest.pop(0) for _ in range(n)]
        table_out, class_out, gain_out, sums = (rest.pop(0) for _ in range(4))
        owns, halves, ones, twos, threes = ([rest.pop(0) for _ in items] for _ in range(5))
        near, far = ([rest.pop(0), rest.pop(0)] for _ in range(2))
        lined, given, own, half, small_in, small_out, tops, gained_all, mine, every, *rest = rest
        ssem, rsem, lsem = rest
        place = Place(dims)
        z, y, x, c = (place.z, place.y, place.x, place.c)
        comm = Comm(ssem, rsem, lsem)
        kept = []
        for i, (a, span, cols, _) in enumerate(items):
            kept.append(comm.keep(parts[a].at[:, :, :, c, span, cols], owns[i]))
        greet(place, all_offsets(dims))
        pair, got_one, got_two, third = ({}, {}, {}, {})

        def set_out(g):
            for i in order[g] if g < len(order) else []:
                a, span, cols, _ = items[i]
                pair[i] = comm.send(parts[a].at[:, :, :, 1 - c, span, cols], halves[i], place.dev(c=1))

        def back(axis, t):
            return place.ys(ny - t) if axis == "y" else place.xs(nx - t)

        def first_add(g):
            for i in order[g]:
                pair[i].wait_recv()
                comm.done(kept[i])
                add_blocks(halves[i], [halves[i], owns[i]])

        def first_send(g):
            for i in order[g]:
                axis = items[i][3]
                got_one[i] = [
                    comm.send(
                        halves[i].at[:, back(axis, t)] if axis == "y" else halves[i].at[:, :, back(axis, t)],
                        ones[i].at[t - 1],
                        place.dev(**{axis: t}),
                    )
                    for t in range(1, sizes[axis])
                ]

        def second_step(g):
            for i in order[g]:
                axis = items[i][3]
                other = "x" if axis == "y" else "y"
                for copy in got_one[i]:
                    copy.wait_recv()
                held = halves[i].at[:, y] if axis == "y" else halves[i].at[:, :, x]
                add_blocks(held, [held] + [ones[i].at[t] for t in range(ones[i].shape[0])])
                got_two[i] = [
                    comm.send(
                        halves[i].at[:, y, back("x", t)] if other == "x" else halves[i].at[:, back("y", t), x],
                        twos[i].at[t - 1],
                        place.dev(**{other: t}),
                    )
                    for t in range(1, sizes[other])
                ]

        def third_step(g):
            for i in order[g]:
                for copy in got_two[i]:
                    copy.wait_recv()
                held = halves[i].at[:, y, x]
                add_blocks(held, [held] + [twos[i].at[t] for t in range(twos[i].shape[0])])
                third[i] = [
                    comm.send(halves[i].at[place.zs(nz - s), y, x], threes[i].at[s - 1], place.dev(z=s))
                    for s in range(1, nz)
                ]

        def last_step(g):
            for i in order[g]:
                a, span, cols, _ = items[i]
                for copy in third[i]:
                    copy.wait_recv()
                terms = [halves[i].at[z, y, x]] + [threes[i].at[s] for s in range(nz - 1)]
                add_blocks(outs[a].at[span, cols], terms)

        flat = []
        first = lax.broadcasted_iota(jnp.int32, (1, length), 1) == 0
        for s in range(nz):
            codes = [meta_in[place.zs(s), y, x, part, pl.ds(c, 1), :] for part in range(2)]
            codes = pltpu.roll(jnp.concatenate(codes, axis=1) - z * (2 * plane * device_codes), 1, 1)
            flat.append(jnp.where(first, -1, codes))
        flat = jnp.concatenate(flat, axis=1)

        def product(into, core):
            @pl.loop(0, plane)
            def _(j):
                code = lax.broadcasted_iota(jnp.int32, (device_codes, nz * length), 0)
                pick = code + (j * 2 + core) * device_codes == flat
                pick = jnp.where(pick, 1.0, 0.0).astype(BF)
                value = matmul(pick, lined[...].reshape(nz * length, width))
                into[j // nx, j % nx] = value.astype(BF)

        set_out(0)
        set_out(1)
        lane = lax.broadcasted_iota(jnp.int32, (8, 128), 1)
        top = jnp.concatenate([rows_in[0:1], gains_in[0:3], jnp.zeros((4, width), F32)], axis=0)
        for d in range(2 * nz * plane):
            k, core = divmod(d, 2)
            piece = pltpu.roll(top, (width - columns * d) % width, 1)[:, :128]
            small_in[k // plane, k // nx % ny, k % nx, core] = jnp.where(lane < columns, piece, 0.0)
        waits = small_exchange(comm, place, lambda *spot: small_in.at[spot], small_out, False)
        small_out[z, y, x, c] = small_in[z, y, x, c]
        lined[0] = rows_in[...].astype(BF)
        lines = [comm.send(lined.at[0], lined.at[s], place.dev(z=s)) for s in range(1, nz)]
        count = len(order)
        for g in range(count):
            first_add(g)
            set_out(g + 2)
            if g >= 2:
                second_step(g - 2)
            first_send(g)
            if g >= 3:
                third_step(g - 3)
        for copy in lines:
            copy.wait_recv()
        product(given, 1 - c)
        table_pair = comm.send(given, half, place.dev(c=1))
        second_step(count - 2)
        product(own, c)
        if count > 2:
            third_step(count - 3)
        second_step(count - 1)
        table_pair.wait_recv()
        add_blocks(half, [half, own])
        parts_of = [pl.ds(0, device_codes // 2), pl.ds(device_codes // 2, device_codes // 2)]
        came = [
            [
                comm.send(half.at[:, back("x", t), parts_of[0]], near[0].at[t - 1], place.dev(x=t))
                for t in range(1, nx)
            ],
            [
                comm.send(half.at[back("y", t), :, parts_of[1]], near[1].at[t - 1], place.dev(y=t))
                for t in range(1, ny)
            ],
        ]
        third_step(count - 2)
        third_step(count - 1)

        for copy in waits:
            copy.wait_recv()
        gained_all[...] = jnp.zeros_like(gained_all)
        tops[...] = jnp.zeros_like(tops)

        @pl.loop(0, nz)
        def _(k):
            for j in range(ny):
                for i in range(nx):
                    for core in range(2):
                        at = ((k * ny + j) * nx + i) * 2 + core
                        tops[pl.ds(at, 1), :] = small_out[k, j, i, core, 0:1, :]
                        gained_all[...] += small_out[k, j, i, core]

        high = -(-classes // 128) * 128
        value = jnp.zeros((128, high), F32)
        for r in range(label_rows):
            labels = jnp.zeros((1, 128), jnp.int32)
            for k in range(nz * plane):
                labels = labels + meta_in[k // plane, k // nx % ny, k % nx, 0, 5 + r : 6 + r, :]
            at = lax.broadcasted_iota(jnp.int32, (high, 128), 1) + 128 * r
            pick = lax.broadcasted_iota(jnp.int32, (high, 128), 0) == labels
            pick = jnp.where(pick & (at < 2 * nz * plane), 1.0, 0.0)
            value = value + lax.dot_general(
                tops[128 * r : 128 * r + 128],
                pick,
                (((0,), (1,)), ((), ())),
                precision=lax.Precision.HIGHEST,
                preferred_element_type=F32,
            )
        class_out[...] = value[:columns, :classes]
        gain_out[...] = gained_all[1:4, :columns]
        row = lax.broadcasted_iota(jnp.int32, gained_all.shape, 0)
        gained = jnp.where((row >= 1) & (row < 4), gained_all[...], 0.0)
        square = jnp.sum(value * value) + jnp.sum(gained * gained)
        share = head_in[...].astype(F32)
        square = square + jnp.sum(share * share)
        for g in range(count - 1):
            last_step(g)

        for copy in came[0] + came[1]:
            copy.wait_recv()
        for h, held in ((0, half.at[:, x, parts_of[0]]), (1, half.at[y, :, parts_of[1]])):
            add_blocks(held, [held] + [near[h].at[t] for t in range(near[h].shape[0])])
        came = [
            comm.send(half.at[back("y", t), x, parts_of[0]], far[0].at[t - 1], place.dev(y=t))
            for t in range(1, ny)
        ]
        came += [
            comm.send(half.at[y, back("x", t), parts_of[1]], far[1].at[t - 1], place.dev(x=t))
            for t in range(1, nx)
        ]
        last_step(count - 1)
        for a in range(n):
            square = square + jnp.sum(outs[a][...] * outs[a][...])
        for copy in came:
            copy.wait_recv()
        for h in range(2):
            terms = [half.at[y, x, parts_of[h]]] + [far[h].at[t] for t in range(far[h].shape[0])]
            add_blocks(table_out.at[parts_of[h]], terms)
        square = square + jnp.sum(table_out[...] * table_out[...])
        first = (lax.broadcasted_iota(jnp.int32, mine.shape, 0) == 0) & (
            lax.broadcasted_iota(jnp.int32, mine.shape, 1) == 0
        )
        mine[...] = partial_in[...] + jnp.where(first, square, 0.0)
        for copy in small_exchange(comm, place, lambda *spot: mine, every, False):
            copy.wait_recv()
        every[z, y, x, c] = mine[...]
        sums[...] = jnp.zeros_like(sums)

        @pl.loop(0, nz)
        def _(k):
            for j in range(ny):
                for i in range(nx):
                    sums[...] += every[k, j, i, 0] + every[k, j, i, 1]

        comm.finish()

    total = len(items) * (ny + nx - 1 + nz - 1) + nz + 2 * (ny + nx) + 2 * small_sends(dims)
    cuts = [(span.stop - span.start, cols.stop - cols.start) for _, span, cols, _ in items]
    near_far = [(ny, nx) if item[3] == "y" else (nx, ny) for item in items]
    part = (device_codes // 2, width)
    scratch = [pltpu.VMEM((nz, ny, nx) + t, BF) for t in cuts] * 2
    scratch += [pltpu.VMEM((u - 1, nz, v) + t, BF) for t, (u, v) in zip(cuts, near_far)]
    scratch += [pltpu.VMEM((v - 1, nz) + t, BF) for t, (u, v) in zip(cuts, near_far)]
    scratch += [pltpu.VMEM((nz - 1,) + t, BF) for t in cuts]
    scratch += [
        pltpu.VMEM((nx - 1, ny) + part, BF),
        pltpu.VMEM((ny - 1, nx) + part, BF),
        pltpu.VMEM((ny - 1,) + part, BF),
        pltpu.VMEM((nx - 1,) + part, BF),
        pltpu.VMEM((nz, length, width), BF),
        pltpu.VMEM((ny, nx) + block, BF),
        pltpu.VMEM((ny, nx) + block, BF),
        pltpu.VMEM((ny, nx) + block, BF),
        pltpu.VMEM(dims + (2, 8, 128), F32),
        pltpu.VMEM(dims + (2, 8, 128), F32),
        pltpu.VMEM((128 * label_rows, 128), F32),
        pltpu.VMEM((8, 128), F32),
        pltpu.VMEM(partial.shape, F32),
        pltpu.VMEM(dims + (2,) + partial.shape, F32),
        sems(total),
        sems(total),
        sems(len(items)),
    ]
    outs = [shape(t, F32) for t in shapes]
    outs += [shape(block, F32), shape((columns, classes), F32), shape((3, columns), F32)]
    outs += [shape(partial.shape, F32)]
    return call(
        kernel, outs, [ANY] * n + [VMEM] * 5, [VMEM] * (n + 4), scratch,
        cid, "scatter_all", (*grads, rows, gains, metas, head, partial), 60 * 2**20,
    )


def head_all(dims, middle, gain, metas, head, expand_w, shrink_w, images, cid):
    nz, ny, nx = dims
    length, width = middle.shape
    inner = shrink_w.shape[0]
    pieces = inner // PIECE
    columns = head.shape[1]
    lanes = min(columns, 128)
    groups = columns // lanes
    plane = ny * nx
    blocks = 2 * plane
    keep = columns >= 128
    shared = columns == PIECE and nz * length >= width and blocks >= 2 * pieces

    def kernel(*refs):
        middle_in, gain_in, meta_in, head_in, expand_in, shrink_in, *rest = refs
        top_out, head_out, loss_out, both_out, final_out, *rest = rest
        whole, marks_in, wide, lined, turned, peaks, totals, picks, exps, grads, *rest = rest
        columned, partial, back, coming, mine, every, given, half, ssem, rsem, lsem = rest
        place = Place(dims)
        z, y, x, c = (place.z, place.y, place.x, place.c)
        greet(place, line_offsets(dims))
        comm = Comm(ssem, rsem, lsem)
        room, loads = ({}, {})

        def load(j):
            room[j] = grads.at[j, pl.ds(0, width)] if shared else wide.at[j // pieces]
            loads[j] = comm.keep(expand_in.at[:, pl.ds(PIECE * j, PIECE)], room[j])

        for j in range(2 * pieces) if shared else []:
            load(j)
        whole[c, y, x] = head_in[...].astype(BF)
        gather = PlaneGather(comm, place)
        for first, start in (("x", 0), ("y", width // 2)):
            part = pl.ds(start, width // 2)
            gather.spread(lambda yy, xx, part=part: whole.at[c, yy, xx, part], first)
        normed = norm_forward(middle_in[...], gain_in[1:2])[0].astype(BF)
        total = middle_in[...]
        for j in range(pieces):
            at = slice(PIECE * j, PIECE * (j + 1))
            for k in (j, pieces + j):
                if not shared:
                    load(k)
                comm.done(loads[k])
            gate, up = (matmul(normed, room[j][...]), matmul(normed, room[pieces + j][...]))
            both_out[:, at] = gate
            both_out[:, inner + PIECE * j : inner + PIECE * (j + 1)] = up
            hidden = (gate * jax.nn.sigmoid(gate) * up).astype(BF)
            total = total + matmul(hidden, shrink_in[at])
        final_out[...] = total
        lined[0] = norm_forward(total, gain_in[2:3])[0].astype(BF)
        turns = sorted(range(1, nz), key=lambda s: min(s, nz - s))
        arriving = {s: comm.send(lined.at[0], lined.at[s], place.dev(z=s)) for s in turns[:2]}
        turned[:, 0:length] = lined[0].T
        for s in range(nz):
            for part in range(2):
                codes = meta_in[place.zs(s), y, x, part, pl.ds(c, 1), :].astype(F32)
                tall = jnp.broadcast_to(codes, (128, 128)).T.astype(jnp.int32)
                marks_in[s, 128 * part : 128 * part + 128] = tall[:, :lanes] - z * (blocks * columns)
        gather.forward()
        for s in turns[:2]:
            comm.gone(arriving[s])
        for s in turns[2:]:
            arriving[s] = comm.send(lined.at[0], lined.at[s], place.dev(z=s))
        gather.settle()
        gather.arrive()

        def block(k):
            return whole[k // plane, k // nx % ny, k % nx]

        def split(value):
            return [value[:, lanes * q : lanes * (q + 1)] for q in range(groups)]

        def hits(s, k):
            base = (k % plane * 2 + k // plane) * columns
            lane = lax.broadcasted_iota(jnp.int32, (length, lanes), 1) + base
            return [lane + lanes * q == marks_in[s] for q in range(groups)]

        def logits_of(s, k):
            return matmul(lined[s], block(k))

        def forward(s):
            at = pl.ds(s * length, length)
            peaks[...] = jnp.full_like(peaks, -jnp.inf)
            totals[...] = jnp.zeros_like(totals)
            picks[...] = jnp.zeros_like(picks)

            @pl.loop(0, blocks // 2)
            def _(pair):
                high, found = (peaks[...], picks[...])
                for k in (2 * pair, 2 * pair + 1):
                    logits = logits_of(s, k)
                    if keep:
                        exps[k, at] = logits
                    for piece, hit in zip(split(logits), hits(s, k)):
                        high = jnp.maximum(high, piece)
                        found = found + jnp.where(hit, piece, 0.0)
                peaks[...] = high
                picks[...] = found

            peak = jnp.max(peaks[...], axis=1, keepdims=True)
            peaks[...] = jnp.broadcast_to(peak, (length, lanes))

            @pl.loop(0, blocks // 2)
            def _(pair):
                total = totals[...]
                for k in (2 * pair, 2 * pair + 1):
                    logits = exps[k, at] if keep else logits_of(s, k)
                    for q, piece in enumerate(split(logits)):
                        power = jnp.exp(piece - peaks[...])
                        if keep:
                            exps[k, at, lanes * q : lanes * (q + 1)] = power
                        total = total + power
                totals[...] = total

            if not keep:
                exps[s] = peaks[...]
            lane = lax.broadcasted_iota(jnp.int32, (length, 128), 1)
            total = jnp.sum(totals[...], axis=1, keepdims=True)
            found = jnp.sum(picks[...], axis=1, keepdims=True)
            table = jnp.where(lane == 0, peak, jnp.where(lane == 1, total, found))
            mine[place.zs(s)] = table.T[:8]

        forward(0)
        for s in turns:
            arriving[s].wait_recv()
            turned[:, s * length : (s + 1) * length] = lined[s].T
            forward(s)
        stats = [comm.send(mine, every.at[s], place.dev(z=s)) for s in range(1, nz)]
        every[0] = mine[...]
        for copy in stats:
            copy.wait_recv()

        def backward(s):
            at = pl.ds(s * length, length)
            held = [every[q, place.zs(s)] for q in range(nz)]
            peak = held[0][0:1]
            for other in held[1:]:
                peak = jnp.maximum(peak, other[0:1])
            total = sum(other[1:2] * jnp.exp(other[0:1] - peak) for other in held)
            zz = place.zs(s)
            mask = [meta_in[zz, y, x, part, pl.ds(images + c, 1), :] for part in range(2)]
            mask = jnp.concatenate(mask, axis=1).astype(F32)
            tail = meta_in[zz, y, x, 0, 4:5, :]
            lane = lax.broadcasted_iota(jnp.int32, (1, 128), 1)
            tall = jnp.sum(jnp.where(lane == images + c, tail, 0).astype(F32), axis=1, keepdims=True)
            place_of = lax.broadcasted_iota(jnp.int32, (1, length), 1).astype(F32)
            weight = jnp.where(place_of < GRID * tall, mask, 0.0)
            if s == 0:
                found = sum(other[2:3] for other in held)
                loss = (peak + jnp.log(total) - found) * weight
                lane = lax.broadcasted_iota(jnp.int32, (8, 128), 1)
                row = lax.broadcasted_iota(jnp.int32, (8, 128), 0)
                sums = jnp.where(lane == 1, jnp.sum(loss, axis=1, keepdims=True), 0.0)
                sums = sums + jnp.where(lane == 2, jnp.sum(weight, axis=1, keepdims=True), 0.0)
                loss_out[...] = jnp.where(row == 0, sums, 0.0)
            scale = weight / total * jnp.exp(held[0][0:1] - peak)
            tall = jnp.concatenate([scale, weight, jnp.zeros((126, length), F32)], axis=0).T
            columned[0] = jnp.broadcast_to(tall[:, 0:1], (length, lanes))
            columned[1] = jnp.broadcast_to(tall[:, 1:2], (length, lanes))
            partial[...] = jnp.zeros_like(partial)

            @pl.loop(0, blocks // 2)
            def _(pair):
                added = partial[...]
                for k in (2 * pair, 2 * pair + 1):
                    if keep:
                        powers = split(exps[k, at])
                    else:
                        powers = [jnp.exp(piece - exps[s]) for piece in split(logits_of(s, k))]
                    parts = []
                    for power, hit in zip(powers, hits(s, k)):
                        grad = power * columned[0] - jnp.where(hit, columned[1], 0.0)
                        parts.append(grad.astype(BF))
                    grad = jnp.concatenate(parts, axis=1) if groups > 1 else parts[0]
                    grads[k, at] = grad
                    added = added + times_turned(grad, block(k))
                partial[...] = added

        coming_in = []
        for s in range(1, nz):
            backward(s)
            back[s - 1] = partial[...].astype(BF)
            coming_in.append(comm.send(back.at[s - 1], coming.at[s - 1], place.dev(z=nz - s)))
        backward(0)

        def weights(into, core):
            @pl.loop(0, plane)
            def _(j):
                into[j // nx, j % nx] = matmul(turned[...], grads[core * plane + j]).astype(BF)

        weights(given, 1 - c)
        pair = comm.send(given, half, place.dev(c=1))
        weights(head_out, c)
        pair.wait_recv()
        add_blocks(head_out, [head_out, half])
        for copy in coming_in:
            copy.wait_recv()
        total = partial[...]
        for s in range(nz - 1):
            total = total + coming[s].astype(F32)
        top_out[...] = total
        comm.finish()

    count = 3 * (nz - 1) + 2 * (2 * plane - 1) + 1
    scratch = [
        pltpu.VMEM((2, ny, nx) + head.shape, BF),
        pltpu.VMEM((nz, length, lanes), jnp.int32),
        pltpu.VMEM((16, 128) if shared else (2, width, PIECE), BF),
        pltpu.VMEM((nz, length, width), BF),
        pltpu.VMEM((width, nz * length), BF),
        pltpu.VMEM((length, lanes), F32),
        pltpu.VMEM((length, lanes), F32),
        pltpu.VMEM((length, lanes), F32),
        pltpu.VMEM((blocks, nz * length, columns) if keep else (nz, length, lanes), F32),
        pltpu.VMEM((blocks, nz * length, columns), BF),
        pltpu.VMEM((2, length, lanes), F32),
        pltpu.VMEM((length, width), F32),
        pltpu.VMEM((nz - 1, length, width), BF),
        pltpu.VMEM((nz - 1, length, width), BF),
        pltpu.VMEM((nz, 8, length), F32),
        pltpu.VMEM((nz, nz, 8, length), F32),
        pltpu.VMEM((ny, nx) + head.shape, BF),
        pltpu.VMEM((ny, nx) + head.shape, BF),
        sems(count),
        sems(count),
        sems(2 * pieces),
    ]
    outs = [
        shape((length, width), F32),
        shape((ny, nx) + head.shape, BF),
        shape((8, 128), F32),
        shape((length, 2 * inner), F32),
        shape((length, width), F32),
    ]
    return call(
        kernel, outs, [VMEM] * 4 + [ANY, VMEM], [VMEM] * 5, scratch,
        cid, "head_all", (middle, gain, metas, head, expand_w, shrink_w), 63 * 2**20,
    )


def matmul(left, right):
    return jnp.dot(left, right, preferred_element_type=F32)


def norm_forward(values, gain):
    inverse = lax.rsqrt(jnp.mean(values * values, axis=-1, keepdims=True) + EPS_NORM)
    normed = values * inverse
    return (normed * gain, normed, inverse)


def norm_backward(grad, normed, inverse, gain):
    scaled = grad * gain
    inner = jnp.mean(scaled * normed, axis=-1, keepdims=True)
    return (inverse * (scaled - normed * inner), jnp.sum(grad * normed, axis=0))


def turned(value, low):
    return jnp.where(low, -pltpu.roll(value, 112, 1), pltpu.roll(value, 16, 1))


def low_quarters(rows):
    return lax.broadcasted_iota(jnp.int32, (rows, 128), 1) % 32 < 16


def left_half(rows):
    return lax.broadcasted_iota(jnp.int32, (rows, 128), 1) < HD


def times_turned(left, right):
    return lax.dot_general(left, right, (((1,), (1,)), ((), ())), preferred_element_type=F32)


def turned_times(left, right):
    return lax.dot_general(left, right, (((0,), (0,)), ((), ())), preferred_element_type=F32)


def attention_steps(start, gain, angles, allowed, weights, mix, held, probs, out):
    length, width = start.shape
    normed = norm_forward(start[...], gain[0:1])[0].astype(BF)
    low, left = (low_quarters(length), left_half(length))
    for k in range(3):
        value = matmul(normed, weights(k))
        for p in range(width // 128):
            piece = value[:, 128 * p : 128 * p + 128]
            if k < 2:
                piece = piece * angles[0] + turned(piece, low) * angles[1]
            held[k, :, 128 * p : 128 * p + 128] = piece.astype(BF)
        yield
    for p in range(width // 128):
        at = slice(128 * p, 128 * p + 128)
        query, keys, values = (held[0, :, at], held[1, :, at], held[2, :, at])
        parts = []
        for side in range(2):
            own = jnp.where(left == (side == 0), query, jnp.zeros_like(query))
            scores = times_turned(own, keys) * HD ** (-0.5)
            scores = jnp.where(allowed[...] > 0, scores, NEGATIVE_FILL)
            power = jnp.exp(scores - jnp.max(scores, axis=1, keepdims=True))
            power = power / jnp.sum(power, axis=1, keepdims=True)
            probs[2 * p + side] = power
            parts.append(matmul(power.astype(BF), values))
        held[3, :, at] = jnp.where(left, parts[0], parts[1]).astype(BF)
        yield
    out[...] = start[...] + matmul(held[3], mix())
    yield


def attention_back_steps(start, gain, angles, weights, mix, held, probs, grad_mid, put, out, gains):
    length, width = start.shape
    low, left = (low_quarters(length), left_half(length))
    back = grad_mid[...].astype(BF)
    put(3, turned_times(held[3], back))
    grad_out = times_turned(back, mix()).astype(BF)
    yield
    grads = [[], [], []]
    for p in range(width // 128):
        at = slice(128 * p, 128 * p + 128)
        query, keys, values, grad = (held[0, :, at], held[1, :, at], held[2, :, at], grad_out[:, at])
        parts = []
        for side in range(2):
            own = jnp.where(left == (side == 0), grad, jnp.zeros_like(grad))
            grad_probs = times_turned(own, values)
            power = probs[2 * p + side]
            inner = jnp.sum(power * grad_probs, axis=1, keepdims=True)
            score = (power * (grad_probs - inner)).astype(BF)
            parts.append(
                (
                    matmul(score, keys) * HD ** (-0.5),
                    turned_times(score, query) * HD ** (-0.5),
                    turned_times(power.astype(BF), grad),
                )
            )
        for k in range(3):
            value = jnp.where(left, parts[0][k], parts[1][k]).astype(BF)
            if k < 2:
                value = value.astype(F32)
                value = (value * angles[0] - turned(value * angles[1], low)).astype(BF)
            grads[k].append(value)
        yield
    gain_row = gain[0:1]
    normed_gain, normed, inverse = norm_forward(start[...], gain_row)
    normed_gain = normed_gain.astype(BF)
    total = jnp.zeros((length, width), F32)
    for k in range(3):
        grad = jnp.concatenate(grads[k], axis=1)
        put(k, turned_times(normed_gain, grad))
        total = total + times_turned(grad, weights(k))
        yield
    grad, gain_grad = norm_backward(total, normed, inverse, gain_row)
    gains[0:1] = gain_grad.reshape(1, width)
    out[...] = grad_mid[...] + grad
    yield


def local_call(kernel, outs, args, scratch, name, flops, spaces=None):
    spaces = [VMEM] * len(args) if spaces is None else spaces
    return pl.pallas_call(
        kernel,
        out_shape=outs,
        in_specs=spaces,
        out_specs=[VMEM] * len(outs),
        scratch_shapes=scratch,
        compiler_params=pltpu.CompilerParams(vmem_limit_bytes=60 * 2**20),
        cost_estimate=pl.CostEstimate(flops=flops, bytes_accessed=2**24, transcendentals=0),
        name=name,
    )(*args)


def attention_forward(start, gain, angles, allowed, qkv_w, mix_w):
    length, width = start.shape

    def kernel(start, gain, angles, allowed, qkv, mix, held, probs, out):
        def weights(k):
            return qkv[:, width * k : width * (k + 1)]

        drain(attention_steps(start, gain, angles, allowed, weights, lambda: mix[...], held, probs, out))

    outs = [
        shape((4, length, width), BF),
        shape((width // HD, length, length), F32),
        shape((length, width), F32),
    ]
    args = (start, gain, angles, allowed, qkv_w, mix_w)
    return local_call(kernel, outs, args, [], "attention_forward", 2**31)


def feed_back_steps(grad_top, final, middle, both, gain, expand, shrink, grad_expand, grad_shrink, out, gains):
    length, width = middle.shape
    inner = shrink.shape[0]
    _, normed, inverse = norm_forward(final[...], gain[2:3])
    grad_final, gain_top = norm_backward(grad_top[...], normed, inverse, gain[2:3])
    back = grad_final.astype(BF)
    low, normed, inverse = norm_forward(middle[...], gain[1:2])
    low = low.astype(BF)
    total = jnp.zeros((length, width), F32)
    for k in range(inner // PIECE):
        at = slice(PIECE * k, PIECE * (k + 1))
        up_at = slice(inner + PIECE * k, inner + PIECE * (k + 1))
        gate, up = (both[:, at], both[:, up_at])
        sigma = jax.nn.sigmoid(gate)
        hidden = (gate * sigma * up).astype(BF)
        grad_shrink[at] = turned_times(hidden, back).astype(BF)
        grad = times_turned(back, shrink[at])
        grad_gate = (grad * up * sigma * (1.0 + gate * (1.0 - sigma))).astype(BF)
        grad_up = (grad * gate * sigma).astype(BF)
        grad_expand[:, at] = turned_times(low, grad_gate).astype(BF)
        grad_expand[:, up_at] = turned_times(low, grad_up).astype(BF)
        total = total + times_turned(grad_gate, expand[:, at])
        total = total + times_turned(grad_up, expand[:, up_at])
        yield
    grad_middle, gain_two = norm_backward(total, normed, inverse, gain[1:2])
    out[...] = grad_final + grad_middle
    gains[...] = jnp.zeros_like(gains)
    gains[1:2] = gain_two.reshape(1, width)
    gains[2:3] = gain_top.reshape(1, width)
    yield


def layer_backward(dims, grad_top, final, middle, both, gain, expand_w, shrink_w, start, angles, attention, head, cid):
    nz, ny, nx = dims
    length, width = middle.shape
    deep, columns = head.shape[2:]
    later = len(attention)

    def kernel(*refs):
        grad_top, final, middle, both, gain, expand, shrink, start, angles, head_in, *rest = refs
        sources, rest = (rest[:later], rest[later:])
        expand_out, shrink_out, grad_qkv, grad_mix, start_out, gains, head_out, *rest = rest
        qkv, mix, held, probs, *rest = rest
        grad_expand, grad_shrink, grad_mid, *rest = rest
        near, mids, fars, (ssem, rsem, lsem) = (rest[0:2], rest[2:4], rest[4:6], rest[6:])
        place = Place(dims)
        y, x = (place.y, place.x)
        comm = Comm(ssem, rsem, lsem)
        loads = [comm.keep(src, dst) for src, dst in zip(sources, (qkv, mix, held, probs))]
        greet(place, [off for off in line_offsets(dims) if off[1] or off[2]])
        parts = (pl.ds(0, deep // 2), pl.ds(deep // 2, deep // 2))
        by_x = [(t, place.xs(nx - t), place.dev(x=t)) for t in range(1, nx)]
        by_y = [(t, place.ys(ny - t), place.dev(y=t)) for t in range(1, ny)]
        came = [comm.send(head_in.at[:, to, parts[0]], near[0].at[t - 1], dev) for t, to, dev in by_x]
        came += [comm.send(head_in.at[to, :, parts[1]], near[1].at[t - 1], dev) for t, to, dev in by_y]
        drain(
            feed_back_steps(
                grad_top, final, middle, both, gain, expand, shrink, grad_expand, grad_shrink, grad_mid, gains
            )
        )
        comm.keep(grad_expand, expand_out)
        comm.keep(grad_shrink, shrink_out)
        for copy in came:
            copy.wait_recv()
        add_blocks(mids[0], [head_in.at[:, x, parts[0]]] + [near[0].at[t] for t in range(nx - 1)])
        add_blocks(mids[1], [head_in.at[y, :, parts[1]]] + [near[1].at[t] for t in range(ny - 1)])
        came = [comm.send(mids[0].at[to], fars[0].at[t - 1], dev) for t, to, dev in by_y]
        came += [comm.send(mids[1].at[to], fars[1].at[t - 1], dev) for t, to, dev in by_x]
        for copy in loads:
            comm.done(copy)

        def weights(k):
            return qkv[:, width * k : width * (k + 1)]

        def put(k, value):
            if k == 3:
                grad_mix[...] = value.astype(BF)
            else:
                grad_qkv[:, width * k : width * (k + 1)] = value.astype(BF)

        drain(
            attention_back_steps(
                start, gain, angles, weights, lambda: mix[...], held, probs, grad_mid, put, start_out, gains
            )
        )
        for copy in came:
            copy.wait_recv()
        for part, mid, far in ((parts[0], mids[0].at[y], fars[0]), (parts[1], mids[1].at[x], fars[1])):
            add_blocks(head_out.at[part], [mid] + [far.at[t] for t in range(far.shape[0])])
        comm.finish()

    count = 2 * (ny + nx)
    half = (deep // 2, columns)
    outs = [
        shape(expand_w.shape, BF),
        shape(shrink_w.shape, BF),
        shape(attention[0].shape, BF),
        shape(attention[1].shape, BF),
        shape((length, width), F32),
        shape((8, width), F32),
        shape(head.shape[2:], F32),
    ]
    scratch = [pltpu.VMEM(v.shape, v.dtype) for v in attention]
    scratch += [pltpu.VMEM(expand_w.shape, BF), pltpu.VMEM(shrink_w.shape, BF)]
    scratch += [
        pltpu.VMEM((length, width), F32),
        pltpu.VMEM((nx - 1, ny) + half, BF),
        pltpu.VMEM((ny - 1, nx) + half, BF),
        pltpu.VMEM((ny,) + half, BF),
        pltpu.VMEM((nx,) + half, BF),
        pltpu.VMEM((ny - 1,) + half, BF),
        pltpu.VMEM((nx - 1,) + half, BF),
        sems(count),
        sems(count),
        sems(later + 2),
    ]
    args = (grad_top, final, middle, both, gain, expand_w, shrink_w, start, angles, head, *attention)
    return call(
        kernel, outs, [VMEM] * 10 + [ANY] * later, [ANY] * 2 + [VMEM] * 5, scratch,
        cid, "layer_backward", args, 60 * 2**20,
    )


def rope_tables(length, width):
    quarter = width // 4
    places = np.arange(length)
    freq = np.float32(10000.0) ** (-np.arange(quarter, dtype=np.float32) / np.float32(quarter))
    row_angle = (places // GRID).astype(np.float32)[:, None] * freq
    col_angle = (places % GRID).astype(np.float32)[:, None] * freq
    angles = np.concatenate([row_angle, row_angle, col_angle, col_angle] * (128 // width), axis=-1)
    return jnp.asarray(np.stack([np.cos(angles), np.sin(angles)]).astype(np.float32))


def adam_update(master, drift, square, grad, rate, decay):
    moment = BETA_ONE * drift + (1.0 - BETA_ONE) * grad
    second = BETA_TWO * square + (1.0 - BETA_TWO) * grad * grad
    stride = (
        moment / (1.0 - BETA_ONE**STEP) / (jnp.sqrt(second / (1.0 - BETA_TWO**STEP)) + ADAM_EPS)
    )
    return (master - rate * (stride + decay * master), moment, second)


def adam_all(masters, drifts, squares, grads, sums, rates, decays):
    n = len(masters)
    pieces = []
    for i, master in enumerate(masters):
        rows = master.shape[0]
        cut = rows // 4 if rows % 32 == 0 and rows >= 256 else rows
        pieces += [(i, k, min(cut, rows)) for k in range(0, rows, cut)]

    def kernel(*refs):
        ins = [refs[n * k : n * (k + 1)] for k in range(4)]
        sums_in = refs[4 * n]
        outs = [refs[4 * n + 1 + n * k : 4 * n + 1 + n * (k + 1)] for k in range(3)]
        sums_out = refs[7 * n + 1 : 7 * n + 4]
        rest = refs[7 * n + 4 :]
        held = [rest[n * k : n * (k + 1)] for k in range(4)]
        in_sems, out_sems = rest[4 * n :]
        loads, stores = ([], [])
        for p, (i, at, size) in enumerate(pieces):
            span = pl.ds(at, size)
            loads.append(
                [
                    pltpu.make_async_copy(ins[k][i].at[span], held[k][i].at[span], in_sems.at[p, k])
                    for k in range(4)
                ]
            )
        ahead = 3
        for p in range(ahead):
            for copy in loads[p]:
                copy.start()
        row = sums_in[0:1]
        norm = jnp.sqrt(row[:, 0:1]) / row[:, 2:3]
        factor = CLIP_NORM / jnp.maximum(norm, CLIP_NORM) / row[:, 2:3]
        for out, value in zip(sums_out, (norm, row[:, 1:2], row[:, 2:3])):
            out[...] = value

        def update(i, span):
            fresh, moment, second = adam_update(
                held[0][i][span],
                held[1][i][span],
                held[2][i][span],
                held[3][i][span] * factor,
                rates[i],
                decays[i],
            )
            held[0][i][span], held[1][i][span], held[2][i][span] = (fresh, moment, second)

        for p, (i, at, size) in enumerate(pieces):
            for copy in loads[p]:
                copy.wait()
            if p + ahead < len(pieces):
                for copy in loads[p + ahead]:
                    copy.start()
            strip = 32 if size % 32 == 0 else 8
            if size % strip:
                update(i, slice(at, at + size))
            else:

                @pl.loop(0, size // strip)
                def _(k, i=i, at=at, strip=strip):
                    update(i, pl.ds(pl.multiple_of(at + strip * k, strip), strip))

            span = pl.ds(at, size)
            for k in range(3):
                copy = pltpu.make_async_copy(held[k][i].at[span], outs[k][i].at[span], out_sems.at[p, k])
                copy.start()
                stores.append(copy)
        for copy in stores:
            copy.wait()

    return pl.pallas_call(
        kernel,
        out_shape=[shape(v.shape, F32) for v in masters] * 3 + [shape((1, 1), F32)] * 3,
        in_specs=[ANY] * (4 * n) + [VMEM],
        out_specs=[ANY] * (3 * n) + [VMEM] * 3,
        scratch_shapes=[pltpu.VMEM(v.shape, F32) for v in masters] * 4
        + [pltpu.SemaphoreType.DMA((len(pieces), 4)), pltpu.SemaphoreType.DMA((len(pieces), 3))],
        compiler_params=pltpu.CompilerParams(vmem_limit_bytes=62 * 2**20),
        name="adam_all",
    )(*masters, *drifts, *squares, *grads, sums)


def block_form(rows, columns):
    return (rows, columns) if rows % 8 == 0 else (rows * columns // 128, 128)


FIRST_AXES = ("x", "x", "y", "x")


def on_device(dims, *args):
    labels, targets, heights, loss_mask = args[:4]
    masters, drifts, squares = (args[4:12], args[12:20], args[20:28])
    class_table, code_table, attend_in, attend_mix, expand_in, shrink_out, head_weight, norm_gains = masters
    images, local_len = targets.shape
    length = local_len * 2

    layers = (attend_in, attend_mix, expand_in, shrink_out)
    *weights, start, gain, metas, allowed = gather_all(
        dims, layers, FIRST_AXES, code_table, class_table.T, norm_gains, labels, targets, heights, loss_mask, 0
    )
    qkv_w, mix_w, expand_w, shrink_w = (v.reshape(-1, v.shape[-1]) for v in weights)

    angles = rope_tables(length, HD)
    held, probs, middle = attention_forward(start, gain, angles, allowed, qkv_w, mix_w)
    grad_top, grad_head, partial, both, final = head_all(
        dims, middle, gain, metas, head_weight, expand_w, shrink_w, images, 2
    )
    grad_expand, grad_shrink, grad_qkv, grad_mix, grad_start, gain_grads, grad_head = layer_backward(
        dims, grad_top, final, middle, both, gain, expand_w, shrink_w, start, angles,
        (qkv_w, mix_w, held, probs), grad_head, 3,
    )

    grads_in = []
    for grad, shard in zip((grad_qkv, grad_mix, grad_expand, grad_shrink), layers):
        grads_in.append(grad.reshape(dims + (2,) + block_form(*shard.shape)))
    *layer_shares, code_share, class_share, gain_share, sums = scatter_all(
        dims,
        grads_in,
        FIRST_AXES,
        grad_start,
        gain_grads,
        metas,
        grad_head,
        partial,
        code_table.shape[0],
        class_table.shape[0],
        4,
    )
    layer_shares = [g.reshape(v.shape) for g, v in zip(layer_shares, layers)]
    shares = (class_share, code_share, *layer_shares, grad_head, gain_share)

    def laid(members):
        return (members[0].T, *members[1:])

    updated = adam_all(laid(masters), laid(drifts), laid(squares), shares, sums, RATES, DECAYS)
    sums = updated[24:]
    updated = tuple(member for k in range(3) for member in laid(updated[8 * k : 8 * k + 8]))
    return updated + tuple(member.reshape(()) for member in sums)


def solution(mesh):
    rows, columns = (P(("dp", "seq"), None), P(None, ("dp", "seq")))
    eight = (columns, rows, rows, rows, rows, rows, columns, columns)
    return jax.shard_map(
        functools.partial(on_device, dims_of(mesh.shape["dp"])),
        mesh=mesh,
        in_specs=(P("dp"), P("dp", "seq"), P("dp"), P("dp", "seq")) + eight * 3,
        out_specs=eight * 3 + (P(), P(), P()),
        check_vma=False,
    )
```
